32 devices in a mesh: dp: 16 (over z, x, core), seq: 2 (over y).
Axes of the slice: x: 2, y: 2, z: 4, core: 2. Of those that a mesh axis runs over, the one named last changes fastest.
Arguments:
- tokens: bfloat16 [32, 1024, 1024], P('dp', 'seq'), may hold values from -6 to 6
- text_states: bfloat16 [32, 256, 1024], P('dp', 'seq'), may hold values from -6 to 6
- unit_length: int32 [32], P('dp'), may hold values from 512 to 1024, as said below
- text_length: int32 [32], P('dp'), may hold values from 64 to 256, as said below
- cotangent: bfloat16 [32, 1024, 1024], P('dp', 'seq'), may hold values from -6 to 6
- attn_gain: bfloat16 [1024], P(('dp', 'seq')), may hold values from 0.5 to 1.5
- attn_shift: bfloat16 [1024], P(('dp', 'seq')), may hold values from -1 to 1
- attn_inputs: bfloat16 [1024, 3072], P(('dp', 'seq')), may hold values from -0.1875 to 0.1875
- attn_qbias: bfloat16 [1024], P(('dp', 'seq')), may hold values from -1 to 1
- attn_vbias: bfloat16 [1024], P(('dp', 'seq')), may hold values from -1 to 1
- attn_output: bfloat16 [1024, 1024], P(('dp', 'seq')), may hold values from -0.75 to 0.75
- attn_obias: bfloat16 [1024], P(('dp', 'seq')), may hold values from -1 to 1
- cross_gain: bfloat16 [1024], P(('dp', 'seq')), may hold values from 0.5 to 1.5
- cross_shift: bfloat16 [1024], P(('dp', 'seq')), may hold values from -1 to 1
- cross_query: bfloat16 [1024, 1024], P(('dp', 'seq')), may hold values from -0.1875 to 0.1875
- cross_qbias: bfloat16 [1024], P(('dp', 'seq')), may hold values from -1 to 1
- cross_keyval: bfloat16 [1024, 2048], P(('dp', 'seq')), may hold values from -0.1875 to 0.1875
- cross_vbias: bfloat16 [1024], P(('dp', 'seq')), may hold values from -1 to 1
- cross_output: bfloat16 [1024, 1024], P(('dp', 'seq')), may hold values from -0.375 to 0.375
- cross_obias: bfloat16 [1024], P(('dp', 'seq')), may hold values from -1 to 1
- ffn_gain: bfloat16 [1024], P(('dp', 'seq')), may hold values from 0.5 to 1.5
- ffn_shift: bfloat16 [1024], P(('dp', 'seq')), may hold values from -1 to 1
- ffn_up: bfloat16 [1024, 4096], P(('dp', 'seq')), may hold values from -0.1875 to 0.1875
- ffn_upbias: bfloat16 [4096], P(('dp', 'seq')), may hold values from -1 to 1
- ffn_down: bfloat16 [4096, 1024], P(('dp', 'seq')), may hold values from -0.125 to 0.125
- ffn_downbias: bfloat16 [1024], P(('dp', 'seq')), may hold values from -1 to 1
- final_gain: bfloat16 [1024], P(('dp', 'seq')), may hold values from 0.5 to 1.5
- final_shift: bfloat16 [1024], P(('dp', 'seq')), may hold values from -1 to 1
Outputs:
- layer_out: bfloat16 [32, 1024, 1024], P('dp', 'seq')
- tokens_grad: bfloat16 [32, 1024, 1024], P('dp', 'seq')
- text_grad: bfloat16 [32, 256, 1024], P('dp', 'seq')
- grad_attn_gain: float32 [1024], P(('dp', 'seq'))
- grad_attn_shift: float32 [1024], P(('dp', 'seq'))
- grad_attn_inputs: float32 [1024, 3072], P(('dp', 'seq'))
- grad_attn_qbias: float32 [1024], P(('dp', 'seq'))
- grad_attn_vbias: float32 [1024], P(('dp', 'seq'))
- grad_attn_output: float32 [1024, 1024], P(('dp', 'seq'))
- grad_attn_obias: float32 [1024], P(('dp', 'seq'))
- grad_cross_gain: float32 [1024], P(('dp', 'seq'))
- grad_cross_shift: float32 [1024], P(('dp', 'seq'))
- grad_cross_query: float32 [1024, 1024], P(('dp', 'seq'))
- grad_cross_qbias: float32 [1024], P(('dp', 'seq'))
- grad_cross_keyval: float32 [1024, 2048], P(('dp', 'seq'))
- grad_cross_vbias: float32 [1024], P(('dp', 'seq'))
- grad_cross_output: float32 [1024, 1024], P(('dp', 'seq'))
- grad_cross_obias: float32 [1024], P(('dp', 'seq'))
- grad_ffn_gain: float32 [1024], P(('dp', 'seq'))
- grad_ffn_shift: float32 [1024], P(('dp', 'seq'))
- grad_ffn_up: float32 [1024, 4096], P(('dp', 'seq'))
- grad_ffn_upbias: float32 [4096], P(('dp', 'seq'))
- grad_ffn_down: float32 [4096, 1024], P(('dp', 'seq'))
- grad_ffn_downbias: float32 [1024], P(('dp', 'seq'))
- grad_final_gain: float32 [1024], P(('dp', 'seq'))
- grad_final_shift: float32 [1024], P(('dp', 'seq'))
The draws below stay inside these ranges and needn't reach their ends.
Inputs may be any that keep to these rules, and one draw needn't show every extreme that they name: `unit_length`: each is 512, 768 or 1024; among the 2 sequences of each index of dp one has 1024 and another 1024//2. `text_length`: some sequence has 256 and another 256//4.
All inputs are finite; a program needn't handle non-finite values.
Results may differ from the reference program's by a relative error of at most 0.035.
Values may be sent and summed in bfloat16 or wider, within the bound.
A program may use at most 320 MiB of HBM per device.

```python
import math
import jax
import jax.numpy as jnp
from jax import lax

D = 1024
FF = 4096
HEADS = 16
HEAD_DIM = 64
TXT = 256
LEN = 1024
SEQS = 2
SEQ_ALL = 32


def draw_unit_length(key, part):
    key = jax.random.fold_in(key, 11)
    key_values, key_pick = jax.random.split(key)
    group_count = SEQ_ALL // SEQS
    lengths = jax.random.randint(key_values, (group_count, SEQS), 2, 5) * (LEN // 4)
    chosen = jax.random.randint(key_pick, (group_count, 1), 0, SEQS)
    slot_index = jnp.arange(SEQS)[None, :]
    lengths = jnp.where(slot_index == (chosen + 1) % SEQS, LEN // 2, lengths)
    lengths = jnp.where(slot_index == chosen, LEN, lengths)
    return lengths.reshape(SEQ_ALL).astype(jnp.int32)


def draw_text_length(key, part):
    key = jax.random.fold_in(key, 23)
    key_values, key_pick = jax.random.split(key)
    lengths = jax.random.randint(key_values, (SEQ_ALL,), TXT // 4, TXT + 1)
    chosen = jax.random.randint(key_pick, (), 0, SEQ_ALL)
    slot_index = jnp.arange(SEQ_ALL)
    lengths = jnp.where(slot_index == (chosen + 1) % SEQ_ALL, TXT // 4, lengths)
    lengths = jnp.where(slot_index == chosen, TXT, lengths)
    return lengths.astype(jnp.int32)


def shard_levels(rng, dims, pieces, low, largest):
    def one(position, parts):
        heights = jax.random.uniform(jax.random.fold_in(jax.random.fold_in(rng, 6), position), (parts,), jnp.float32, low / len(pieces), largest / len(pieces))
        return jnp.repeat(jnp.exp(heights), dims[position] // parts).reshape((-1,) + (1,) * (len(dims) - position - 1))

    level = one(*pieces[0])
    for cut in pieces[1:]:
        level = level * one(*cut)
    return level


def bell_draw(rng, shape, width, most, shards=(), kind=jnp.bfloat16):
    entries = jax.random.normal(rng, shape, jnp.float32) * width
    if len(shards) > 0:
        entries = shard_levels(rng, shape, shards, -0.22, 0.18) * entries
    return jnp.clip(entries, min=-most, max=most).astype(kind)


def setup_inputs(seed: int = 0) -> dict:
    key_list = jax.random.split(jax.random.key(seed), 29)
    tokens = bell_draw(key_list[0], (SEQ_ALL, LEN, D), 1.0, 6.0, ((0, 16), (1, 2)))
    text_states = bell_draw(key_list[1], (SEQ_ALL, TXT, D), 1.0, 6.0, ((0, 16), (1, 2)))
    unit_length = draw_unit_length(jax.random.fold_in(key_list[28], 71), 0)
    text_length = draw_text_length(jax.random.fold_in(key_list[28], 71), 0)
    cotangent = bell_draw(key_list[4], (SEQ_ALL, LEN, D), 1.0, 6.0, ((0, 16), (1, 2)))
    attn_gain = jnp.clip(1.0 + 0.1 * jax.random.normal(key_list[5], (D,), jnp.float32), 0.5, 1.5).astype(jnp.bfloat16)
    attn_shift = bell_draw(key_list[6], (D,), 0.2, 1.0, ((0, 32),))
    attn_inputs = bell_draw(key_list[7], (D, 3 * D), D ** -0.5, 0.1875, ((0, 32),))
    attn_qbias = bell_draw(key_list[8], (D,), 0.2, 1.0, ((0, 32),))
    attn_vbias = bell_draw(key_list[9], (D,), 0.2, 1.0, ((0, 32),))
    attn_output = bell_draw(key_list[10], (D, D), (D // 16) ** -0.5, 0.75, ((0, 32),))
    attn_obias = bell_draw(key_list[11], (D,), 0.2, 1.0, ((0, 32),))
    cross_gain = jnp.clip(1.0 + 0.1 * jax.random.normal(key_list[12], (D,), jnp.float32), 0.5, 1.5).astype(jnp.bfloat16)
    cross_shift = bell_draw(key_list[13], (D,), 0.2, 1.0, ((0, 32),))
    cross_query = bell_draw(key_list[14], (D, D), D ** -0.5, 0.1875, ((0, 32),))
    cross_qbias = bell_draw(key_list[15], (D,), 0.2, 1.0, ((0, 32),))
    cross_keyval = bell_draw(key_list[16], (D, 2 * D), D ** -0.5, 0.1875, ((0, 32),))
    cross_vbias = bell_draw(key_list[17], (D,), 0.2, 1.0, ((0, 32),))
    cross_output = bell_draw(key_list[18], (D, D), (D // 4) ** -0.5, 0.375, ((0, 32),))
    cross_obias = bell_draw(key_list[19], (D,), 0.2, 1.0, ((0, 32),))
    ffn_gain = jnp.clip(1.0 + 0.1 * jax.random.normal(key_list[20], (D,), jnp.float32), 0.5, 1.5).astype(jnp.bfloat16)
    ffn_shift = bell_draw(key_list[21], (D,), 0.2, 1.0, ((0, 32),))
    ffn_up = bell_draw(key_list[22], (D, FF), D ** -0.5, 0.1875, ((0, 32),))
    ffn_upbias = bell_draw(key_list[23], (FF,), 0.2, 1.0, ((0, 32),))
    ffn_down = bell_draw(key_list[24], (FF, D), (FF // 2) ** -0.5, 0.125, ((0, 32),))
    ffn_downbias = bell_draw(key_list[25], (D,), 0.2, 1.0, ((0, 32),))
    final_gain = jnp.clip(1.0 + 0.1 * jax.random.normal(key_list[26], (D,), jnp.float32), 0.5, 1.5).astype(jnp.bfloat16)
    final_shift = bell_draw(key_list[27], (D,), 0.2, 1.0, ((0, 32),))
    return {"tokens": tokens, "text_states": text_states, "unit_length": unit_length, "text_length": text_length, "cotangent": cotangent, "attn_gain": attn_gain, "attn_shift": attn_shift, "attn_inputs": attn_inputs, "attn_qbias": attn_qbias, "attn_vbias": attn_vbias, "attn_output": attn_output, "attn_obias": attn_obias, "cross_gain": cross_gain, "cross_shift": cross_shift, "cross_query": cross_query, "cross_qbias": cross_qbias, "cross_keyval": cross_keyval, "cross_vbias": cross_vbias, "cross_output": cross_output, "cross_obias": cross_obias, "ffn_gain": ffn_gain, "ffn_shift": ffn_shift, "ffn_up": ffn_up, "ffn_upbias": ffn_upbias, "ffn_down": ffn_down, "ffn_downbias": ffn_downbias, "final_gain": final_gain, "final_shift": final_shift}


EPSILON = 1e-05
PRECISE = lax.Precision.HIGHEST

@jax.custom_vjp
def low(v):
    return lax.optimization_barrier(v.astype(jnp.bfloat16)).astype(jnp.float32)

@jax.custom_vjp
def low_back(v):
    return v

def low_keep(v):
    return (low(v), None)

def low_pass(kept, grad):
    return (grad,)

def back_keep(v):
    return (v, None)

def back_low(kept, grad):
    return (low(grad),)
low.defvjp(low_keep, low_pass)
low_back.defvjp(back_keep, back_low)

def layer_norm(values, norm_gain, norm_shift):
    center = values - lax.optimization_barrier(jnp.mean(values, axis=-1, keepdims=True))
    spread = lax.optimization_barrier(jnp.mean(center * center, axis=-1, keepdims=True))
    return center * lax.rsqrt(spread + EPSILON) * norm_gain + norm_shift

def matmul(left_side, right_side):
    return jnp.dot(left_side, right_side, precision=PRECISE)

def heads_view(matrix):
    return matrix.reshape(matrix.shape[0], HEADS, HEAD_DIM)

def attend(queries, key_rows, value_rows, allowed):
    score_scale = 1.0 / math.sqrt(HEAD_DIM)
    scores = jnp.einsum('qhd,khd->hqk', heads_view(queries), heads_view(key_rows), precision=PRECISE) * score_scale
    scores = low_back(scores)
    scores = jnp.where(allowed[None], scores, -1e+30)
    row_max = lax.optimization_barrier(jnp.max(scores, axis=-1, keepdims=True))
    weights = jnp.exp(scores - row_max)
    weights = low(weights / lax.optimization_barrier(jnp.sum(weights, axis=-1, keepdims=True)))
    mixed_rows = jnp.einsum('hqk,khd->qhd', weights, heads_view(value_rows), precision=PRECISE)
    return low(low_back(mixed_rows.reshape(queries.shape[0], D)))

def sequence_layer(params, token_seq, text_seq, unit_count, text_count):
    a_gain, a_shift, a_inputs, a_qbias, a_vbias, a_output, a_obias, c_gain, c_shift, c_query, c_qbias, c_keyval, c_vbias, c_output, c_obias, f_gain, f_shift, f_up, f_upbias, f_down, f_downbias, z_gain, z_shift = params
    zero_bias = jnp.zeros((D,), jnp.float32)
    positions = jnp.arange(LEN)
    normed = low(layer_norm(token_seq, a_gain, a_shift))
    joined = matmul(normed, a_inputs) + jnp.concatenate([a_qbias, zero_bias, a_vbias])
    joined = low(low_back(joined))
    causal = positions[None, :] <= positions[:, None]
    self_mixed = attend(joined[:, :D], joined[:, D:2 * D], joined[:, 2 * D:], causal)
    after_self = token_seq + low_back(matmul(self_mixed, a_output) + a_obias)
    normed = low(layer_norm(after_self, c_gain, c_shift))
    cross_q = low(low_back(matmul(normed, c_query) + c_qbias))
    cross_kv = low(low_back(matmul(text_seq, c_keyval) + jnp.concatenate([zero_bias, c_vbias])))
    text_allowed = jnp.broadcast_to((jnp.arange(TXT) < text_count)[None, :], (LEN, TXT))
    cross_blended_rows = attend(cross_q, cross_kv[:, :D], cross_kv[:, D:], text_allowed)
    after_cross = after_self + low_back(matmul(cross_blended_rows, c_output) + c_obias)
    normed = low(layer_norm(after_cross, f_gain, f_shift))
    ffn_inner = low_back(matmul(normed, f_up) + f_upbias)
    active = low(jax.nn.gelu(ffn_inner))
    after_ffn = after_cross + low_back(matmul(active, f_down) + f_downbias)
    valid_rows = (positions < unit_count).astype(jnp.float32)[:, None]
    return layer_norm(after_ffn, z_gain, z_shift) * valid_rows

def reference(tokens, text_states, unit_length, text_length, cotangent, attn_gain, attn_shift, attn_inputs, attn_qbias, attn_vbias, attn_output, attn_obias, cross_gain, cross_shift, cross_query, cross_qbias, cross_keyval, cross_vbias, cross_output, cross_obias, ffn_gain, ffn_shift, ffn_up, ffn_upbias, ffn_down, ffn_downbias, final_gain, final_shift):
    weights_in = (attn_gain, attn_shift, attn_inputs, attn_qbias, attn_vbias, attn_output, attn_obias, cross_gain, cross_shift, cross_query, cross_qbias, cross_keyval, cross_vbias, cross_output, cross_obias, ffn_gain, ffn_shift, ffn_up, ffn_upbias, ffn_down, ffn_downbias, final_gain, final_shift)
    params = tuple((weight_item.astype(jnp.float32) for weight_item in weights_in))

    def forward(token_values, text_values, param_values):

        def one_sequence(packed):
            return sequence_layer(param_values, packed[0], packed[1], packed[2], packed[3])
        return lax.map(jax.checkpoint(one_sequence), (token_values, text_values, unit_length, text_length))
    layer_out, pullback = jax.vjp(forward, tokens.astype(jnp.float32), text_states.astype(jnp.float32), params)
    grad_tokens, grad_text, weight_grads = pullback(cotangent.astype(jnp.float32))
    return (layer_out.astype(jnp.bfloat16), grad_tokens.astype(jnp.bfloat16), grad_text.astype(jnp.bfloat16), weight_grads[0], weight_grads[1], weight_grads[2], weight_grads[3], weight_grads[4], weight_grads[5], weight_grads[6], weight_grads[7], weight_grads[8], weight_grads[9], weight_grads[10], weight_grads[11], weight_grads[12], weight_grads[13], weight_grads[14], weight_grads[15], weight_grads[16], weight_grads[17], weight_grads[18], weight_grads[19], weight_grads[20], weight_grads[21], weight_grads[22])
```

```python
import functools
import math

import jax
import jax.numpy as jnp
from jax import lax
from jax.experimental import pallas as pl
from jax.experimental.pallas import tpu as pltpu
from jax.sharding import PartitionSpec as P

HEADS = 16
HEAD_DIM = 64


EPSILON = 1e-05
MASKED = -1e30


def layer_norm(values, norm_gain, norm_shift):
    center = values - jnp.mean(values, axis=-1, keepdims=True)
    spread = jnp.mean(center * center, axis=-1, keepdims=True)
    return center * lax.rsqrt(spread + EPSILON) * norm_gain + norm_shift


def norm_back(values, norm_gain, norm_shift, upstream):
    result, pullback = jax.vjp(layer_norm, values, norm_gain, norm_shift)
    return pullback(upstream)


def rows_dot(left_side, right_side):
    return jnp.dot(left_side, right_side, preferred_element_type=jnp.float32)


def left_dot(left_side, right_side):
    return lax.dot_general(
        left_side, right_side, (((0,), (0,)), ((), ())), preferred_element_type=jnp.float32
    )


def right_dot(left_side, right_side):
    return lax.dot_general(
        left_side, right_side, (((1,), (1,)), ((), ())), preferred_element_type=jnp.float32
    )


def heads_of(matrix):
    return matrix.reshape(matrix.shape[0], HEADS, HEAD_DIM)


def attend_forward(queries, key_rows, value_rows, allowed):
    score_scale = 1.0 / math.sqrt(HEAD_DIM)
    scores = (
        jnp.einsum(
            "qhd,khd->hqk",
            heads_of(queries),
            heads_of(key_rows),
            preferred_element_type=jnp.float32,
        )
        * score_scale
    )
    scores = jnp.where(allowed[None], scores, MASKED)
    row_max = jnp.max(scores, axis=-1, keepdims=True)
    weights = jnp.exp(scores - row_max)
    row_total = jnp.sum(weights, axis=-1, keepdims=True)
    weights = (weights / row_total).astype(jnp.bfloat16)
    mixed_rows = jnp.einsum(
        "hqk,khd->qhd", weights, heads_of(value_rows), preferred_element_type=jnp.float32
    )
    logsum = (row_max + jnp.log(row_total))[..., 0]
    return (mixed_rows.reshape(queries.shape[0], -1).astype(jnp.bfloat16), logsum)


def attend_back(queries, key_rows, value_rows, allowed, logsum, upstream):
    score_scale = 1.0 / math.sqrt(HEAD_DIM)
    query_heads = heads_of(queries)
    key_heads = heads_of(key_rows)
    upstream_heads = heads_of(upstream)
    scores = (
        jnp.einsum("qhd,khd->hqk", query_heads, key_heads, preferred_element_type=jnp.float32)
        * score_scale
    )
    scores = jnp.where(allowed[None], scores, MASKED)
    weights = jnp.exp(scores - logsum[..., None])
    grad_weights = jnp.einsum(
        "qhd,khd->hqk", upstream_heads, heads_of(value_rows), preferred_element_type=jnp.float32
    )
    row_delta = jnp.sum(weights * grad_weights, axis=-1, keepdims=True)
    grad_scores = (weights * (grad_weights - row_delta)).astype(jnp.bfloat16)
    grad_query = (
        jnp.einsum("hqk,khd->qhd", grad_scores, key_heads, preferred_element_type=jnp.float32)
        * score_scale
    )
    grad_key = (
        jnp.einsum("hqk,qhd->khd", grad_scores, query_heads, preferred_element_type=jnp.float32)
        * score_scale
    )
    grad_value = jnp.einsum(
        "hqk,qhd->khd",
        weights.astype(jnp.bfloat16),
        upstream_heads,
        preferred_element_type=jnp.float32,
    )
    key_count = key_rows.shape[0]
    return (
        grad_query.reshape(queries.shape[0], -1),
        grad_key.reshape(key_count, -1),
        grad_value.reshape(key_count, -1),
    )


def to_float(values):
    return values.astype(jnp.float32)


def on_device(
    tokens,
    text_states,
    unit_length,
    text_length,
    cotangent,
    attn_gain,
    attn_shift,
    attn_inputs,
    attn_qbias,
    attn_vbias,
    attn_output,
    attn_obias,
    cross_gain,
    cross_shift,
    cross_query,
    cross_qbias,
    cross_keyval,
    cross_vbias,
    cross_output,
    cross_obias,
    ffn_gain,
    ffn_shift,
    ffn_up,
    ffn_upbias,
    ffn_down,
    ffn_downbias,
    final_gain,
    final_shift,
):
    seq_count, local_len, model_width = tokens.shape
    row_count = seq_count * local_len
    first_pos = lax.axis_index("seq") * local_len
    zero_bias = jnp.zeros((model_width,), jnp.float32)
    (
        a_gain_full,
        a_shift_full,
        attention_input_weight_whole,
        a_qbias_full,
        a_vbias_full,
        a_output_full,
        a_obias_full,
    ) = (
        lax.all_gather(attn_gain, ("dp", "seq"), axis=0, tiled=True),
        lax.all_gather(attn_shift, ("dp", "seq"), axis=0, tiled=True),
        lax.all_gather(attn_inputs, ("dp", "seq"), axis=0, tiled=True),
        lax.all_gather(attn_qbias, ("dp", "seq"), axis=0, tiled=True),
        lax.all_gather(attn_vbias, ("dp", "seq"), axis=0, tiled=True),
        lax.all_gather(attn_output, ("dp", "seq"), axis=0, tiled=True),
        lax.all_gather(attn_obias, ("dp", "seq"), axis=0, tiled=True),
    )
    inputs = to_float(tokens).reshape(row_count, model_width)
    normed_one = layer_norm(inputs, to_float(a_gain_full), to_float(a_shift_full)).astype(
        jnp.bfloat16
    )
    joined = rows_dot(normed_one, attention_input_weight_whole) + jnp.concatenate(
        [to_float(a_qbias_full), zero_bias, to_float(a_vbias_full)]
    )
    joined = joined.astype(jnp.bfloat16)
    self_queries = joined[:, :model_width].reshape(seq_count, local_len, model_width)
    keyval_local = joined[:, model_width:].reshape(seq_count, local_len, 2 * model_width)
    self_keyval = lax.all_gather(keyval_local, "seq", axis=1, tiled=True)
    full_len = self_keyval.shape[1]
    causal = jnp.arange(full_len)[None, :] <= (first_pos + jnp.arange(local_len))[:, None]

    def self_forward(packed):
        seq_queries, seq_keyval = packed
        return attend_forward(
            seq_queries, seq_keyval[:, :model_width], seq_keyval[:, model_width:], causal
        )

    self_mixed, self_logsum = lax.map(self_forward, (self_queries, self_keyval))
    self_flat = self_mixed.reshape(row_count, model_width)
    after_self = inputs + rows_dot(self_flat, a_output_full) + to_float(a_obias_full)
    (
        c_gain_full,
        c_shift_full,
        c_query_full,
        c_qbias_full,
        c_keyval_full,
        cross_value_bias_whole,
        c_output_full,
        c_obias_full,
    ) = (
        lax.all_gather(cross_gain, ("dp", "seq"), axis=0, tiled=True),
        lax.all_gather(cross_shift, ("dp", "seq"), axis=0, tiled=True),
        lax.all_gather(cross_query, ("dp", "seq"), axis=0, tiled=True),
        lax.all_gather(cross_qbias, ("dp", "seq"), axis=0, tiled=True),
        lax.all_gather(cross_keyval, ("dp", "seq"), axis=0, tiled=True),
        lax.all_gather(cross_vbias, ("dp", "seq"), axis=0, tiled=True),
        lax.all_gather(cross_output, ("dp", "seq"), axis=0, tiled=True),
        lax.all_gather(cross_obias, ("dp", "seq"), axis=0, tiled=True),
    )
    normed_two = layer_norm(after_self, to_float(c_gain_full), to_float(c_shift_full)).astype(
        jnp.bfloat16
    )
    cross_queries = (rows_dot(normed_two, c_query_full) + to_float(c_qbias_full)).astype(
        jnp.bfloat16
    )
    cross_queries = cross_queries.reshape(seq_count, local_len, model_width)
    keyval_bias = jnp.concatenate([zero_bias, to_float(cross_value_bias_whole)])
    text_whole = lax.all_gather(text_states, "seq", axis=1, tiled=True)
    cross_kv = (rows_dot(text_whole.reshape(-1, model_width), c_keyval_full) + keyval_bias).astype(
        jnp.bfloat16
    )
    cross_kv = cross_kv.reshape(seq_count, -1, 2 * model_width)
    text_total = cross_kv.shape[1]
    text_allowed = jnp.arange(text_total)[None, :] < text_length[:, None]

    def cross_forward(packed):
        seq_queries, seq_keyval, seq_allowed = packed
        allowed = jnp.broadcast_to(seq_allowed[None, :], (local_len, text_total))
        return attend_forward(
            seq_queries, seq_keyval[:, :model_width], seq_keyval[:, model_width:], allowed
        )

    cross_blended_rows, cross_logsum = lax.map(
        cross_forward, (cross_queries, cross_kv, text_allowed)
    )
    cross_flat = cross_blended_rows.reshape(row_count, model_width)
    after_cross = after_self + rows_dot(cross_flat, c_output_full) + to_float(c_obias_full)
    (
        f_gain_full,
        feedforward_shift_whole,
        f_up_full,
        f_upbias_full,
        f_down_full,
        f_downbias_full,
        z_gain_full,
        z_shift_full,
    ) = (
        lax.all_gather(ffn_gain, ("dp", "seq"), axis=0, tiled=True),
        lax.all_gather(ffn_shift, ("dp", "seq"), axis=0, tiled=True),
        lax.all_gather(ffn_up, ("dp", "seq"), axis=0, tiled=True),
        lax.all_gather(ffn_upbias, ("dp", "seq"), axis=0, tiled=True),
        lax.all_gather(ffn_down, ("dp", "seq"), axis=0, tiled=True),
        lax.all_gather(ffn_downbias, ("dp", "seq"), axis=0, tiled=True),
        lax.all_gather(final_gain, ("dp", "seq"), axis=0, tiled=True),
        lax.all_gather(final_shift, ("dp", "seq"), axis=0, tiled=True),
    )
    normed_three = layer_norm(
        after_cross, to_float(f_gain_full), to_float(feedforward_shift_whole)
    ).astype(jnp.bfloat16)
    ffn_inner = rows_dot(normed_three, f_up_full) + to_float(f_upbias_full)
    active = jax.nn.gelu(ffn_inner).astype(jnp.bfloat16)
    after_ffn = after_cross + rows_dot(active, f_down_full) + to_float(f_downbias_full)
    valid_rows = ((first_pos + jnp.arange(local_len))[None, :] < unit_length[:, None]).astype(
        jnp.float32
    )
    valid_rows = valid_rows.reshape(row_count, 1)
    final_norm = layer_norm(after_ffn, to_float(z_gain_full), to_float(z_shift_full))
    layer_out = (
        (final_norm * valid_rows).astype(jnp.bfloat16).reshape(seq_count, local_len, model_width)
    )
    (
        f_gain_full,
        feedforward_shift_whole,
        f_up_full,
        f_upbias_full,
        f_down_full,
        f_downbias_full,
        z_gain_full,
        z_shift_full,
    ) = (
        lax.all_gather(ffn_gain, ("dp", "seq"), axis=0, tiled=True),
        lax.all_gather(ffn_shift, ("dp", "seq"), axis=0, tiled=True),
        lax.all_gather(ffn_up, ("dp", "seq"), axis=0, tiled=True),
        lax.all_gather(ffn_upbias, ("dp", "seq"), axis=0, tiled=True),
        lax.all_gather(ffn_down, ("dp", "seq"), axis=0, tiled=True),
        lax.all_gather(ffn_downbias, ("dp", "seq"), axis=0, tiled=True),
        lax.all_gather(final_gain, ("dp", "seq"), axis=0, tiled=True),
        lax.all_gather(final_shift, ("dp", "seq"), axis=0, tiled=True),
    )
    upstream = to_float(cotangent).reshape(row_count, model_width) * valid_rows
    grad_after_ffn, grad_zgain, grad_zshift = norm_back(
        after_ffn, to_float(z_gain_full), to_float(z_shift_full), upstream
    )
    grad_branch = grad_after_ffn.astype(jnp.bfloat16)
    grad_down = left_dot(active, grad_branch)
    grad_downbias = jnp.sum(to_float(grad_branch), axis=0)
    grad_active = right_dot(grad_branch, f_down_full)
    inner_value, gelu_back = jax.vjp(jax.nn.gelu, ffn_inner)
    grad_inner = gelu_back(grad_active)[0].astype(jnp.bfloat16)
    grad_up = left_dot(normed_three, grad_inner)
    grad_upbias = jnp.sum(to_float(grad_inner), axis=0)
    grad_normed_three = right_dot(grad_inner, f_up_full)
    grad_cross_norm, grad_fgain, grad_fshift = norm_back(
        after_cross, to_float(f_gain_full), to_float(feedforward_shift_whole), grad_normed_three
    )
    grad_after_cross = grad_after_ffn + grad_cross_norm
    ffn_sums = (
        lax.psum_scatter(grad_fgain, ("dp", "seq"), scatter_dimension=0, tiled=True),
        lax.psum_scatter(grad_fshift, ("dp", "seq"), scatter_dimension=0, tiled=True),
        lax.psum_scatter(grad_up, ("dp", "seq"), scatter_dimension=0, tiled=True),
        lax.psum_scatter(grad_upbias, ("dp", "seq"), scatter_dimension=0, tiled=True),
        lax.psum_scatter(grad_down, ("dp", "seq"), scatter_dimension=0, tiled=True),
        lax.psum_scatter(grad_downbias, ("dp", "seq"), scatter_dimension=0, tiled=True),
        lax.psum_scatter(grad_zgain, ("dp", "seq"), scatter_dimension=0, tiled=True),
        lax.psum_scatter(grad_zshift, ("dp", "seq"), scatter_dimension=0, tiled=True),
    )
    (
        c_gain_full,
        c_shift_full,
        c_query_full,
        c_qbias_full,
        c_keyval_full,
        cross_value_bias_whole,
        c_output_full,
        c_obias_full,
    ) = (
        lax.all_gather(cross_gain, ("dp", "seq"), axis=0, tiled=True),
        lax.all_gather(cross_shift, ("dp", "seq"), axis=0, tiled=True),
        lax.all_gather(cross_query, ("dp", "seq"), axis=0, tiled=True),
        lax.all_gather(cross_qbias, ("dp", "seq"), axis=0, tiled=True),
        lax.all_gather(cross_keyval, ("dp", "seq"), axis=0, tiled=True),
        lax.all_gather(cross_vbias, ("dp", "seq"), axis=0, tiled=True),
        lax.all_gather(cross_output, ("dp", "seq"), axis=0, tiled=True),
        lax.all_gather(cross_obias, ("dp", "seq"), axis=0, tiled=True),
    )
    cross_branch_gradient = grad_after_cross.astype(jnp.bfloat16)
    grad_coutput = left_dot(cross_flat, cross_branch_gradient)
    grad_cobias = jnp.sum(to_float(cross_branch_gradient), axis=0)
    grad_cross_mixed = right_dot(cross_branch_gradient, c_output_full).astype(jnp.bfloat16)
    grad_cross_mixed = grad_cross_mixed.reshape(seq_count, local_len, model_width)

    def cross_backward(packed):
        seq_queries, seq_keyval, seq_allowed, sequence_log_sum_exp, seq_upstream = packed
        allowed = jnp.broadcast_to(seq_allowed[None, :], (local_len, text_total))
        return attend_back(
            seq_queries,
            seq_keyval[:, :model_width],
            seq_keyval[:, model_width:],
            allowed,
            sequence_log_sum_exp,
            seq_upstream,
        )

    grad_cq, grad_ck, grad_cv = lax.map(
        cross_backward, (cross_queries, cross_kv, text_allowed, cross_logsum, grad_cross_mixed)
    )
    grad_ckv = lax.psum_scatter(
        jnp.concatenate([grad_ck, grad_cv], axis=-1).astype(jnp.bfloat16),
        "seq",
        scatter_dimension=1,
        tiled=True,
    ).astype(jnp.float32)
    grad_ckv = grad_ckv.astype(jnp.bfloat16).reshape(-1, 2 * model_width)
    grad_ckeyval = left_dot(text_states.reshape(-1, model_width), grad_ckv)
    grad_cvbias = jnp.sum(to_float(grad_ckv[:, model_width:]), axis=0)
    text_grad = right_dot(grad_ckv, c_keyval_full).astype(jnp.bfloat16).reshape(text_states.shape)
    grad_cq_low = grad_cq.reshape(row_count, model_width).astype(jnp.bfloat16)
    grad_cquery = left_dot(normed_two, grad_cq_low)
    grad_cqbias = jnp.sum(to_float(grad_cq_low), axis=0)
    grad_normed_two = right_dot(grad_cq_low, c_query_full)
    grad_self_norm, grad_cgain, grad_cshift = norm_back(
        after_self, to_float(c_gain_full), to_float(c_shift_full), grad_normed_two
    )
    grad_after_self = grad_after_cross + grad_self_norm
    cross_sums = (
        lax.psum_scatter(grad_cgain, ("dp", "seq"), scatter_dimension=0, tiled=True),
        lax.psum_scatter(grad_cshift, ("dp", "seq"), scatter_dimension=0, tiled=True),
        lax.psum_scatter(grad_cquery, ("dp", "seq"), scatter_dimension=0, tiled=True),
        lax.psum_scatter(grad_cqbias, ("dp", "seq"), scatter_dimension=0, tiled=True),
        lax.psum_scatter(grad_ckeyval, ("dp", "seq"), scatter_dimension=0, tiled=True),
        lax.psum_scatter(grad_cvbias, ("dp", "seq"), scatter_dimension=0, tiled=True),
        lax.psum_scatter(grad_coutput, ("dp", "seq"), scatter_dimension=0, tiled=True),
        lax.psum_scatter(grad_cobias, ("dp", "seq"), scatter_dimension=0, tiled=True),
    )
    (
        a_gain_full,
        a_shift_full,
        attention_input_weight_whole,
        a_qbias_full,
        a_vbias_full,
        a_output_full,
        a_obias_full,
    ) = (
        lax.all_gather(attn_gain, ("dp", "seq"), axis=0, tiled=True),
        lax.all_gather(attn_shift, ("dp", "seq"), axis=0, tiled=True),
        lax.all_gather(attn_inputs, ("dp", "seq"), axis=0, tiled=True),
        lax.all_gather(attn_qbias, ("dp", "seq"), axis=0, tiled=True),
        lax.all_gather(attn_vbias, ("dp", "seq"), axis=0, tiled=True),
        lax.all_gather(attn_output, ("dp", "seq"), axis=0, tiled=True),
        lax.all_gather(attn_obias, ("dp", "seq"), axis=0, tiled=True),
    )
    grad_self_branch = grad_after_self.astype(jnp.bfloat16)
    grad_aoutput = left_dot(self_flat, grad_self_branch)
    grad_aobias = jnp.sum(to_float(grad_self_branch), axis=0)
    grad_self_mixed = right_dot(grad_self_branch, a_output_full).astype(jnp.bfloat16)
    grad_self_mixed = grad_self_mixed.reshape(seq_count, local_len, model_width)

    def self_backward(packed):
        seq_queries, seq_keyval, sequence_log_sum_exp, seq_upstream = packed
        return attend_back(
            seq_queries,
            seq_keyval[:, :model_width],
            seq_keyval[:, model_width:],
            causal,
            sequence_log_sum_exp,
            seq_upstream,
        )

    gradient_self_query, grad_sk, grad_sv = lax.map(
        self_backward, (self_queries, self_keyval, self_logsum, grad_self_mixed)
    )
    gradient_self_keyvalue = lax.psum_scatter(
        jnp.concatenate([grad_sk, grad_sv], axis=-1).astype(jnp.bfloat16),
        "seq",
        scatter_dimension=1,
        tiled=True,
    ).astype(jnp.float32)
    grad_joined = (
        jnp.concatenate([gradient_self_query, gradient_self_keyvalue], axis=-1)
        .reshape(row_count, 3 * model_width)
        .astype(jnp.bfloat16)
    )
    grad_ainputs = left_dot(normed_one, grad_joined)
    grad_aqbias = jnp.sum(to_float(grad_joined[:, :model_width]), axis=0)
    grad_avbias = jnp.sum(to_float(grad_joined[:, 2 * model_width :]), axis=0)
    grad_normed_one = right_dot(grad_joined, attention_input_weight_whole)
    grad_input_norm, grad_again, grad_ashift = norm_back(
        inputs, to_float(a_gain_full), to_float(a_shift_full), grad_normed_one
    )
    tokens_grad = (
        (grad_after_self + grad_input_norm)
        .astype(jnp.bfloat16)
        .reshape(seq_count, local_len, model_width)
    )
    attn_sums = (
        lax.psum_scatter(grad_again, ("dp", "seq"), scatter_dimension=0, tiled=True),
        lax.psum_scatter(grad_ashift, ("dp", "seq"), scatter_dimension=0, tiled=True),
        lax.psum_scatter(grad_ainputs, ("dp", "seq"), scatter_dimension=0, tiled=True),
        lax.psum_scatter(grad_aqbias, ("dp", "seq"), scatter_dimension=0, tiled=True),
        lax.psum_scatter(grad_avbias, ("dp", "seq"), scatter_dimension=0, tiled=True),
        lax.psum_scatter(grad_aoutput, ("dp", "seq"), scatter_dimension=0, tiled=True),
        lax.psum_scatter(grad_aobias, ("dp", "seq"), scatter_dimension=0, tiled=True),
    )
    return (layer_out, tokens_grad, text_grad, *attn_sums, *cross_sums, *ffn_sums)


MESH_ID = pl.DeviceIdType.MESH
ANYWHERE = pl.BlockSpec(memory_space=pl.ANY)
VMEM_LIMIT = 56 * 2**20


class Place:
    def __init__(self, depth):
        group = lax.axis_index("dp")
        self.depth = depth
        self.z = group // 4
        self.x = lax.rem(group // 2, 2)
        self.core = lax.rem(group, 2)
        self.y = lax.axis_index("seq")

    def device(self, z, x, core, y):
        return {"dp": (z * 2 + x) * 2 + core, "seq": y}

    def along_z(self, step):
        return self.device(lax.rem(self.z + step, self.depth), self.x, self.core, self.y)

    def across_x(self):
        return self.device(self.z, 1 - self.x, self.core, self.y)

    def across_y(self):
        return self.device(self.z, self.x, self.core, 1 - self.y)

    def sibling(self):
        return self.device(self.z, self.x, 1 - self.core, self.y)

    def along(self, axis):
        if axis == "z":
            return [self.along_z(step) for step in range(1, self.depth)]
        return [self.across_x() if axis == "x" else self.across_y()]

    def greet(self):
        partners = [self.along_z(step) for step in range(1, self.depth)]
        partners += [self.across_x(), self.across_y(), self.sibling()]
        barrier = pltpu.get_barrier_semaphore()
        for partner in partners:
            pl.semaphore_signal(barrier, inc=1, device_id=partner, device_id_type=MESH_ID)
        pl.semaphore_wait(barrier, len(partners))


def remote(source, target, sems, item, index, device):
    send, receive = sems
    return pltpu.make_async_remote_copy(
        src_ref=source,
        dst_ref=target,
        send_sem=send.at[item, index],
        recv_sem=receive.at[item, index],
        device_id=device,
        device_id_type=MESH_ID,
    )


def pipelined(phase_lists):
    count = max(len(phases) + first for first, phases in enumerate(phase_lists))
    stages = []
    for turn in range(count):
        work = [
            phases[turn - first]
            for first, phases in enumerate(phase_lists)
            if 0 <= turn - first < len(phases)
        ]
        stages.append(work)
    return stages


ORDERS = (("z", "x", "y"), ("z", "y", "x"))


def gather_phases(place, shard, whole, rows, cols, sems, local, stop, item):
    half = rows.size // 2
    halves = (pl.ds(rows.start, half), pl.ds(rows.start + half, half))
    here = {"z": place.z, "x": place.x, "y": place.y}
    every = slice(None)

    def view(done, some_rows, core):
        at = {axis: every if axis in done else here[axis] for axis in here}
        return whole.at[at["z"], at["x"], core, at["y"], some_rows, cols]

    def copies(phase):
        made = []
        if phase == 3:
            both = view("zxy", rows, place.core)
            return [remote(both, both, sems, item, 2 * place.depth + 2, place.sibling())]
        slot = sum(len(place.along(o[p])) for o in ORDERS for p in range(phase))
        for some_rows, order in zip(halves, ORDERS):
            target = view(order[:phase], some_rows, place.core)
            source = shard.at[some_rows, cols] if phase == 0 else target
            for device in place.along(order[phase]):
                made.append(remote(source, target, sems, item, slot, device))
                slot += 1
        return made

    def take():
        return pltpu.make_async_copy(shard.at[rows, cols], stop, local.at[item, 0])

    def put():
        return pltpu.make_async_copy(stop, view("", rows, place.core), local.at[item, 1])

    def start(phase):
        for copy in copies(phase):
            copy.start()

    def wait(phase):
        for copy in copies(phase):
            copy.wait()

    def opening():
        start(0)
        take().start()
        take().wait()
        put().start()

    def turn(phase):
        def run():
            wait(phase - 1)
            if phase == 1:
                put().wait()
            start(phase)

        return run

    return [opening, turn(1), turn(2), turn(3), lambda: wait(3)]


def swap_phases(place, source, target, sems, local, stop, item):
    y = place.y

    def away():
        return remote(source.at[1 - y], target.at[y], sems, item, 0, place.across_y())

    def take():
        return pltpu.make_async_copy(source.at[y], stop, local.at[item, 0])

    def put():
        return pltpu.make_async_copy(stop, target.at[y], local.at[item, 1])

    def opening():
        away().start()
        take().start()

    def middle():
        take().wait()
        put().start()

    def closing():
        put().wait()
        away().wait()

    return [opening, middle, closing]


def sum_scratch(depth, slots, items, rows, cols, dtype):
    half = rows // 2
    return [
        pltpu.VMEM((slots, depth, 2, 2, rows, cols), dtype),
        pltpu.VMEM((items, depth, 2, 2, rows, cols), dtype),
        pltpu.VMEM((items, depth, 2, half, cols), dtype),
        pltpu.VMEM((items, depth, half, cols), dtype),
        pltpu.VMEM((items, depth - 1, half, cols), dtype),
        pltpu.VMEM((items, depth, 2, half, cols), dtype),
        pltpu.VMEM((items, depth - 1, 2, half, cols), dtype),
        pltpu.VMEM((items, half, cols), dtype),
    ]


def sum_phases(place, source, result, rows, cols, bufs, sems, local, item, slots):
    own = bufs[0].at[item % slots]
    came, a_y, a_x, a_z, b_x, b_z, b_y = (buf.at[item] for buf in bufs[1:])
    depth = place.depth
    half = rows.size // 2
    low, high = pl.ds(0, half), pl.ds(half, half)
    z, x, core, y = place.z, place.x, place.core, place.y
    every = slice(None)

    def load():
        return pltpu.make_async_copy(
            source.at[every, every, core, every, rows, cols], own, local.at[item, 0]
        )

    def send(a, b, index, device):
        return remote(a, b, sems, item, index, device)

    def copies(phase):
        if phase == 0:
            theirs = source.at[every, every, 1 - core, every, rows, cols]
            return [send(theirs, came, 0, place.sibling())]
        if phase == 1:
            return [
                send(own.at[every, every, 1 - y, low], a_y, 1, place.across_y()),
                send(own.at[every, 1 - x, every, high], b_x, 2, place.across_x()),
            ]
        if phase == 2:
            return [send(a_y.at[every, 1 - x], a_x, 3, place.across_x())] + [
                send(
                    b_x.at[lax.rem(z + step, depth)], b_z.at[step - 1], 3 + step,
                    place.along_z(step),
                )
                for step in range(1, depth)
            ]
        return [send(b_z.at[0, 1 - y], b_y, 3 + depth, place.across_y())] + [
            send(
                a_x.at[lax.rem(z + step, depth)], a_z.at[step - 1], 3 + depth + step,
                place.along_z(step),
            )
            for step in range(1, depth)
        ]

    def start(phase):
        for copy in copies(phase):
            copy.start()

    def wait(phase):
        for copy in copies(phase):
            copy.wait()

    def opening():
        load().start()
        start(0)

    def after_core():
        load().wait()
        wait(0)

        @pl.loop(0, depth)
        def _(k):
            for i in range(2):
                for j in range(2):
                    own[k, i, j] = own[k, i, j] + came[k, i, j]

        start(1)

    def after_one():
        wait(1)

        @pl.loop(0, depth)
        def _(k):
            for i in range(2):
                a_y[k, i] = a_y[k, i] + own[k, i, y, low]
                b_x[k, i] = b_x[k, i] + own[k, x, i, high]

        start(2)

    def wide(values):
        return values.astype(jnp.float32)

    def after_two():
        wait(2)

        @pl.loop(0, depth)
        def _(k):
            a_x[k] = a_x[k] + a_y[k, x]

        for i in range(2):
            total = wide(b_x[z, i])
            for step in range(1, depth):
                total = total + wide(b_z[step - 1, i])
            b_z[0, i] = total.astype(b_z.dtype)
        start(3)

    def closing():
        wait(3)
        total = wide(a_x[z])
        for step in range(1, depth):
            total = total + wide(a_z[step - 1])
        result[pl.ds(rows.start, half), cols] = total
        result[pl.ds(rows.start + half, half), cols] = wide(b_z[0, y]) + wide(b_y[...])

    return [opening, after_core, after_one, after_two, closing]


def copy_sems(items, depth):
    width = 2 * depth + 3
    return [
        pltpu.SemaphoreType.DMA((items, width)),
        pltpu.SemaphoreType.DMA((items, width)),
        pltpu.SemaphoreType.DMA((items, 2)),
    ]


ITEM = 1024


def weight_items(shape):
    rows, cols = shape
    return [
        (pl.ds(r, 32), pl.ds(c, min(ITEM, cols)))
        for r in range(0, rows, 32)
        for c in range(0, cols, min(ITEM, cols))
    ]


def merged(stage_lists):
    count = max(len(stages) for stages in stage_lists)
    return [
        [one for stages in stage_lists if turn < len(stages) for one in stages[turn]]
        for turn in range(count)
    ]


class Swap:
    def __init__(self, depth, arrays):
        self.depth = depth
        self.arrays = list(arrays)
        self.in_specs = [ANYWHERE] * len(arrays)
        self.out_shape = [jax.ShapeDtypeStruct(a.shape, a.dtype) for a in arrays]
        self.out_specs = [ANYWHERE] * len(arrays)
        self.scratch = copy_sems(len(arrays), depth)
        self.scratch += [pltpu.VMEM(a.shape[1:], a.dtype) for a in arrays]

    def stages(self, place, ins, outs, scratch):
        phases = [
            swap_phases(place, a, b, scratch[:2], scratch[2], scratch[3 + k], k)
            for k, (a, b) in enumerate(zip(ins, outs))
        ]
        opening, middle, closing = (list(part) for part in zip(*phases))
        return [opening, middle, [], [], closing]

    def finish(self, results):
        return list(results)


class Gather:
    def __init__(self, depth, shards):
        self.depth = depth
        self.arrays = list(shards)
        self.order = [
            (index, rows, cols)
            for index, shard in enumerate(shards)
            for rows, cols in weight_items(shard.shape)
        ]
        self.in_specs = [ANYWHERE] * len(shards)
        self.out_shape = [
            jax.ShapeDtypeStruct((depth, 2, 2, 2) + s.shape, s.dtype) for s in shards
        ]
        self.out_specs = [ANYWHERE] * len(shards)
        self.scratch = copy_sems(len(self.order), depth)
        self.scratch += [
            pltpu.VMEM((rows.size, cols.size), shards[index].dtype)
            for index, rows, cols in self.order
        ]

    def stages(self, place, ins, outs, scratch):
        return pipelined(
            [
                gather_phases(
                    place, ins[index], outs[index], rows, cols, scratch[:2], scratch[2],
                    scratch[3 + item], item,
                )
                for item, (index, rows, cols) in enumerate(self.order)
            ]
        )

    def finish(self, results):
        return [r.reshape(-1, r.shape[-1]) for r in results]


SLOTS = 4


class Total:
    def __init__(self, depth, grads):
        self.depth = depth
        shards = depth * 8
        shapes = [(g.shape[0] // shards, g.shape[1]) for g in grads]
        self.arrays = [g.reshape((depth, 2, 2, 2) + s) for g, s in zip(grads, shapes)]
        self.order = [
            (index, rows, cols)
            for index, shape in enumerate(shapes)
            for rows, cols in weight_items(shape)
        ]
        self.in_specs = [ANYWHERE] * len(grads)
        self.out_shape = [jax.ShapeDtypeStruct(s, jnp.float32) for s in shapes]
        self.out_specs = [whole_block(s) for s in shapes]
        rows, cols = self.order[0][1].size, self.order[0][2].size
        self.slots = min(SLOTS, len(self.order))
        self.scratch = copy_sems(len(self.order), depth) + sum_scratch(
            depth, self.slots, len(self.order), rows, cols, grads[0].dtype
        )

    def stages(self, place, ins, outs, scratch):
        return pipelined(
            [
                sum_phases(
                    place, ins[index], outs[index], rows, cols, scratch[3:], scratch[:2],
                    scratch[2], item, self.slots,
                )
                for item, (index, rows, cols) in enumerate(self.order)
            ]
        )

    def finish(self, results):
        return list(results)


def whole_block(shape):
    return pl.BlockSpec(shape, lambda *_: (0,) * len(shape))


def hosted(name, number, comms, steps, body, args, in_specs, out_shape, out_specs, scratch):
    depth = comms[0].depth
    all_args = list(args)
    all_in, all_shape, all_out, all_scratch = (
        list(in_specs), list(out_shape), list(out_specs), list(scratch),
    )
    for comm in comms:
        all_args += comm.arrays
        all_in += comm.in_specs
        all_shape += comm.out_shape
        all_out += comm.out_specs
        all_scratch += comm.scratch

    def kernel(*refs):
        refs = list(refs)

        def take(count):
            taken = refs[:count]
            del refs[:count]
            return taken

        own_in = take(len(args))
        comm_in = [take(len(comm.arrays)) for comm in comms]
        own_out = take(len(out_shape))
        comm_out = [take(len(comm.out_shape)) for comm in comms]
        own_scratch = take(len(scratch))
        comm_scratch = [take(len(comm.scratch)) for comm in comms]
        place = Place(depth)
        stages = merged(
            [
                comm.stages(place, a, b, c)
                for comm, a, b, c in zip(comms, comm_in, comm_out, comm_scratch)
            ]
        )
        step = pl.program_id(0)

        @pl.when(step == 0)
        def _():
            place.greet()

        spread = max(1, len(stages) - 1)
        for at in range(steps):
            due = [k for k in range(len(stages) - 1) if k * steps // spread == at]
            if due:

                @pl.when(step == at)
                def _(due=due):
                    for k in due:
                        for one in reversed(stages[k]):
                            one()

        if body is not None:
            body(*own_in, *own_out, *own_scratch)

        @pl.when(step == steps - 1)
        def _():
            for one in reversed(stages[-1]):
                one()

    results = pl.pallas_call(
        kernel,
        grid=(steps,),
        out_shape=all_shape,
        in_specs=all_in,
        out_specs=all_out,
        scratch_shapes=all_scratch,
        compiler_params=pltpu.CompilerParams(
            collective_id=number, has_side_effects=True, vmem_limit_bytes=VMEM_LIMIT
        ),
        name=name,
    )(*all_args)
    results = list(results)
    own = results[: len(out_shape)]
    results = results[len(out_shape) :]
    finished = []
    for comm in comms:
        finished.append(comm.finish(results[: len(comm.out_shape)]))
        results = results[len(comm.out_shape) :]
    return own, finished


def only(name, number, comms):
    return hosted(name, number, comms, 1, None, [], [], [], [], [])[1]


QB=256
def nt(a,b): return lax.dot_general(a,b,(((1,),(1,)),((),())),preferred_element_type=jnp.float32)
def nn(a,b): return jnp.dot(a,b,preferred_element_type=jnp.float32)
def half_mask(rows):
    lane=lax.broadcasted_iota(jnp.int32,(rows,128),1)
    return lane<64
def pick(block,h,first):
    zero=jnp.zeros_like(block)
    return jnp.where(first,block,zero) if h==0 else jnp.where(first,zero,block)
def scores(keys, queries, diagonal, bias):
    s = nt(keys, queries)
    if diagonal:
        r = lax.broadcasted_iota(jnp.int32, s.shape, 0)
        c = lax.broadcasted_iota(jnp.int32, s.shape, 1)
        s = jnp.where(r <= c, s, MASKED)
    if bias is not None:
        s = s + bias
    return s


def segments(causal,qb,keys):
    if not causal: return [(0,keys,False)]
    out=[]
    if qb>0: out.append((0,qb*QB,False))
    out.append((qb*QB,(qb+1)*QB,True))
    return out
def attend_pair(causal, rows, keys, get_q, get_k, get_v, bias, put, lse_ref):
    vt = get_v(0, keys).T
    first = half_mask(QB)
    for qb in range(rows // QB):
        sl = slice(qb * QB, (qb + 1) * QB)
        q = get_q(qb * QB, (qb + 1) * QB) * jnp.bfloat16(0.125)
        outs = []
        for h in (0, 1):
            qs = pick(q, h, first)
            segs = segments(causal, qb, keys)
            ss = [scores(get_k(lo, hi), qs, d, bias) for lo, hi, d in segs]
            m = functools.reduce(jnp.maximum, [jnp.max(s, axis=0, keepdims=True) for s in ss])
            ps = [jnp.exp(s - m) for s in ss]
            l = functools.reduce(jnp.add, [jnp.sum(p, axis=0, keepdims=True) for p in ps])
            ot = functools.reduce(
                jnp.add,
                [
                    nn(vt[h * 64 : (h + 1) * 64, lo:hi], p.astype(jnp.bfloat16))
                    for p, (lo, hi, _) in zip(ps, segs)
                ],
            )
            outs.append(ot * (1.0 / l))
            lse_ref[h : h + 1, sl] = m + jnp.log(l)
        put(sl, jnp.concatenate(outs, axis=0).T.astype(jnp.bfloat16))


def bwd_body(causal,q_ref,k_ref,v_ref,bias,o_ref,do_ref,lse_ref,dq_ref,dk_ref,dv_ref,dk_acc,dv_acc):
    rows=q_ref.shape[0]; keys=k_ref.shape[0]
    kt=(k_ref[...]*jnp.bfloat16(0.125)).T
    first=half_mask(QB)
    nq=rows//QB
    order=list(range(nq))[::-1] if causal else list(range(nq))
    started=set()
    for qb in order:
        sl=slice(qb*QB,(qb+1)*QB)
        q=q_ref[sl,:]*jnp.bfloat16(0.125)
        do=do_ref[sl,:]
        dt=(do.astype(jnp.float32)*o_ref[sl,:].astype(jnp.float32)).T
        outs=[]
        segs=segments(causal,qb,keys)
        new={}
        for h in (0,1):
            qs=pick(q,h,first); doh=pick(do,h,first)
            delta=jnp.sum(dt[h*64:(h+1)*64,:],axis=0,keepdims=True)
            lse=lse_ref[0,h:h+1,sl]
            dqt=None
            for lo,hi,d in segs:
                p=jnp.exp(scores(k_ref[lo:hi,:],qs,d,bias)-lse)
                dp=nt(v_ref[lo:hi,:],doh)
                ds=(p*(dp-delta)).astype(jnp.bfloat16)
                t=nn(kt[h*64:(h+1)*64,lo:hi],ds)
                dqt=t if dqt is None else dqt+t
                a=nn(p.astype(jnp.bfloat16),doh); b=nn(ds,qs)
                if (lo,hi) in new: new[(lo,hi)]=(new[(lo,hi)][0]+a,new[(lo,hi)][1]+b)
                else: new[(lo,hi)]=(a,b)
            outs.append(dqt)
        dq_ref[sl,:]=jnp.concatenate(outs,axis=0).T.astype(jnp.bfloat16)
        for (lo,hi),(a,b) in new.items():
            if qb==order[0]:
                dv_acc[lo:hi,:]=a; dk_acc[lo:hi,:]=b
            else:
                dv_acc[lo:hi,:]+=a; dk_acc[lo:hi,:]+=b
    dk_ref[...]=dk_acc[...].astype(jnp.bfloat16)
    dv_ref[...]=dv_acc[...].astype(jnp.bfloat16)
def self_attend_back(qkv,o,do,lse,number,comms):
    R=qkv.shape[0]; D=qkv.shape[1]//3; n=D//128
    def body(q,k,v,o,do,lse,dq,dk,dv,ka,va): bwd_body(True,q,k,v,None,o,do,lse,dq,dk,dv,ka,va)
    blk=pl.BlockSpec((R,128),lambda j:(0,j))
    return hosted("self_attend_back",number,comms,n,body,[qkv]*3+[o,do,lse],
        [pl.BlockSpec((R,128),lambda j,i=i:(0,j+n*i)) for i in range(3)]+[blk,blk,pl.BlockSpec((1,2,R),lambda j:(j,0,0))],
        [jax.ShapeDtypeStruct((R,D),jnp.bfloat16)]*3,[blk]*3,[pltpu.VMEM((R,128),jnp.float32)]*2)
def cross_attend_back(q,kv,bias,o,do,lse,number,comms):
    R,D=q.shape; T=kv.shape[0]; n=D//128
    def body(q,k,v,b,o,do,lse,dq,dk,dv,ka,va): bwd_body(False,q,k,v,jnp.concatenate([b[...]]*2,axis=1),o,do,lse,dq,dk,dv,ka,va)
    blk=pl.BlockSpec((R,128),lambda j:(0,j)); tb=pl.BlockSpec((T,128),lambda j:(0,j))
    return hosted("cross_attend_back",number,comms,n,body,[q,kv,kv,bias,o,do,lse],
        [blk]+[pl.BlockSpec((T,128),lambda j,i=i:(0,j+n*i)) for i in range(2)]+[pl.BlockSpec((T,128),lambda j:(0,0)),blk,blk,pl.BlockSpec((1,2,R),lambda j:(j,0,0))],
        [jax.ShapeDtypeStruct((R,D),jnp.bfloat16)]+[jax.ShapeDtypeStruct((T,D),jnp.bfloat16)]*2,[blk,tb,tb],[pltpu.VMEM((T,128),jnp.float32)]*2)


BLOCK = 256
MATMUL_ROWS = 512
RING = 6

VECTOR_COUNT = 15
(
    A_GAIN, A_SHIFT, A_QBIAS, A_VBIAS, A_OBIAS, C_GAIN, C_SHIFT, C_QBIAS, C_VBIAS, C_OBIAS,
    F_GAIN, F_SHIFT, F_DOWNBIAS, Z_GAIN, Z_SHIFT,
) = range(VECTOR_COUNT)
F_UPBIAS = VECTOR_COUNT


def block_rows(index, size):
    return pl.ds(pl.multiple_of(index * size, size), size)


def lanes(index, size):
    return pl.ds(pl.multiple_of(index * size, size), size)


def center_and_scale(values):
    center = values - jnp.mean(values, axis=-1, keepdims=True)
    spread = jnp.mean(center * center, axis=-1, keepdims=True)
    scale = lax.rsqrt(spread + EPSILON)
    return center * scale, scale


def norm_pull(unit, scale, pulled):
    inner = jnp.mean(pulled * unit, axis=-1, keepdims=True)
    return scale * (pulled - jnp.mean(pulled, axis=-1, keepdims=True) - unit * inner)


def gelu_and_slope(values):
    root = math.sqrt(2.0 / math.pi)
    square = values * values
    bend = jnp.tanh(root * (values + 0.044715 * (values * square)))
    rise = root * (1.0 + 3.0 * 0.044715 * square)
    result = 0.5 * values * (1.0 + bend)
    slope = 0.5 * (1.0 + bend) + 0.5 * values * ((1.0 - bend * bend) * rise)
    return result, slope


def spread_vectors(packed):
    rows = packed.shape[0]
    width = rows
    lane = lax.broadcasted_iota(jnp.int32, (128, width), 1)
    source = lax.broadcasted_iota(jnp.int32, (128, width), 0)
    select = jnp.where(lax.rem(lane, 32) == source, 1.0, 0.0).astype(jnp.bfloat16)
    wide = jnp.dot(packed, select, preferred_element_type=jnp.float32)
    row = lax.broadcasted_iota(jnp.int32, (rows, width), 0)
    lane = lax.broadcasted_iota(jnp.int32, (rows, width), 1)
    wide = jnp.where(row // 32 == lane // 32, wide, 0.0)
    return jnp.sum(wide.reshape(rows // 32, 32, width), axis=0)


class Copies:
    def __init__(self, sems):
        self.sems = sems
        self.open = {}
        self.used = 0

    def start(self, source, target):
        copy = pltpu.make_async_copy(source, target, self.sems.at[self.used])
        self.used += 1
        copy.start()
        return copy


def forward_kernel(depth, sizes, *refs):
    refs = list(refs)

    def take(count):
        taken = refs[:count]
        del refs[:count]
        return taken

    shard_count = len(sizes)
    tokens, texts, cots, unit_length, text_length = take(5)
    shards = take(shard_count)
    wholes = take(shard_count)
    (
        o_tokens, o_text, o_h1, o_qkv, o_o1, o_after_self, o_h2, o_cq, o_ckv, o_o2,
        o_after_cross, o_h3, o_active, o_slope, o_gaf, o_gbr, o_layer,
    ) = take(17)
    vec, lse1, lse2, zgrads = take(4)
    tok, txt, cot, x, o1, cq, ckv, o2, resid, h2, ring, slopes, packed = take(13)
    stops = take(sum(len(weight_items(s)) for s in sizes))
    send, receive, local, sw_send, sw_receive, sw_local, loads, outs = take(8)

    place = Place(depth)
    y = place.y
    rows = resid.shape[0]
    width = resid.shape[1]
    part = rows // 2
    copies = Copies(outs)
    phases, chunks, item = [], [], 0
    for index, size in enumerate(sizes):
        for r, c in weight_items(size):
            phase = gather_phases(
                place, shards[index], wholes[index], r, c, (send, receive), local, stops[item], item
            )
            phases.append(phase)
            if index > 0:
                chunks.append((wholes[index], c))
            item += 1
    first = phases[0]
    stages = pipelined(phases[1:])
    stages = [([first[k]] if k < len(first) else []) + s for k, s in enumerate(stages)]

    def swapping(k, source, target):
        def away():
            return remote(source.at[1 - y], target.at[y], (sw_send, sw_receive), k, 0, place.across_y())

        def home():
            return pltpu.make_async_copy(source.at[y], target.at[y], sw_local.at[k])

        def opening():
            away().start()
            home().start()

        def closing():
            away().wait()
            home().wait()

        return opening, closing

    token_swap = swapping(0, tokens, tok)
    text_swap = swapping(1, texts, txt)
    cot_swap = swapping(2, cots, cot)

    def load(chunk):
        whole, cols = chunks[chunk]
        return pltpu.make_async_copy(
            whole.at[:, :, :, :, :, cols], ring.at[chunk % RING], loads.at[chunk]
        )

    def stage(k):
        for one in reversed(stages[k]):
            one()
        if k >= 4:
            load(k - 4).start()

    def weight(chunk):
        return ring[chunk % RING].reshape(width, width)

    def row(index):
        return vec[index : index + 1, :]

    def looped(count, body, due=()):
        @pl.loop(0, count)
        def _(j):
            for at, k in due:

                @pl.when(j == at)
                def _(k=k):
                    stage(k)

            body(j)

    place.greet()
    token_swap[0]()
    for k in range(3):
        stage(k)
    text_swap[0]()
    stage(3)
    stage(4)
    pack = pltpu.make_async_copy(wholes[0], packed, outs.at[copies.used])
    copies.used += 1
    pack.start()
    pack.wait()
    vec[...] = spread_vectors(packed[...].reshape(-1, 128))
    token_swap[1]()
    done_tokens = copies.start(tok, o_tokens)

    def token_block(b):
        half = b // (part // BLOCK)
        inner = lax.rem(b, part // BLOCK)
        return tok[half, block_rows(inner, BLOCK), :].astype(jnp.float32)

    def norm_one(b):
        unit, _ = center_and_scale(token_block(b))
        at = block_rows(b, BLOCK)
        x[at, 3 * width :] = (unit * row(A_GAIN) + row(A_SHIFT)).astype(jnp.bfloat16)
        resid[at, :] = token_block(b)

    looped(rows // BLOCK, norm_one)
    done_h1 = copies.start(x.at[:, pl.ds(3 * width, width)], o_h1)

    def project(chunk):
        bias = (row(A_QBIAS), None, row(A_VBIAS))[chunk]
        load(chunk).wait()

        def block(b):
            at = block_rows(b, MATMUL_ROWS)
            value = nn(x[at, 3 * width :], weight(chunk))
            if bias is not None:
                value = value + bias
            x[at, chunk * width : (chunk + 1) * width] = value.astype(jnp.bfloat16)

        looped(rows // MATMUL_ROWS, block)

    project(0)
    stage(5)
    project(1)
    stage(6)
    project(2)
    done_qkv = copies.start(x.at[:, pl.ds(0, 3 * width)], o_qkv)
    pairs = width // 128

    def self_pair(j):
        def part_of(base):
            return lambda lo, hi: x[lo:hi, lanes(j + base * pairs, 128)]

        def put(sl, value):
            o1[sl, lanes(j, 128)] = value

        attend_pair(
            True, rows, rows, part_of(0), part_of(1), part_of(2), None, put, lse1.at[j]
        )

    looped(pairs, self_pair, ((2, 7), (4, 8), (7, 9)))
    done_o1 = copies.start(o1, o_o1)
    load(3).wait()

    def out_block(b):
        at = block_rows(b, MATMUL_ROWS)
        resid[at, :] = resid[at, :] + nn(o1[at, :], weight(3)) + row(A_OBIAS)

    looped(rows // MATMUL_ROWS, out_block)
    done_after_self = copies.start(resid, o_after_self)

    def norm_two(b):
        at = block_rows(b, BLOCK)
        unit, _ = center_and_scale(resid[at, :])
        h2[at, :] = (unit * row(C_GAIN) + row(C_SHIFT)).astype(jnp.bfloat16)

    looped(rows // BLOCK, norm_two)
    done_h2 = copies.start(h2, o_h2)
    stage(10)
    load(4).wait()

    def cq_block(b):
        at = block_rows(b, MATMUL_ROWS)
        cq[at, :] = (nn(h2[at, :], weight(4)) + row(C_QBIAS)).astype(jnp.bfloat16)

    looped(rows // MATMUL_ROWS, cq_block)
    done_cq = copies.start(cq, o_cq)
    text_swap[1]()
    cot_swap[0]()
    done_text = copies.start(txt, o_text)
    text = txt[...].reshape(-1, width)
    text_rows = text.shape[0]
    load(5).wait()
    ckv[:, :width] = nn(text, weight(5)).astype(jnp.bfloat16)
    load(6).wait()
    ckv[:, width:] = (nn(text, weight(6)) + row(C_VBIAS)).astype(jnp.bfloat16)
    done_ckv = copies.start(ckv, o_ckv)
    bias = text_mask(text_rows, text_length[y])

    def cross_pair(j):
        def put(sl, value):
            o2[sl, lanes(j, 128)] = value

        attend_pair(
            False, rows, text_rows,
            lambda lo, hi: cq[lo:hi, lanes(j, 128)],
            lambda lo, hi: ckv[lo:hi, lanes(j, 128)],
            lambda lo, hi: ckv[lo:hi, lanes(j + pairs, 128)],
            bias, put, lse2.at[j],
        )

    looped(pairs, cross_pair, ((1, 11), (4, 12), (7, 13)))
    done_o2 = copies.start(o2, o_o2)
    load(7).wait()
    done_after_self.wait()

    def cross_out_block(b):
        at = block_rows(b, MATMUL_ROWS)
        resid[at, :] = resid[at, :] + nn(o2[at, :], weight(7)) + row(C_OBIAS)

    looped(rows // MATMUL_ROWS, cross_out_block)
    done_after_cross = copies.start(resid, o_after_cross)
    done_o1.wait()
    h3 = o1

    def norm_three(b):
        at = block_rows(b, BLOCK)
        unit, _ = center_and_scale(resid[at, :])
        h3[at, :] = (unit * row(F_GAIN) + row(F_SHIFT)).astype(jnp.bfloat16)

    looped(rows // BLOCK, norm_three)
    done_h3 = copies.start(h3, o_h3)
    done_h1.wait()
    done_qkv.wait()
    waiting = []

    def up(q):
        load(8 + q).wait()
        slope_at = slopes.at[q % 2]

        def block(b):
            at = block_rows(b, BLOCK)
            inner = nn(h3[at, :], weight(8 + q)) + row(F_UPBIAS + q)
            active, slope = gelu_and_slope(inner)
            x[at, q * width : (q + 1) * width] = active.astype(jnp.bfloat16)
            slope_at[at, :] = slope.astype(jnp.bfloat16)

        if q >= 2:
            waiting[q - 2].wait()
        looped(rows // BLOCK, block)
        span = pl.ds(q * width, width)
        waiting.append(copies.start(slope_at, o_slope.at[:, span]))

    stage(14)
    up(0)
    up(1)
    stage(15)
    up(2)
    up(3)
    done_active = copies.start(x, o_active)
    done_after_cross.wait()

    def down(q):
        load(12 + q).wait()

        def block(b):
            at = block_rows(b, MATMUL_ROWS)
            resid[at, :] += nn(x[at, q * width : (q + 1) * width], weight(12 + q))

        looped(rows // MATMUL_ROWS, block)

    for q in range(4):
        stage(16 + q)
        down(q)
    cot_swap[1]()
    done_cq.wait()
    done_o2.wait()
    valid_count = unit_length[y]
    zgrads[...] = jnp.zeros_like(zgrads)
    gbr, layer = cq, o2

    def last_block(b):
        at = block_rows(b, BLOCK)
        unit, scale = center_and_scale(resid[at, :] + row(F_DOWNBIAS))
        position = b * BLOCK + lax.broadcasted_iota(jnp.int32, (BLOCK, 1), 0)
        valid = jnp.where(position < valid_count, 1.0, 0.0)
        layer[at, :] = ((unit * row(Z_GAIN) + row(Z_SHIFT)) * valid).astype(jnp.bfloat16)
        half = b // (part // BLOCK)
        inner = lax.rem(b, part // BLOCK)
        upstream = cot[half, block_rows(inner, BLOCK), :].astype(jnp.float32) * valid
        zgrads[0:1, :] += jnp.sum(upstream * unit, axis=0, keepdims=True)
        zgrads[1:2, :] += jnp.sum(upstream, axis=0, keepdims=True)
        grad = norm_pull(unit, scale, upstream * row(Z_GAIN))
        low = grad.astype(jnp.bfloat16)
        gbr[at, :] = low
        zgrads[2:3, :] += jnp.sum(low.astype(jnp.float32), axis=0, keepdims=True)
        resid[at, :] = grad

    looped(rows // BLOCK, last_block)
    ending = [
        copies.start(resid, o_gaf), copies.start(gbr, o_gbr), copies.start(layer, o_layer),
    ]
    ending += [done_tokens, done_h2, done_text, done_ckv, done_h3, done_active]
    for copy in ending + waiting[2:]:
        copy.wait()


def text_mask(text_rows, count):
    position = lax.broadcasted_iota(jnp.int32, (text_rows, QB), 0)
    return jnp.where(position < count, 0.0, MASKED)


def forward(depth, number, tokens, texts, cots, unit_length, text_length, shards):
    rows, width = 2 * tokens.shape[1], tokens.shape[2]
    text_rows = 2 * texts.shape[1]
    hidden = 4 * width
    pairs = width // 128
    sizes = [s.shape for s in shards]
    items = sum(len(weight_items(s)) for s in sizes)
    low, full = jnp.bfloat16, jnp.float32

    def shape(*dims, kind=low):
        return jax.ShapeDtypeStruct(dims, kind)

    def vmem(*dims, kind=low):
        return pltpu.VMEM(dims, kind)

    big = shape(rows, width)
    exact = shape(rows, width, kind=full)
    outs = [shape(depth, 2, 2, 2, *s) for s in sizes]
    outs += [
        shape(*tokens.shape), shape(*texts.shape), big, shape(rows, 3 * width), big, exact, big, big,
        shape(text_rows, 2 * width), big, exact, big, shape(rows, hidden), shape(rows, hidden),
        exact, big, big,
    ]
    small = [
        shape(32, width, kind=full), shape(pairs, 2, rows, kind=full),
        shape(pairs, 2, rows, kind=full), shape(8, width, kind=full),
    ]
    scratch = [
        vmem(*tokens.shape), vmem(*texts.shape), vmem(*cots.shape), vmem(rows, hidden),
        vmem(rows, width), vmem(rows, width), vmem(text_rows, 2 * width), vmem(rows, width),
        vmem(rows, width, kind=full), vmem(rows, width), vmem(RING, depth, 2, 2, 2, 32, width),
        vmem(2, rows, width), vmem(depth, 2, 2, 2, *sizes[0]),
    ]
    scratch += [vmem(r.size, c.size) for s in sizes for r, c in weight_items(s)]
    scratch += copy_sems(items, depth)
    scratch += [
        pltpu.SemaphoreType.DMA((3, 1)), pltpu.SemaphoreType.DMA((3, 1)),
        pltpu.SemaphoreType.DMA((3,)), pltpu.SemaphoreType.DMA((items,)),
        pltpu.SemaphoreType.DMA((32,)),
    ]
    memory = pl.BlockSpec(memory_space=pltpu.SMEM)
    results = pl.pallas_call(
        functools.partial(forward_kernel, depth, sizes),
        out_shape=outs + small,
        in_specs=[ANYWHERE] * 3 + [memory] * 2 + [ANYWHERE] * len(shards),
        out_specs=[ANYWHERE] * len(outs) + [pl.BlockSpec(memory_space=pltpu.VMEM)] * len(small),
        scratch_shapes=scratch,
        compiler_params=pltpu.CompilerParams(
            collective_id=number, has_side_effects=True, vmem_limit_bytes=VMEM_LIMIT
        ),
        name="forward",
    )(tokens, texts, cots, unit_length, text_length, *shards)
    return list(results[: len(sizes)]), list(results[len(sizes) :])


def pack_vectors(vectors, wide):
    packed = jnp.concatenate([jnp.stack(vectors), wide.reshape(4, -1)])
    return jnp.pad(packed, ((0, 32 - packed.shape[0]), (0, 128 - packed.shape[1])))


def pack_vector_grads(vectors, shards):
    parts = jnp.concatenate([v.reshape(-1, shards, v.shape[-1] // shards) for v in vectors])
    parts = jnp.swapaxes(parts, 0, 1)
    parts = jnp.pad(parts, ((0, 0), (0, 32 - parts.shape[1]), (0, 128 - parts.shape[2])))
    return parts.reshape(-1, 128)


def half(values):
    return values.astype(jnp.bfloat16)


def paired_layer(
    depth,
    tokens,
    text_states,
    unit_length,
    text_length,
    cotangent,
    attn_gain,
    attn_shift,
    attn_inputs,
    attn_qbias,
    attn_vbias,
    attn_output,
    attn_obias,
    cross_gain,
    cross_shift,
    cross_query,
    cross_qbias,
    cross_keyval,
    cross_vbias,
    cross_output,
    cross_obias,
    ffn_gain,
    ffn_shift,
    ffn_up,
    ffn_upbias,
    ffn_down,
    ffn_downbias,
    final_gain,
    final_shift,
):
    part_len, width = tokens.shape[1:]
    share = attn_gain.shape[0]
    text_part = text_states.shape[1]
    rows = 2 * part_len
    me = lax.axis_index("seq")
    packed = pack_vectors(
        [
            attn_gain, attn_shift, attn_qbias, attn_vbias, attn_obias, cross_gain, cross_shift,
            cross_qbias, cross_vbias, cross_obias, ffn_gain, ffn_shift, ffn_downbias, final_gain,
            final_shift,
        ],
        ffn_upbias,
    )
    shards = depth * 8
    up_shard = ffn_up.reshape(share, shards, 4, share).swapaxes(1, 2).reshape(share, -1)
    wholes, kept = forward(
        depth, 0, tokens, text_states, cotangent, unit_length, text_length,
        [packed, attn_inputs, attn_output, cross_query, cross_keyval, cross_output, up_shard]
        + [ffn_down[q * share : (q + 1) * share] for q in range(4)],
    )
    w_in, w_out, w_cq, w_ckv, w_co, w_up, *w_downs = [
        w.reshape(-1, w.shape[-1]) for w in wholes[1:]
    ]
    w_down = jnp.concatenate(w_downs)
    (
        token_seq, text_seq, normed_one, joined, self_mixed, after_self, normed_two, cross_queries,
        cross_kv, cross_mixed, after_cross, normed_three, active, slope, grad_after_ffn,
        grad_branch, layer_out, vec, self_logsum, cross_logsum, zgrads,
    ) = kept
    inputs = to_float(token_seq).reshape(rows, width)
    text = text_seq.reshape(2 * text_part, width)
    allowed = jnp.arange(2 * text_part)[:, None] < text_length[me]
    text_bias = jnp.broadcast_to(jnp.where(allowed, 0.0, MASKED), (2 * text_part, 128))
    grad_zgain, grad_zshift, grad_downbias = zgrads[0], zgrads[1], zgrads[2]

    grad_down = half(left_dot(active, grad_branch))
    grad_active = right_dot(grad_branch, w_down)
    grad_inner = half(grad_active * to_float(slope))
    grad_up = half(left_dot(normed_three, grad_inner))
    grad_upbias = jnp.sum(to_float(grad_inner), axis=0)
    grad_normed_three = right_dot(grad_inner, w_up)
    grad_cross_norm, grad_fgain, grad_fshift = norm_back(
        after_cross, vec[F_GAIN], vec[F_SHIFT], grad_normed_three
    )
    grad_after_cross = grad_after_ffn + grad_cross_norm

    cross_branch = half(grad_after_cross)
    grad_coutput = half(left_dot(cross_mixed, cross_branch))
    grad_cobias = jnp.sum(to_float(cross_branch), axis=0)
    grad_cross_mixed = half(right_dot(cross_branch, w_co))
    (grad_cq, grad_ck, grad_cv), ((s_up, *s_downs), (layer_out,)) = cross_attend_back(
        cross_queries, cross_kv, text_bias, cross_mixed, grad_cross_mixed, cross_logsum, 3,
        [Total(depth, [grad_up, *jnp.split(grad_down, 4)]), Swap(depth, [layer_out.reshape(2, part_len, width)])],
    )
    grad_ckv = jnp.concatenate([grad_ck, grad_cv], axis=-1)
    grad_ckeyval = half(left_dot(text, grad_ckv))
    grad_cvbias = jnp.sum(to_float(grad_cv), axis=0)
    text_grad = half(right_dot(grad_ckv, w_ckv))
    grad_cquery = half(left_dot(normed_two, grad_cq))
    grad_cqbias = jnp.sum(to_float(grad_cq), axis=0)
    grad_normed_two = right_dot(grad_cq, w_cq)
    grad_self_norm, grad_cgain, grad_cshift = norm_back(
        after_self, vec[C_GAIN], vec[C_SHIFT], grad_normed_two
    )
    grad_after_self = grad_after_cross + grad_self_norm

    self_branch = half(grad_after_self)
    grad_aoutput = half(left_dot(self_mixed, self_branch))
    grad_aobias = jnp.sum(to_float(self_branch), axis=0)
    grad_self_mixed = half(right_dot(self_branch, w_out))
    (grad_q, grad_k, grad_v), ((s_ckv, s_cq, s_co), (text_grad,)) = self_attend_back(
        joined, self_mixed, grad_self_mixed, self_logsum, 4,
        [
            Total(depth, [grad_ckeyval, grad_cquery, grad_coutput]),
            Swap(depth, [text_grad.reshape(2, text_part, width)]),
        ],
    )
    grad_joined = jnp.concatenate([grad_q, grad_k, grad_v], axis=-1)
    grad_ainputs = half(left_dot(normed_one, grad_joined))
    grad_aqbias = jnp.sum(to_float(grad_q), axis=0)
    grad_avbias = jnp.sum(to_float(grad_v), axis=0)
    grad_normed_one = right_dot(grad_joined, w_in)
    grad_input_norm, grad_again, grad_ashift = norm_back(
        inputs, vec[A_GAIN], vec[A_SHIFT], grad_normed_one
    )
    tokens_grad = half(grad_after_self + grad_input_norm)

    small = pack_vector_grads(
        [
            grad_again, grad_ashift, grad_aqbias, grad_avbias, grad_aobias, grad_cgain,
            grad_cshift, grad_cqbias, grad_cvbias, grad_cobias, grad_fgain, grad_fshift,
            grad_downbias, grad_zgain, grad_zshift, grad_upbias.reshape(4, -1),
        ],
        shards,
    )
    (s_in, s_out), (s_small,), (tokens_grad,) = only(
        "sum_last", 5,
        [
            Total(depth, [grad_ainputs, grad_aoutput]),
            Total(depth, [small]),
            Swap(depth, [tokens_grad.reshape(2, part_len, width)]),
        ],
    )
    s_up = s_up.reshape(share, 4, shards, share).swapaxes(1, 2).reshape(share, -1)
    s_down = jnp.concatenate(s_downs)
    s_upbias = s_small[VECTOR_COUNT : VECTOR_COUNT + 4, :share].reshape(-1)
    v = [s_small[i, :share] for i in range(VECTOR_COUNT)]
    return (
        layer_out, tokens_grad, text_grad, v[A_GAIN], v[A_SHIFT], s_in, v[A_QBIAS], v[A_VBIAS],
        s_out, v[A_OBIAS], v[C_GAIN], v[C_SHIFT], s_cq, v[C_QBIAS], s_ckv, v[C_VBIAS], s_co,
        v[C_OBIAS], v[F_GAIN], v[F_SHIFT], s_up, s_upbias, s_down, v[F_DOWNBIAS], v[Z_GAIN],
        v[Z_SHIFT],
    )


def solution(mesh):
    in_specs = (
        P("dp", "seq", None),
        P("dp", "seq", None),
        P("dp"),
        P("dp"),
        P("dp", "seq", None),
        P(("dp", "seq")),
        P(("dp", "seq")),
        P(("dp", "seq"), None),
        P(("dp", "seq")),
        P(("dp", "seq")),
        P(("dp", "seq"), None),
        P(("dp", "seq")),
        P(("dp", "seq")),
        P(("dp", "seq")),
        P(("dp", "seq"), None),
        P(("dp", "seq")),
        P(("dp", "seq"), None),
        P(("dp", "seq")),
        P(("dp", "seq"), None),
        P(("dp", "seq")),
        P(("dp", "seq")),
        P(("dp", "seq")),
        P(("dp", "seq"), None),
        P(("dp", "seq")),
        P(("dp", "seq"), None),
        P(("dp", "seq")),
        P(("dp", "seq")),
        P(("dp", "seq")),
    )
    out_specs = (
        P("dp", "seq", None),
        P("dp", "seq", None),
        P("dp", "seq", None),
        P(("dp", "seq")),
        P(("dp", "seq")),
        P(("dp", "seq"), None),
        P(("dp", "seq")),
        P(("dp", "seq")),
        P(("dp", "seq"), None),
        P(("dp", "seq")),
        P(("dp", "seq")),
        P(("dp", "seq")),
        P(("dp", "seq"), None),
        P(("dp", "seq")),
        P(("dp", "seq"), None),
        P(("dp", "seq")),
        P(("dp", "seq"), None),
        P(("dp", "seq")),
        P(("dp", "seq")),
        P(("dp", "seq")),
        P(("dp", "seq"), None),
        P(("dp", "seq")),
        P(("dp", "seq"), None),
        P(("dp", "seq")),
        P(("dp", "seq")),
        P(("dp", "seq")),
    )
    groups, seq_parts = mesh.shape["dp"], mesh.shape["seq"]

    def layer(*arguments):
        shard = arguments[5].shape[0]
        parts = arguments[0].shape[0]
        if seq_parts == 2 and parts == 2 and groups % 4 == 0 and shard % 32 == 0:
            return paired_layer(groups // 4, *arguments)
        return on_device(*arguments)

    return jax.shard_map(
        layer, mesh=mesh, in_specs=in_specs, out_specs=out_specs, check_vma=False
    )
```

```python
import functools
import math

import jax
import jax.numpy as jnp
from jax import lax
from jax.experimental import pallas as pl
from jax.experimental.pallas import tpu as pltpu
from jax.sharding import PartitionSpec as P

HEADS = 16
HEAD_DIM = 64


EPSILON = 1e-05
MASKED = -1e30


def layer_norm(values, norm_gain, norm_shift):
    center = values - jnp.mean(values, axis=-1, keepdims=True)
    spread = jnp.mean(center * center, axis=-1, keepdims=True)
    return center * lax.rsqrt(spread + EPSILON) * norm_gain + norm_shift


def norm_back(values, norm_gain, norm_shift, upstream):
    result, pullback = jax.vjp(layer_norm, values, norm_gain, norm_shift)
    return pullback(upstream)


def rows_dot(left_side, right_side):
    return jnp.dot(left_side, right_side, preferred_element_type=jnp.float32)


def left_dot(left_side, right_side):
    return lax.dot_general(
        left_side, right_side, (((0,), (0,)), ((), ())), preferred_element_type=jnp.float32
    )


def right_dot(left_side, right_side):
    return lax.dot_general(
        left_side, right_side, (((1,), (1,)), ((), ())), preferred_element_type=jnp.float32
    )


def heads_of(matrix):
    return matrix.reshape(matrix.shape[0], HEADS, HEAD_DIM)


def attend_forward(queries, key_rows, value_rows, allowed):
    score_scale = 1.0 / math.sqrt(HEAD_DIM)
    scores = (
        jnp.einsum(
            "qhd,khd->hqk",
            heads_of(queries),
            heads_of(key_rows),
            preferred_element_type=jnp.float32,
        )
        * score_scale
    )
    scores = jnp.where(allowed[None], scores, MASKED)
    row_max = jnp.max(scores, axis=-1, keepdims=True)
    weights = jnp.exp(scores - row_max)
    row_total = jnp.sum(weights, axis=-1, keepdims=True)
    weights = (weights / row_total).astype(jnp.bfloat16)
    mixed_rows = jnp.einsum(
        "hqk,khd->qhd", weights, heads_of(value_rows), preferred_element_type=jnp.float32
    )
    logsum = (row_max + jnp.log(row_total))[..., 0]
    return (mixed_rows.reshape(queries.shape[0], -1).astype(jnp.bfloat16), logsum)


def attend_back(queries, key_rows, value_rows, allowed, logsum, upstream):
    score_scale = 1.0 / math.sqrt(HEAD_DIM)
    query_heads = heads_of(queries)
    key_heads = heads_of(key_rows)
    upstream_heads = heads_of(upstream)
    scores = (
        jnp.einsum("qhd,khd->hqk", query_heads, key_heads, preferred_element_type=jnp.float32)
        * score_scale
    )
    scores = jnp.where(allowed[None], scores, MASKED)
    weights = jnp.exp(scores - logsum[..., None])
    grad_weights = jnp.einsum(
        "qhd,khd->hqk", upstream_heads, heads_of(value_rows), preferred_element_type=jnp.float32
    )
    row_delta = jnp.sum(weights * grad_weights, axis=-1, keepdims=True)
    grad_scores = (weights * (grad_weights - row_delta)).astype(jnp.bfloat16)
    grad_query = (
        jnp.einsum("hqk,khd->qhd", grad_scores, key_heads, preferred_element_type=jnp.float32)
        * score_scale
    )
    grad_key = (
        jnp.einsum("hqk,qhd->khd", grad_scores, query_heads, preferred_element_type=jnp.float32)
        * score_scale
    )
    grad_value = jnp.einsum(
        "hqk,qhd->khd",
        weights.astype(jnp.bfloat16),
        upstream_heads,
        preferred_element_type=jnp.float32,
    )
    key_count = key_rows.shape[0]
    return (
        grad_query.reshape(queries.shape[0], -1),
        grad_key.reshape(key_count, -1),
        grad_value.reshape(key_count, -1),
    )


def to_float(values):
    return values.astype(jnp.float32)


def on_device(
    tokens,
    text_states,
    unit_length,
    text_length,
    cotangent,
    attn_gain,
    attn_shift,
    attn_inputs,
    attn_qbias,
    attn_vbias,
    attn_output,
    attn_obias,
    cross_gain,
    cross_shift,
    cross_query,
    cross_qbias,
    cross_keyval,
    cross_vbias,
    cross_output,
    cross_obias,
    ffn_gain,
    ffn_shift,
    ffn_up,
    ffn_upbias,
    ffn_down,
    ffn_downbias,
    final_gain,
    final_shift,
):
    seq_count, local_len, model_width = tokens.shape
    row_count = seq_count * local_len
    first_pos = lax.axis_index("seq") * local_len
    zero_bias = jnp.zeros((model_width,), jnp.float32)
    (
        a_gain_full,
        a_shift_full,
        attention_input_weight_whole,
        a_qbias_full,
        a_vbias_full,
        a_output_full,
        a_obias_full,
    ) = (
        lax.all_gather(attn_gain, ("dp", "seq"), axis=0, tiled=True),
        lax.all_gather(attn_shift, ("dp", "seq"), axis=0, tiled=True),
        lax.all_gather(attn_inputs, ("dp", "seq"), axis=0, tiled=True),
        lax.all_gather(attn_qbias, ("dp", "seq"), axis=0, tiled=True),
        lax.all_gather(attn_vbias, ("dp", "seq"), axis=0, tiled=True),
        lax.all_gather(attn_output, ("dp", "seq"), axis=0, tiled=True),
        lax.all_gather(attn_obias, ("dp", "seq"), axis=0, tiled=True),
    )
    inputs = to_float(tokens).reshape(row_count, model_width)
    normed_one = layer_norm(inputs, to_float(a_gain_full), to_float(a_shift_full)).astype(
        jnp.bfloat16
    )
    joined = rows_dot(normed_one, attention_input_weight_whole) + jnp.concatenate(
        [to_float(a_qbias_full), zero_bias, to_float(a_vbias_full)]
    )
    joined = joined.astype(jnp.bfloat16)
    self_queries = joined[:, :model_width].reshape(seq_count, local_len, model_width)
    keyval_local = joined[:, model_width:].reshape(seq_count, local_len, 2 * model_width)
    self_keyval = lax.all_gather(keyval_local, "seq", axis=1, tiled=True)
    full_len = self_keyval.shape[1]
    causal = jnp.arange(full_len)[None, :] <= (first_pos + jnp.arange(local_len))[:, None]

    def self_forward(packed):
        seq_queries, seq_keyval = packed
        return attend_forward(
            seq_queries, seq_keyval[:, :model_width], seq_keyval[:, model_width:], causal
        )

    self_mixed, self_logsum = lax.map(self_forward, (self_queries, self_keyval))
    self_flat = self_mixed.reshape(row_count, model_width)
    after_self = inputs + rows_dot(self_flat, a_output_full) + to_float(a_obias_full)
    (
        c_gain_full,
        c_shift_full,
        c_query_full,
        c_qbias_full,
        c_keyval_full,
        cross_value_bias_whole,
        c_output_full,
        c_obias_full,
    ) = (
        lax.all_gather(cross_gain, ("dp", "seq"), axis=0, tiled=True),
        lax.all_gather(cross_shift, ("dp", "seq"), axis=0, tiled=True),
        lax.all_gather(cross_query, ("dp", "seq"), axis=0, tiled=True),
        lax.all_gather(cross_qbias, ("dp", "seq"), axis=0, tiled=True),
        lax.all_gather(cross_keyval, ("dp", "seq"), axis=0, tiled=True),
        lax.all_gather(cross_vbias, ("dp", "seq"), axis=0, tiled=True),
        lax.all_gather(cross_output, ("dp", "seq"), axis=0, tiled=True),
        lax.all_gather(cross_obias, ("dp", "seq"), axis=0, tiled=True),
    )
    normed_two = layer_norm(after_self, to_float(c_gain_full), to_float(c_shift_full)).astype(
        jnp.bfloat16
    )
    cross_queries = (rows_dot(normed_two, c_query_full) + to_float(c_qbias_full)).astype(
        jnp.bfloat16
    )
    cross_queries = cross_queries.reshape(seq_count, local_len, model_width)
    keyval_bias = jnp.concatenate([zero_bias, to_float(cross_value_bias_whole)])
    text_whole = lax.all_gather(text_states, "seq", axis=1, tiled=True)
    cross_kv = (rows_dot(text_whole.reshape(-1, model_width), c_keyval_full) + keyval_bias).astype(
        jnp.bfloat16
    )
    cross_kv = cross_kv.reshape(seq_count, -1, 2 * model_width)
    text_total = cross_kv.shape[1]
    text_allowed = jnp.arange(text_total)[None, :] < text_length[:, None]

    def cross_forward(packed):
        seq_queries, seq_keyval, seq_allowed = packed
        allowed = jnp.broadcast_to(seq_allowed[None, :], (local_len, text_total))
        return attend_forward(
            seq_queries, seq_keyval[:, :model_width], seq_keyval[:, model_width:], allowed
        )

    cross_blended_rows, cross_logsum = lax.map(
        cross_forward, (cross_queries, cross_kv, text_allowed)
    )
    cross_flat = cross_blended_rows.reshape(row_count, model_width)
    after_cross = after_self + rows_dot(cross_flat, c_output_full) + to_float(c_obias_full)
    (
        f_gain_full,
        feedforward_shift_whole,
        f_up_full,
        f_upbias_full,
        f_down_full,
        f_downbias_full,
        z_gain_full,
        z_shift_full,
    ) = (
        lax.all_gather(ffn_gain, ("dp", "seq"), axis=0, tiled=True),
        lax.all_gather(ffn_shift, ("dp", "seq"), axis=0, tiled=True),
        lax.all_gather(ffn_up, ("dp", "seq"), axis=0, tiled=True),
        lax.all_gather(ffn_upbias, ("dp", "seq"), axis=0, tiled=True),
        lax.all_gather(ffn_down, ("dp", "seq"), axis=0, tiled=True),
        lax.all_gather(ffn_downbias, ("dp", "seq"), axis=0, tiled=True),
        lax.all_gather(final_gain, ("dp", "seq"), axis=0, tiled=True),
        lax.all_gather(final_shift, ("dp", "seq"), axis=0, tiled=True),
    )
    normed_three = layer_norm(
        after_cross, to_float(f_gain_full), to_float(feedforward_shift_whole)
    ).astype(jnp.bfloat16)
    ffn_inner = rows_dot(normed_three, f_up_full) + to_float(f_upbias_full)
    active = jax.nn.gelu(ffn_inner).astype(jnp.bfloat16)
    after_ffn = after_cross + rows_dot(active, f_down_full) + to_float(f_downbias_full)
    valid_rows = ((first_pos + jnp.arange(local_len))[None, :] < unit_length[:, None]).astype(
        jnp.float32
    )
    valid_rows = valid_rows.reshape(row_count, 1)
    final_norm = layer_norm(after_ffn, to_float(z_gain_full), to_float(z_shift_full))
    layer_out = (
        (final_norm * valid_rows).astype(jnp.bfloat16).reshape(seq_count, local_len, model_width)
    )
    (
        f_gain_full,
        feedforward_shift_whole,
        f_up_full,
        f_upbias_full,
        f_down_full,
        f_downbias_full,
        z_gain_full,
        z_shift_full,
    ) = (
        lax.all_gather(ffn_gain, ("dp", "seq"), axis=0, tiled=True),
        lax.all_gather(ffn_shift, ("dp", "seq"), axis=0, tiled=True),
        lax.all_gather(ffn_up, ("dp", "seq"), axis=0, tiled=True),
        lax.all_gather(ffn_upbias, ("dp", "seq"), axis=0, tiled=True),
        lax.all_gather(ffn_down, ("dp", "seq"), axis=0, tiled=True),
        lax.all_gather(ffn_downbias, ("dp", "seq"), axis=0, tiled=True),
        lax.all_gather(final_gain, ("dp", "seq"), axis=0, tiled=True),
        lax.all_gather(final_shift, ("dp", "seq"), axis=0, tiled=True),
    )
    upstream = to_float(cotangent).reshape(row_count, model_width) * valid_rows
    grad_after_ffn, grad_zgain, grad_zshift = norm_back(
        after_ffn, to_float(z_gain_full), to_float(z_shift_full), upstream
    )
    grad_branch = grad_after_ffn.astype(jnp.bfloat16)
    grad_down = left_dot(active, grad_branch)
    grad_downbias = jnp.sum(to_float(grad_branch), axis=0)
    grad_active = right_dot(grad_branch, f_down_full)
    inner_value, gelu_back = jax.vjp(jax.nn.gelu, ffn_inner)
    grad_inner = gelu_back(grad_active)[0].astype(jnp.bfloat16)
    grad_up = left_dot(normed_three, grad_inner)
    grad_upbias = jnp.sum(to_float(grad_inner), axis=0)
    grad_normed_three = right_dot(grad_inner, f_up_full)
    grad_cross_norm, grad_fgain, grad_fshift = norm_back(
        after_cross, to_float(f_gain_full), to_float(feedforward_shift_whole), grad_normed_three
    )
    grad_after_cross = grad_after_ffn + grad_cross_norm
    ffn_sums = (
        lax.psum_scatter(grad_fgain, ("dp", "seq"), scatter_dimension=0, tiled=True),
        lax.psum_scatter(grad_fshift, ("dp", "seq"), scatter_dimension=0, tiled=True),
        lax.psum_scatter(grad_up, ("dp", "seq"), scatter_dimension=0, tiled=True),
        lax.psum_scatter(grad_upbias, ("dp", "seq"), scatter_dimension=0, tiled=True),
        lax.psum_scatter(grad_down, ("dp", "seq"), scatter_dimension=0, tiled=True),
        lax.psum_scatter(grad_downbias, ("dp", "seq"), scatter_dimension=0, tiled=True),
        lax.psum_scatter(grad_zgain, ("dp", "seq"), scatter_dimension=0, tiled=True),
        lax.psum_scatter(grad_zshift, ("dp", "seq"), scatter_dimension=0, tiled=True),
    )
    (
        c_gain_full,
        c_shift_full,
        c_query_full,
        c_qbias_full,
        c_keyval_full,
        cross_value_bias_whole,
        c_output_full,
        c_obias_full,
    ) = (
        lax.all_gather(cross_gain, ("dp", "seq"), axis=0, tiled=True),
        lax.all_gather(cross_shift, ("dp", "seq"), axis=0, tiled=True),
        lax.all_gather(cross_query, ("dp", "seq"), axis=0, tiled=True),
        lax.all_gather(cross_qbias, ("dp", "seq"), axis=0, tiled=True),
        lax.all_gather(cross_keyval, ("dp", "seq"), axis=0, tiled=True),
        lax.all_gather(cross_vbias, ("dp", "seq"), axis=0, tiled=True),
        lax.all_gather(cross_output, ("dp", "seq"), axis=0, tiled=True),
        lax.all_gather(cross_obias, ("dp", "seq"), axis=0, tiled=True),
    )
    cross_branch_gradient = grad_after_cross.astype(jnp.bfloat16)
    grad_coutput = left_dot(cross_flat, cross_branch_gradient)
    grad_cobias = jnp.sum(to_float(cross_branch_gradient), axis=0)
    grad_cross_mixed = right_dot(cross_branch_gradient, c_output_full).astype(jnp.bfloat16)
    grad_cross_mixed = grad_cross_mixed.reshape(seq_count, local_len, model_width)

    def cross_backward(packed):
        seq_queries, seq_keyval, seq_allowed, sequence_log_sum_exp, seq_upstream = packed
        allowed = jnp.broadcast_to(seq_allowed[None, :], (local_len, text_total))
        return attend_back(
            seq_queries,
            seq_keyval[:, :model_width],
            seq_keyval[:, model_width:],
            allowed,
            sequence_log_sum_exp,
            seq_upstream,
        )

    grad_cq, grad_ck, grad_cv = lax.map(
        cross_backward, (cross_queries, cross_kv, text_allowed, cross_logsum, grad_cross_mixed)
    )
    grad_ckv = lax.psum_scatter(
        jnp.concatenate([grad_ck, grad_cv], axis=-1).astype(jnp.bfloat16),
        "seq",
        scatter_dimension=1,
        tiled=True,
    ).astype(jnp.float32)
    grad_ckv = grad_ckv.astype(jnp.bfloat16).reshape(-1, 2 * model_width)
    grad_ckeyval = left_dot(text_states.reshape(-1, model_width), grad_ckv)
    grad_cvbias = jnp.sum(to_float(grad_ckv[:, model_width:]), axis=0)
    text_grad = right_dot(grad_ckv, c_keyval_full).astype(jnp.bfloat16).reshape(text_states.shape)
    grad_cq_low = grad_cq.reshape(row_count, model_width).astype(jnp.bfloat16)
    grad_cquery = left_dot(normed_two, grad_cq_low)
    grad_cqbias = jnp.sum(to_float(grad_cq_low), axis=0)
    grad_normed_two = right_dot(grad_cq_low, c_query_full)
    grad_self_norm, grad_cgain, grad_cshift = norm_back(
        after_self, to_float(c_gain_full), to_float(c_shift_full), grad_normed_two
    )
    grad_after_self = grad_after_cross + grad_self_norm
    cross_sums = (
        lax.psum_scatter(grad_cgain, ("dp", "seq"), scatter_dimension=0, tiled=True),
        lax.psum_scatter(grad_cshift, ("dp", "seq"), scatter_dimension=0, tiled=True),
        lax.psum_scatter(grad_cquery, ("dp", "seq"), scatter_dimension=0, tiled=True),
        lax.psum_scatter(grad_cqbias, ("dp", "seq"), scatter_dimension=0, tiled=True),
        lax.psum_scatter(grad_ckeyval, ("dp", "seq"), scatter_dimension=0, tiled=True),
        lax.psum_scatter(grad_cvbias, ("dp", "seq"), scatter_dimension=0, tiled=True),
        lax.psum_scatter(grad_coutput, ("dp", "seq"), scatter_dimension=0, tiled=True),
        lax.psum_scatter(grad_cobias, ("dp", "seq"), scatter_dimension=0, tiled=True),
    )
    (
        a_gain_full,
        a_shift_full,
        attention_input_weight_whole,
        a_qbias_full,
        a_vbias_full,
        a_output_full,
        a_obias_full,
    ) = (
        lax.all_gather(attn_gain, ("dp", "seq"), axis=0, tiled=True),
        lax.all_gather(attn_shift, ("dp", "seq"), axis=0, tiled=True),
        lax.all_gather(attn_inputs, ("dp", "seq"), axis=0, tiled=True),
        lax.all_gather(attn_qbias, ("dp", "seq"), axis=0, tiled=True),
        lax.all_gather(attn_vbias, ("dp", "seq"), axis=0, tiled=True),
        lax.all_gather(attn_output, ("dp", "seq"), axis=0, tiled=True),
        lax.all_gather(attn_obias, ("dp", "seq"), axis=0, tiled=True),
    )
    grad_self_branch = grad_after_self.astype(jnp.bfloat16)
    grad_aoutput = left_dot(self_flat, grad_self_branch)
    grad_aobias = jnp.sum(to_float(grad_self_branch), axis=0)
    grad_self_mixed = right_dot(grad_self_branch, a_output_full).astype(jnp.bfloat16)
    grad_self_mixed = grad_self_mixed.reshape(seq_count, local_len, model_width)

    def self_backward(packed):
        seq_queries, seq_keyval, sequence_log_sum_exp, seq_upstream = packed
        return attend_back(
            seq_queries,
            seq_keyval[:, :model_width],
            seq_keyval[:, model_width:],
            causal,
            sequence_log_sum_exp,
            seq_upstream,
        )

    gradient_self_query, grad_sk, grad_sv = lax.map(
        self_backward, (self_queries, self_keyval, self_logsum, grad_self_mixed)
    )
    gradient_self_keyvalue = lax.psum_scatter(
        jnp.concatenate([grad_sk, grad_sv], axis=-1).astype(jnp.bfloat16),
        "seq",
        scatter_dimension=1,
        tiled=True,
    ).astype(jnp.float32)
    grad_joined = (
        jnp.concatenate([gradient_self_query, gradient_self_keyvalue], axis=-1)
        .reshape(row_count, 3 * model_width)
        .astype(jnp.bfloat16)
    )
    grad_ainputs = left_dot(normed_one, grad_joined)
    grad_aqbias = jnp.sum(to_float(grad_joined[:, :model_width]), axis=0)
    grad_avbias = jnp.sum(to_float(grad_joined[:, 2 * model_width :]), axis=0)
    grad_normed_one = right_dot(grad_joined, attention_input_weight_whole)
    grad_input_norm, grad_again, grad_ashift = norm_back(
        inputs, to_float(a_gain_full), to_float(a_shift_full), grad_normed_one
    )
    tokens_grad = (
        (grad_after_self + grad_input_norm)
        .astype(jnp.bfloat16)
        .reshape(seq_count, local_len, model_width)
    )
    attn_sums = (
        lax.psum_scatter(grad_again, ("dp", "seq"), scatter_dimension=0, tiled=True),
        lax.psum_scatter(grad_ashift, ("dp", "seq"), scatter_dimension=0, tiled=True),
        lax.psum_scatter(grad_ainputs, ("dp", "seq"), scatter_dimension=0, tiled=True),
        lax.psum_scatter(grad_aqbias, ("dp", "seq"), scatter_dimension=0, tiled=True),
        lax.psum_scatter(grad_avbias, ("dp", "seq"), scatter_dimension=0, tiled=True),
        lax.psum_scatter(grad_aoutput, ("dp", "seq"), scatter_dimension=0, tiled=True),
        lax.psum_scatter(grad_aobias, ("dp", "seq"), scatter_dimension=0, tiled=True),
    )
    return (layer_out, tokens_grad, text_grad, *attn_sums, *cross_sums, *ffn_sums)


MESH_ID = pl.DeviceIdType.MESH
ANYWHERE = pl.BlockSpec(memory_space=pl.ANY)
VMEM_LIMIT = 56 * 2**20


class Place:
    def __init__(self, depth):
        group = lax.axis_index("dp")
        self.depth = depth
        self.z = group // 4
        self.x = lax.rem(group // 2, 2)
        self.core = lax.rem(group, 2)
        self.y = lax.axis_index("seq")

    def device(self, z, x, core, y):
        return {"dp": (z * 2 + x) * 2 + core, "seq": y}

    def along_z(self, step):
        return self.device(lax.rem(self.z + step, self.depth), self.x, self.core, self.y)

    def across_x(self):
        return self.device(self.z, 1 - self.x, self.core, self.y)

    def across_y(self):
        return self.device(self.z, self.x, self.core, 1 - self.y)

    def sibling(self):
        return self.device(self.z, self.x, 1 - self.core, self.y)

    def along(self, axis):
        if axis == "z":
            return [self.along_z(step) for step in range(1, self.depth)]
        return [self.across_x() if axis == "x" else self.across_y()]

    def greet(self):
        partners = [self.along_z(step) for step in range(1, self.depth)]
        partners += [self.across_x(), self.across_y(), self.sibling()]
        barrier = pltpu.get_barrier_semaphore()
        for partner in partners:
            pl.semaphore_signal(barrier, inc=1, device_id=partner, device_id_type=MESH_ID)
        pl.semaphore_wait(barrier, len(partners))


def remote(source, target, sems, item, index, device):
    send, receive = sems
    return pltpu.make_async_remote_copy(
        src_ref=source,
        dst_ref=target,
        send_sem=send.at[item, index],
        recv_sem=receive.at[item, index],
        device_id=device,
        device_id_type=MESH_ID,
    )


def pipelined(phase_lists):
    count = max(len(phases) + first for first, phases in enumerate(phase_lists))
    stages = []
    for turn in range(count):
        work = [
            phases[turn - first]
            for first, phases in enumerate(phase_lists)
            if 0 <= turn - first < len(phases)
        ]
        stages.append(work)
    return stages


ORDERS = (("z", "x", "y"), ("z", "y", "x"))


def gather_phases(place, shard, whole, rows, cols, sems, local, stop, item):
    half = rows.size // 2
    halves = (pl.ds(rows.start, half), pl.ds(rows.start + half, half))
    here = {"z": place.z, "x": place.x, "y": place.y}
    every = slice(None)

    def view(done, some_rows, core):
        at = {axis: every if axis in done else here[axis] for axis in here}
        return whole.at[at["z"], at["x"], core, at["y"], some_rows, cols]

    def copies(phase):
        made = []
        if phase == 3:
            both = view("zxy", rows, place.core)
            return [remote(both, both, sems, item, 2 * place.depth + 2, place.sibling())]
        slot = sum(len(place.along(o[p])) for o in ORDERS for p in range(phase))
        for some_rows, order in zip(halves, ORDERS):
            target = view(order[:phase], some_rows, place.core)
            source = shard.at[some_rows, cols] if phase == 0 else target
            for device in place.along(order[phase]):
                made.append(remote(source, target, sems, item, slot, device))
                slot += 1
        return made

    def take():
        return pltpu.make_async_copy(shard.at[rows, cols], stop, local.at[item, 0])

    def put():
        return pltpu.make_async_copy(stop, view("", rows, place.core), local.at[item, 1])

    def start(phase):
        for copy in copies(phase):
            copy.start()

    def wait(phase):
        for copy in copies(phase):
            copy.wait()

    def opening():
        start(0)
        take().start()
        take().wait()
        put().start()

    def turn(phase):
        def run():
            wait(phase - 1)
            if phase == 1:
                put().wait()
            start(phase)

        return run

    return [opening, turn(1), turn(2), turn(3), lambda: wait(3)]


def copy_sems(items, depth):
    width = 2 * depth + 3
    return [
        pltpu.SemaphoreType.DMA((items, width)),
        pltpu.SemaphoreType.DMA((items, width)),
        pltpu.SemaphoreType.DMA((items, 2)),
    ]


ITEM = 1024


def weight_items(shape):
    rows, cols = shape
    return [
        (pl.ds(r, 32), pl.ds(c, min(ITEM, cols)))
        for r in range(0, rows, 32)
        for c in range(0, cols, min(ITEM, cols))
    ]


QB = 256


def nt(a,b): return lax.dot_general(a,b,(((1,),(1,)),((),())),preferred_element_type=jnp.float32)
def nn(a,b): return jnp.dot(a,b,preferred_element_type=jnp.float32)
def half_mask(rows):
    lane=lax.broadcasted_iota(jnp.int32,(rows,128),1)
    return lane<64
def pick(block,h,first):
    zero=jnp.zeros_like(block)
    return jnp.where(first,block,zero) if h==0 else jnp.where(first,zero,block)
def scores(keys, queries, diagonal, bias):
    s = nt(keys, queries)
    if diagonal:
        r = lax.broadcasted_iota(jnp.int32, s.shape, 0)
        c = lax.broadcasted_iota(jnp.int32, s.shape, 1)
        s = jnp.where(r <= c, s, MASKED)
    if bias is not None:
        s = s + bias
    return s


def segments(causal,qb,keys):
    if not causal: return [(0,keys,False)]
    out=[]
    if qb>0: out.append((0,qb*QB,False))
    out.append((qb*QB,(qb+1)*QB,True))
    return out
def attend_pair(causal, rows, keys, get_q, get_k, get_v, bias, put, lse_ref):
    vt = get_v(0, keys).T
    first = half_mask(QB)
    for qb in range(rows // QB):
        sl = slice(qb * QB, (qb + 1) * QB)
        q = get_q(qb * QB, (qb + 1) * QB) * jnp.bfloat16(0.125)
        outs = []
        for h in (0, 1):
            qs = pick(q, h, first)
            segs = segments(causal, qb, keys)
            ss = [scores(get_k(lo, hi), qs, d, bias) for lo, hi, d in segs]
            m = functools.reduce(jnp.maximum, [jnp.max(s, axis=0, keepdims=True) for s in ss])
            ps = [jnp.exp(s - m) for s in ss]
            l = functools.reduce(jnp.add, [jnp.sum(p, axis=0, keepdims=True) for p in ps])
            ot = functools.reduce(
                jnp.add,
                [
                    nn(vt[h * 64 : (h + 1) * 64, lo:hi], p.astype(jnp.bfloat16))
                    for p, (lo, hi, _) in zip(ps, segs)
                ],
            )
            outs.append(ot * (1.0 / l))
            lse_ref[h : h + 1, sl] = m + jnp.log(l)
        put(sl, jnp.concatenate(outs, axis=0).T.astype(jnp.bfloat16))


def attend_back_pair(
    causal, rows, keys, get_q, get_k, get_v, get_o, get_do, lse_ref, bias, put_dq, put_dk, put_dv,
    dk_acc, dv_acc,
):
    kt = (get_k(0, keys) * jnp.bfloat16(0.125)).T
    first = half_mask(QB)
    order = list(range(rows // QB))
    if causal:
        order = order[::-1]
    for qb in order:
        sl = slice(qb * QB, (qb + 1) * QB)
        q = get_q(sl.start, sl.stop) * jnp.bfloat16(0.125)
        do = get_do(sl.start, sl.stop)
        dt = (do.astype(jnp.float32) * get_o(sl.start, sl.stop).astype(jnp.float32)).T
        outs, new = [], {}
        for h in (0, 1):
            qs, doh = pick(q, h, first), pick(do, h, first)
            delta = jnp.sum(dt[h * 64 : (h + 1) * 64, :], axis=0, keepdims=True)
            lse = lse_ref[h : h + 1, sl]
            dqt = None
            for lo, hi, diagonal in segments(causal, qb, keys):
                p = jnp.exp(scores(get_k(lo, hi), qs, diagonal, bias) - lse)
                dp = nt(get_v(lo, hi), doh)
                ds = (p * (dp - delta)).astype(jnp.bfloat16)
                part = nn(kt[h * 64 : (h + 1) * 64, lo:hi], ds)
                dqt = part if dqt is None else dqt + part
                dv, dk = nn(p.astype(jnp.bfloat16), doh), nn(ds, qs)
                if (lo, hi) in new:
                    dv, dk = new[lo, hi][0] + dv, new[lo, hi][1] + dk
                new[lo, hi] = (dv, dk)
            outs.append(dqt)
        put_dq(sl, jnp.concatenate(outs, axis=0).T.astype(jnp.bfloat16))
        for (lo, hi), (dv, dk) in new.items():
            if qb == order[0]:
                dv_acc[lo:hi, :] = dv
                dk_acc[lo:hi, :] = dk
            else:
                dv_acc[lo:hi, :] += dv
                dk_acc[lo:hi, :] += dk
    put_dk(dk_acc[0:keys, :].astype(jnp.bfloat16))
    put_dv(dv_acc[0:keys, :].astype(jnp.bfloat16))


BLOCK = 256
MATMUL_ROWS = 512
RING = 6

VECTOR_COUNT = 15
(
    A_GAIN, A_SHIFT, A_QBIAS, A_VBIAS, A_OBIAS, C_GAIN, C_SHIFT, C_QBIAS, C_VBIAS, C_OBIAS,
    F_GAIN, F_SHIFT, F_DOWNBIAS, Z_GAIN, Z_SHIFT,
) = range(VECTOR_COUNT)
F_UPBIAS = VECTOR_COUNT


def block_rows(index, size):
    return pl.ds(pl.multiple_of(index * size, size), size)


def lanes(index, size):
    return pl.ds(pl.multiple_of(index * size, size), size)


def center_and_scale(values):
    center = values - jnp.mean(values, axis=-1, keepdims=True)
    spread = jnp.mean(center * center, axis=-1, keepdims=True)
    scale = lax.rsqrt(spread + EPSILON)
    return center * scale, scale


def norm_pull(unit, scale, pulled):
    inner = jnp.mean(pulled * unit, axis=-1, keepdims=True)
    return scale * (pulled - jnp.mean(pulled, axis=-1, keepdims=True) - unit * inner)


def gelu_and_slope(values):
    root = math.sqrt(2.0 / math.pi)
    square = values * values
    bend = jnp.tanh(root * (values + 0.044715 * (values * square)))
    rise = root * (1.0 + 3.0 * 0.044715 * square)
    result = 0.5 * values * (1.0 + bend)
    slope = 0.5 * (1.0 + bend) + 0.5 * values * ((1.0 - bend * bend) * rise)
    return result, slope


def spread_vectors(packed):
    rows = packed.shape[0]
    width = rows
    lane = lax.broadcasted_iota(jnp.int32, (128, width), 1)
    source = lax.broadcasted_iota(jnp.int32, (128, width), 0)
    select = jnp.where(lax.rem(lane, 32) == source, 1.0, 0.0).astype(jnp.bfloat16)
    wide = jnp.dot(packed, select, preferred_element_type=jnp.float32)
    row = lax.broadcasted_iota(jnp.int32, (rows, width), 0)
    lane = lax.broadcasted_iota(jnp.int32, (rows, width), 1)
    wide = jnp.where(row // 32 == lane // 32, wide, 0.0)
    return jnp.sum(wide.reshape(rows // 32, 32, width), axis=0)


class Copies:
    def __init__(self, sems):
        self.sems = sems
        self.open = {}
        self.used = 0

    def start(self, source, target):
        copy = pltpu.make_async_copy(source, target, self.sems.at[self.used])
        self.used += 1
        copy.start()
        return copy


def forward_kernel(depth, sizes, *refs):
    refs = list(refs)

    def take(count):
        taken = refs[:count]
        del refs[:count]
        return taken

    shard_count = len(sizes)
    tokens, texts, cots, unit_length, text_length = take(5)
    shards = take(shard_count)
    wholes = take(shard_count)
    (
        o_tokens, o_text, o_h1, o_qkv, o_o1, o_after_self, o_h2, o_cq, o_ckv, o_o2,
        o_after_cross, o_h3, o_active, o_slope, o_gaf, o_gbr, o_layer,
    ) = take(17)
    vec, lse1, lse2, zgrads = take(4)
    tok, txt, cot, x, o1, cq, ckv, o2, resid, h2, ring, slopes, packed = take(13)
    stops = take(sum(len(weight_items(s)) for s in sizes))
    send, receive, local, sw_send, sw_receive, sw_local, loads, outs = take(8)

    place = Place(depth)
    y = place.y
    rows = resid.shape[0]
    width = resid.shape[1]
    part = rows // 2
    copies = Copies(outs)
    phases, chunks, item = [], [], 0
    for index, size in enumerate(sizes):
        for r, c in weight_items(size):
            phase = gather_phases(
                place, shards[index], wholes[index], r, c, (send, receive), local, stops[item], item
            )
            phases.append(phase)
            if index > 0:
                chunks.append((wholes[index], c))
            item += 1
    first = phases[0]
    stages = pipelined(phases[1:])
    stages = [([first[k]] if k < len(first) else []) + s for k, s in enumerate(stages)]

    def swapping(k, source, target):
        def away():
            return remote(source.at[1 - y], target.at[y], (sw_send, sw_receive), k, 0, place.across_y())

        def home():
            return pltpu.make_async_copy(source.at[y], target.at[y], sw_local.at[k])

        def opening():
            away().start()
            home().start()

        def closing():
            away().wait()
            home().wait()

        return opening, closing

    token_swap = swapping(0, tokens, tok)
    text_swap = swapping(1, texts, txt)
    cot_swap = swapping(2, cots, cot)

    def load(chunk):
        whole, cols = chunks[chunk]
        return pltpu.make_async_copy(
            whole.at[:, :, :, :, :, cols], ring.at[chunk % RING], loads.at[chunk]
        )

    def stage(k):
        for one in reversed(stages[k]):
            one()
        if k >= 4:
            load(k - 4).start()

    def weight(chunk):
        return ring[chunk % RING].reshape(width, width)

    def row(index):
        return vec[index : index + 1, :]

    def looped(count, body, due=()):
        @pl.loop(0, count)
        def _(j):
            for at, k in due:

                @pl.when(j == at)
                def _(k=k):
                    stage(k)

            body(j)

    place.greet()
    token_swap[0]()
    for k in range(3):
        stage(k)
    text_swap[0]()
    stage(3)
    stage(4)
    pack = pltpu.make_async_copy(wholes[0], packed, outs.at[copies.used])
    copies.used += 1
    pack.start()
    pack.wait()
    vec[...] = spread_vectors(packed[...].reshape(-1, 128))
    token_swap[1]()
    done_tokens = copies.start(tok, o_tokens)

    def token_block(b):
        half = b // (part // BLOCK)
        inner = lax.rem(b, part // BLOCK)
        return tok[half, block_rows(inner, BLOCK), :].astype(jnp.float32)

    def norm_one(b):
        unit, _ = center_and_scale(token_block(b))
        at = block_rows(b, BLOCK)
        x[at, 3 * width :] = (unit * row(A_GAIN) + row(A_SHIFT)).astype(jnp.bfloat16)
        resid[at, :] = token_block(b)

    looped(rows // BLOCK, norm_one)
    done_h1 = copies.start(x.at[:, pl.ds(3 * width, width)], o_h1)

    def project(chunk):
        bias = (row(A_QBIAS), None, row(A_VBIAS))[chunk]
        load(chunk).wait()

        def block(b):
            at = block_rows(b, MATMUL_ROWS)
            value = nn(x[at, 3 * width :], weight(chunk))
            if bias is not None:
                value = value + bias
            x[at, chunk * width : (chunk + 1) * width] = value.astype(jnp.bfloat16)

        looped(rows // MATMUL_ROWS, block)

    project(0)
    stage(5)
    project(1)
    stage(6)
    project(2)
    done_qkv = copies.start(x.at[:, pl.ds(0, 3 * width)], o_qkv)
    pairs = width // 128

    def self_pair(j):
        def part_of(base):
            return lambda lo, hi: x[lo:hi, lanes(j + base * pairs, 128)]

        def put(sl, value):
            o1[sl, lanes(j, 128)] = value

        attend_pair(
            True, rows, rows, part_of(0), part_of(1), part_of(2), None, put, lse1.at[j]
        )

    looped(pairs, self_pair, ((2, 7), (4, 8), (7, 9)))
    done_o1 = copies.start(o1, o_o1)
    load(3).wait()

    def out_block(b):
        at = block_rows(b, MATMUL_ROWS)
        resid[at, :] = resid[at, :] + nn(o1[at, :], weight(3)) + row(A_OBIAS)

    looped(rows // MATMUL_ROWS, out_block)
    done_after_self = copies.start(resid, o_after_self)

    def norm_two(b):
        at = block_rows(b, BLOCK)
        unit, _ = center_and_scale(resid[at, :])
        h2[at, :] = (unit * row(C_GAIN) + row(C_SHIFT)).astype(jnp.bfloat16)

    looped(rows // BLOCK, norm_two)
    done_h2 = copies.start(h2, o_h2)
    stage(10)
    load(4).wait()

    def cq_block(b):
        at = block_rows(b, MATMUL_ROWS)
        cq[at, :] = (nn(h2[at, :], weight(4)) + row(C_QBIAS)).astype(jnp.bfloat16)

    looped(rows // MATMUL_ROWS, cq_block)
    done_cq = copies.start(cq, o_cq)
    text_swap[1]()
    cot_swap[0]()
    done_text = copies.start(txt, o_text)
    text = txt[...].reshape(-1, width)
    text_rows = text.shape[0]
    load(5).wait()
    ckv[:, :width] = nn(text, weight(5)).astype(jnp.bfloat16)
    load(6).wait()
    ckv[:, width:] = (nn(text, weight(6)) + row(C_VBIAS)).astype(jnp.bfloat16)
    done_ckv = copies.start(ckv, o_ckv)
    bias = text_mask(text_rows, text_length[y])

    def cross_pair(j):
        def put(sl, value):
            o2[sl, lanes(j, 128)] = value

        attend_pair(
            False, rows, text_rows,
            lambda lo, hi: cq[lo:hi, lanes(j, 128)],
            lambda lo, hi: ckv[lo:hi, lanes(j, 128)],
            lambda lo, hi: ckv[lo:hi, lanes(j + pairs, 128)],
            bias, put, lse2.at[j],
        )

    looped(pairs, cross_pair, ((1, 11), (4, 12), (7, 13)))
    done_o2 = copies.start(o2, o_o2)
    load(7).wait()
    done_after_self.wait()

    def cross_out_block(b):
        at = block_rows(b, MATMUL_ROWS)
        resid[at, :] = resid[at, :] + nn(o2[at, :], weight(7)) + row(C_OBIAS)

    looped(rows // MATMUL_ROWS, cross_out_block)
    done_after_cross = copies.start(resid, o_after_cross)
    done_o1.wait()
    h3 = o1

    def norm_three(b):
        at = block_rows(b, BLOCK)
        unit, _ = center_and_scale(resid[at, :])
        h3[at, :] = (unit * row(F_GAIN) + row(F_SHIFT)).astype(jnp.bfloat16)

    looped(rows // BLOCK, norm_three)
    done_h3 = copies.start(h3, o_h3)
    done_h1.wait()
    done_qkv.wait()
    waiting = []

    def up(q):
        load(8 + q).wait()
        slope_at = slopes.at[q % 2]

        def block(b):
            at = block_rows(b, BLOCK)
            inner = nn(h3[at, :], weight(8 + q)) + row(F_UPBIAS + q)
            active, slope = gelu_and_slope(inner)
            x[at, q * width : (q + 1) * width] = active.astype(jnp.bfloat16)
            slope_at[at, :] = slope.astype(jnp.bfloat16)

        if q >= 2:
            waiting[q - 2].wait()
        looped(rows // BLOCK, block)
        span = pl.ds(q * width, width)
        waiting.append(copies.start(slope_at, o_slope.at[:, span]))

    stage(14)
    up(0)
    up(1)
    stage(15)
    up(2)
    up(3)
    done_active = copies.start(x, o_active)
    done_after_cross.wait()

    def down(q):
        load(12 + q).wait()

        def block(b):
            at = block_rows(b, MATMUL_ROWS)
            resid[at, :] += nn(x[at, q * width : (q + 1) * width], weight(12 + q))

        looped(rows // MATMUL_ROWS, block)

    for q in range(4):
        stage(16 + q)
        down(q)
    cot_swap[1]()
    done_cq.wait()
    done_o2.wait()
    valid_count = unit_length[y]
    zgrads[...] = jnp.zeros_like(zgrads)
    gbr, layer = cq, o2

    def last_block(b):
        at = block_rows(b, BLOCK)
        unit, scale = center_and_scale(resid[at, :] + row(F_DOWNBIAS))
        position = b * BLOCK + lax.broadcasted_iota(jnp.int32, (BLOCK, 1), 0)
        valid = jnp.where(position < valid_count, 1.0, 0.0)
        layer[at, :] = ((unit * row(Z_GAIN) + row(Z_SHIFT)) * valid).astype(jnp.bfloat16)
        half = b // (part // BLOCK)
        inner = lax.rem(b, part // BLOCK)
        upstream = cot[half, block_rows(inner, BLOCK), :].astype(jnp.float32) * valid
        zgrads[0:1, :] += jnp.sum(upstream * unit, axis=0, keepdims=True)
        zgrads[1:2, :] += jnp.sum(upstream, axis=0, keepdims=True)
        grad = norm_pull(unit, scale, upstream * row(Z_GAIN))
        low = grad.astype(jnp.bfloat16)
        gbr[at, :] = low
        zgrads[2:3, :] += jnp.sum(low.astype(jnp.float32), axis=0, keepdims=True)
        resid[at, :] = grad

    looped(rows // BLOCK, last_block)
    ending = [
        copies.start(resid, o_gaf), copies.start(gbr, o_gbr), copies.start(layer, o_layer),
    ]
    ending += [done_tokens, done_h2, done_text, done_ckv, done_h3, done_active]
    for copy in ending + waiting[2:]:
        copy.wait()


def text_mask(text_rows, count):
    position = lax.broadcasted_iota(jnp.int32, (text_rows, QB), 0)
    return jnp.where(position < count, 0.0, MASKED)


def forward(depth, number, tokens, texts, cots, unit_length, text_length, shards):
    rows, width = 2 * tokens.shape[1], tokens.shape[2]
    text_rows = 2 * texts.shape[1]
    hidden = 4 * width
    pairs = width // 128
    sizes = [s.shape for s in shards]
    items = sum(len(weight_items(s)) for s in sizes)
    low, full = jnp.bfloat16, jnp.float32

    def shape(*dims, kind=low):
        return jax.ShapeDtypeStruct(dims, kind)

    def vmem(*dims, kind=low):
        return pltpu.VMEM(dims, kind)

    big = shape(rows, width)
    exact = shape(rows, width, kind=full)
    outs = [shape(depth, 2, 2, 2, *s) for s in sizes]
    outs += [
        shape(*tokens.shape), shape(*texts.shape), big, shape(rows, 3 * width), big, exact, big, big,
        shape(text_rows, 2 * width), big, exact, big, shape(rows, hidden), shape(rows, hidden),
        exact, big, big,
    ]
    small = [
        shape(32, width, kind=full), shape(pairs, 2, rows, kind=full),
        shape(pairs, 2, rows, kind=full), shape(8, width, kind=full),
    ]
    scratch = [
        vmem(*tokens.shape), vmem(*texts.shape), vmem(*cots.shape), vmem(rows, hidden),
        vmem(rows, width), vmem(rows, width), vmem(text_rows, 2 * width), vmem(rows, width),
        vmem(rows, width, kind=full), vmem(rows, width), vmem(RING, depth, 2, 2, 2, 32, width),
        vmem(2, rows, width), vmem(depth, 2, 2, 2, *sizes[0]),
    ]
    scratch += [vmem(r.size, c.size) for s in sizes for r, c in weight_items(s)]
    scratch += copy_sems(items, depth)
    scratch += [
        pltpu.SemaphoreType.DMA((3, 1)), pltpu.SemaphoreType.DMA((3, 1)),
        pltpu.SemaphoreType.DMA((3,)), pltpu.SemaphoreType.DMA((items,)),
        pltpu.SemaphoreType.DMA((32,)),
    ]
    memory = pl.BlockSpec(memory_space=pltpu.SMEM)
    results = pl.pallas_call(
        functools.partial(forward_kernel, depth, sizes),
        out_shape=outs + small,
        in_specs=[ANYWHERE] * 3 + [memory] * 2 + [ANYWHERE] * len(shards),
        out_specs=[ANYWHERE] * len(outs) + [pl.BlockSpec(memory_space=pltpu.VMEM)] * len(small),
        scratch_shapes=scratch,
        compiler_params=pltpu.CompilerParams(
            collective_id=number, has_side_effects=True, vmem_limit_bytes=VMEM_LIMIT
        ),
        name="forward",
    )(tokens, texts, cots, unit_length, text_length, *shards)
    return list(results[: len(sizes)]), list(results[len(sizes) :])


BACK_RING = 3
WEIGHT_RING = 2
NORM_BLOCK = 128


def ring_scratch(depth, slots, rows, cols, dtype):
    half = rows // 2
    return [
        pltpu.VMEM((slots, depth, 2, 2, 2, rows, cols), dtype),
        pltpu.VMEM((min(slots, 2), depth, 2, 2, rows, cols), dtype),
        pltpu.VMEM((slots, depth, 2, half, cols), dtype),
        pltpu.VMEM((slots, depth, half, cols), dtype),
        pltpu.VMEM((slots, depth - 1, half, cols), dtype),
        pltpu.VMEM((slots, depth, 2, half, cols), dtype),
        pltpu.VMEM((slots, depth - 1, 2, half, cols), dtype),
        pltpu.VMEM((slots, half, cols), dtype),
    ]


def piece_phases(place, put_result, bufs, sems, item):
    slots, depth = bufs[0].shape[0], bufs[0].shape[1]
    slot = item % slots
    piece = bufs[0].at[slot]
    came = bufs[1].at[item % bufs[1].shape[0]]
    a_y, a_x, a_z, b_x, b_z, b_y = (buf.at[slot] for buf in bufs[2:])
    half = bufs[7].shape[1]
    low, high = pl.ds(0, half), pl.ds(half, half)
    z, x, core, y = place.z, place.x, place.core, place.y
    every = slice(None)

    def send(a, b, index, device):
        return remote(a, b, sems, item, index, device)

    def copies(phase):
        if phase == 0:
            return [send(piece.at[every, every, 1 - core], came, 0, place.sibling())]
        if phase == 1:
            return [
                send(piece.at[every, every, core, 1 - y, low], a_y, 1, place.across_y()),
                send(piece.at[every, 1 - x, core, every, high], b_x, 2, place.across_x()),
            ]
        if phase == 2:
            return [send(a_y.at[every, 1 - x], a_x, 3, place.across_x())] + [
                send(
                    b_x.at[lax.rem(z + step, depth)], b_z.at[step - 1], 3 + step,
                    place.along_z(step),
                )
                for step in range(1, depth)
            ]
        return [send(b_z.at[0, 1 - y], b_y, 3 + depth, place.across_y())] + [
            send(
                a_x.at[lax.rem(z + step, depth)], a_z.at[step - 1], 3 + depth + step,
                place.along_z(step),
            )
            for step in range(1, depth)
        ]

    def start(phase):
        for copy in copies(phase):
            copy.start()

    def wait(phase):
        for copy in copies(phase):
            copy.wait()

    def wide(values):
        return values.astype(jnp.float32)

    def after_core():
        wait(0)

        @pl.loop(0, depth)
        def _(k):
            for i in range(2):
                for j in range(2):
                    piece[k, i, core, j] = piece[k, i, core, j] + came[k, i, j]

        start(1)

    def after_one():
        wait(1)

        @pl.loop(0, depth)
        def _(k):
            for i in range(2):
                a_y[k, i] = a_y[k, i] + piece[k, i, core, y, low]
                b_x[k, i] = b_x[k, i] + piece[k, x, core, i, high]

        start(2)

    def after_two():
        wait(2)

        @pl.loop(0, depth)
        def _(k):
            a_x[k] = a_x[k] + a_y[k, x]

        for i in range(2):
            total = wide(b_x[z, i])
            for step in range(1, depth):
                total = total + wide(b_z[step - 1, i])
            b_z[0, i] = total.astype(b_z.dtype)
        start(3)

    def closing():
        wait(3)
        total = wide(a_x[z])
        for step in range(1, depth):
            total = total + wide(a_z[step - 1])
        put_result(low, total)
        put_result(high, wide(b_z[0, y]) + wide(b_y[...]))

    return [lambda: start(0), after_core, after_one, after_two, closing]


def gather_vectors(vectors, first, shards):
    width = vectors.shape[1]
    row = first + lax.broadcasted_iota(jnp.int32, (shards, 32, width), 0)
    lane = lax.broadcasted_iota(jnp.int32, (shards, 32, width), 2)
    parts = jnp.where(row == lane // 32, vectors[None], 0.0).reshape(shards * 32, width)
    source = lax.broadcasted_iota(jnp.int32, (width, 128), 0)
    lane = lax.broadcasted_iota(jnp.int32, (width, 128), 1)
    select = jnp.where(lax.rem(source, 32) == lane, 1.0, 0.0)
    return jnp.dot(
        parts, select, precision=lax.Precision.HIGHEST, preferred_element_type=jnp.float32
    )


def backward_kernel(depth, *refs):
    refs = list(refs)

    def take(count):
        taken = refs[:count]
        del refs[:count]
        return taken

    w_in, w_out, w_cq, w_ckv, w_co, w_up = take(6)
    w_downs = take(4)
    (
        i_tokens, i_text, i_h1, i_qkv, i_o1, i_after_self, i_h2, i_cq, i_ckv, i_o2, i_after_cross,
        i_h3, i_active, i_slope, i_gaf, i_gbr, i_layer,
    ) = take(17)
    vec, lse1, lse2, zgrads, text_length = take(5)
    o_layer, o_tokens, o_text = take(3)
    s_in, s_out, s_cq, s_ckv, s_co, s_up = take(6)
    s_downs = take(4)
    (s_small,) = take(1)
    p, q_buf, resid, dh, low, h3, extra, ckv, dckv, text, tgrad, src, vg, ka, va = take(15)
    ring = take(1)[0]
    bufs = take(8)
    small_bufs = take(8)
    sems = take(2)
    small_sems = take(2)
    swap_send, swap_receive, swap_local, loads, fetches = take(5)

    place = Place(depth)
    y = place.y
    rows, width = resid.shape
    part = rows // 2
    pairs = width // 128
    shards = depth * 8
    text_rows = ckv.shape[0]
    fetched = Copies(fetches)
    fetch = fetched.start

    targets = [(s, 0) for s in s_downs] + [(s_up, c) for c in range(4)]
    targets += [(s_co, 0), (s_cq, 0), (s_ckv, 0), (s_ckv, 1), (s_out, 0)]
    targets += [(s_in, c) for c in range(3)]

    def keeping(target, column):
        def put(some_rows, value):
            target[some_rows, column * width : (column + 1) * width] = value

        return put

    phases = [
        piece_phases(place, keeping(target, column), bufs, sems, item)
        for item, (target, column) in enumerate(targets)
    ]

    def put_small(some_rows, value):
        s_small[some_rows, :] = value

    small_phases = piece_phases(place, put_small, small_bufs, small_sems, 0)
    stages = pipelined(phases + [small_phases])

    def stage(k):
        for one in stages[k]:
            one()

    def produce(item, get_left, right):
        piece = bufs[0].at[item % BACK_RING]

        @pl.loop(0, 2)
        def _(b):
            value = left_dot(get_left(lanes(b, width // 2)), right())
            value = value.astype(jnp.bfloat16).reshape(depth // 2, 2, 2, 2, width // shards, width)
            piece[pl.ds(b * (depth // 2), depth // 2)] = value

        stage(item)

    order = []
    for k in range(4):
        order += [(w_downs[k], 0), (w_up, k)]
    order += [(w_co, 0), (w_ckv, 0), (w_ckv, 1), (w_cq, 0), (w_out, 0)]
    order += [(w_in, c) for c in range(3)]

    def load(n):
        whole, column = order[n]
        return pltpu.make_async_copy(
            whole.at[:, :, :, :, :, pl.ds(column * width, width)],
            ring.at[n % WEIGHT_RING],
            loads.at[n],
        )

    def weight(n):
        return ring[n % WEIGHT_RING].reshape(width, width)

    def ready(n):
        load(n).wait()

    def finished(n):
        if n + WEIGHT_RING < len(order):
            load(n + WEIGHT_RING).start()

    def row(index):
        return vec[index : index + 1, :]

    def add_row(index, value):
        vg[index : index + 1, :] += jnp.sum(value, axis=0, keepdims=True)

    def looped(count, body):
        @pl.loop(0, count)
        def _(j):
            body(j)

    def by_blocks(body, size=MATMUL_ROWS):
        looped(rows // size, lambda b: body(block_rows(b, size)))

    def column(buf, k):
        return lambda some_lanes: buf[:, pl.ds(k * width + some_lanes.start, some_lanes.size)]

    def plain(buf):
        return lambda some_lanes: buf[:, some_lanes]

    def norm_step(source, gain, shift, next_bias):
        blocks = rows // NORM_BLOCK

        def bring(b, slot):
            return pltpu.make_async_copy(
                source.at[block_rows(b, NORM_BLOCK), :], src.at[slot], swap_local.at[3 + slot]
            )

        bring(0, 0).start()

        def step(b):
            slot = lax.rem(b, 2)
            bring(b, slot).wait()

            @pl.when(b + 1 < blocks)
            def _():
                bring(b + 1, 1 - slot).start()

            at = block_rows(b, NORM_BLOCK)
            unit, scale = center_and_scale(src[slot])
            pulled = dh[at, :]
            add_row(gain, pulled * unit)
            add_row(shift, pulled)
            total = resid[at, :] + norm_pull(unit, scale, pulled * row(gain))
            resid[at, :] = total
            rounded = total.astype(jnp.bfloat16)
            low[at, :] = rounded
            add_row(next_bias, rounded.astype(jnp.float32))

        looped(blocks, step)

    def swap_out(k, get_source, target, local_source):
        def away():
            return remote(
                get_source(1 - y), target.at[y], (swap_send, swap_receive), k, 0, place.across_y()
            )

        def home():
            return pltpu.make_async_copy(local_source, target.at[y], swap_local.at[k])

        return away, home

    place.greet()
    for n in range(WEIGHT_RING):
        load(n).start()
    got_low = fetch(i_gbr, low)
    got_active = [
        fetch(i_active.at[:, pl.ds(k * width, width)], p.at[:, pl.ds(k * width, width)])
        for k in range(4)
    ]
    got_slope = [
        fetch(i_slope.at[:, pl.ds(k * width, width)], q_buf.at[:, pl.ds(k * width, width)])
        for k in range(4)
    ]
    got_resid = fetch(i_gaf, resid)
    got_h3 = fetch(i_h3, h3)
    keep = extra.at[pl.ds(0, part)]
    got_keep = fetch(i_layer.at[y], keep)
    got_ckv = fetch(i_ckv, ckv)
    got_text = fetch(i_text, text)
    vg[...] = jnp.zeros_like(vg)
    vg[Z_GAIN : Z_GAIN + 1, :] = zgrads[0:1, :]
    vg[Z_SHIFT : Z_SHIFT + 1, :] = zgrads[1:2, :]
    vg[F_DOWNBIAS : F_DOWNBIAS + 1, :] = zgrads[2:3, :]
    layer_away, layer_home = swap_out(0, lambda k: i_layer.at[k], o_layer, keep)
    layer_away().start()

    got_low.wait()
    for k in range(4):
        got_active[k].wait()
        produce(k, column(p, k), lambda: low[...])
        n = 2 * k
        got_slope[k].wait()
        ready(n)
        span = slice(k * width, (k + 1) * width)

        def inner_block(b, n=n, span=span, k=k):
            at = block_rows(b, BLOCK)
            grad = nt(low[at, :], weight(n)) * q_buf[at, span].astype(jnp.float32)
            rounded = grad.astype(jnp.bfloat16)
            q_buf[at, span] = rounded
            add_row(F_UPBIAS + k, rounded.astype(jnp.float32))

        looped(rows // BLOCK, inner_block)
        finished(n)
        ready(n + 1)

        def up_block(at, n=n, span=span, k=k):
            value = nt(q_buf[at, span], weight(n + 1))
            dh[at, :] = value if k == 0 else dh[at, :] + value

        by_blocks(up_block)
        finished(n + 1)
    cq_at, o2_at, do2_at, h2_at = (slice(k * width, (k + 1) * width) for k in range(4))
    got_cq = fetch(i_cq, p.at[:, pl.ds(0, width)])
    got_o2 = fetch(i_o2, p.at[:, pl.ds(width, width)])
    got_h2 = fetch(i_h2, p.at[:, pl.ds(3 * width, width)])
    got_resid.wait()
    norm_step(i_after_cross, F_GAIN, F_SHIFT, C_OBIAS)
    got_keep.wait()
    layer_home().start()

    got_h3.wait()
    produce(4, plain(h3), lambda: q_buf[:, 0:width])
    ready(8)

    def do2_block(at):
        p[at, do2_at] = nt(low[at, :], weight(8)).astype(jnp.bfloat16)

    by_blocks(do2_block)
    finished(8)
    got_cq.wait()
    got_o2.wait()
    got_ckv.wait()
    bias = text_mask(text_rows, text_length[y])
    dcq = extra
    layer_home().wait()

    def pair_lanes(buf, j, base):
        return lambda lo, hi: buf[lo:hi, lanes(j + base * pairs, 128)]

    def cross_pair(j):
        for at, k in ((2, 1), (5, 2)):

            @pl.when(j == at)
            def _(k=k):
                produce(4 + k, plain(h3), lambda: q_buf[:, k * width : (k + 1) * width])

        def put_dq(sl, value):
            dcq[sl, lanes(j, 128)] = value
            vg[C_QBIAS : C_QBIAS + 1, lanes(j, 128)] += jnp.sum(
                value.astype(jnp.float32), axis=0, keepdims=True
            )

        def put_dk(value):
            dckv[:, lanes(j, 128)] = value

        def put_dv(value):
            dckv[:, lanes(j + pairs, 128)] = value
            vg[C_VBIAS : C_VBIAS + 1, lanes(j, 128)] = jnp.sum(
                value.astype(jnp.float32), axis=0, keepdims=True
            )

        attend_back_pair(
            False, rows, text_rows, pair_lanes(p, j, 0), pair_lanes(ckv, j, 0),
            pair_lanes(ckv, j, 1), pair_lanes(p, j, 1), pair_lanes(p, j, 2), lse2.at[j], bias,
            put_dq, put_dk, put_dv, ka, va,
        )

    looped(pairs, cross_pair)
    produce(7, plain(h3), lambda: q_buf[:, 3 * width : 4 * width])
    got_o1 = fetch(i_o1, q_buf.at[:, pl.ds(3 * width, width)])
    ready(9)
    text_value = nt(dckv[:, :width], weight(9))
    finished(9)
    ready(10)
    text_value = text_value + nt(dckv[:, width:], weight(10))
    finished(10)
    tgrad[...] = text_value.astype(jnp.bfloat16).reshape(tgrad.shape)
    text_away, text_home = swap_out(1, lambda k: tgrad.at[k], o_text, tgrad.at[y])
    text_away().start()
    text_home().start()
    ready(11)

    def dh2_block(at):
        dh[at, :] = nt(dcq[at, :], weight(11))

    by_blocks(dh2_block)
    finished(11)
    produce(8, column(p, 1), lambda: low[...])
    norm_step(i_after_self, C_GAIN, C_SHIFT, A_OBIAS)
    got_h2.wait()
    produce(9, column(p, 3), lambda: dcq[...])
    got_qkv = fetch(i_qkv, p.at[:, pl.ds(0, 3 * width)])
    got_h1 = fetch(i_h1, p.at[:, pl.ds(3 * width, width)])
    got_tokens = fetch(i_tokens, h3)

    ready(12)
    do1 = extra

    def do1_block(at):
        do1[at, :] = nt(low[at, :], weight(12)).astype(jnp.bfloat16)

    by_blocks(do1_block)
    finished(12)
    got_text.wait()

    def text_lanes(some_lanes):
        return text[:, :, some_lanes].reshape(text_rows, some_lanes.size)

    produce(10, text_lanes, lambda: dckv[:, :width])
    got_qkv.wait()
    got_o1.wait()

    def self_pair(j):
        @pl.when(j == 2)
        def _():
            produce(11, text_lanes, lambda: dckv[:, width:])

        @pl.when(j == 4)
        def _():
            produce(12, column(q_buf, 3), lambda: low[...])

        def put_dq(sl, value):
            q_buf[sl, lanes(j, 128)] = value
            vg[A_QBIAS : A_QBIAS + 1, lanes(j, 128)] += jnp.sum(
                value.astype(jnp.float32), axis=0, keepdims=True
            )

        def put_dk(value):
            q_buf[:, lanes(j + pairs, 128)] = value

        def put_dv(value):
            q_buf[:, lanes(j + 2 * pairs, 128)] = value
            vg[A_VBIAS : A_VBIAS + 1, lanes(j, 128)] = jnp.sum(
                value.astype(jnp.float32), axis=0, keepdims=True
            )

        attend_back_pair(
            True, rows, rows, pair_lanes(p, j, 0), pair_lanes(p, j, 1), pair_lanes(p, j, 2),
            pair_lanes(q_buf, j, 3), lambda lo, hi: do1[lo:hi, lanes(j, 128)], lse1.at[j], None,
            put_dq, put_dk, put_dv, ka, va,
        )

    looped(pairs, self_pair)
    got_h1.wait()
    for c in range(3):
        produce(13 + c, column(p, 3), lambda c=c: q_buf[:, c * width : (c + 1) * width])
        ready(13 + c)

        def dh1_block(at, c=c):
            value = nt(q_buf[at, c * width : (c + 1) * width], weight(13 + c))
            dh[at, :] = value if c == 0 else dh[at, :] + value

        by_blocks(dh1_block)
        finished(13 + c)
    got_tokens.wait()
    grads = low

    def last_block(b):
        at = block_rows(b, BLOCK)
        half = b // (part // BLOCK)
        inner = block_rows(lax.rem(b, part // BLOCK), BLOCK)
        unit, scale = center_and_scale(h3[at, :].astype(jnp.float32))
        pulled = dh[at, :]
        add_row(A_GAIN, pulled * unit)
        add_row(A_SHIFT, pulled)
        total = resid[at, :] + norm_pull(unit, scale, pulled * row(A_GAIN))
        grads[at, :] = total.astype(jnp.bfloat16)

    looped(rows // BLOCK, last_block)
    tokens_away, tokens_home = swap_out(
        2,
        lambda k: grads.at[block_rows(k, part), :],
        o_tokens,
        grads.at[block_rows(y, part), :],
    )
    tokens_away().start()
    tokens_home().start()

    @pl.loop(0, depth)
    def _(k):
        some = gather_vectors(vg[...], k * 8, 8)
        small_bufs[0][0, k] = some.reshape(small_bufs[0].shape[2:])

    for k in range(16, len(stages)):
        stage(k)
    for copy in (
        layer_away(), text_away(), text_home(), tokens_away(), tokens_home(),
    ):
        copy.wait()


def backward(depth, number, wholes, kept, text_length):
    (
        token_seq, text_seq, normed_one, joined, self_mixed, after_self, normed_two, cross_queries,
        cross_kv, cross_mixed, after_cross, normed_three, active, slope, grad_after_ffn,
        grad_branch, layer_out, vec, lse1, lse2, zgrads,
    ) = kept
    rows, width = self_mixed.shape
    text_rows = cross_kv.shape[0]
    hidden = active.shape[1]
    share = width // (depth * 8)
    half = (2, rows // 2, width)
    low, full = jnp.bfloat16, jnp.float32
    operands = [
        token_seq.reshape(rows, width), text_seq, normed_one, joined, self_mixed, after_self,
        normed_two, cross_queries, cross_kv, cross_mixed, after_cross, normed_three, active, slope,
        grad_after_ffn, grad_branch, layer_out.reshape(half),
    ]

    def vmem(*dims, kind=low):
        return pltpu.VMEM(dims, kind)

    results_low = [jax.ShapeDtypeStruct(s, low) for s in (half, half, text_seq.shape)]
    columns = [w.shape[-1] for w in wholes] + [128]
    sums = [jax.ShapeDtypeStruct((share, c), full) for c in columns]
    scratch = [
        vmem(rows, hidden), vmem(rows, hidden), vmem(rows, width, kind=full),
        vmem(rows, width, kind=full), vmem(rows, width), vmem(rows, width), vmem(rows, width),
        vmem(text_rows, 2 * width), vmem(text_rows, 2 * width), vmem(*text_seq.shape),
        vmem(*text_seq.shape), vmem(2, NORM_BLOCK, width, kind=full),
        vmem(32, width, kind=full), vmem(rows, 128, kind=full), vmem(rows, 128, kind=full),
        vmem(WEIGHT_RING, depth, 2, 2, 2, share, width),
    ]
    scratch += ring_scratch(depth, BACK_RING, share, width, low)
    scratch += ring_scratch(depth, 1, share, 128, full)
    pieces = sum(c // width for c in columns)
    scratch += copy_sems(pieces, depth)[:2] + copy_sems(1, depth)[:2]
    scratch += [
        pltpu.SemaphoreType.DMA((3, 1)), pltpu.SemaphoreType.DMA((3, 1)),
        pltpu.SemaphoreType.DMA((5,)), pltpu.SemaphoreType.DMA((16,)),
        pltpu.SemaphoreType.DMA((32,)),
    ]
    in_vmem = pl.BlockSpec(memory_space=pltpu.VMEM)
    results = pl.pallas_call(
        functools.partial(backward_kernel, depth),
        out_shape=results_low + sums,
        in_specs=[ANYWHERE] * (len(wholes) + len(operands))
        + [in_vmem] * 4
        + [pl.BlockSpec(memory_space=pltpu.SMEM)],
        out_specs=[ANYWHERE] * 3 + [in_vmem] * len(sums),
        scratch_shapes=scratch,
        compiler_params=pltpu.CompilerParams(
            collective_id=number, has_side_effects=True, vmem_limit_bytes=BACK_VMEM_LIMIT
        ),
        name="backward",
    )(*wholes, *operands, vec, lse1, lse2, zgrads, text_length)
    return list(results[:3]), list(results[3:])


BACK_VMEM_LIMIT = 61 * 2**20


def pack_vectors(vectors, wide):
    packed = jnp.concatenate([jnp.stack(vectors), wide.reshape(4, -1)])
    return jnp.pad(packed, ((0, 32 - packed.shape[0]), (0, 128 - packed.shape[1])))


def paired_layer(
    depth,
    tokens,
    text_states,
    unit_length,
    text_length,
    cotangent,
    attn_gain,
    attn_shift,
    attn_inputs,
    attn_qbias,
    attn_vbias,
    attn_output,
    attn_obias,
    cross_gain,
    cross_shift,
    cross_query,
    cross_qbias,
    cross_keyval,
    cross_vbias,
    cross_output,
    cross_obias,
    ffn_gain,
    ffn_shift,
    ffn_up,
    ffn_upbias,
    ffn_down,
    ffn_downbias,
    final_gain,
    final_shift,
):
    share = attn_gain.shape[0]
    packed = pack_vectors(
        [
            attn_gain, attn_shift, attn_qbias, attn_vbias, attn_obias, cross_gain, cross_shift,
            cross_qbias, cross_vbias, cross_obias, ffn_gain, ffn_shift, ffn_downbias, final_gain,
            final_shift,
        ],
        ffn_upbias,
    )
    shards = depth * 8
    up_shard = ffn_up.reshape(share, shards, 4, share).swapaxes(1, 2).reshape(share, -1)
    wholes, kept = forward(
        depth, 0, tokens, text_states, cotangent, unit_length, text_length,
        [packed, attn_inputs, attn_output, cross_query, cross_keyval, cross_output, up_shard]
        + [ffn_down[q * share : (q + 1) * share] for q in range(4)],
    )
    (layer_out, tokens_grad, text_grad), sums = backward(depth, 1, wholes[1:], kept, text_length)
    s_in, s_out, s_cq, s_ckv, s_co, s_up, *s_downs, s_small = sums
    s_up = s_up.reshape(share, 4, shards, share).swapaxes(1, 2).reshape(share, -1)
    s_down = jnp.concatenate(s_downs)
    s_upbias = s_small[VECTOR_COUNT : VECTOR_COUNT + 4, :share].reshape(-1)
    v = [s_small[i, :share] for i in range(VECTOR_COUNT)]
    return (
        layer_out, tokens_grad, text_grad, v[A_GAIN], v[A_SHIFT], s_in, v[A_QBIAS], v[A_VBIAS],
        s_out, v[A_OBIAS], v[C_GAIN], v[C_SHIFT], s_cq, v[C_QBIAS], s_ckv, v[C_VBIAS], s_co,
        v[C_OBIAS], v[F_GAIN], v[F_SHIFT], s_up, s_upbias, s_down, v[F_DOWNBIAS], v[Z_GAIN],
        v[Z_SHIFT],
    )


def solution(mesh):
    in_specs = (
        P("dp", "seq", None),
        P("dp", "seq", None),
        P("dp"),
        P("dp"),
        P("dp", "seq", None),
        P(("dp", "seq")),
        P(("dp", "seq")),
        P(("dp", "seq"), None),
        P(("dp", "seq")),
        P(("dp", "seq")),
        P(("dp", "seq"), None),
        P(("dp", "seq")),
        P(("dp", "seq")),
        P(("dp", "seq")),
        P(("dp", "seq"), None),
        P(("dp", "seq")),
        P(("dp", "seq"), None),
        P(("dp", "seq")),
        P(("dp", "seq"), None),
        P(("dp", "seq")),
        P(("dp", "seq")),
        P(("dp", "seq")),
        P(("dp", "seq"), None),
        P(("dp", "seq")),
        P(("dp", "seq"), None),
        P(("dp", "seq")),
        P(("dp", "seq")),
        P(("dp", "seq")),
    )
    out_specs = (
        P("dp", "seq", None),
        P("dp", "seq", None),
        P("dp", "seq", None),
        P(("dp", "seq")),
        P(("dp", "seq")),
        P(("dp", "seq"), None),
        P(("dp", "seq")),
        P(("dp", "seq")),
        P(("dp", "seq"), None),
        P(("dp", "seq")),
        P(("dp", "seq")),
        P(("dp", "seq")),
        P(("dp", "seq"), None),
        P(("dp", "seq")),
        P(("dp", "seq"), None),
        P(("dp", "seq")),
        P(("dp", "seq"), None),
        P(("dp", "seq")),
        P(("dp", "seq")),
        P(("dp", "seq")),
        P(("dp", "seq"), None),
        P(("dp", "seq")),
        P(("dp", "seq"), None),
        P(("dp", "seq")),
        P(("dp", "seq")),
        P(("dp", "seq")),
    )
    groups, seq_parts = mesh.shape["dp"], mesh.shape["seq"]

    def layer(*arguments):
        shard = arguments[5].shape[0]
        parts = arguments[0].shape[0]
        if seq_parts == 2 and parts == 2 and groups % 4 == 0 and shard % 32 == 0:
            return paired_layer(groups // 4, *arguments)
        return on_device(*arguments)

    return jax.shard_map(
        layer, mesh=mesh, in_specs=in_specs, out_specs=out_specs, check_vma=False
    )
```

```python
import functools
import math

import jax
import jax.numpy as jnp
from jax import lax
from jax.experimental import pallas as pl
from jax.experimental.pallas import tpu as pltpu
from jax.sharding import PartitionSpec as P

HEADS = 16
HEAD_DIM = 64


EPSILON = 1e-05
MASKED = -1e30


def layer_norm(values, norm_gain, norm_shift):
    center = values - jnp.mean(values, axis=-1, keepdims=True)
    spread = jnp.mean(center * center, axis=-1, keepdims=True)
    return center * lax.rsqrt(spread + EPSILON) * norm_gain + norm_shift


def norm_back(values, norm_gain, norm_shift, upstream):
    result, pullback = jax.vjp(layer_norm, values, norm_gain, norm_shift)
    return pullback(upstream)


def rows_dot(left_side, right_side):
    return jnp.dot(left_side, right_side, preferred_element_type=jnp.float32)


def left_dot(left_side, right_side):
    return lax.dot_general(
        left_side, right_side, (((0,), (0,)), ((), ())), preferred_element_type=jnp.float32
    )


def right_dot(left_side, right_side):
    return lax.dot_general(
        left_side, right_side, (((1,), (1,)), ((), ())), preferred_element_type=jnp.float32
    )


def heads_of(matrix):
    return matrix.reshape(matrix.shape[0], HEADS, HEAD_DIM)


def attend_forward(queries, key_rows, value_rows, allowed):
    score_scale = 1.0 / math.sqrt(HEAD_DIM)
    scores = (
        jnp.einsum(
            "qhd,khd->hqk",
            heads_of(queries),
            heads_of(key_rows),
            preferred_element_type=jnp.float32,
        )
        * score_scale
    )
    scores = jnp.where(allowed[None], scores, MASKED)
    row_max = jnp.max(scores, axis=-1, keepdims=True)
    weights = jnp.exp(scores - row_max)
    row_total = jnp.sum(weights, axis=-1, keepdims=True)
    weights = (weights / row_total).astype(jnp.bfloat16)
    mixed_rows = jnp.einsum(
        "hqk,khd->qhd", weights, heads_of(value_rows), preferred_element_type=jnp.float32
    )
    logsum = (row_max + jnp.log(row_total))[..., 0]
    return (mixed_rows.reshape(queries.shape[0], -1).astype(jnp.bfloat16), logsum)


def attend_back(queries, key_rows, value_rows, allowed, logsum, upstream):
    score_scale = 1.0 / math.sqrt(HEAD_DIM)
    query_heads = heads_of(queries)
    key_heads = heads_of(key_rows)
    upstream_heads = heads_of(upstream)
    scores = (
        jnp.einsum("qhd,khd->hqk", query_heads, key_heads, preferred_element_type=jnp.float32)
        * score_scale
    )
    scores = jnp.where(allowed[None], scores, MASKED)
    weights = jnp.exp(scores - logsum[..., None])
    grad_weights = jnp.einsum(
        "qhd,khd->hqk", upstream_heads, heads_of(value_rows), preferred_element_type=jnp.float32
    )
    row_delta = jnp.sum(weights * grad_weights, axis=-1, keepdims=True)
    grad_scores = (weights * (grad_weights - row_delta)).astype(jnp.bfloat16)
    grad_query = (
        jnp.einsum("hqk,khd->qhd", grad_scores, key_heads, preferred_element_type=jnp.float32)
        * score_scale
    )
    grad_key = (
        jnp.einsum("hqk,qhd->khd", grad_scores, query_heads, preferred_element_type=jnp.float32)
        * score_scale
    )
    grad_value = jnp.einsum(
        "hqk,qhd->khd",
        weights.astype(jnp.bfloat16),
        upstream_heads,
        preferred_element_type=jnp.float32,
    )
    key_count = key_rows.shape[0]
    return (
        grad_query.reshape(queries.shape[0], -1),
        grad_key.reshape(key_count, -1),
        grad_value.reshape(key_count, -1),
    )


def to_float(values):
    return values.astype(jnp.float32)


def on_device(
    tokens,
    text_states,
    unit_length,
    text_length,
    cotangent,
    attn_gain,
    attn_shift,
    attn_inputs,
    attn_qbias,
    attn_vbias,
    attn_output,
    attn_obias,
    cross_gain,
    cross_shift,
    cross_query,
    cross_qbias,
    cross_keyval,
    cross_vbias,
    cross_output,
    cross_obias,
    ffn_gain,
    ffn_shift,
    ffn_up,
    ffn_upbias,
    ffn_down,
    ffn_downbias,
    final_gain,
    final_shift,
):
    seq_count, local_len, model_width = tokens.shape
    row_count = seq_count * local_len
    first_pos = lax.axis_index("seq") * local_len
    zero_bias = jnp.zeros((model_width,), jnp.float32)
    (
        a_gain_full,
        a_shift_full,
        attention_input_weight_whole,
        a_qbias_full,
        a_vbias_full,
        a_output_full,
        a_obias_full,
    ) = (
        lax.all_gather(attn_gain, ("dp", "seq"), axis=0, tiled=True),
        lax.all_gather(attn_shift, ("dp", "seq"), axis=0, tiled=True),
        lax.all_gather(attn_inputs, ("dp", "seq"), axis=0, tiled=True),
        lax.all_gather(attn_qbias, ("dp", "seq"), axis=0, tiled=True),
        lax.all_gather(attn_vbias, ("dp", "seq"), axis=0, tiled=True),
        lax.all_gather(attn_output, ("dp", "seq"), axis=0, tiled=True),
        lax.all_gather(attn_obias, ("dp", "seq"), axis=0, tiled=True),
    )
    inputs = to_float(tokens).reshape(row_count, model_width)
    normed_one = layer_norm(inputs, to_float(a_gain_full), to_float(a_shift_full)).astype(
        jnp.bfloat16
    )
    joined = rows_dot(normed_one, attention_input_weight_whole) + jnp.concatenate(
        [to_float(a_qbias_full), zero_bias, to_float(a_vbias_full)]
    )
    joined = joined.astype(jnp.bfloat16)
    self_queries = joined[:, :model_width].reshape(seq_count, local_len, model_width)
    keyval_local = joined[:, model_width:].reshape(seq_count, local_len, 2 * model_width)
    self_keyval = lax.all_gather(keyval_local, "seq", axis=1, tiled=True)
    full_len = self_keyval.shape[1]
    causal = jnp.arange(full_len)[None, :] <= (first_pos + jnp.arange(local_len))[:, None]

    def self_forward(packed):
        seq_queries, seq_keyval = packed
        return attend_forward(
            seq_queries, seq_keyval[:, :model_width], seq_keyval[:, model_width:], causal
        )

    self_mixed, self_logsum = lax.map(self_forward, (self_queries, self_keyval))
    self_flat = self_mixed.reshape(row_count, model_width)
    after_self = inputs + rows_dot(self_flat, a_output_full) + to_float(a_obias_full)
    (
        c_gain_full,
        c_shift_full,
        c_query_full,
        c_qbias_full,
        c_keyval_full,
        cross_value_bias_whole,
        c_output_full,
        c_obias_full,
    ) = (
        lax.all_gather(cross_gain, ("dp", "seq"), axis=0, tiled=True),
        lax.all_gather(cross_shift, ("dp", "seq"), axis=0, tiled=True),
        lax.all_gather(cross_query, ("dp", "seq"), axis=0, tiled=True),
        lax.all_gather(cross_qbias, ("dp", "seq"), axis=0, tiled=True),
        lax.all_gather(cross_keyval, ("dp", "seq"), axis=0, tiled=True),
        lax.all_gather(cross_vbias, ("dp", "seq"), axis=0, tiled=True),
        lax.all_gather(cross_output, ("dp", "seq"), axis=0, tiled=True),
        lax.all_gather(cross_obias, ("dp", "seq"), axis=0, tiled=True),
    )
    normed_two = layer_norm(after_self, to_float(c_gain_full), to_float(c_shift_full)).astype(
        jnp.bfloat16
    )
    cross_queries = (rows_dot(normed_two, c_query_full) + to_float(c_qbias_full)).astype(
        jnp.bfloat16
    )
    cross_queries = cross_queries.reshape(seq_count, local_len, model_width)
    keyval_bias = jnp.concatenate([zero_bias, to_float(cross_value_bias_whole)])
    text_whole = lax.all_gather(text_states, "seq", axis=1, tiled=True)
    cross_kv = (rows_dot(text_whole.reshape(-1, model_width), c_keyval_full) + keyval_bias).astype(
        jnp.bfloat16
    )
    cross_kv = cross_kv.reshape(seq_count, -1, 2 * model_width)
    text_total = cross_kv.shape[1]
    text_allowed = jnp.arange(text_total)[None, :] < text_length[:, None]

    def cross_forward(packed):
        seq_queries, seq_keyval, seq_allowed = packed
        allowed = jnp.broadcast_to(seq_allowed[None, :], (local_len, text_total))
        return attend_forward(
            seq_queries, seq_keyval[:, :model_width], seq_keyval[:, model_width:], allowed
        )

    cross_blended_rows, cross_logsum = lax.map(
        cross_forward, (cross_queries, cross_kv, text_allowed)
    )
    cross_flat = cross_blended_rows.reshape(row_count, model_width)
    after_cross = after_self + rows_dot(cross_flat, c_output_full) + to_float(c_obias_full)
    (
        f_gain_full,
        feedforward_shift_whole,
        f_up_full,
        f_upbias_full,
        f_down_full,
        f_downbias_full,
        z_gain_full,
        z_shift_full,
    ) = (
        lax.all_gather(ffn_gain, ("dp", "seq"), axis=0, tiled=True),
        lax.all_gather(ffn_shift, ("dp", "seq"), axis=0, tiled=True),
        lax.all_gather(ffn_up, ("dp", "seq"), axis=0, tiled=True),
        lax.all_gather(ffn_upbias, ("dp", "seq"), axis=0, tiled=True),
        lax.all_gather(ffn_down, ("dp", "seq"), axis=0, tiled=True),
        lax.all_gather(ffn_downbias, ("dp", "seq"), axis=0, tiled=True),
        lax.all_gather(final_gain, ("dp", "seq"), axis=0, tiled=True),
        lax.all_gather(final_shift, ("dp", "seq"), axis=0, tiled=True),
    )
    normed_three = layer_norm(
        after_cross, to_float(f_gain_full), to_float(feedforward_shift_whole)
    ).astype(jnp.bfloat16)
    ffn_inner = rows_dot(normed_three, f_up_full) + to_float(f_upbias_full)
    active = jax.nn.gelu(ffn_inner).astype(jnp.bfloat16)
    after_ffn = after_cross + rows_dot(active, f_down_full) + to_float(f_downbias_full)
    valid_rows = ((first_pos + jnp.arange(local_len))[None, :] < unit_length[:, None]).astype(
        jnp.float32
    )
    valid_rows = valid_rows.reshape(row_count, 1)
    final_norm = layer_norm(after_ffn, to_float(z_gain_full), to_float(z_shift_full))
    layer_out = (
        (final_norm * valid_rows).astype(jnp.bfloat16).reshape(seq_count, local_len, model_width)
    )
    (
        f_gain_full,
        feedforward_shift_whole,
        f_up_full,
        f_upbias_full,
        f_down_full,
        f_downbias_full,
        z_gain_full,
        z_shift_full,
    ) = (
        lax.all_gather(ffn_gain, ("dp", "seq"), axis=0, tiled=True),
        lax.all_gather(ffn_shift, ("dp", "seq"), axis=0, tiled=True),
        lax.all_gather(ffn_up, ("dp", "seq"), axis=0, tiled=True),
        lax.all_gather(ffn_upbias, ("dp", "seq"), axis=0, tiled=True),
        lax.all_gather(ffn_down, ("dp", "seq"), axis=0, tiled=True),
        lax.all_gather(ffn_downbias, ("dp", "seq"), axis=0, tiled=True),
        lax.all_gather(final_gain, ("dp", "seq"), axis=0, tiled=True),
        lax.all_gather(final_shift, ("dp", "seq"), axis=0, tiled=True),
    )
    upstream = to_float(cotangent).reshape(row_count, model_width) * valid_rows
    grad_after_ffn, grad_zgain, grad_zshift = norm_back(
        after_ffn, to_float(z_gain_full), to_float(z_shift_full), upstream
    )
    grad_branch = grad_after_ffn.astype(jnp.bfloat16)
    grad_down = left_dot(active, grad_branch)
    grad_downbias = jnp.sum(to_float(grad_branch), axis=0)
    grad_active = right_dot(grad_branch, f_down_full)
    inner_value, gelu_back = jax.vjp(jax.nn.gelu, ffn_inner)
    grad_inner = gelu_back(grad_active)[0].astype(jnp.bfloat16)
    grad_up = left_dot(normed_three, grad_inner)
    grad_upbias = jnp.sum(to_float(grad_inner), axis=0)
    grad_normed_three = right_dot(grad_inner, f_up_full)
    grad_cross_norm, grad_fgain, grad_fshift = norm_back(
        after_cross, to_float(f_gain_full), to_float(feedforward_shift_whole), grad_normed_three
    )
    grad_after_cross = grad_after_ffn + grad_cross_norm
    ffn_sums = (
        lax.psum_scatter(grad_fgain, ("dp", "seq"), scatter_dimension=0, tiled=True),
        lax.psum_scatter(grad_fshift, ("dp", "seq"), scatter_dimension=0, tiled=True),
        lax.psum_scatter(grad_up, ("dp", "seq"), scatter_dimension=0, tiled=True),
        lax.psum_scatter(grad_upbias, ("dp", "seq"), scatter_dimension=0, tiled=True),
        lax.psum_scatter(grad_down, ("dp", "seq"), scatter_dimension=0, tiled=True),
        lax.psum_scatter(grad_downbias, ("dp", "seq"), scatter_dimension=0, tiled=True),
        lax.psum_scatter(grad_zgain, ("dp", "seq"), scatter_dimension=0, tiled=True),
        lax.psum_scatter(grad_zshift, ("dp", "seq"), scatter_dimension=0, tiled=True),
    )
    (
        c_gain_full,
        c_shift_full,
        c_query_full,
        c_qbias_full,
        c_keyval_full,
        cross_value_bias_whole,
        c_output_full,
        c_obias_full,
    ) = (
        lax.all_gather(cross_gain, ("dp", "seq"), axis=0, tiled=True),
        lax.all_gather(cross_shift, ("dp", "seq"), axis=0, tiled=True),
        lax.all_gather(cross_query, ("dp", "seq"), axis=0, tiled=True),
        lax.all_gather(cross_qbias, ("dp", "seq"), axis=0, tiled=True),
        lax.all_gather(cross_keyval, ("dp", "seq"), axis=0, tiled=True),
        lax.all_gather(cross_vbias, ("dp", "seq"), axis=0, tiled=True),
        lax.all_gather(cross_output, ("dp", "seq"), axis=0, tiled=True),
        lax.all_gather(cross_obias, ("dp", "seq"), axis=0, tiled=True),
    )
    cross_branch_gradient = grad_after_cross.astype(jnp.bfloat16)
    grad_coutput = left_dot(cross_flat, cross_branch_gradient)
    grad_cobias = jnp.sum(to_float(cross_branch_gradient), axis=0)
    grad_cross_mixed = right_dot(cross_branch_gradient, c_output_full).astype(jnp.bfloat16)
    grad_cross_mixed = grad_cross_mixed.reshape(seq_count, local_len, model_width)

    def cross_backward(packed):
        seq_queries, seq_keyval, seq_allowed, sequence_log_sum_exp, seq_upstream = packed
        allowed = jnp.broadcast_to(seq_allowed[None, :], (local_len, text_total))
        return attend_back(
            seq_queries,
            seq_keyval[:, :model_width],
            seq_keyval[:, model_width:],
            allowed,
            sequence_log_sum_exp,
            seq_upstream,
        )

    grad_cq, grad_ck, grad_cv = lax.map(
        cross_backward, (cross_queries, cross_kv, text_allowed, cross_logsum, grad_cross_mixed)
    )
    grad_ckv = lax.psum_scatter(
        jnp.concatenate([grad_ck, grad_cv], axis=-1).astype(jnp.bfloat16),
        "seq",
        scatter_dimension=1,
        tiled=True,
    ).astype(jnp.float32)
    grad_ckv = grad_ckv.astype(jnp.bfloat16).reshape(-1, 2 * model_width)
    grad_ckeyval = left_dot(text_states.reshape(-1, model_width), grad_ckv)
    grad_cvbias = jnp.sum(to_float(grad_ckv[:, model_width:]), axis=0)
    text_grad = right_dot(grad_ckv, c_keyval_full).astype(jnp.bfloat16).reshape(text_states.shape)
    grad_cq_low = grad_cq.reshape(row_count, model_width).astype(jnp.bfloat16)
    grad_cquery = left_dot(normed_two, grad_cq_low)
    grad_cqbias = jnp.sum(to_float(grad_cq_low), axis=0)
    grad_normed_two = right_dot(grad_cq_low, c_query_full)
    grad_self_norm, grad_cgain, grad_cshift = norm_back(
        after_self, to_float(c_gain_full), to_float(c_shift_full), grad_normed_two
    )
    grad_after_self = grad_after_cross + grad_self_norm
    cross_sums = (
        lax.psum_scatter(grad_cgain, ("dp", "seq"), scatter_dimension=0, tiled=True),
        lax.psum_scatter(grad_cshift, ("dp", "seq"), scatter_dimension=0, tiled=True),
        lax.psum_scatter(grad_cquery, ("dp", "seq"), scatter_dimension=0, tiled=True),
        lax.psum_scatter(grad_cqbias, ("dp", "seq"), scatter_dimension=0, tiled=True),
        lax.psum_scatter(grad_ckeyval, ("dp", "seq"), scatter_dimension=0, tiled=True),
        lax.psum_scatter(grad_cvbias, ("dp", "seq"), scatter_dimension=0, tiled=True),
        lax.psum_scatter(grad_coutput, ("dp", "seq"), scatter_dimension=0, tiled=True),
        lax.psum_scatter(grad_cobias, ("dp", "seq"), scatter_dimension=0, tiled=True),
    )
    (
        a_gain_full,
        a_shift_full,
        attention_input_weight_whole,
        a_qbias_full,
        a_vbias_full,
        a_output_full,
        a_obias_full,
    ) = (
        lax.all_gather(attn_gain, ("dp", "seq"), axis=0, tiled=True),
        lax.all_gather(attn_shift, ("dp", "seq"), axis=0, tiled=True),
        lax.all_gather(attn_inputs, ("dp", "seq"), axis=0, tiled=True),
        lax.all_gather(attn_qbias, ("dp", "seq"), axis=0, tiled=True),
        lax.all_gather(attn_vbias, ("dp", "seq"), axis=0, tiled=True),
        lax.all_gather(attn_output, ("dp", "seq"), axis=0, tiled=True),
        lax.all_gather(attn_obias, ("dp", "seq"), axis=0, tiled=True),
    )
    grad_self_branch = grad_after_self.astype(jnp.bfloat16)
    grad_aoutput = left_dot(self_flat, grad_self_branch)
    grad_aobias = jnp.sum(to_float(grad_self_branch), axis=0)
    grad_self_mixed = right_dot(grad_self_branch, a_output_full).astype(jnp.bfloat16)
    grad_self_mixed = grad_self_mixed.reshape(seq_count, local_len, model_width)

    def self_backward(packed):
        seq_queries, seq_keyval, sequence_log_sum_exp, seq_upstream = packed
        return attend_back(
            seq_queries,
            seq_keyval[:, :model_width],
            seq_keyval[:, model_width:],
            causal,
            sequence_log_sum_exp,
            seq_upstream,
        )

    gradient_self_query, grad_sk, grad_sv = lax.map(
        self_backward, (self_queries, self_keyval, self_logsum, grad_self_mixed)
    )
    gradient_self_keyvalue = lax.psum_scatter(
        jnp.concatenate([grad_sk, grad_sv], axis=-1).astype(jnp.bfloat16),
        "seq",
        scatter_dimension=1,
        tiled=True,
    ).astype(jnp.float32)
    grad_joined = (
        jnp.concatenate([gradient_self_query, gradient_self_keyvalue], axis=-1)
        .reshape(row_count, 3 * model_width)
        .astype(jnp.bfloat16)
    )
    grad_ainputs = left_dot(normed_one, grad_joined)
    grad_aqbias = jnp.sum(to_float(grad_joined[:, :model_width]), axis=0)
    grad_avbias = jnp.sum(to_float(grad_joined[:, 2 * model_width :]), axis=0)
    grad_normed_one = right_dot(grad_joined, attention_input_weight_whole)
    grad_input_norm, grad_again, grad_ashift = norm_back(
        inputs, to_float(a_gain_full), to_float(a_shift_full), grad_normed_one
    )
    tokens_grad = (
        (grad_after_self + grad_input_norm)
        .astype(jnp.bfloat16)
        .reshape(seq_count, local_len, model_width)
    )
    attn_sums = (
        lax.psum_scatter(grad_again, ("dp", "seq"), scatter_dimension=0, tiled=True),
        lax.psum_scatter(grad_ashift, ("dp", "seq"), scatter_dimension=0, tiled=True),
        lax.psum_scatter(grad_ainputs, ("dp", "seq"), scatter_dimension=0, tiled=True),
        lax.psum_scatter(grad_aqbias, ("dp", "seq"), scatter_dimension=0, tiled=True),
        lax.psum_scatter(grad_avbias, ("dp", "seq"), scatter_dimension=0, tiled=True),
        lax.psum_scatter(grad_aoutput, ("dp", "seq"), scatter_dimension=0, tiled=True),
        lax.psum_scatter(grad_aobias, ("dp", "seq"), scatter_dimension=0, tiled=True),
    )
    return (layer_out, tokens_grad, text_grad, *attn_sums, *cross_sums, *ffn_sums)


MESH_ID = pl.DeviceIdType.MESH
ANYWHERE = pl.BlockSpec(memory_space=pl.ANY)
VMEM_LIMIT = 56 * 2**20


class Place:
    def __init__(self, depth):
        group = lax.axis_index("dp")
        self.depth = depth
        self.z = group // 4
        self.x = lax.rem(group // 2, 2)
        self.core = lax.rem(group, 2)
        self.y = lax.axis_index("seq")

    def device(self, z, x, core, y):
        return {"dp": (z * 2 + x) * 2 + core, "seq": y}

    def along_z(self, step):
        return self.device(lax.rem(self.z + step, self.depth), self.x, self.core, self.y)

    def across_x(self):
        return self.device(self.z, 1 - self.x, self.core, self.y)

    def across_y(self):
        return self.device(self.z, self.x, self.core, 1 - self.y)

    def sibling(self):
        return self.device(self.z, self.x, 1 - self.core, self.y)

    def along(self, axis):
        if axis == "z":
            return [self.along_z(step) for step in range(1, self.depth)]
        return [self.across_x() if axis == "x" else self.across_y()]

    def greet(self):
        partners = [self.along_z(step) for step in range(1, self.depth)]
        partners += [self.across_x(), self.across_y(), self.sibling()]
        barrier = pltpu.get_barrier_semaphore()
        for partner in partners:
            pl.semaphore_signal(barrier, inc=1, device_id=partner, device_id_type=MESH_ID)
        pl.semaphore_wait(barrier, len(partners))


def remote(source, target, sems, item, index, device):
    send, receive = sems
    return pltpu.make_async_remote_copy(
        src_ref=source,
        dst_ref=target,
        send_sem=send.at[item, index],
        recv_sem=receive.at[item, index],
        device_id=device,
        device_id_type=MESH_ID,
    )


def pipelined(phase_lists, stride):
    stages = []
    for first, phases in enumerate(phase_lists):
        for p, phase in enumerate(phases):
            turn = first + stride * p
            while len(stages) <= turn:
                stages.append([])
            stages[turn].append(phase)
    return stages


ORDERS = (("z", "x", "y"), ("y", "z", "x"))


def gather_phases(place, shard, whole, rows, cols, sems, local, stop, item):
    half = rows.size // 2
    halves = (pl.ds(rows.start, half), pl.ds(rows.start + half, half))
    here = {"z": place.z, "x": place.x, "y": place.y}
    every = slice(None)

    def view(done, some_rows, core):
        at = {axis: every if axis in done else here[axis] for axis in here}
        return whole.at[at["z"], at["x"], core, at["y"], some_rows, cols]

    def copies(phase):
        made = []
        if phase == 3:
            both = view("zxy", rows, place.core)
            return [remote(both, both, sems, item, 2 * place.depth + 2, place.sibling())]
        slot = sum(len(place.along(o[p])) for o in ORDERS for p in range(phase))
        for some_rows, order in zip(halves, ORDERS):
            target = view(order[:phase], some_rows, place.core)
            source = shard.at[some_rows, cols] if phase == 0 else target
            for device in place.along(order[phase]):
                made.append(remote(source, target, sems, item, slot, device))
                slot += 1
        return made

    def take():
        return pltpu.make_async_copy(shard.at[rows, cols], stop, local.at[item, 0])

    def put():
        return pltpu.make_async_copy(stop, view("", rows, place.core), local.at[item, 1])

    def start(phase):
        for copy in copies(phase):
            copy.start()

    def wait(phase):
        for copy in copies(phase):
            copy.wait()

    def opening():
        start(0)
        take().start()
        take().wait()
        put().start()

    def turn(phase):
        def run():
            wait(phase - 1)
            if phase == 1:
                put().wait()
            start(phase)

        return run

    return [opening, turn(1), turn(2), turn(3), lambda: wait(3)]


def copy_sems(items, depth):
    width = 2 * depth + 3
    return [
        pltpu.SemaphoreType.DMA((items, width)),
        pltpu.SemaphoreType.DMA((items, width)),
        pltpu.SemaphoreType.DMA((items, 2)),
    ]


ITEM = 512


def weight_items(shape):
    rows, cols = shape
    return [
        (pl.ds(r, 32), pl.ds(c, min(ITEM, cols)))
        for r in range(0, rows, 32)
        for c in range(0, cols, min(ITEM, cols))
    ]


def nt(a, b):
    return lax.dot_general(a, b, (((1,), (1,)), ((), ())), preferred_element_type=jnp.float32)


def nn(a, b):
    return jnp.dot(a, b, preferred_element_type=jnp.float32)


def half_mask(rows):
    return lax.broadcasted_iota(jnp.int32, (rows, 128), 1) < 64


def pick(block, head, first):
    zero = jnp.zeros_like(block)
    return jnp.where(first, block, zero) if head == 0 else jnp.where(first, zero, block)


def segments(causal, qb, keys, size):
    if not causal:
        return [(0, keys, False)]
    diagonal = [(qb * size, (qb + 1) * size, True)]
    return [(0, qb * size, False)] * (qb > 0) + diagonal


def both(block, first):
    return jnp.concatenate([pick(block, 0, first), pick(block, 1, first)], axis=0)


def diagonal_mask(scored, size):
    r = lax.broadcasted_iota(jnp.int32, scored.shape, 0)
    c = lax.broadcasted_iota(jnp.int32, scored.shape, 1)
    return jnp.where(r <= lax.rem(c, size), scored, MASKED)


def attend_pair(causal, rows, keys, size, get_q, get_k, get_v, bias, put, lse_ref):
    vt = get_v(0, keys).T
    first = half_mask(size)
    for qb in range(rows // size):
        sl = slice(qb * size, (qb + 1) * size)
        qs = both(get_q(sl.start, sl.stop) * jnp.bfloat16(0.125), first)
        parts = []
        for lo, hi, diagonal in segments(causal, qb, keys, size):
            s = nt(get_k(lo, hi), qs)
            if diagonal:
                s = diagonal_mask(s, size)
            if bias is not None:
                s = s + jnp.concatenate([bias] * (2 * size // 128), axis=1)
            parts.append((lo, hi, s))
        m = functools.reduce(jnp.maximum, [jnp.max(s, axis=0, keepdims=True) for _, _, s in parts])
        total, out = None, None
        for lo, hi, s in parts:
            p = jnp.exp(s - m)
            l = jnp.sum(p, axis=0, keepdims=True)
            o = nn(vt[:, lo:hi], p.astype(jnp.bfloat16))
            total = l if total is None else total + l
            out = o if out is None else out + o
        lse = m + jnp.log(total)
        lse_ref[0:1, sl] = lse[:, :size]
        lse_ref[1:2, sl] = lse[:, size:]
        out = out * (1.0 / total)
        out = jnp.concatenate([out[:64, :size], out[64:, size:]], axis=0).T
        put(sl, out.astype(jnp.bfloat16))


def attend_back_pair(
    causal, rows, keys, size, get_q, get_k, get_v, get_o, get_do, lse_ref, bias, put_dq, put_dk,
    put_dv, dk_acc, dv_acc,
):
    kt = (get_k(0, keys) * jnp.bfloat16(0.125)).T
    first = half_mask(size)
    order = list(range(rows // size))
    if causal:
        order = order[::-1]
    for qb in order:
        sl = slice(qb * size, (qb + 1) * size)
        qs = both(get_q(sl.start, sl.stop) * jnp.bfloat16(0.125), first)
        do = get_do(sl.start, sl.stop)
        dos = both(do, first)
        dt = (do.astype(jnp.float32) * get_o(sl.start, sl.stop).astype(jnp.float32)).T
        delta = jnp.concatenate(
            [
                jnp.sum(dt[:64], axis=0, keepdims=True),
                jnp.sum(dt[64:], axis=0, keepdims=True),
            ],
            axis=1,
        )
        lse = jnp.concatenate([lse_ref[0:1, sl], lse_ref[1:2, sl]], axis=1)
        dq = None
        for lo, hi, diagonal in segments(causal, qb, keys, size):
            s = nt(get_k(lo, hi), qs)
            if diagonal:
                s = diagonal_mask(s, size)
            if bias is not None:
                s = s + jnp.concatenate([bias] * (2 * size // 128), axis=1)
            dp = nt(get_v(lo, hi), dos)
            p = jnp.exp(s - lse)
            ds = (p * (dp - delta)).astype(jnp.bfloat16)
            dv = nn(p.astype(jnp.bfloat16), dos)
            dk = nn(ds, qs)
            part = nn(kt[:, lo:hi], ds)
            dq = part if dq is None else dq + part
            if qb == order[0]:
                dv_acc[lo:hi, :] = dv
                dk_acc[lo:hi, :] = dk
            else:
                dv_acc[lo:hi, :] += dv
                dk_acc[lo:hi, :] += dk
        dq = jnp.concatenate([dq[:64, :size], dq[64:, size:]], axis=0).T
        put_dq(sl, dq.astype(jnp.bfloat16))
    put_dk(dk_acc[0:keys, :].astype(jnp.bfloat16))
    put_dv(dv_acc[0:keys, :].astype(jnp.bfloat16))


BLOCK = 256
MATMUL_ROWS = 512
RING = 6

VECTOR_COUNT = 15
(
    A_GAIN, A_SHIFT, A_QBIAS, A_VBIAS, A_OBIAS, C_GAIN, C_SHIFT, C_QBIAS, C_VBIAS, C_OBIAS,
    F_GAIN, F_SHIFT, F_DOWNBIAS, Z_GAIN, Z_SHIFT,
) = range(VECTOR_COUNT)
F_UPBIAS = VECTOR_COUNT
UP_INDEX, DOWN_INDEX = 6, 7
STRIDE = 3
SWAP_PIECES = 16
SELF_QUERIES, CROSS_QUERIES = 512, 1024


def block_rows(index, size):
    return pl.ds(pl.multiple_of(index * size, size), size)


def lanes(index, size):
    return pl.ds(pl.multiple_of(index * size, size), size)


def center_and_scale(values):
    center = values - jnp.mean(values, axis=-1, keepdims=True)
    spread = jnp.mean(center * center, axis=-1, keepdims=True)
    scale = lax.rsqrt(spread + EPSILON)
    return center * scale, scale


def norm_pull(unit, scale, pulled):
    inner = jnp.mean(pulled * unit, axis=-1, keepdims=True)
    return scale * (pulled - jnp.mean(pulled, axis=-1, keepdims=True) - unit * inner)


def gelu_and_slope(values):
    root = math.sqrt(2.0 / math.pi)
    square = values * values
    bend = jnp.tanh(root * (values + 0.044715 * (values * square)))
    rise = root * (1.0 + 3.0 * 0.044715 * square)
    result = 0.5 * values * (1.0 + bend)
    slope = 0.5 * (1.0 + bend) + 0.5 * values * ((1.0 - bend * bend) * rise)
    return result, slope


def spread_vectors(packed):
    rows = packed.shape[0]
    width = rows
    lane = lax.broadcasted_iota(jnp.int32, (128, width), 1)
    source = lax.broadcasted_iota(jnp.int32, (128, width), 0)
    select = jnp.where(lax.rem(lane, 32) == source, 1.0, 0.0).astype(jnp.bfloat16)
    wide = jnp.dot(packed, select, preferred_element_type=jnp.float32)
    row = lax.broadcasted_iota(jnp.int32, (rows, width), 0)
    lane = lax.broadcasted_iota(jnp.int32, (rows, width), 1)
    wide = jnp.where(row // 32 == lane // 32, wide, 0.0)
    return jnp.sum(wide.reshape(rows // 32, 32, width), axis=0)


def quarter_columns(values, width, back=False):
    share = 32
    per = 128 // share
    shards = width // share
    lane = lax.broadcasted_iota(jnp.int32, (values.shape[0], 128), 1) // share
    blocks = [values[:, k * 128 : (k + 1) * 128] for k in range(4 * shards * share // 128)]
    result = []
    for k in range(len(blocks)):
        total = None
        for j in range(per):
            if back:
                source, held = blocks[j * (shards // per) + k // per], k % per
            else:
                source, held = blocks[per * (k % (shards // per)) + j], k // (shards // per)
            moved = source if held == j else pltpu.roll(source, (j - held) * share % 128, 1)
            total = moved if total is None else jnp.where(lane == j, moved, total)
        result.append(total)
    return jnp.concatenate(result, axis=1)


def arrange_columns(target, source, sem, width):
    copy = pltpu.make_async_copy(source, target, sem)
    copy.start()
    copy.wait()
    values = target[...].astype(jnp.float32)
    target[...] = quarter_columns(values, width).astype(target.dtype)


class Copies:
    def __init__(self, sems):
        self.sems = sems
        self.open = {}
        self.used = 0

    def start(self, source, target):
        copy = pltpu.make_async_copy(source, target, self.sems.at[self.used])
        self.used += 1
        copy.start()
        return copy


def forward_kernel(depth, sizes, *refs):
    refs = list(refs)

    def take(count):
        taken = refs[:count]
        del refs[:count]
        return taken

    shard_count = len(sizes)
    tokens, texts, cots, unit_length, text_length = take(5)
    shards = take(7 + 1)
    wholes = take(shard_count)
    (
        o_tokens, o_text, o_h1, o_qkv, o_o1, o_after_self, o_h2, o_cq, o_ckv, o_o2,
        o_after_cross, o_h3, o_active, o_slope, o_gaf, o_gbr, o_layer,
    ) = take(17)
    vec, lse1, lse2, zgrads = take(4)
    tok, txt, cot, x, o1, cq, ckv, o2, resid, h2, ring, slopes, packed = take(13)
    stops = take(sum(len(weight_items(s)) for s in sizes))
    send, receive, local, sw_send, sw_receive, sw_local, loads, outs = take(8)
    (up_stop, up_sem) = take(2)

    place = Place(depth)
    y = place.y
    rows = resid.shape[0]
    width = resid.shape[1]
    part = rows // 2
    copies = Copies(outs)
    sources = list(shards[:DOWN_INDEX])
    sources[UP_INDEX] = up_stop
    share = sizes[0][0]
    sources += [shards[DOWN_INDEX].at[pl.ds(q * share, share)] for q in range(4)]
    phases, chunks, item = [], [], 0
    for index, size in enumerate(sizes):
        for r, c in weight_items(size):
            phases.append(
                gather_phases(
                    place, sources[index], wholes[index], r, c, (send, receive), local,
                    stops[item], item,
                )
            )
            if index > 0 and c.start % width == 0:
                chunks.append((wholes[index], pl.ds(c.start, width)))
            item += 1
    stages = pipelined(phases[1:], STRIDE)
    for k, phase in enumerate(phases[0]):
        stages[STRIDE * k].append(phase)

    def swapping(k, source, target, count, first):
        size = source.shape[1] // count

        def away(i):
            piece = pl.ds(i * size, size)
            return remote(
                source.at[1 - y, piece], target.at[y, piece], (sw_send, sw_receive), k, i,
                place.across_y(),
            )

        home = pltpu.make_async_copy(source.at[y], target.at[y], sw_local.at[k])
        for i in range(count):
            stages[first + i].append(lambda i=i: away(i).start())
        stages[first].append(home.start)

        def closing():
            home.wait()
            for i in range(count):
                away(i).wait()

        return closing

    token_swap = swapping(0, tokens, tok, 8, 0)
    text_swap = swapping(1, texts, txt, 2, 10)
    cot_swap = swapping(2, cots, cot, SWAP_PIECES, 22)

    def load(chunk):
        whole, cols = chunks[chunk]
        return pltpu.make_async_copy(
            whole.at[:, :, :, :, :, cols], ring.at[chunk % RING], loads.at[chunk]
        )

    ran = []

    def stage(k):
        assert len(ran) == k
        ran.append(k)
        for one in stages[k]:
            one()
        ready = k - 4 * STRIDE
        if ready > 0 and ready % 2 == 1:
            load(ready // 2).start()

    def weight(chunk):
        return ring[chunk % RING].reshape(width, width)

    def row(index):
        return vec[index : index + 1, :]

    def looped(count, body, due=()):
        @pl.loop(0, count)
        def _(j):
            for at, k in due:

                @pl.when(j == at)
                def _(k=k):
                    stage(k)

            body(j)

    place.greet()
    for k in range(4):
        stage(k)
    arrange_columns(up_stop, shards[UP_INDEX], up_sem, width)
    for k in range(4, 14):
        stage(k)
    pack = pltpu.make_async_copy(wholes[0], packed, outs.at[copies.used])
    copies.used += 1
    pack.start()
    pack.wait()
    vec[...] = spread_vectors(packed[...].reshape(-1, 128))
    token_swap()
    done_tokens = copies.start(tok, o_tokens)

    def token_block(b):
        half = b // (part // BLOCK)
        inner = lax.rem(b, part // BLOCK)
        return tok[half, block_rows(inner, BLOCK), :].astype(jnp.float32)

    def norm_one(b):
        unit, _ = center_and_scale(token_block(b))
        at = block_rows(b, BLOCK)
        x[at, 3 * width :] = (unit * row(A_GAIN) + row(A_SHIFT)).astype(jnp.bfloat16)
        resid[at, :] = token_block(b)

    looped(rows // BLOCK, norm_one)
    done_h1 = copies.start(x.at[:, pl.ds(3 * width, width)], o_h1)

    def project(chunk):
        bias = (row(A_QBIAS), None, row(A_VBIAS))[chunk]
        load(chunk).wait()

        def block(b):
            at = block_rows(b, MATMUL_ROWS)
            value = nn(x[at, 3 * width :], weight(chunk))
            if bias is not None:
                value = value + bias
            x[at, chunk * width : (chunk + 1) * width] = value.astype(jnp.bfloat16)

        looped(rows // MATMUL_ROWS, block)

    stage(14)
    project(0)
    stage(15)
    project(1)
    stage(16)
    stage(17)
    project(2)
    done_qkv = copies.start(x.at[:, pl.ds(0, 3 * width)], o_qkv)
    pairs = width // 128

    def self_pair(j):
        def part_of(base):
            return lambda lo, hi: x[lo:hi, lanes(j + base * pairs, 128)]

        def put(sl, value):
            o1[sl, lanes(j, 128)] = value

        attend_pair(
            True, rows, rows, min(SELF_QUERIES, rows), part_of(0), part_of(1), part_of(2), None, put, lse1.at[j]
        )

    looped(pairs, self_pair, ((1, 18), (2, 19), (4, 20), (5, 21), (7, 22)))
    done_o1 = copies.start(o1, o_o1)
    load(3).wait()

    def out_block(b):
        at = block_rows(b, MATMUL_ROWS)
        resid[at, :] = resid[at, :] + nn(o1[at, :], weight(3)) + row(A_OBIAS)

    looped(rows // MATMUL_ROWS, out_block)
    stage(23)
    done_after_self = copies.start(resid, o_after_self)

    def norm_two(b):
        at = block_rows(b, BLOCK)
        unit, _ = center_and_scale(resid[at, :])
        h2[at, :] = (unit * row(C_GAIN) + row(C_SHIFT)).astype(jnp.bfloat16)

    looped(rows // BLOCK, norm_two)
    done_h2 = copies.start(h2, o_h2)
    stage(24)
    load(4).wait()

    def cq_block(b):
        at = block_rows(b, MATMUL_ROWS)
        cq[at, :] = (nn(h2[at, :], weight(4)) + row(C_QBIAS)).astype(jnp.bfloat16)

    looped(rows // MATMUL_ROWS, cq_block)
    done_cq = copies.start(cq, o_cq)
    text_swap()
    done_text = copies.start(txt, o_text)
    text = txt[...].reshape(-1, width)
    text_rows = text.shape[0]
    stage(25)
    load(5).wait()
    ckv[:, :width] = nn(text, weight(5)).astype(jnp.bfloat16)
    load(6).wait()
    ckv[:, width:] = (nn(text, weight(6)) + row(C_VBIAS)).astype(jnp.bfloat16)
    done_ckv = copies.start(ckv, o_ckv)
    bias = text_mask(text_rows, text_length[y])

    def cross_pair(j):
        def put(sl, value):
            o2[sl, lanes(j, 128)] = value

        attend_pair(
            False, rows, text_rows, min(CROSS_QUERIES, rows),
            lambda lo, hi: cq[lo:hi, lanes(j, 128)],
            lambda lo, hi: ckv[lo:hi, lanes(j, 128)],
            lambda lo, hi: ckv[lo:hi, lanes(j + pairs, 128)],
            bias, put, lse2.at[j],
        )

    looped(pairs, cross_pair, ((1, 26), (4, 27), (6, 28)))
    done_o2 = copies.start(o2, o_o2)
    load(7).wait()
    done_after_self.wait()

    def cross_out_block(b):
        at = block_rows(b, MATMUL_ROWS)
        resid[at, :] = resid[at, :] + nn(o2[at, :], weight(7)) + row(C_OBIAS)

    looped(rows // MATMUL_ROWS, cross_out_block)
    stage(29)
    done_after_cross = copies.start(resid, o_after_cross)
    done_o1.wait()
    h3 = o1

    def norm_three(b):
        at = block_rows(b, BLOCK)
        unit, _ = center_and_scale(resid[at, :])
        h3[at, :] = (unit * row(F_GAIN) + row(F_SHIFT)).astype(jnp.bfloat16)

    looped(rows // BLOCK, norm_three)
    done_h3 = copies.start(h3, o_h3)
    done_h1.wait()
    done_qkv.wait()
    waiting = []

    def up(q):
        load(8 + q).wait()
        slope_at = slopes.at[q % 2]

        def block(b):
            at = block_rows(b, BLOCK)
            inner = nn(h3[at, :], weight(8 + q)) + row(F_UPBIAS + q)
            active, slope = gelu_and_slope(inner)
            x[at, q * width : (q + 1) * width] = active.astype(jnp.bfloat16)
            slope_at[at, :] = slope.astype(jnp.bfloat16)

        if q >= 2:
            waiting[q - 2].wait()
        looped(rows // BLOCK, block)
        span = pl.ds(q * width, width)
        waiting.append(copies.start(slope_at, o_slope.at[:, span]))

    stage(30)
    stage(31)
    up(0)
    stage(32)
    stage(33)
    up(1)
    stage(34)
    up(2)
    stage(35)
    stage(36)
    up(3)
    stage(37)
    done_active = copies.start(x, o_active)
    done_after_cross.wait()

    def down(q):
        load(12 + q).wait()

        def block(b):
            at = block_rows(b, MATMUL_ROWS)
            resid[at, :] += nn(x[at, q * width : (q + 1) * width], weight(12 + q))

        looped(rows // MATMUL_ROWS, block)

    for q in range(4):
        down(q)
        if q < 3:
            stage(38 + 2 * q)
            stage(39 + 2 * q)
    cot_swap()
    done_cq.wait()
    done_o2.wait()
    valid_count = unit_length[y]
    zgrads[...] = jnp.zeros_like(zgrads)
    gbr, layer = cq, o2

    def last_block(b):
        at = block_rows(b, BLOCK)
        unit, scale = center_and_scale(resid[at, :] + row(F_DOWNBIAS))
        position = b * BLOCK + lax.broadcasted_iota(jnp.int32, (BLOCK, 1), 0)
        valid = jnp.where(position < valid_count, 1.0, 0.0)
        layer[at, :] = ((unit * row(Z_GAIN) + row(Z_SHIFT)) * valid).astype(jnp.bfloat16)
        half = b // (part // BLOCK)
        inner = lax.rem(b, part // BLOCK)
        upstream = cot[half, block_rows(inner, BLOCK), :].astype(jnp.float32) * valid
        zgrads[0:1, :] += jnp.sum(upstream * unit, axis=0, keepdims=True)
        zgrads[1:2, :] += jnp.sum(upstream, axis=0, keepdims=True)
        grad = norm_pull(unit, scale, upstream * row(Z_GAIN))
        low = grad.astype(jnp.bfloat16)
        gbr[at, :] = low
        zgrads[2:3, :] += jnp.sum(low.astype(jnp.float32), axis=0, keepdims=True)
        resid[at, :] = grad

    looped(rows // BLOCK, last_block)
    ending = [
        copies.start(resid, o_gaf), copies.start(gbr, o_gbr), copies.start(layer, o_layer),
    ]
    ending += [done_tokens, done_h2, done_text, done_ckv, done_h3, done_active]
    for copy in ending + waiting[2:]:
        copy.wait()


def text_mask(text_rows, count):
    position = lax.broadcasted_iota(jnp.int32, (text_rows, 128), 0)
    return jnp.where(position < count, 0.0, MASKED)


def forward(depth, number, tokens, texts, cots, unit_length, text_length, shards):
    rows, width = 2 * tokens.shape[1], tokens.shape[2]
    text_rows = 2 * texts.shape[1]
    hidden = 4 * width
    pairs = width // 128
    share = shards[0].shape[0]
    sizes = [s.shape for s in shards[:DOWN_INDEX]] + [(share, width)] * 4
    items = sum(len(weight_items(s)) for s in sizes)
    low, full = jnp.bfloat16, jnp.float32

    def shape(*dims, kind=low):
        return jax.ShapeDtypeStruct(dims, kind)

    def vmem(*dims, kind=low):
        return pltpu.VMEM(dims, kind)

    big = shape(rows, width)
    exact = shape(rows, width, kind=full)
    outs = [shape(depth, 2, 2, 2, *s) for s in sizes]
    outs += [
        shape(*tokens.shape), shape(*texts.shape), big, shape(rows, 3 * width), big, exact, big, big,
        shape(text_rows, 2 * width), big, exact, big, shape(rows, hidden), shape(rows, hidden),
        exact, big, big,
    ]
    small = [
        shape(32, width, kind=full), shape(pairs, 2, rows, kind=full),
        shape(pairs, 2, rows, kind=full), shape(8, width, kind=full),
    ]
    scratch = [
        vmem(*tokens.shape), vmem(*texts.shape), vmem(*cots.shape), vmem(rows, hidden),
        vmem(rows, width), vmem(rows, width), vmem(text_rows, 2 * width), vmem(rows, width),
        vmem(rows, width, kind=full), vmem(rows, width), vmem(RING, depth, 2, 2, 2, 32, width),
        vmem(2, rows, width), vmem(depth, 2, 2, 2, *sizes[0]),
    ]
    scratch += [vmem(r.size, c.size) for s in sizes for r, c in weight_items(s)]
    scratch += copy_sems(items, depth)
    scratch += [
        pltpu.SemaphoreType.DMA((3, SWAP_PIECES)), pltpu.SemaphoreType.DMA((3, SWAP_PIECES)),
        pltpu.SemaphoreType.DMA((3,)), pltpu.SemaphoreType.DMA((items,)),
        pltpu.SemaphoreType.DMA((32,)), vmem(*sizes[UP_INDEX]), pltpu.SemaphoreType.DMA,
    ]
    memory = pl.BlockSpec(memory_space=pltpu.SMEM)
    results = pl.pallas_call(
        functools.partial(forward_kernel, depth, sizes),
        out_shape=outs + small,
        in_specs=[ANYWHERE] * 3 + [memory] * 2 + [ANYWHERE] * len(shards),
        out_specs=[ANYWHERE] * len(outs) + [pl.BlockSpec(memory_space=pltpu.VMEM)] * len(small),
        scratch_shapes=scratch,
        compiler_params=pltpu.CompilerParams(
            collective_id=number, has_side_effects=True, vmem_limit_bytes=VMEM_LIMIT
        ),
        name="forward",
    )(tokens, texts, cots, unit_length, text_length, *shards)
    return list(results[: len(sizes)]), list(results[len(sizes) :])


BACK_STRIDE = 2
BACK_RING = 3 * BACK_STRIDE
BACK_QUERIES = 256
WEIGHT_RING = 3
NORM_BLOCK = 128


def ring_scratch(depth, slots, rows, cols, dtype):
    half = rows // 2
    return [
        pltpu.VMEM((slots, depth, 2, 2, 2, rows, cols), dtype),
        pltpu.VMEM((min(slots, 2 * BACK_STRIDE), depth, 2, 2, rows, cols), dtype),
        pltpu.VMEM((slots, depth, 2, half, cols), dtype),
        pltpu.VMEM((slots, depth, half, cols), dtype),
        pltpu.VMEM((slots, depth - 1, half, cols), dtype),
        pltpu.VMEM((slots, depth, 2, half, cols), dtype),
        pltpu.VMEM((slots, depth - 1, 2, half, cols), dtype),
        pltpu.VMEM((slots, half, cols), dtype),
    ]


def piece_phases(place, put_result, bufs, sems, item):
    slots, depth = bufs[0].shape[0], bufs[0].shape[1]
    slot = item % slots
    piece = bufs[0].at[slot]
    came = bufs[1].at[item % bufs[1].shape[0]]
    a_y, a_x, a_z, b_x, b_z, b_y = (buf.at[slot] for buf in bufs[2:])
    half = bufs[7].shape[1]
    low, high = pl.ds(0, half), pl.ds(half, half)
    z, x, core, y = place.z, place.x, place.core, place.y
    every = slice(None)

    def send(a, b, index, device):
        return remote(a, b, sems, item, index, device)

    def copies(phase):
        if phase == 0:
            return [send(piece.at[every, every, 1 - core], came, 0, place.sibling())]
        if phase == 1:
            return [
                send(piece.at[every, every, core, 1 - y, low], a_y, 1, place.across_y()),
                send(piece.at[every, 1 - x, core, every, high], b_x, 2, place.across_x()),
            ]
        if phase == 2:
            return [send(a_y.at[every, 1 - x], a_x, 3, place.across_x())] + [
                send(
                    b_x.at[lax.rem(z + step, depth)], b_z.at[step - 1], 3 + step,
                    place.along_z(step),
                )
                for step in range(1, depth)
            ]
        return [send(b_z.at[0, 1 - y], b_y, 3 + depth, place.across_y())] + [
            send(
                a_x.at[lax.rem(z + step, depth)], a_z.at[step - 1], 3 + depth + step,
                place.along_z(step),
            )
            for step in range(1, depth)
        ]

    def start(phase):
        for copy in copies(phase):
            copy.start()

    def wait(phase):
        for copy in copies(phase):
            copy.wait()

    def wide(values):
        return values.astype(jnp.float32)

    def after_core():
        wait(0)

        @pl.loop(0, depth)
        def _(k):
            for i in range(2):
                for j in range(2):
                    piece[k, i, core, j] = piece[k, i, core, j] + came[k, i, j]

        start(1)

    def after_one():
        wait(1)

        @pl.loop(0, depth)
        def _(k):
            for i in range(2):
                a_y[k, i] = a_y[k, i] + piece[k, i, core, y, low]
                b_x[k, i] = b_x[k, i] + piece[k, x, core, i, high]

        start(2)

    def after_two():
        wait(2)

        @pl.loop(0, depth)
        def _(k):
            a_x[k] = a_x[k] + a_y[k, x]

        for i in range(2):
            total = wide(b_x[z, i])
            for step in range(1, depth):
                total = total + wide(b_z[step - 1, i])
            b_z[0, i] = total.astype(b_z.dtype)
        start(3)

    def closing():
        wait(3)
        total = wide(a_x[z])
        for step in range(1, depth):
            total = total + wide(a_z[step - 1])
        put_result(low, total)
        put_result(high, wide(b_z[0, y]) + wide(b_y[...]))

    return [lambda: start(0), after_core, after_one, after_two, closing]


def gather_vectors(vectors, first, shards):
    width = vectors.shape[1]
    row = first + lax.broadcasted_iota(jnp.int32, (shards, 32, width), 0)
    lane = lax.broadcasted_iota(jnp.int32, (shards, 32, width), 2)
    parts = jnp.where(row == lane // 32, vectors[None], 0.0).reshape(shards * 32, width)
    source = lax.broadcasted_iota(jnp.int32, (width, 128), 0)
    lane = lax.broadcasted_iota(jnp.int32, (width, 128), 1)
    select = jnp.where(lax.rem(source, 32) == lane, 1.0, 0.0)
    return jnp.dot(
        parts, select, precision=lax.Precision.HIGHEST, preferred_element_type=jnp.float32
    )


def backward_kernel(depth, *refs):
    refs = list(refs)

    def take(count):
        taken = refs[:count]
        del refs[:count]
        return taken

    w_in, w_out, w_cq, w_ckv, w_co, w_up = take(6)
    w_downs = take(4)
    (
        i_tokens, i_text, i_h1, i_qkv, i_o1, i_after_self, i_h2, i_cq, i_ckv, i_o2, i_after_cross,
        i_h3, i_active, i_slope, i_gaf, i_gbr, i_layer,
    ) = take(17)
    vec, lse1, lse2, zgrads, text_length = take(5)
    o_layer, o_tokens, o_text = take(3)
    s_in, s_out, s_cq, s_ckv, s_co, s_up, s_down, s_small = take(8)
    p, q_buf, resid, dh, low, h3, extra, ckv, dckv, text, tgrad, src, vg, ka, va = take(15)
    ring = take(1)[0]
    bufs = take(8)
    small_bufs = take(8)
    sems = take(2)
    small_sems = take(2)
    swap_send, swap_receive, swap_local, loads, fetches = take(5)

    place = Place(depth)
    y = place.y
    rows, width = resid.shape
    part_rows = rows // 2
    pairs = width // 128
    shards = depth * 8
    text_rows = ckv.shape[0]
    fetched = Copies(fetches)
    fetch = fetched.start

    half_width = width // 2
    targets = [(s_down, q, h) for q in range(4) for h in (0, 1)]
    targets += [(s_co, 0, h) for h in (0, 1)]
    targets += [(s_up, 0, h) for h in range(8)]
    targets += [(s_cq, 0, h) for h in (0, 1)]
    targets += [(s_ckv, 0, h) for h in range(4)]
    targets += [(s_out, 0, h) for h in (0, 1)]
    targets += [(s_in, 0, 2 * c + h) for h in (0, 1) for c in range(3)]
    share = width // shards

    def keeping(target, quarter, column):
        def put(some_rows, value):
            at = pl.ds(quarter * share + some_rows.start, some_rows.size)
            target[at, column * half_width : (column + 1) * half_width] = value

        return put

    phases = [
        piece_phases(place, keeping(*target), bufs, sems, item)
        for item, target in enumerate(targets)
    ]

    def put_small(some_rows, value):
        s_small[some_rows, :] = value

    small_phases = piece_phases(place, put_small, small_bufs, small_sems, 0)
    stages = pipelined(phases + [[lambda: None] + small_phases[1:]], BACK_STRIDE)
    ran = []

    def stage(k):
        assert len(ran) == k
        ran.append(k)
        for one in stages[k]:
            one()

    def produce(item, get_left, *rights):
        @pl.loop(0, 2)
        def _(b):
            right = [get() for get in rights]
            right = right[0] if len(right) == 1 else jnp.concatenate(right, axis=1)
            value = left_dot(get_left(lanes(b, half_width)), right).astype(jnp.bfloat16)
            for k in range(len(rights)):
                some = value[:, k * half_width : (k + 1) * half_width]
                piece = bufs[0].at[(item + k) % BACK_RING]
                piece[pl.ds(b * (depth // 2), depth // 2)] = some.reshape(
                    depth // 2, 2, 2, 2, share, half_width
                )

        stage(item)

    def part(buf, k):
        return lambda: buf[:, k * half_width : (k + 1) * half_width]

    def halves(buf, k):
        return part(buf, 2 * k), part(buf, 2 * k + 1)

    order = []
    for k in range(4):
        order += [(w_downs[k], 0), (w_up, k)]
    order += [(w_co, 0), (w_ckv, 0), (w_ckv, 1), (w_cq, 0), (w_out, 0)]
    order += [(w_in, c) for c in range(3)]

    def load(n):
        whole, column = order[n]
        return pltpu.make_async_copy(
            whole.at[:, :, :, :, :, pl.ds(column * width, width)],
            ring.at[n % WEIGHT_RING],
            loads.at[n],
        )

    def weight(n):
        return ring[n % WEIGHT_RING].reshape(width, width)

    def ready(n):
        load(n).wait()

    def finished(n):
        if n + WEIGHT_RING < len(order):
            load(n + WEIGHT_RING).start()

    def row(index):
        return vec[index : index + 1, :]

    def add_row(index, value):
        vg[index : index + 1, :] += jnp.sum(value, axis=0, keepdims=True)

    def looped(count, body):
        @pl.loop(0, count)
        def _(j):
            body(j)

    def by_blocks(body, size=MATMUL_ROWS):
        looped(rows // size, lambda b: body(block_rows(b, size)))

    def column(buf, k):
        return lambda some_lanes: buf[:, pl.ds(k * width + some_lanes.start, some_lanes.size)]

    def plain(buf):
        return lambda some_lanes: buf[:, some_lanes]

    def norm_step(source, gain, shift, next_bias):
        blocks = rows // NORM_BLOCK

        def bring(b, slot):
            return pltpu.make_async_copy(
                source.at[block_rows(b, NORM_BLOCK), :], src.at[slot], swap_local.at[3 + slot]
            )

        bring(0, 0).start()

        def step(b):
            slot = lax.rem(b, 2)
            bring(b, slot).wait()

            @pl.when(b + 1 < blocks)
            def _():
                bring(b + 1, 1 - slot).start()

            at = block_rows(b, NORM_BLOCK)
            unit, scale = center_and_scale(src[slot])
            pulled = dh[at, :]
            add_row(gain, pulled * unit)
            add_row(shift, pulled)
            total = resid[at, :] + norm_pull(unit, scale, pulled * row(gain))
            resid[at, :] = total
            rounded = total.astype(jnp.bfloat16)
            low[at, :] = rounded
            add_row(next_bias, rounded.astype(jnp.float32))

        looped(blocks, step)

    def swap_out(k, get_source, target, local_source):
        def away():
            return remote(
                get_source(1 - y), target.at[y], (swap_send, swap_receive), k, 0, place.across_y()
            )

        def home():
            return pltpu.make_async_copy(local_source, target.at[y], swap_local.at[k])

        return away, home

    place.greet()
    for n in range(WEIGHT_RING):
        load(n).start()
    got_low = fetch(i_gbr, low)
    got_active = [
        fetch(i_active.at[:, pl.ds(k * width, width)], p.at[:, pl.ds(k * width, width)])
        for k in range(4)
    ]
    got_slope = [
        fetch(i_slope.at[:, pl.ds(k * width, width)], q_buf.at[:, pl.ds(k * width, width)])
        for k in range(4)
    ]
    got_resid = fetch(i_gaf, resid)
    got_h3 = fetch(i_h3, h3)
    keep = extra.at[pl.ds(0, part_rows)]
    got_keep = fetch(i_layer.at[y], keep)
    got_ckv = fetch(i_ckv, ckv)
    got_text = fetch(i_text, text)
    vg[...] = jnp.zeros_like(vg)
    vg[Z_GAIN : Z_GAIN + 1, :] = zgrads[0:1, :]
    vg[Z_SHIFT : Z_SHIFT + 1, :] = zgrads[1:2, :]
    vg[F_DOWNBIAS : F_DOWNBIAS + 1, :] = zgrads[2:3, :]
    layer_count = 16
    layer_size = part_rows // layer_count

    def layer_away(i):
        piece = pl.ds(i * layer_size, layer_size)
        return remote(
            i_layer.at[1 - y, piece], o_layer.at[y, piece], (swap_send, swap_receive), 0, i,
            place.across_y(),
        )

    layer_home = pltpu.make_async_copy(keep, o_layer.at[y], swap_local.at[0])
    for i in range(layer_count):
        stages[1 + i].append(lambda i=i: layer_away(i).start())

    got_low.wait()
    for k in range(4):
        got_active[k].wait()
        produce(2 * k, column(p, k), *halves(low, 0))
        n = 2 * k
        got_slope[k].wait()
        ready(n)
        span = slice(k * width, (k + 1) * width)

        def inner_block(b, n=n, span=span, k=k):
            at = block_rows(b, BLOCK)
            grad = nt(low[at, :], weight(n)) * q_buf[at, span].astype(jnp.float32)
            rounded = grad.astype(jnp.bfloat16)
            q_buf[at, span] = rounded
            add_row(F_UPBIAS + k, rounded.astype(jnp.float32))

        looped(rows // BLOCK, inner_block)
        finished(n)
        stage(2 * k + 1)
        ready(n + 1)

        def up_block(at, n=n, span=span, k=k):
            value = nt(q_buf[at, span], weight(n + 1))
            dh[at, :] = value if k == 0 else dh[at, :] + value

        by_blocks(up_block)
        finished(n + 1)
    cq_at, o2_at, do2_at, h2_at = (slice(k * width, (k + 1) * width) for k in range(4))
    got_cq = fetch(i_cq, p.at[:, pl.ds(0, width)])
    got_o2 = fetch(i_o2, p.at[:, pl.ds(width, width)])
    got_h2 = fetch(i_h2, p.at[:, pl.ds(3 * width, width)])
    got_resid.wait()
    norm_step(i_after_cross, F_GAIN, F_SHIFT, C_OBIAS)
    got_keep.wait()
    layer_home.start()

    got_o2.wait()
    produce(8, column(p, 1), *halves(low, 0))
    ready(8)

    def do2_block(at):
        p[at, do2_at] = nt(low[at, :], weight(8)).astype(jnp.bfloat16)

    by_blocks(do2_block)
    finished(8)
    stage(9)
    got_cq.wait()
    got_h3.wait()
    got_ckv.wait()
    bias = text_mask(text_rows, text_length[y])
    dcq = extra
    layer_home.wait()

    def pair_lanes(buf, j, base):
        return lambda lo, hi: buf[lo:hi, lanes(j + base * pairs, 128)]

    def cross_pair(j):
        for at, k in ((0, 10), (2, 11), (3, 12), (5, 13), (7, 14)):

            @pl.when(j == at)
            def _(k=k):
                if k % 2 == 0:
                    produce(k, plain(h3), *halves(q_buf, (k - 10) // 2))
                else:
                    stage(k)

        def put_dq(sl, value):
            dcq[sl, lanes(j, 128)] = value
            vg[C_QBIAS : C_QBIAS + 1, lanes(j, 128)] += jnp.sum(
                value.astype(jnp.float32), axis=0, keepdims=True
            )

        def put_dk(value):
            dckv[:, lanes(j, 128)] = value

        def put_dv(value):
            dckv[:, lanes(j + pairs, 128)] = value
            vg[C_VBIAS : C_VBIAS + 1, lanes(j, 128)] = jnp.sum(
                value.astype(jnp.float32), axis=0, keepdims=True
            )

        attend_back_pair(
            False, rows, text_rows, BACK_QUERIES, pair_lanes(p, j, 0), pair_lanes(ckv, j, 0),
            pair_lanes(ckv, j, 1), pair_lanes(p, j, 1), pair_lanes(p, j, 2), lse2.at[j], bias,
            put_dq, put_dk, put_dv, ka, va,
        )

    looped(pairs, cross_pair)
    got_qkv = fetch(i_qkv, p.at[:, pl.ds(0, 3 * width)])
    stage(15)
    ready(9)
    text_value = nt(dckv[:, :width], weight(9))
    finished(9)
    ready(10)
    text_value = text_value + nt(dckv[:, width:], weight(10))
    finished(10)
    tgrad[...] = text_value.astype(jnp.bfloat16).reshape(tgrad.shape)
    text_away, text_home = swap_out(1, lambda k: tgrad.at[k], o_text, tgrad.at[y])
    text_away().start()
    text_home().start()
    produce(16, plain(h3), *halves(q_buf, 3))
    ready(11)

    def dh2_block(at):
        dh[at, :] = nt(dcq[at, :], weight(11))

    by_blocks(dh2_block)
    finished(11)
    stage(17)
    got_o1 = fetch(i_o1, q_buf.at[:, pl.ds(3 * width, width)])
    got_tokens = fetch(i_tokens, h3)
    norm_step(i_after_self, C_GAIN, C_SHIFT, A_OBIAS)
    got_h2.wait()
    produce(18, column(p, 3), *halves(dcq, 0))
    got_h1 = fetch(i_h1, p.at[:, pl.ds(3 * width, width)])

    ready(12)
    do1 = extra

    def do1_block(at):
        do1[at, :] = nt(low[at, :], weight(12)).astype(jnp.bfloat16)

    by_blocks(do1_block)
    finished(12)
    stage(19)
    got_text.wait()

    def text_lanes(some_lanes):
        return text[:, :, some_lanes].reshape(text_rows, some_lanes.size)

    got_qkv.wait()
    got_o1.wait()

    def self_pair(j):
        def put_dq(sl, value):
            q_buf[sl, lanes(j, 128)] = value
            vg[A_QBIAS : A_QBIAS + 1, lanes(j, 128)] += jnp.sum(
                value.astype(jnp.float32), axis=0, keepdims=True
            )

        def put_dk(value):
            q_buf[:, lanes(j + pairs, 128)] = value

        def put_dv(value):
            q_buf[:, lanes(j + 2 * pairs, 128)] = value
            vg[A_VBIAS : A_VBIAS + 1, lanes(j, 128)] = jnp.sum(
                value.astype(jnp.float32), axis=0, keepdims=True
            )

        attend_back_pair(
            True, rows, rows, BACK_QUERIES, pair_lanes(p, j, 0), pair_lanes(p, j, 1), pair_lanes(p, j, 2),
            pair_lanes(q_buf, j, 3), lambda lo, hi: do1[lo:hi, lanes(j, 128)], lse1.at[j], None,
            put_dq, put_dk, put_dv, ka, va,
        )

    half_pairs = pairs // 2

    def first_half(j):
        for k in range(4):

            @pl.when(j == k)
            def _(k=k):
                if k % 2 == 0:
                    produce(20 + k, text_lanes, *halves(dckv, k // 2))
                else:
                    stage(20 + k)

        self_pair(j)

    looped(half_pairs, first_half)
    got_h1.wait()

    def second_half(j):
        @pl.when(j == 0)
        def _():
            produce(24, column(q_buf, 3), *halves(low, 0))

        @pl.when(j == 1)
        def _():
            stage(25)

        @pl.when(j == 2)
        def _():
            produce(26, column(p, 3), part(q_buf, 0), part(q_buf, 2))
            stage(27)

        @pl.when(j == 3)
        def _():
            produce(28, column(p, 3), part(q_buf, 4))

        self_pair(j + half_pairs)

    looped(half_pairs, second_half)

    grads = low

    def rows_of(half, b):
        return pl.ds(pl.multiple_of(half * part_rows + b * BLOCK, BLOCK), BLOCK)

    def dh1_block(half, c):
        def block(b):
            at = rows_of(half, b)
            value = nt(q_buf[at, c * width : (c + 1) * width], weight(13 + c))
            dh[at, :] = value if c == 0 else dh[at, :] + value

        return block

    def last_block(half):
        def block(b):
            at = rows_of(half, b)
            unit, scale = center_and_scale(h3[at, :].astype(jnp.float32))
            pulled = dh[at, :]
            add_row(A_GAIN, pulled * unit)
            add_row(A_SHIFT, pulled)
            total = resid[at, :] + norm_pull(unit, scale, pulled * row(A_GAIN))
            grads[at, :] = total.astype(jnp.bfloat16)

        return block

    tokens_away, tokens_home = swap_out(
        2,
        lambda k: grads.at[block_rows(k, part_rows), :],
        o_tokens,
        grads.at[block_rows(y, part_rows), :],
    )
    count = part_rows // BLOCK
    produce(29, column(p, 3), part(q_buf, 1), part(q_buf, 3))
    got_tokens.wait()
    for c in range(3):
        ready(13 + c)
        looped(count, dh1_block(1 - y, c))
    stage(30)
    looped(count, last_block(1 - y))
    tokens_away().start()
    produce(31, column(p, 3), part(q_buf, 5))
    for c in range(3):
        looped(count, dh1_block(y, c))
    stage(32)
    looped(count, last_block(y))
    tokens_home().start()

    @pl.loop(0, depth)
    def _(k):
        some = gather_vectors(vg[...], k * 8, 8)
        small_bufs[0][0, k] = some.reshape(small_bufs[0].shape[2:])

    small_phases[0]()
    for k in range(33, len(stages)):
        stage(k)
    values = s_up[...]
    s_up[...] = quarter_columns(values, width, back=True)
    for copy in (
        *[layer_away(i) for i in range(layer_count)], text_away(), text_home(), tokens_away(), tokens_home(),
    ):
        copy.wait()


def backward(depth, number, wholes, kept, text_length):
    (
        token_seq, text_seq, normed_one, joined, self_mixed, after_self, normed_two, cross_queries,
        cross_kv, cross_mixed, after_cross, normed_three, active, slope, grad_after_ffn,
        grad_branch, layer_out, vec, lse1, lse2, zgrads,
    ) = kept
    rows, width = self_mixed.shape
    text_rows = cross_kv.shape[0]
    hidden = active.shape[1]
    share = width // (depth * 8)
    half = (2, rows // 2, width)
    low, full = jnp.bfloat16, jnp.float32
    operands = [
        token_seq.reshape(rows, width), text_seq, normed_one, joined, self_mixed, after_self,
        normed_two, cross_queries, cross_kv, cross_mixed, after_cross, normed_three, active, slope,
        grad_after_ffn, grad_branch, layer_out.reshape(half),
    ]

    def vmem(*dims, kind=low):
        return pltpu.VMEM(dims, kind)

    results_low = [jax.ShapeDtypeStruct(s, low) for s in (half, half, text_seq.shape)]
    columns = [w.shape[-1] for w in wholes[:6]]
    sums = [jax.ShapeDtypeStruct((share, c), full) for c in columns]
    sums += [jax.ShapeDtypeStruct((4 * share, width), full), jax.ShapeDtypeStruct((share, 128), full)]
    scratch = [
        vmem(rows, hidden), vmem(rows, hidden), vmem(rows, width, kind=full),
        vmem(rows, width, kind=full), vmem(rows, width), vmem(rows, width), vmem(rows, width),
        vmem(text_rows, 2 * width), vmem(text_rows, 2 * width), vmem(*text_seq.shape),
        vmem(*text_seq.shape), vmem(2, NORM_BLOCK, width, kind=full),
        vmem(32, width, kind=full), vmem(rows, 128, kind=full), vmem(rows, 128, kind=full),
        vmem(WEIGHT_RING, depth, 2, 2, 2, share, width),
    ]
    scratch += ring_scratch(depth, BACK_RING, share, width // 2, low)
    scratch += ring_scratch(depth, 1, share, 128, full)
    pieces = 2 * (sum(c // width for c in columns) + 4)
    scratch += copy_sems(pieces, depth)[:2] + copy_sems(1, depth)[:2]
    scratch += [
        pltpu.SemaphoreType.DMA((3, 16)), pltpu.SemaphoreType.DMA((3, 16)),
        pltpu.SemaphoreType.DMA((5,)), pltpu.SemaphoreType.DMA((16,)),
        pltpu.SemaphoreType.DMA((32,)),
    ]
    in_vmem = pl.BlockSpec(memory_space=pltpu.VMEM)
    results = pl.pallas_call(
        functools.partial(backward_kernel, depth),
        out_shape=results_low + sums,
        in_specs=[ANYWHERE] * (len(wholes) + len(operands))
        + [in_vmem] * 4
        + [pl.BlockSpec(memory_space=pltpu.SMEM)],
        out_specs=[ANYWHERE] * 3 + [in_vmem] * len(sums),
        scratch_shapes=scratch,
        compiler_params=pltpu.CompilerParams(
            collective_id=number, has_side_effects=True, vmem_limit_bytes=BACK_VMEM_LIMIT
        ),
        name="backward",
    )(*wholes, *operands, vec, lse1, lse2, zgrads, text_length)
    return list(results[:3]), list(results[3:])


BACK_VMEM_LIMIT = 61 * 2**20


def pack_vectors(vectors, wide):
    packed = jnp.concatenate([jnp.stack(vectors), wide.reshape(4, -1)])
    return jnp.pad(packed, ((0, 32 - packed.shape[0]), (0, 128 - packed.shape[1])))


def paired_layer(
    depth,
    tokens,
    text_states,
    unit_length,
    text_length,
    cotangent,
    attn_gain,
    attn_shift,
    attn_inputs,
    attn_qbias,
    attn_vbias,
    attn_output,
    attn_obias,
    cross_gain,
    cross_shift,
    cross_query,
    cross_qbias,
    cross_keyval,
    cross_vbias,
    cross_output,
    cross_obias,
    ffn_gain,
    ffn_shift,
    ffn_up,
    ffn_upbias,
    ffn_down,
    ffn_downbias,
    final_gain,
    final_shift,
):
    share = attn_gain.shape[0]
    packed = pack_vectors(
        [
            attn_gain, attn_shift, attn_qbias, attn_vbias, attn_obias, cross_gain, cross_shift,
            cross_qbias, cross_vbias, cross_obias, ffn_gain, ffn_shift, ffn_downbias, final_gain,
            final_shift,
        ],
        ffn_upbias,
    )
    wholes, kept = forward(
        depth, 0, tokens, text_states, cotangent, unit_length, text_length,
        [
            packed, attn_inputs, attn_output, cross_query, cross_keyval, cross_output, ffn_up,
            ffn_down,
        ],
    )
    (layer_out, tokens_grad, text_grad), sums = backward(depth, 1, wholes[1:], kept, text_length)
    s_in, s_out, s_cq, s_ckv, s_co, s_up, s_down, s_small = sums
    s_upbias = s_small[VECTOR_COUNT : VECTOR_COUNT + 4, :share].reshape(-1)
    v = [s_small[i, :share] for i in range(VECTOR_COUNT)]
    return (
        layer_out, tokens_grad, text_grad, v[A_GAIN], v[A_SHIFT], s_in, v[A_QBIAS], v[A_VBIAS],
        s_out, v[A_OBIAS], v[C_GAIN], v[C_SHIFT], s_cq, v[C_QBIAS], s_ckv, v[C_VBIAS], s_co,
        v[C_OBIAS], v[F_GAIN], v[F_SHIFT], s_up, s_upbias, s_down, v[F_DOWNBIAS], v[Z_GAIN],
        v[Z_SHIFT],
    )


def solution(mesh):
    in_specs = (
        P("dp", "seq", None),
        P("dp", "seq", None),
        P("dp"),
        P("dp"),
        P("dp", "seq", None),
        P(("dp", "seq")),
        P(("dp", "seq")),
        P(("dp", "seq"), None),
        P(("dp", "seq")),
        P(("dp", "seq")),
        P(("dp", "seq"), None),
        P(("dp", "seq")),
        P(("dp", "seq")),
        P(("dp", "seq")),
        P(("dp", "seq"), None),
        P(("dp", "seq")),
        P(("dp", "seq"), None),
        P(("dp", "seq")),
        P(("dp", "seq"), None),
        P(("dp", "seq")),
        P(("dp", "seq")),
        P(("dp", "seq")),
        P(("dp", "seq"), None),
        P(("dp", "seq")),
        P(("dp", "seq"), None),
        P(("dp", "seq")),
        P(("dp", "seq")),
        P(("dp", "seq")),
    )
    out_specs = (
        P("dp", "seq", None),
        P("dp", "seq", None),
        P("dp", "seq", None),
        P(("dp", "seq")),
        P(("dp", "seq")),
        P(("dp", "seq"), None),
        P(("dp", "seq")),
        P(("dp", "seq")),
        P(("dp", "seq"), None),
        P(("dp", "seq")),
        P(("dp", "seq")),
        P(("dp", "seq")),
        P(("dp", "seq"), None),
        P(("dp", "seq")),
        P(("dp", "seq"), None),
        P(("dp", "seq")),
        P(("dp", "seq"), None),
        P(("dp", "seq")),
        P(("dp", "seq")),
        P(("dp", "seq")),
        P(("dp", "seq"), None),
        P(("dp", "seq")),
        P(("dp", "seq"), None),
        P(("dp", "seq")),
        P(("dp", "seq")),
        P(("dp", "seq")),
    )
    groups, seq_parts = mesh.shape["dp"], mesh.shape["seq"]

    def layer(*arguments):
        shard = arguments[5].shape[0]
        parts = arguments[0].shape[0]
        if seq_parts == 2 and parts == 2 and groups % 4 == 0 and shard % 32 == 0:
            return paired_layer(groups // 4, *arguments)
        return on_device(*arguments)

    return jax.shard_map(
        layer, mesh=mesh, in_specs=in_specs, out_specs=out_specs, check_vma=False
    )
```

```python
import functools
import math

import jax
import jax.numpy as jnp
from jax import lax
from jax.experimental import pallas as pl
from jax.experimental.pallas import tpu as pltpu
from jax.sharding import PartitionSpec as P

HEADS = 16
HEAD_DIM = 64


EPSILON = 1e-05
MASKED = -1e30


def layer_norm(values, norm_gain, norm_shift):
    center = values - jnp.mean(values, axis=-1, keepdims=True)
    spread = jnp.mean(center * center, axis=-1, keepdims=True)
    return center * lax.rsqrt(spread + EPSILON) * norm_gain + norm_shift


def norm_back(values, norm_gain, norm_shift, upstream):
    result, pullback = jax.vjp(layer_norm, values, norm_gain, norm_shift)
    return pullback(upstream)


def rows_dot(left_side, right_side):
    return jnp.dot(left_side, right_side, preferred_element_type=jnp.float32)


def left_dot(left_side, right_side):
    return lax.dot_general(
        left_side, right_side, (((0,), (0,)), ((), ())), preferred_element_type=jnp.float32
    )


def right_dot(left_side, right_side):
    return lax.dot_general(
        left_side, right_side, (((1,), (1,)), ((), ())), preferred_element_type=jnp.float32
    )


def heads_of(matrix):
    return matrix.reshape(matrix.shape[0], HEADS, HEAD_DIM)


def attend_forward(queries, key_rows, value_rows, allowed):
    score_scale = 1.0 / math.sqrt(HEAD_DIM)
    scores = (
        jnp.einsum(
            "qhd,khd->hqk",
            heads_of(queries),
            heads_of(key_rows),
            preferred_element_type=jnp.float32,
        )
        * score_scale
    )
    scores = jnp.where(allowed[None], scores, MASKED)
    row_max = jnp.max(scores, axis=-1, keepdims=True)
    weights = jnp.exp(scores - row_max)
    row_total = jnp.sum(weights, axis=-1, keepdims=True)
    weights = (weights / row_total).astype(jnp.bfloat16)
    mixed_rows = jnp.einsum(
        "hqk,khd->qhd", weights, heads_of(value_rows), preferred_element_type=jnp.float32
    )
    logsum = (row_max + jnp.log(row_total))[..., 0]
    return (mixed_rows.reshape(queries.shape[0], -1).astype(jnp.bfloat16), logsum)


def attend_back(queries, key_rows, value_rows, allowed, logsum, upstream):
    score_scale = 1.0 / math.sqrt(HEAD_DIM)
    query_heads = heads_of(queries)
    key_heads = heads_of(key_rows)
    upstream_heads = heads_of(upstream)
    scores = (
        jnp.einsum("qhd,khd->hqk", query_heads, key_heads, preferred_element_type=jnp.float32)
        * score_scale
    )
    scores = jnp.where(allowed[None], scores, MASKED)
    weights = jnp.exp(scores - logsum[..., None])
    grad_weights = jnp.einsum(
        "qhd,khd->hqk", upstream_heads, heads_of(value_rows), preferred_element_type=jnp.float32
    )
    row_delta = jnp.sum(weights * grad_weights, axis=-1, keepdims=True)
    grad_scores = (weights * (grad_weights - row_delta)).astype(jnp.bfloat16)
    grad_query = (
        jnp.einsum("hqk,khd->qhd", grad_scores, key_heads, preferred_element_type=jnp.float32)
        * score_scale
    )
    grad_key = (
        jnp.einsum("hqk,qhd->khd", grad_scores, query_heads, preferred_element_type=jnp.float32)
        * score_scale
    )
    grad_value = jnp.einsum(
        "hqk,qhd->khd",
        weights.astype(jnp.bfloat16),
        upstream_heads,
        preferred_element_type=jnp.float32,
    )
    key_count = key_rows.shape[0]
    return (
        grad_query.reshape(queries.shape[0], -1),
        grad_key.reshape(key_count, -1),
        grad_value.reshape(key_count, -1),
    )


def to_float(values):
    return values.astype(jnp.float32)


def on_device(
    tokens,
    text_states,
    unit_length,
    text_length,
    cotangent,
    attn_gain,
    attn_shift,
    attn_inputs,
    attn_qbias,
    attn_vbias,
    attn_output,
    attn_obias,
    cross_gain,
    cross_shift,
    cross_query,
    cross_qbias,
    cross_keyval,
    cross_vbias,
    cross_output,
    cross_obias,
    ffn_gain,
    ffn_shift,
    ffn_up,
    ffn_upbias,
    ffn_down,
    ffn_downbias,
    final_gain,
    final_shift,
):
    seq_count, local_len, model_width = tokens.shape
    row_count = seq_count * local_len
    first_pos = lax.axis_index("seq") * local_len
    zero_bias = jnp.zeros((model_width,), jnp.float32)
    (
        a_gain_full,
        a_shift_full,
        attention_input_weight_whole,
        a_qbias_full,
        a_vbias_full,
        a_output_full,
        a_obias_full,
    ) = (
        lax.all_gather(attn_gain, ("dp", "seq"), axis=0, tiled=True),
        lax.all_gather(attn_shift, ("dp", "seq"), axis=0, tiled=True),
        lax.all_gather(attn_inputs, ("dp", "seq"), axis=0, tiled=True),
        lax.all_gather(attn_qbias, ("dp", "seq"), axis=0, tiled=True),
        lax.all_gather(attn_vbias, ("dp", "seq"), axis=0, tiled=True),
        lax.all_gather(attn_output, ("dp", "seq"), axis=0, tiled=True),
        lax.all_gather(attn_obias, ("dp", "seq"), axis=0, tiled=True),
    )
    inputs = to_float(tokens).reshape(row_count, model_width)
    normed_one = layer_norm(inputs, to_float(a_gain_full), to_float(a_shift_full)).astype(
        jnp.bfloat16
    )
    joined = rows_dot(normed_one, attention_input_weight_whole) + jnp.concatenate(
        [to_float(a_qbias_full), zero_bias, to_float(a_vbias_full)]
    )
    joined = joined.astype(jnp.bfloat16)
    self_queries = joined[:, :model_width].reshape(seq_count, local_len, model_width)
    keyval_local = joined[:, model_width:].reshape(seq_count, local_len, 2 * model_width)
    self_keyval = lax.all_gather(keyval_local, "seq", axis=1, tiled=True)
    full_len = self_keyval.shape[1]
    causal = jnp.arange(full_len)[None, :] <= (first_pos + jnp.arange(local_len))[:, None]

    def self_forward(packed):
        seq_queries, seq_keyval = packed
        return attend_forward(
            seq_queries, seq_keyval[:, :model_width], seq_keyval[:, model_width:], causal
        )

    self_mixed, self_logsum = lax.map(self_forward, (self_queries, self_keyval))
    self_flat = self_mixed.reshape(row_count, model_width)
    after_self = inputs + rows_dot(self_flat, a_output_full) + to_float(a_obias_full)
    (
        c_gain_full,
        c_shift_full,
        c_query_full,
        c_qbias_full,
        c_keyval_full,
        cross_value_bias_whole,
        c_output_full,
        c_obias_full,
    ) = (
        lax.all_gather(cross_gain, ("dp", "seq"), axis=0, tiled=True),
        lax.all_gather(cross_shift, ("dp", "seq"), axis=0, tiled=True),
        lax.all_gather(cross_query, ("dp", "seq"), axis=0, tiled=True),
        lax.all_gather(cross_qbias, ("dp", "seq"), axis=0, tiled=True),
        lax.all_gather(cross_keyval, ("dp", "seq"), axis=0, tiled=True),
        lax.all_gather(cross_vbias, ("dp", "seq"), axis=0, tiled=True),
        lax.all_gather(cross_output, ("dp", "seq"), axis=0, tiled=True),
        lax.all_gather(cross_obias, ("dp", "seq"), axis=0, tiled=True),
    )
    normed_two = layer_norm(after_self, to_float(c_gain_full), to_float(c_shift_full)).astype(
        jnp.bfloat16
    )
    cross_queries = (rows_dot(normed_two, c_query_full) + to_float(c_qbias_full)).astype(
        jnp.bfloat16
    )
    cross_queries = cross_queries.reshape(seq_count, local_len, model_width)
    keyval_bias = jnp.concatenate([zero_bias, to_float(cross_value_bias_whole)])
    text_whole = lax.all_gather(text_states, "seq", axis=1, tiled=True)
    cross_kv = (rows_dot(text_whole.reshape(-1, model_width), c_keyval_full) + keyval_bias).astype(
        jnp.bfloat16
    )
    cross_kv = cross_kv.reshape(seq_count, -1, 2 * model_width)
    text_total = cross_kv.shape[1]
    text_allowed = jnp.arange(text_total)[None, :] < text_length[:, None]

    def cross_forward(packed):
        seq_queries, seq_keyval, seq_allowed = packed
        allowed = jnp.broadcast_to(seq_allowed[None, :], (local_len, text_total))
        return attend_forward(
            seq_queries, seq_keyval[:, :model_width], seq_keyval[:, model_width:], allowed
        )

    cross_blended_rows, cross_logsum = lax.map(
        cross_forward, (cross_queries, cross_kv, text_allowed)
    )
    cross_flat = cross_blended_rows.reshape(row_count, model_width)
    after_cross = after_self + rows_dot(cross_flat, c_output_full) + to_float(c_obias_full)
    (
        f_gain_full,
        feedforward_shift_whole,
        f_up_full,
        f_upbias_full,
        f_down_full,
        f_downbias_full,
        z_gain_full,
        z_shift_full,
    ) = (
        lax.all_gather(ffn_gain, ("dp", "seq"), axis=0, tiled=True),
        lax.all_gather(ffn_shift, ("dp", "seq"), axis=0, tiled=True),
        lax.all_gather(ffn_up, ("dp", "seq"), axis=0, tiled=True),
        lax.all_gather(ffn_upbias, ("dp", "seq"), axis=0, tiled=True),
        lax.all_gather(ffn_down, ("dp", "seq"), axis=0, tiled=True),
        lax.all_gather(ffn_downbias, ("dp", "seq"), axis=0, tiled=True),
        lax.all_gather(final_gain, ("dp", "seq"), axis=0, tiled=True),
        lax.all_gather(final_shift, ("dp", "seq"), axis=0, tiled=True),
    )
    normed_three = layer_norm(
        after_cross, to_float(f_gain_full), to_float(feedforward_shift_whole)
    ).astype(jnp.bfloat16)
    ffn_inner = rows_dot(normed_three, f_up_full) + to_float(f_upbias_full)
    active = jax.nn.gelu(ffn_inner).astype(jnp.bfloat16)
    after_ffn = after_cross + rows_dot(active, f_down_full) + to_float(f_downbias_full)
    valid_rows = ((first_pos + jnp.arange(local_len))[None, :] < unit_length[:, None]).astype(
        jnp.float32
    )
    valid_rows = valid_rows.reshape(row_count, 1)
    final_norm = layer_norm(after_ffn, to_float(z_gain_full), to_float(z_shift_full))
    layer_out = (
        (final_norm * valid_rows).astype(jnp.bfloat16).reshape(seq_count, local_len, model_width)
    )
    (
        f_gain_full,
        feedforward_shift_whole,
        f_up_full,
        f_upbias_full,
        f_down_full,
        f_downbias_full,
        z_gain_full,
        z_shift_full,
    ) = (
        lax.all_gather(ffn_gain, ("dp", "seq"), axis=0, tiled=True),
        lax.all_gather(ffn_shift, ("dp", "seq"), axis=0, tiled=True),
        lax.all_gather(ffn_up, ("dp", "seq"), axis=0, tiled=True),
        lax.all_gather(ffn_upbias, ("dp", "seq"), axis=0, tiled=True),
        lax.all_gather(ffn_down, ("dp", "seq"), axis=0, tiled=True),
        lax.all_gather(ffn_downbias, ("dp", "seq"), axis=0, tiled=True),
        lax.all_gather(final_gain, ("dp", "seq"), axis=0, tiled=True),
        lax.all_gather(final_shift, ("dp", "seq"), axis=0, tiled=True),
    )
    upstream = to_float(cotangent).reshape(row_count, model_width) * valid_rows
    grad_after_ffn, grad_zgain, grad_zshift = norm_back(
        after_ffn, to_float(z_gain_full), to_float(z_shift_full), upstream
    )
    grad_branch = grad_after_ffn.astype(jnp.bfloat16)
    grad_down = left_dot(active, grad_branch)
    grad_downbias = jnp.sum(to_float(grad_branch), axis=0)
    grad_active = right_dot(grad_branch, f_down_full)
    inner_value, gelu_back = jax.vjp(jax.nn.gelu, ffn_inner)
    grad_inner = gelu_back(grad_active)[0].astype(jnp.bfloat16)
    grad_up = left_dot(normed_three, grad_inner)
    grad_upbias = jnp.sum(to_float(grad_inner), axis=0)
    grad_normed_three = right_dot(grad_inner, f_up_full)
    grad_cross_norm, grad_fgain, grad_fshift = norm_back(
        after_cross, to_float(f_gain_full), to_float(feedforward_shift_whole), grad_normed_three
    )
    grad_after_cross = grad_after_ffn + grad_cross_norm
    ffn_sums = (
        lax.psum_scatter(grad_fgain, ("dp", "seq"), scatter_dimension=0, tiled=True),
        lax.psum_scatter(grad_fshift, ("dp", "seq"), scatter_dimension=0, tiled=True),
        lax.psum_scatter(grad_up, ("dp", "seq"), scatter_dimension=0, tiled=True),
        lax.psum_scatter(grad_upbias, ("dp", "seq"), scatter_dimension=0, tiled=True),
        lax.psum_scatter(grad_down, ("dp", "seq"), scatter_dimension=0, tiled=True),
        lax.psum_scatter(grad_downbias, ("dp", "seq"), scatter_dimension=0, tiled=True),
        lax.psum_scatter(grad_zgain, ("dp", "seq"), scatter_dimension=0, tiled=True),
        lax.psum_scatter(grad_zshift, ("dp", "seq"), scatter_dimension=0, tiled=True),
    )
    (
        c_gain_full,
        c_shift_full,
        c_query_full,
        c_qbias_full,
        c_keyval_full,
        cross_value_bias_whole,
        c_output_full,
        c_obias_full,
    ) = (
        lax.all_gather(cross_gain, ("dp", "seq"), axis=0, tiled=True),
        lax.all_gather(cross_shift, ("dp", "seq"), axis=0, tiled=True),
        lax.all_gather(cross_query, ("dp", "seq"), axis=0, tiled=True),
        lax.all_gather(cross_qbias, ("dp", "seq"), axis=0, tiled=True),
        lax.all_gather(cross_keyval, ("dp", "seq"), axis=0, tiled=True),
        lax.all_gather(cross_vbias, ("dp", "seq"), axis=0, tiled=True),
        lax.all_gather(cross_output, ("dp", "seq"), axis=0, tiled=True),
        lax.all_gather(cross_obias, ("dp", "seq"), axis=0, tiled=True),
    )
    cross_branch_gradient = grad_after_cross.astype(jnp.bfloat16)
    grad_coutput = left_dot(cross_flat, cross_branch_gradient)
    grad_cobias = jnp.sum(to_float(cross_branch_gradient), axis=0)
    grad_cross_mixed = right_dot(cross_branch_gradient, c_output_full).astype(jnp.bfloat16)
    grad_cross_mixed = grad_cross_mixed.reshape(seq_count, local_len, model_width)

    def cross_backward(packed):
        seq_queries, seq_keyval, seq_allowed, sequence_log_sum_exp, seq_upstream = packed
        allowed = jnp.broadcast_to(seq_allowed[None, :], (local_len, text_total))
        return attend_back(
            seq_queries,
            seq_keyval[:, :model_width],
            seq_keyval[:, model_width:],
            allowed,
            sequence_log_sum_exp,
            seq_upstream,
        )

    grad_cq, grad_ck, grad_cv = lax.map(
        cross_backward, (cross_queries, cross_kv, text_allowed, cross_logsum, grad_cross_mixed)
    )
    grad_ckv = lax.psum_scatter(
        jnp.concatenate([grad_ck, grad_cv], axis=-1).astype(jnp.bfloat16),
        "seq",
        scatter_dimension=1,
        tiled=True,
    ).astype(jnp.float32)
    grad_ckv = grad_ckv.astype(jnp.bfloat16).reshape(-1, 2 * model_width)
    grad_ckeyval = left_dot(text_states.reshape(-1, model_width), grad_ckv)
    grad_cvbias = jnp.sum(to_float(grad_ckv[:, model_width:]), axis=0)
    text_grad = right_dot(grad_ckv, c_keyval_full).astype(jnp.bfloat16).reshape(text_states.shape)
    grad_cq_low = grad_cq.reshape(row_count, model_width).astype(jnp.bfloat16)
    grad_cquery = left_dot(normed_two, grad_cq_low)
    grad_cqbias = jnp.sum(to_float(grad_cq_low), axis=0)
    grad_normed_two = right_dot(grad_cq_low, c_query_full)
    grad_self_norm, grad_cgain, grad_cshift = norm_back(
        after_self, to_float(c_gain_full), to_float(c_shift_full), grad_normed_two
    )
    grad_after_self = grad_after_cross + grad_self_norm
    cross_sums = (
        lax.psum_scatter(grad_cgain, ("dp", "seq"), scatter_dimension=0, tiled=True),
        lax.psum_scatter(grad_cshift, ("dp", "seq"), scatter_dimension=0, tiled=True),
        lax.psum_scatter(grad_cquery, ("dp", "seq"), scatter_dimension=0, tiled=True),
        lax.psum_scatter(grad_cqbias, ("dp", "seq"), scatter_dimension=0, tiled=True),
        lax.psum_scatter(grad_ckeyval, ("dp", "seq"), scatter_dimension=0, tiled=True),
        lax.psum_scatter(grad_cvbias, ("dp", "seq"), scatter_dimension=0, tiled=True),
        lax.psum_scatter(grad_coutput, ("dp", "seq"), scatter_dimension=0, tiled=True),
        lax.psum_scatter(grad_cobias, ("dp", "seq"), scatter_dimension=0, tiled=True),
    )
    (
        a_gain_full,
        a_shift_full,
        attention_input_weight_whole,
        a_qbias_full,
        a_vbias_full,
        a_output_full,
        a_obias_full,
    ) = (
        lax.all_gather(attn_gain, ("dp", "seq"), axis=0, tiled=True),
        lax.all_gather(attn_shift, ("dp", "seq"), axis=0, tiled=True),
        lax.all_gather(attn_inputs, ("dp", "seq"), axis=0, tiled=True),
        lax.all_gather(attn_qbias, ("dp", "seq"), axis=0, tiled=True),
        lax.all_gather(attn_vbias, ("dp", "seq"), axis=0, tiled=True),
        lax.all_gather(attn_output, ("dp", "seq"), axis=0, tiled=True),
        lax.all_gather(attn_obias, ("dp", "seq"), axis=0, tiled=True),
    )
    grad_self_branch = grad_after_self.astype(jnp.bfloat16)
    grad_aoutput = left_dot(self_flat, grad_self_branch)
    grad_aobias = jnp.sum(to_float(grad_self_branch), axis=0)
    grad_self_mixed = right_dot(grad_self_branch, a_output_full).astype(jnp.bfloat16)
    grad_self_mixed = grad_self_mixed.reshape(seq_count, local_len, model_width)

    def self_backward(packed):
        seq_queries, seq_keyval, sequence_log_sum_exp, seq_upstream = packed
        return attend_back(
            seq_queries,
            seq_keyval[:, :model_width],
            seq_keyval[:, model_width:],
            causal,
            sequence_log_sum_exp,
            seq_upstream,
        )

    gradient_self_query, grad_sk, grad_sv = lax.map(
        self_backward, (self_queries, self_keyval, self_logsum, grad_self_mixed)
    )
    gradient_self_keyvalue = lax.psum_scatter(
        jnp.concatenate([grad_sk, grad_sv], axis=-1).astype(jnp.bfloat16),
        "seq",
        scatter_dimension=1,
        tiled=True,
    ).astype(jnp.float32)
    grad_joined = (
        jnp.concatenate([gradient_self_query, gradient_self_keyvalue], axis=-1)
        .reshape(row_count, 3 * model_width)
        .astype(jnp.bfloat16)
    )
    grad_ainputs = left_dot(normed_one, grad_joined)
    grad_aqbias = jnp.sum(to_float(grad_joined[:, :model_width]), axis=0)
    grad_avbias = jnp.sum(to_float(grad_joined[:, 2 * model_width :]), axis=0)
    grad_normed_one = right_dot(grad_joined, attention_input_weight_whole)
    grad_input_norm, grad_again, grad_ashift = norm_back(
        inputs, to_float(a_gain_full), to_float(a_shift_full), grad_normed_one
    )
    tokens_grad = (
        (grad_after_self + grad_input_norm)
        .astype(jnp.bfloat16)
        .reshape(seq_count, local_len, model_width)
    )
    attn_sums = (
        lax.psum_scatter(grad_again, ("dp", "seq"), scatter_dimension=0, tiled=True),
        lax.psum_scatter(grad_ashift, ("dp", "seq"), scatter_dimension=0, tiled=True),
        lax.psum_scatter(grad_ainputs, ("dp", "seq"), scatter_dimension=0, tiled=True),
        lax.psum_scatter(grad_aqbias, ("dp", "seq"), scatter_dimension=0, tiled=True),
        lax.psum_scatter(grad_avbias, ("dp", "seq"), scatter_dimension=0, tiled=True),
        lax.psum_scatter(grad_aoutput, ("dp", "seq"), scatter_dimension=0, tiled=True),
        lax.psum_scatter(grad_aobias, ("dp", "seq"), scatter_dimension=0, tiled=True),
    )
    return (layer_out, tokens_grad, text_grad, *attn_sums, *cross_sums, *ffn_sums)


MESH_ID = pl.DeviceIdType.MESH
ANYWHERE = pl.BlockSpec(memory_space=pl.ANY)
VMEM_LIMIT = 56 * 2**20


class Place:
    def __init__(self, depth):
        group = lax.axis_index("dp")
        self.depth = depth
        self.z = group // 4
        self.x = lax.rem(group // 2, 2)
        self.core = lax.rem(group, 2)
        self.y = lax.axis_index("seq")

    def device(self, z, x, core, y):
        return {"dp": (z * 2 + x) * 2 + core, "seq": y}

    def along_z(self, step):
        return self.device(lax.rem(self.z + step, self.depth), self.x, self.core, self.y)

    def across_x(self):
        return self.device(self.z, 1 - self.x, self.core, self.y)

    def across_y(self):
        return self.device(self.z, self.x, self.core, 1 - self.y)

    def sibling(self):
        return self.device(self.z, self.x, 1 - self.core, self.y)

    def along(self, axis):
        if axis == "z":
            return [self.along_z(step) for step in range(1, self.depth)]
        return [self.across_x() if axis == "x" else self.across_y()]

    def greet(self):
        partners = [self.along_z(step) for step in range(1, self.depth)]
        partners += [self.across_x(), self.across_y(), self.sibling()]
        barrier = pltpu.get_barrier_semaphore()
        for partner in partners:
            pl.semaphore_signal(barrier, inc=1, device_id=partner, device_id_type=MESH_ID)
        pl.semaphore_wait(barrier, len(partners))


def remote(source, target, sems, item, index, device):
    send, receive = sems
    return pltpu.make_async_remote_copy(
        src_ref=source,
        dst_ref=target,
        send_sem=send.at[item, index],
        recv_sem=receive.at[item, index],
        device_id=device,
        device_id_type=MESH_ID,
    )


def pipelined(phase_lists, stride):
    stages = []
    for first, phases in enumerate(phase_lists):
        for p, phase in enumerate(phases):
            turn = first + stride * p
            while len(stages) <= turn:
                stages.append([])
            stages[turn].append(phase)
    return stages


ORDERS = (("z", "x", "y"), ("y", "z", "x"))


def gather_phases(place, shard, whole, rows, cols, sems, local, stop, item):
    half = rows.size // 2
    halves = (pl.ds(rows.start, half), pl.ds(rows.start + half, half))
    here = {"z": place.z, "x": place.x, "y": place.y}
    every = slice(None)

    def view(done, some_rows, core):
        at = {axis: every if axis in done else here[axis] for axis in here}
        return whole.at[at["z"], at["x"], core, at["y"], some_rows, cols]

    def copies(phase):
        made = []
        if phase == 3:
            both = view("zxy", rows, place.core)
            return [remote(both, both, sems, item, 2 * place.depth + 2, place.sibling())]
        slot = sum(len(place.along(o[p])) for o in ORDERS for p in range(phase))
        for some_rows, order in zip(halves, ORDERS):
            target = view(order[:phase], some_rows, place.core)
            source = shard.at[some_rows, cols] if phase == 0 else target
            for device in place.along(order[phase]):
                made.append(remote(source, target, sems, item, slot, device))
                slot += 1
        return made

    def take():
        return pltpu.make_async_copy(shard.at[rows, cols], stop, local.at[item, 0])

    def put():
        return pltpu.make_async_copy(stop, view("", rows, place.core), local.at[item, 1])

    def start(phase):
        for copy in copies(phase):
            copy.start()

    def wait(phase):
        for copy in copies(phase):
            copy.wait()

    def opening():
        start(0)
        take().start()
        take().wait()
        put().start()

    def turn(phase):
        def run():
            wait(phase - 1)
            if phase == 1:
                put().wait()
            start(phase)

        return run

    return [opening, turn(1), turn(2), turn(3), lambda: wait(3)]


def copy_sems(items, depth):
    width = 2 * depth + 3
    return [
        pltpu.SemaphoreType.DMA((items, width)),
        pltpu.SemaphoreType.DMA((items, width)),
        pltpu.SemaphoreType.DMA((items, 2)),
    ]


ITEM = 512


def weight_items(shape):
    rows, cols = shape
    return [
        (pl.ds(r, 32), pl.ds(c, min(ITEM, cols)))
        for r in range(0, rows, 32)
        for c in range(0, cols, min(ITEM, cols))
    ]


def nt(a, b):
    return lax.dot_general(a, b, (((1,), (1,)), ((), ())), preferred_element_type=jnp.float32)


def nn(a, b):
    return jnp.dot(a, b, preferred_element_type=jnp.float32)


def half_mask(rows):
    return lax.broadcasted_iota(jnp.int32, (rows, 128), 1) < 64


def pick(block, head, first):
    zero = jnp.zeros_like(block)
    return jnp.where(first, block, zero) if head == 0 else jnp.where(first, zero, block)


MOST_KEYS = 256


def segments(causal, qb, keys, size, most):
    if not causal:
        return [(0, keys, False)]
    first = qb * size
    before = [(lo, min(lo + most, first), False) for lo in range(0, first, most)]
    return before + [(first, first + size, True)]


def both(block, first):
    return jnp.concatenate([pick(block, 0, first), pick(block, 1, first)], axis=0)


def diagonal_mask(scored, size):
    r = lax.broadcasted_iota(jnp.int32, scored.shape, 0)
    c = lax.broadcasted_iota(jnp.int32, scored.shape, 1)
    return jnp.where(r <= lax.rem(c, size), scored, MASKED)


def attend_pair(causal, rows, keys, size, get_q, get_k, get_v, bias, put, lse_ref):
    vt = get_v(0, keys).T
    first = half_mask(size)
    for qb in range(rows // size):
        sl = slice(qb * size, (qb + 1) * size)
        qs = both(get_q(sl.start, sl.stop) * jnp.bfloat16(0.125), first)
        parts = []
        for lo, hi, diagonal in segments(causal, qb, keys, size, MOST_KEYS):
            s = nt(get_k(lo, hi), qs)
            if diagonal:
                s = diagonal_mask(s, size)
            if bias is not None:
                s = s + jnp.concatenate([bias] * (2 * size // 128), axis=1)
            parts.append((lo, hi, s))
        m = functools.reduce(jnp.maximum, [jnp.max(s, axis=0, keepdims=True) for _, _, s in parts])
        total, out = None, None
        for lo, hi, s in parts:
            p = jnp.exp(s - m)
            l = jnp.sum(p, axis=0, keepdims=True)
            o = nn(vt[:, lo:hi], p.astype(jnp.bfloat16))
            total = l if total is None else total + l
            out = o if out is None else out + o
        lse = m + jnp.log(total)
        lse_ref[0:1, sl] = lse[:, :size]
        lse_ref[1:2, sl] = lse[:, size:]
        out = out * (1.0 / total)
        out = jnp.concatenate([out[:64, :size], out[64:, size:]], axis=0).T
        put(sl, out.astype(jnp.bfloat16))


def attend_back_pair(
    causal, rows, keys, size, get_q, get_k, get_v, get_o, get_do, lse_ref, bias, put_dq, put_dk,
    put_dv, dk_acc, dv_acc,
):
    kt = (get_k(0, keys) * jnp.bfloat16(0.125)).T
    first = half_mask(size)
    order = list(range(rows // size))
    if causal:
        order = order[::-1]
    for qb in order:
        sl = slice(qb * size, (qb + 1) * size)
        qs = both(get_q(sl.start, sl.stop) * jnp.bfloat16(0.125), first)
        do = get_do(sl.start, sl.stop)
        dos = both(do, first)
        dt = (do.astype(jnp.float32) * get_o(sl.start, sl.stop).astype(jnp.float32)).T
        delta = jnp.concatenate(
            [
                jnp.sum(dt[:64], axis=0, keepdims=True),
                jnp.sum(dt[64:], axis=0, keepdims=True),
            ],
            axis=1,
        )
        lse = jnp.concatenate([lse_ref[0:1, sl], lse_ref[1:2, sl]], axis=1)
        dq = None
        for lo, hi, diagonal in segments(causal, qb, keys, size, MOST_KEYS):
            s = nt(get_k(lo, hi), qs)
            if diagonal:
                s = diagonal_mask(s, size)
            if bias is not None:
                s = s + jnp.concatenate([bias] * (2 * size // 128), axis=1)
            dp = nt(get_v(lo, hi), dos)
            p = jnp.exp(s - lse)
            ds = (p * (dp - delta)).astype(jnp.bfloat16)
            dv = nn(p.astype(jnp.bfloat16), dos)
            dk = nn(ds, qs)
            part = nn(kt[:, lo:hi], ds)
            dq = part if dq is None else dq + part
            if qb == order[0]:
                dv_acc[lo:hi, :] = dv
                dk_acc[lo:hi, :] = dk
            else:
                dv_acc[lo:hi, :] += dv
                dk_acc[lo:hi, :] += dk
        dq = jnp.concatenate([dq[:64, :size], dq[64:, size:]], axis=0).T
        put_dq(sl, dq.astype(jnp.bfloat16))
    put_dk(dk_acc[0:keys, :].astype(jnp.bfloat16))
    put_dv(dv_acc[0:keys, :].astype(jnp.bfloat16))


BLOCK = 256
MATMUL_ROWS = 512
RING = 6

VECTOR_COUNT = 15
(
    A_GAIN, A_SHIFT, A_QBIAS, A_VBIAS, A_OBIAS, C_GAIN, C_SHIFT, C_QBIAS, C_VBIAS, C_OBIAS,
    F_GAIN, F_SHIFT, F_DOWNBIAS, Z_GAIN, Z_SHIFT,
) = range(VECTOR_COUNT)
F_UPBIAS = VECTOR_COUNT
UP_INDEX, DOWN_INDEX = 6, 7
STRIDE = 3
SWAP_PIECES = 16
SELF_QUERIES, CROSS_QUERIES = 512, 1024


def block_rows(index, size):
    return pl.ds(pl.multiple_of(index * size, size), size)


def lanes(index, size):
    return pl.ds(pl.multiple_of(index * size, size), size)


def center_and_scale(values):
    center = values - jnp.mean(values, axis=-1, keepdims=True)
    spread = jnp.mean(center * center, axis=-1, keepdims=True)
    scale = lax.rsqrt(spread + EPSILON)
    return center * scale, scale


def norm_pull(unit, scale, pulled):
    inner = jnp.mean(pulled * unit, axis=-1, keepdims=True)
    return scale * (pulled - jnp.mean(pulled, axis=-1, keepdims=True) - unit * inner)


def gelu_and_slope(values):
    root = math.sqrt(2.0 / math.pi)
    square = values * values
    bend = jnp.tanh(root * (values + 0.044715 * (values * square)))
    rise = root * (1.0 + 3.0 * 0.044715 * square)
    result = 0.5 * values * (1.0 + bend)
    slope = 0.5 * (1.0 + bend) + 0.5 * values * ((1.0 - bend * bend) * rise)
    return result, slope


def spread_vectors(packed):
    rows = packed.shape[0]
    width = rows
    lane = lax.broadcasted_iota(jnp.int32, (128, width), 1)
    source = lax.broadcasted_iota(jnp.int32, (128, width), 0)
    select = jnp.where(lax.rem(lane, 32) == source, 1.0, 0.0).astype(jnp.bfloat16)
    wide = jnp.dot(packed, select, preferred_element_type=jnp.float32)
    row = lax.broadcasted_iota(jnp.int32, (rows, width), 0)
    lane = lax.broadcasted_iota(jnp.int32, (rows, width), 1)
    wide = jnp.where(row // 32 == lane // 32, wide, 0.0)
    return jnp.sum(wide.reshape(rows // 32, 32, width), axis=0)


def quarter_columns(values, width, back=False):
    share = 32
    per = 128 // share
    shards = width // share
    lane = lax.broadcasted_iota(jnp.int32, (values.shape[0], 128), 1) // share
    blocks = [values[:, k * 128 : (k + 1) * 128] for k in range(4 * shards * share // 128)]
    result = []
    for k in range(len(blocks)):
        total = None
        for j in range(per):
            if back:
                source, held = blocks[j * (shards // per) + k // per], k % per
            else:
                source, held = blocks[per * (k % (shards // per)) + j], k // (shards // per)
            moved = source if held == j else pltpu.roll(source, (j - held) * share % 128, 1)
            total = moved if total is None else jnp.where(lane == j, moved, total)
        result.append(total)
    return jnp.concatenate(result, axis=1)


def arrange_columns(target, source, sem, width):
    copy = pltpu.make_async_copy(source, target, sem)
    copy.start()
    copy.wait()
    values = target[...].astype(jnp.float32)
    target[...] = quarter_columns(values, width).astype(target.dtype)


class Copies:
    def __init__(self, sems):
        self.sems = sems
        self.open = {}
        self.used = 0

    def start(self, source, target):
        copy = pltpu.make_async_copy(source, target, self.sems.at[self.used])
        self.used += 1
        copy.start()
        return copy


def forward_kernel(depth, sizes, *refs):
    refs = list(refs)

    def take(count):
        taken = refs[:count]
        del refs[:count]
        return taken

    shard_count = len(sizes)
    tokens, texts, cots, unit_length, text_length = take(5)
    shards = take(7 + 1)
    wholes = take(shard_count)
    (
        o_tokens, o_text, o_h1, o_qkv, o_o1, o_after_self, o_h2, o_cq, o_ckv, o_o2,
        o_after_cross, o_h3, o_active, o_slope, o_gaf, o_gbr, o_layer,
    ) = take(17)
    vec, lse1, lse2, zgrads = take(4)
    tok, txt, cot, x, o1, cq, ckv, o2, resid, h2, ring, slopes, packed = take(13)
    stops = take(sum(len(weight_items(s)) for s in sizes))
    send, receive, local, sw_send, sw_receive, sw_local, loads, outs = take(8)
    (up_stop, up_sem) = take(2)

    place = Place(depth)
    y = place.y
    rows = resid.shape[0]
    width = resid.shape[1]
    part = rows // 2
    copies = Copies(outs)
    sources = list(shards[:DOWN_INDEX])
    sources[UP_INDEX] = up_stop
    share = sizes[0][0]
    sources += [shards[DOWN_INDEX].at[pl.ds(q * share, share)] for q in range(4)]
    phases, chunks, item = [], [], 0
    for index, size in enumerate(sizes):
        for r, c in weight_items(size):
            phases.append(
                gather_phases(
                    place, sources[index], wholes[index], r, c, (send, receive), local,
                    stops[item], item,
                )
            )
            if index > 0 and c.start % width == 0:
                chunks.append((wholes[index], pl.ds(c.start, width)))
            item += 1
    stages = pipelined(phases[1:], STRIDE)
    for k, phase in enumerate(phases[0]):
        stages[STRIDE * k].append(phase)

    def swapping(k, source, target, count, first):
        size = source.shape[1] // count

        def away(i):
            piece = pl.ds(i * size, size)
            return remote(
                source.at[1 - y, piece], target.at[y, piece], (sw_send, sw_receive), k, i,
                place.across_y(),
            )

        home = pltpu.make_async_copy(source.at[y], target.at[y], sw_local.at[k])
        for i in range(count):
            stages[first + i].append(lambda i=i: away(i).start())
        stages[first].append(home.start)

        def closing():
            home.wait()
            for i in range(count):
                away(i).wait()

        return closing

    token_swap = swapping(0, tokens, tok, 8, 0)
    text_swap = swapping(1, texts, txt, 2, 10)
    cot_swap = swapping(2, cots, cot, SWAP_PIECES, 22)

    def load(chunk):
        whole, cols = chunks[chunk]
        return pltpu.make_async_copy(
            whole.at[:, :, :, :, :, cols], ring.at[chunk % RING], loads.at[chunk]
        )

    ran = []

    def stage(k):
        assert len(ran) == k
        ran.append(k)
        for one in stages[k]:
            one()
        ready = k - 4 * STRIDE
        if ready > 0 and ready % 2 == 1:
            load(ready // 2).start()

    def weight(chunk):
        return ring[chunk % RING].reshape(width, width)

    def row(index):
        return vec[index : index + 1, :]

    def looped(count, body, due=()):
        @pl.loop(0, count)
        def _(j):
            for at, k in due:

                @pl.when(j == at)
                def _(k=k):
                    stage(k)

            body(j)

    place.greet()
    for k in range(4):
        stage(k)
    arrange_columns(up_stop, shards[UP_INDEX], up_sem, width)
    for k in range(4, 14):
        stage(k)
    pack = pltpu.make_async_copy(wholes[0], packed, outs.at[copies.used])
    copies.used += 1
    pack.start()
    pack.wait()
    vec[...] = spread_vectors(packed[...].reshape(-1, 128))
    token_swap()
    done_tokens = copies.start(tok, o_tokens)

    def token_block(b):
        half = b // (part // BLOCK)
        inner = lax.rem(b, part // BLOCK)
        return tok[half, block_rows(inner, BLOCK), :].astype(jnp.float32)

    def norm_one(b):
        unit, _ = center_and_scale(token_block(b))
        at = block_rows(b, BLOCK)
        x[at, 3 * width :] = (unit * row(A_GAIN) + row(A_SHIFT)).astype(jnp.bfloat16)
        resid[at, :] = token_block(b)

    looped(rows // BLOCK, norm_one)
    done_h1 = copies.start(x.at[:, pl.ds(3 * width, width)], o_h1)

    def project(chunk):
        bias = (row(A_QBIAS), None, row(A_VBIAS))[chunk]
        load(chunk).wait()

        def block(b):
            at = block_rows(b, MATMUL_ROWS)
            value = nn(x[at, 3 * width :], weight(chunk))
            if bias is not None:
                value = value + bias
            x[at, chunk * width : (chunk + 1) * width] = value.astype(jnp.bfloat16)

        looped(rows // MATMUL_ROWS, block)

    stage(14)
    project(0)
    stage(15)
    project(1)
    stage(16)
    stage(17)
    project(2)
    done_qkv = copies.start(x.at[:, pl.ds(0, 3 * width)], o_qkv)
    pairs = width // 128

    def self_pair(j):
        def part_of(base):
            return lambda lo, hi: x[lo:hi, lanes(j + base * pairs, 128)]

        def put(sl, value):
            o1[sl, lanes(j, 128)] = value

        attend_pair(
            True, rows, rows, min(SELF_QUERIES, rows), part_of(0), part_of(1), part_of(2), None, put, lse1.at[j]
        )

    looped(pairs, self_pair, ((1, 18), (2, 19), (4, 20), (5, 21), (7, 22)))
    done_o1 = copies.start(o1, o_o1)
    load(3).wait()

    def out_block(b):
        at = block_rows(b, MATMUL_ROWS)
        resid[at, :] = resid[at, :] + nn(o1[at, :], weight(3)) + row(A_OBIAS)

    looped(rows // MATMUL_ROWS, out_block)
    stage(23)
    done_after_self = copies.start(resid, o_after_self)

    def norm_two(b):
        at = block_rows(b, BLOCK)
        unit, _ = center_and_scale(resid[at, :])
        h2[at, :] = (unit * row(C_GAIN) + row(C_SHIFT)).astype(jnp.bfloat16)

    looped(rows // BLOCK, norm_two)
    done_h2 = copies.start(h2, o_h2)
    stage(24)
    load(4).wait()

    def cq_block(b):
        at = block_rows(b, MATMUL_ROWS)
        cq[at, :] = (nn(h2[at, :], weight(4)) + row(C_QBIAS)).astype(jnp.bfloat16)

    looped(rows // MATMUL_ROWS, cq_block)
    done_cq = copies.start(cq, o_cq)
    text_swap()
    done_text = copies.start(txt, o_text)
    text = txt[...].reshape(-1, width)
    text_rows = text.shape[0]
    stage(25)
    load(5).wait()
    ckv[:, :width] = nn(text, weight(5)).astype(jnp.bfloat16)
    load(6).wait()
    ckv[:, width:] = (nn(text, weight(6)) + row(C_VBIAS)).astype(jnp.bfloat16)
    done_ckv = copies.start(ckv, o_ckv)
    bias = text_mask(text_rows, text_length[y])

    def cross_pair(j):
        def put(sl, value):
            o2[sl, lanes(j, 128)] = value

        attend_pair(
            False, rows, text_rows, min(CROSS_QUERIES, rows),
            lambda lo, hi: cq[lo:hi, lanes(j, 128)],
            lambda lo, hi: ckv[lo:hi, lanes(j, 128)],
            lambda lo, hi: ckv[lo:hi, lanes(j + pairs, 128)],
            bias, put, lse2.at[j],
        )

    looped(pairs, cross_pair, ((1, 26), (4, 27), (6, 28)))
    done_o2 = copies.start(o2, o_o2)
    load(7).wait()
    done_after_self.wait()

    def cross_out_block(b):
        at = block_rows(b, MATMUL_ROWS)
        resid[at, :] = resid[at, :] + nn(o2[at, :], weight(7)) + row(C_OBIAS)

    looped(rows // MATMUL_ROWS, cross_out_block)
    stage(29)
    done_after_cross = copies.start(resid, o_after_cross)
    done_o1.wait()
    h3 = o1

    def norm_three(b):
        at = block_rows(b, BLOCK)
        unit, _ = center_and_scale(resid[at, :])
        h3[at, :] = (unit * row(F_GAIN) + row(F_SHIFT)).astype(jnp.bfloat16)

    looped(rows // BLOCK, norm_three)
    done_h3 = copies.start(h3, o_h3)
    done_h1.wait()
    done_qkv.wait()
    waiting = []

    def up(q):
        load(8 + q).wait()
        slope_at = slopes.at[q % 2]

        def block(b):
            at = block_rows(b, BLOCK)
            inner = nn(h3[at, :], weight(8 + q)) + row(F_UPBIAS + q)
            active, slope = gelu_and_slope(inner)
            x[at, q * width : (q + 1) * width] = active.astype(jnp.bfloat16)
            slope_at[at, :] = slope.astype(jnp.bfloat16)

        if q >= 2:
            waiting[q - 2].wait()
        looped(rows // BLOCK, block)
        span = pl.ds(q * width, width)
        waiting.append(copies.start(slope_at, o_slope.at[:, span]))

    stage(30)
    stage(31)
    up(0)
    stage(32)
    stage(33)
    up(1)
    stage(34)
    up(2)
    stage(35)
    stage(36)
    up(3)
    stage(37)
    done_active = copies.start(x, o_active)
    done_after_cross.wait()

    def down(q):
        load(12 + q).wait()

        def block(b):
            at = block_rows(b, MATMUL_ROWS)
            resid[at, :] += nn(x[at, q * width : (q + 1) * width], weight(12 + q))

        looped(rows // MATMUL_ROWS, block)

    for q in range(4):
        down(q)
        if q < 3:
            stage(38 + 2 * q)
            stage(39 + 2 * q)
    cot_swap()
    done_cq.wait()
    done_o2.wait()
    valid_count = unit_length[y]
    zgrads[...] = jnp.zeros_like(zgrads)
    gbr, layer = cq, o2

    def last_block(b):
        at = block_rows(b, BLOCK)
        unit, scale = center_and_scale(resid[at, :] + row(F_DOWNBIAS))
        position = b * BLOCK + lax.broadcasted_iota(jnp.int32, (BLOCK, 1), 0)
        valid = jnp.where(position < valid_count, 1.0, 0.0)
        layer[at, :] = ((unit * row(Z_GAIN) + row(Z_SHIFT)) * valid).astype(jnp.bfloat16)
        half = b // (part // BLOCK)
        inner = lax.rem(b, part // BLOCK)
        upstream = cot[half, block_rows(inner, BLOCK), :].astype(jnp.float32) * valid
        zgrads[0:1, :] += jnp.sum(upstream * unit, axis=0, keepdims=True)
        zgrads[1:2, :] += jnp.sum(upstream, axis=0, keepdims=True)
        grad = norm_pull(unit, scale, upstream * row(Z_GAIN))
        low = grad.astype(jnp.bfloat16)
        gbr[at, :] = low
        zgrads[2:3, :] += jnp.sum(low.astype(jnp.float32), axis=0, keepdims=True)
        resid[at, :] = grad

    ending = []
    for b in range(rows // BLOCK):
        last_block(b)
        at = pl.ds(b * BLOCK, BLOCK)
        ending += [
            copies.start(source.at[at, :], target.at[at, :])
            for source, target in ((resid, o_gaf), (gbr, o_gbr), (layer, o_layer))
        ]
    ending += [done_tokens, done_h2, done_text, done_ckv, done_h3, done_active]
    for copy in ending + waiting[2:]:
        copy.wait()


def text_mask(text_rows, count):
    position = lax.broadcasted_iota(jnp.int32, (text_rows, 128), 0)
    return jnp.where(position < count, 0.0, MASKED)


def forward(depth, number, tokens, texts, cots, unit_length, text_length, shards):
    rows, width = 2 * tokens.shape[1], tokens.shape[2]
    text_rows = 2 * texts.shape[1]
    hidden = 4 * width
    pairs = width // 128
    share = shards[0].shape[0]
    sizes = [s.shape for s in shards[:DOWN_INDEX]] + [(share, width)] * 4
    items = sum(len(weight_items(s)) for s in sizes)
    low, full = jnp.bfloat16, jnp.float32

    def shape(*dims, kind=low):
        return jax.ShapeDtypeStruct(dims, kind)

    def vmem(*dims, kind=low):
        return pltpu.VMEM(dims, kind)

    big = shape(rows, width)
    exact = shape(rows, width, kind=full)
    outs = [shape(depth, 2, 2, 2, *s) for s in sizes]
    outs += [
        shape(*tokens.shape), shape(*texts.shape), big, shape(rows, 3 * width), big, exact, big, big,
        shape(text_rows, 2 * width), big, exact, big, shape(rows, hidden), shape(rows, hidden),
        exact, big, big,
    ]
    small = [
        shape(32, width, kind=full), shape(pairs, 2, rows, kind=full),
        shape(pairs, 2, rows, kind=full), shape(8, width, kind=full),
    ]
    scratch = [
        vmem(*tokens.shape), vmem(*texts.shape), vmem(*cots.shape), vmem(rows, hidden),
        vmem(rows, width), vmem(rows, width), vmem(text_rows, 2 * width), vmem(rows, width),
        vmem(rows, width, kind=full), vmem(rows, width), vmem(RING, depth, 2, 2, 2, 32, width),
        vmem(2, rows, width), vmem(depth, 2, 2, 2, *sizes[0]),
    ]
    scratch += [vmem(r.size, c.size) for s in sizes for r, c in weight_items(s)]
    scratch += copy_sems(items, depth)
    scratch += [
        pltpu.SemaphoreType.DMA((3, SWAP_PIECES)), pltpu.SemaphoreType.DMA((3, SWAP_PIECES)),
        pltpu.SemaphoreType.DMA((3,)), pltpu.SemaphoreType.DMA((items,)),
        pltpu.SemaphoreType.DMA((48,)), vmem(*sizes[UP_INDEX]), pltpu.SemaphoreType.DMA,
    ]
    memory = pl.BlockSpec(memory_space=pltpu.SMEM)
    results = pl.pallas_call(
        functools.partial(forward_kernel, depth, sizes),
        out_shape=outs + small,
        in_specs=[ANYWHERE] * 3 + [memory] * 2 + [ANYWHERE] * len(shards),
        out_specs=[ANYWHERE] * len(outs) + [pl.BlockSpec(memory_space=pltpu.VMEM)] * len(small),
        scratch_shapes=scratch,
        compiler_params=pltpu.CompilerParams(
            collective_id=number, has_side_effects=True, vmem_limit_bytes=VMEM_LIMIT
        ),
        name="forward",
    )(tokens, texts, cots, unit_length, text_length, *shards)
    return list(results[: len(sizes)]), list(results[len(sizes) :])


BACK_STRIDE = 3
BACK_RING = 2 * BACK_STRIDE + 2
BACK_QUERIES = 256
WEIGHT_RING = 2
NORM_BLOCK = 128


def ring_scratch(depth, stride, rows, cols, dtype):
    half = rows // 2
    slots = max(1, 3 * stride)
    return [
        pltpu.VMEM((max(1, 2 * stride + 2 * (stride > 0)), depth, 2, 2, 2, rows, cols), dtype),
        pltpu.VMEM((max(1, 2 * stride), depth, 2, 2, rows, cols), dtype),
        pltpu.VMEM((slots, depth, 2, half, cols), dtype),
        pltpu.VMEM((slots, depth, half, cols), dtype),
        pltpu.VMEM((slots, depth - 1, half, cols), dtype),
        pltpu.VMEM((slots, depth, 2, half, cols), dtype),
        pltpu.VMEM((slots, depth - 1, 2, half, cols), dtype),
        pltpu.VMEM((slots, half, cols), dtype),
    ]


def piece_phases(place, put_result, bufs, sems, item):
    depth = bufs[0].shape[1]
    piece, came, a_y, a_x, a_z, b_x, b_z, b_y = (buf.at[item % buf.shape[0]] for buf in bufs)
    half = bufs[7].shape[1]
    low, high = pl.ds(0, half), pl.ds(half, half)
    z, x, core, y = place.z, place.x, place.core, place.y
    every = slice(None)

    def send(a, b, index, device):
        return remote(a, b, sems, item, index, device)

    def copies(phase):
        if phase == 0:
            return [send(piece.at[every, every, 1 - core], came, 0, place.sibling())]
        if phase == 1:
            return [
                send(piece.at[every, every, core, 1 - y, low], a_y, 1, place.across_y()),
                send(piece.at[every, 1 - x, core, every, high], b_x, 2, place.across_x()),
            ]
        if phase == 2:
            return [send(a_y.at[every, 1 - x], a_x, 3, place.across_x())] + [
                send(
                    b_x.at[lax.rem(z + step, depth)], b_z.at[step - 1], 3 + step,
                    place.along_z(step),
                )
                for step in range(1, depth)
            ]
        return [send(b_z.at[0, 1 - y], b_y, 3 + depth, place.across_y())] + [
            send(
                a_x.at[lax.rem(z + step, depth)], a_z.at[step - 1], 3 + depth + step,
                place.along_z(step),
            )
            for step in range(1, depth)
        ]

    def start(phase):
        for copy in copies(phase):
            copy.start()

    def wait(phase):
        for copy in copies(phase):
            copy.wait()

    def wide(values):
        return values.astype(jnp.float32)

    def after_core():
        wait(0)

        @pl.loop(0, depth)
        def _(k):
            for i in range(2):
                for j in range(2):
                    piece[k, i, core, j] = piece[k, i, core, j] + came[k, i, j]

        start(1)

    def after_one():
        wait(1)

        @pl.loop(0, depth)
        def _(k):
            for i in range(2):
                a_y[k, i] = a_y[k, i] + piece[k, i, core, y, low]
                b_x[k, i] = b_x[k, i] + piece[k, x, core, i, high]

        start(2)

    def after_two():
        wait(2)

        @pl.loop(0, depth)
        def _(k):
            a_x[k] = a_x[k] + a_y[k, x]

        for i in range(2):
            total = wide(b_x[z, i])
            for step in range(1, depth):
                total = total + wide(b_z[step - 1, i])
            b_z[0, i] = total.astype(b_z.dtype)
        start(3)

    def closing():
        wait(3)
        total = wide(a_x[z])
        for step in range(1, depth):
            total = total + wide(a_z[step - 1])
        put_result(low, total)
        put_result(high, wide(b_z[0, y]) + wide(b_y[...]))

    return [lambda: start(0), after_core, after_one, after_two, closing]


def gather_vectors(vectors, first, shards):
    width = vectors.shape[1]
    row = first + lax.broadcasted_iota(jnp.int32, (shards, 32, width), 0)
    lane = lax.broadcasted_iota(jnp.int32, (shards, 32, width), 2)
    parts = jnp.where(row == lane // 32, vectors[None], 0.0).reshape(shards * 32, width)
    source = lax.broadcasted_iota(jnp.int32, (width, 128), 0)
    lane = lax.broadcasted_iota(jnp.int32, (width, 128), 1)
    select = jnp.where(lax.rem(source, 32) == lane, 1.0, 0.0).astype(jnp.bfloat16)
    total = None
    for _ in range(3):
        some = parts.astype(jnp.bfloat16)
        parts = parts - some.astype(jnp.float32)
        value = nn(some, select)
        total = value if total is None else total + value
    return total


def backward_kernel(depth, *refs):
    refs = list(refs)

    def take(count):
        taken = refs[:count]
        del refs[:count]
        return taken

    w_in, w_out, w_cq, w_ckv, w_co, w_up = take(6)
    w_downs = take(4)
    (
        i_tokens, i_text, i_h1, i_qkv, i_o1, i_after_self, i_h2, i_cq, i_ckv, i_o2, i_after_cross,
        i_h3, i_active, i_slope, i_gaf, i_gbr, i_layer,
    ) = take(17)
    vec, lse1, lse2, zgrads, text_length = take(5)
    o_layer, o_tokens, o_text = take(3)
    s_in, s_out, s_cq, s_ckv, s_co, s_up, s_down, s_small = take(8)
    p, q_buf, resid, dh, low, h3, extra, ckv, dckv, text, tgrad, src, vg, ka, va = take(15)
    ring = take(1)[0]
    bufs = take(8)
    small_bufs = take(8)
    sems = take(2)
    small_sems = take(2)
    swap_send, swap_receive, swap_local, loads, fetches = take(5)

    place = Place(depth)
    y = place.y
    rows, width = resid.shape
    part_rows = rows // 2
    pairs = width // 128
    shards = depth * 8
    text_rows = ckv.shape[0]
    fetched = Copies(fetches)
    fetch = fetched.start

    half_width = width // 2
    targets = [(s_down, q, h) for q in range(4) for h in (0, 1)]
    targets += [(s_co, 0, h) for h in (0, 1)]
    targets += [(s_up, 0, h) for h in range(8)]
    targets += [(s_cq, 0, h) for h in (0, 1)]
    targets += [(s_ckv, 0, h) for h in range(4)]
    targets += [(s_out, 0, h) for h in (0, 1)]
    targets += [(s_in, 0, 2 * c + h) for h in (0, 1) for c in range(3)]
    share = width // shards

    def keeping(target, quarter, column):
        def put(some_rows, value):
            at = pl.ds(quarter * share + some_rows.start, some_rows.size)
            target[at, column * half_width : (column + 1) * half_width] = value

        return put

    phases = [
        piece_phases(place, keeping(*target), bufs, sems, item)
        for item, target in enumerate(targets)
    ]

    def put_small(some_rows, value):
        s_small[some_rows, :] = value

    small_phases = piece_phases(place, put_small, small_bufs, small_sems, 0)
    stages = pipelined(phases + [[lambda: None] + small_phases[1:]], BACK_STRIDE)
    ran = []

    def stage(k):
        assert len(ran) == k
        ran.append(k)
        for one in stages[k]:
            one()

    def make(item, get_left, *rights):
        @pl.loop(0, 2)
        def _(b):
            left = get_left(lanes(b, half_width))
            slot = item
            for get in rights:
                value = left_dot(left, get()).astype(jnp.bfloat16)
                for k in range(value.shape[1] // half_width):
                    some = value[:, k * half_width : (k + 1) * half_width]
                    piece = bufs[0].at[slot % BACK_RING]
                    piece[pl.ds(b * (depth // 2), depth // 2)] = some.reshape(
                        depth // 2, 2, 2, 2, share, half_width
                    )
                    slot += 1

    def produce(item, get_left, *rights):
        make(item, get_left, *rights)
        stage(item)

    def part(buf, k):
        return lambda: buf[:, k * half_width : (k + 1) * half_width]

    def halves(buf, k):
        return (lambda: buf[:, k * width : (k + 1) * width],)

    order = []
    for k in range(4):
        order += [(w_downs[k], 0), (w_up, k)]
    order += [(w_co, 0), (w_ckv, 0), (w_ckv, 1), (w_cq, 0), (w_out, 0)]
    order += [(w_in, c) for c in range(3)]

    def load(n):
        whole, column = order[n]
        return pltpu.make_async_copy(
            whole.at[:, :, :, :, :, pl.ds(column * width, width)],
            ring.at[n % WEIGHT_RING],
            loads.at[n],
        )

    def weight(n):
        return ring[n % WEIGHT_RING].reshape(width, width)

    def ready(n):
        load(n).wait()

    def finished(n):
        if n + WEIGHT_RING < len(order):
            load(n + WEIGHT_RING).start()

    def row(index):
        return vec[index : index + 1, :]

    def add_row(index, value):
        vg[index : index + 1, :] += jnp.sum(value, axis=0, keepdims=True)

    def looped(count, body):
        @pl.loop(0, count)
        def _(j):
            body(j)

    def by_blocks(body, size=MATMUL_ROWS):
        looped(rows // size, lambda b: body(block_rows(b, size)))

    def column(buf, k):
        return lambda some_lanes: buf[:, pl.ds(k * width + some_lanes.start, some_lanes.size)]

    def plain(buf):
        return lambda some_lanes: buf[:, some_lanes]

    def norm_step(source, gain, shift, next_bias):
        blocks = rows // NORM_BLOCK

        def bring(b, slot):
            return pltpu.make_async_copy(
                source.at[block_rows(b, NORM_BLOCK), :], src.at[slot], swap_local.at[3 + slot]
            )

        bring(0, 0).start()

        def step(b):
            slot = lax.rem(b, 2)
            bring(b, slot).wait()

            @pl.when(b + 1 < blocks)
            def _():
                bring(b + 1, 1 - slot).start()

            at = block_rows(b, NORM_BLOCK)
            unit, scale = center_and_scale(src[slot])
            pulled = dh[at, :]
            add_row(gain, pulled * unit)
            add_row(shift, pulled)
            total = resid[at, :] + norm_pull(unit, scale, pulled * row(gain))
            resid[at, :] = total
            rounded = total.astype(jnp.bfloat16)
            low[at, :] = rounded
            add_row(next_bias, rounded.astype(jnp.float32))

        looped(blocks, step)

    def swap_out(k, get_source, target, local_source):
        def away():
            return remote(
                get_source(1 - y), target.at[y], (swap_send, swap_receive), k, 0, place.across_y()
            )

        def home():
            return pltpu.make_async_copy(local_source, target.at[y], swap_local.at[k])

        return away, home

    place.greet()
    for n in range(WEIGHT_RING):
        load(n).start()
    got_low = fetch(i_gbr, low)
    got_active = [
        fetch(i_active.at[:, pl.ds(k * width, width)], p.at[:, pl.ds(k * width, width)])
        for k in range(4)
    ]
    got_slope = [
        fetch(i_slope.at[:, pl.ds(k * width, width)], q_buf.at[:, pl.ds(k * width, width)])
        for k in range(4)
    ]
    got_resid = fetch(i_gaf, resid)
    got_h3 = fetch(i_h3, h3)
    keep = extra.at[pl.ds(0, part_rows)]
    got_keep = fetch(i_layer.at[y], keep)
    got_ckv = fetch(i_ckv, ckv)
    got_text = fetch(i_text, text)
    vg[...] = jnp.zeros_like(vg)
    vg[Z_GAIN : Z_GAIN + 1, :] = zgrads[0:1, :]
    vg[Z_SHIFT : Z_SHIFT + 1, :] = zgrads[1:2, :]
    vg[F_DOWNBIAS : F_DOWNBIAS + 1, :] = zgrads[2:3, :]
    layer_count = 16
    layer_size = part_rows // layer_count

    def layer_away(i):
        piece = pl.ds(i * layer_size, layer_size)
        return remote(
            i_layer.at[1 - y, piece], o_layer.at[y, piece], (swap_send, swap_receive), 0, i,
            place.across_y(),
        )

    layer_home = pltpu.make_async_copy(keep, o_layer.at[y], swap_local.at[0])
    for i in range(layer_count):
        if i < 6:
            layer_away(i).start()
        else:
            stages[i - 5].append(lambda i=i: layer_away(i).start())

    got_low.wait()
    for k in range(4):
        got_active[k].wait()
        produce(2 * k, column(p, k), *halves(low, 0))
        n = 2 * k
        got_slope[k].wait()
        ready(n)
        span = slice(k * width, (k + 1) * width)

        def inner_block(at, n=n, span=span, k=k):
            grad = nt(low[at, :], weight(n)) * q_buf[at, span].astype(jnp.float32)
            rounded = grad.astype(jnp.bfloat16)
            q_buf[at, span] = rounded
            add_row(F_UPBIAS + k, rounded.astype(jnp.float32))

        by_blocks(inner_block)
        finished(n)
        stage(2 * k + 1)
        ready(n + 1)

        def up_block(at, n=n, span=span, k=k):
            value = nt(q_buf[at, span], weight(n + 1))
            dh[at, :] = value if k == 0 else dh[at, :] + value

        by_blocks(up_block)
        finished(n + 1)
    cq_at, o2_at, do2_at, h2_at = (slice(k * width, (k + 1) * width) for k in range(4))
    got_cq = fetch(i_cq, p.at[:, pl.ds(0, width)])
    got_o2 = fetch(i_o2, p.at[:, pl.ds(width, width)])
    got_h2 = fetch(i_h2, p.at[:, pl.ds(3 * width, width)])
    got_resid.wait()
    norm_step(i_after_cross, F_GAIN, F_SHIFT, C_OBIAS)
    got_keep.wait()
    layer_home.start()

    got_o2.wait()
    produce(8, column(p, 1), *halves(low, 0))
    ready(8)

    def do2_block(at):
        p[at, do2_at] = nt(low[at, :], weight(8)).astype(jnp.bfloat16)

    by_blocks(do2_block)
    finished(8)
    stage(9)
    got_cq.wait()
    got_h3.wait()
    got_ckv.wait()
    bias = text_mask(text_rows, text_length[y])
    dcq = extra
    layer_home.wait()

    def pair_lanes(buf, j, base):
        return lambda lo, hi: buf[lo:hi, lanes(j + base * pairs, 128)]

    def cross_pair(j):
        for at, k in ((0, 10), (2, 11), (3, 12), (5, 13), (7, 14)):

            @pl.when(j == at)
            def _(k=k):
                if k % 2 == 0:
                    produce(k, plain(h3), *halves(q_buf, (k - 10) // 2))
                else:
                    stage(k)

        def put_dq(sl, value):
            dcq[sl, lanes(j, 128)] = value
            vg[C_QBIAS : C_QBIAS + 1, lanes(j, 128)] += jnp.sum(
                value.astype(jnp.float32), axis=0, keepdims=True
            )

        def put_dk(value):
            dckv[:, lanes(j, 128)] = value

        def put_dv(value):
            dckv[:, lanes(j + pairs, 128)] = value
            vg[C_VBIAS : C_VBIAS + 1, lanes(j, 128)] = jnp.sum(
                value.astype(jnp.float32), axis=0, keepdims=True
            )

        attend_back_pair(
            False, rows, text_rows, BACK_QUERIES, pair_lanes(p, j, 0), pair_lanes(ckv, j, 0),
            pair_lanes(ckv, j, 1), pair_lanes(p, j, 1), pair_lanes(p, j, 2), lse2.at[j], bias,
            put_dq, put_dk, put_dv, ka, va,
        )

    looped(pairs, cross_pair)
    got_qkv = fetch(i_qkv, p.at[:, pl.ds(0, 3 * width)])
    stage(15)
    ready(9)
    text_value = nt(dckv[:, :width], weight(9))
    finished(9)
    ready(10)
    text_value = text_value + nt(dckv[:, width:], weight(10))
    finished(10)
    tgrad[...] = text_value.astype(jnp.bfloat16).reshape(tgrad.shape)
    text_away, text_home = swap_out(1, lambda k: tgrad.at[k], o_text, tgrad.at[y])
    text_away().start()
    text_home().start()
    produce(16, plain(h3), *halves(q_buf, 3))
    ready(11)

    def dh2_block(at):
        dh[at, :] = nt(dcq[at, :], weight(11))

    by_blocks(dh2_block)
    finished(11)
    stage(17)
    got_o1 = fetch(i_o1, q_buf.at[:, pl.ds(3 * width, width)])
    got_tokens = fetch(i_tokens, h3)
    norm_step(i_after_self, C_GAIN, C_SHIFT, A_OBIAS)
    got_h2.wait()
    produce(18, column(p, 3), *halves(dcq, 0))
    got_h1 = fetch(i_h1, p.at[:, pl.ds(3 * width, width)])

    ready(12)
    do1 = extra

    def do1_block(at):
        do1[at, :] = nt(low[at, :], weight(12)).astype(jnp.bfloat16)

    by_blocks(do1_block)
    finished(12)
    stage(19)
    got_text.wait()

    def text_lanes(some_lanes):
        return text[:, :, some_lanes].reshape(text_rows, some_lanes.size)

    got_qkv.wait()
    got_o1.wait()

    def self_pair(j):
        def put_dq(sl, value):
            q_buf[sl, lanes(j, 128)] = value
            vg[A_QBIAS : A_QBIAS + 1, lanes(j, 128)] += jnp.sum(
                value.astype(jnp.float32), axis=0, keepdims=True
            )

        def put_dk(value):
            q_buf[:, lanes(j + pairs, 128)] = value

        def put_dv(value):
            q_buf[:, lanes(j + 2 * pairs, 128)] = value
            vg[A_VBIAS : A_VBIAS + 1, lanes(j, 128)] = jnp.sum(
                value.astype(jnp.float32), axis=0, keepdims=True
            )

        attend_back_pair(
            True, rows, rows, BACK_QUERIES, pair_lanes(p, j, 0), pair_lanes(p, j, 1), pair_lanes(p, j, 2),
            pair_lanes(q_buf, j, 3), lambda lo, hi: do1[lo:hi, lanes(j, 128)], lse1.at[j], None,
            put_dq, put_dk, put_dv, ka, va,
        )

    half_pairs = pairs // 2

    def first_half(j):
        for k in range(4):

            @pl.when(j == k)
            def _(k=k):
                if k % 2 == 0:
                    produce(20 + k, text_lanes, *halves(dckv, k // 2))
                else:
                    stage(20 + k)

        self_pair(j)

    looped(half_pairs, first_half)
    got_h1.wait()

    def second_half(j):
        @pl.when(j == 0)
        def _():
            produce(24, column(q_buf, 3), *halves(low, 0))

        @pl.when(j == 1)
        def _():
            stage(25)

        @pl.when(j == 2)
        def _():
            produce(26, column(p, 3), part(q_buf, 0), part(q_buf, 2))
            stage(27)

        @pl.when(j == 3)
        def _():
            produce(28, column(p, 3), part(q_buf, 4))

        self_pair(j + half_pairs)

    looped(half_pairs, second_half)

    grads = low

    def rows_of(half, b):
        return pl.ds(pl.multiple_of(half * part_rows + b * BLOCK, BLOCK), BLOCK)

    def dh1_block(half, c, first=None):
        fresh = c == 0 if first is None else first

        def block(b):
            at = block_rows(half, part_rows)
            value = nt(q_buf[at, c * width : (c + 1) * width], weight(13 + c))
            dh[at, :] = value if fresh else dh[at, :] + value

        return block

    def last_block(half):
        def block(b):
            at = rows_of(half, b)
            unit, scale = center_and_scale(h3[at, :].astype(jnp.float32))
            pulled = dh[at, :]
            add_row(A_GAIN, pulled * unit)
            add_row(A_SHIFT, pulled)
            total = resid[at, :] + norm_pull(unit, scale, pulled * row(A_GAIN))
            grads[at, :] = total.astype(jnp.bfloat16)

        return block

    token_pieces = 16
    token_size = part_rows // token_pieces

    def tokens_away(i):
        at = pl.multiple_of((1 - y) * part_rows + i * token_size, token_size)
        return remote(
            grads.at[pl.ds(at, token_size), :],
            o_tokens.at[y, pl.ds(i * token_size, token_size)],
            (swap_send, swap_receive), 2, i, place.across_y(),
        )

    tokens_sent = []

    def send_tokens(some):
        for i in range(len(tokens_sent), min(token_pieces, len(tokens_sent) + some)):
            tokens_away(i).start()
            tokens_sent.append(i)

    tokens_home = pltpu.make_async_copy(
        grads.at[block_rows(y, part_rows), :], o_tokens.at[y], swap_local.at[2]
    )
    count = part_rows // BLOCK
    make(29, column(p, 3), part(q_buf, 1), part(q_buf, 3))
    stage(29)
    got_tokens.wait()
    ready(13)
    dh1_block(1 - y, 0)(0)
    load(15).start()
    ready(14)
    dh1_block(1 - y, 1)(0)
    stage(30)
    ready(15)
    dh1_block(1 - y, 2)(0)
    looped(count, last_block(1 - y))
    send_tokens(3)
    make(31, column(p, 3), part(q_buf, 5))
    stage(31)
    send_tokens(2)
    dh1_block(y, 2, True)(0)
    load(13).start()
    dh1_block(y, 1)(0)
    stage(32)
    send_tokens(3)
    ready(13)
    dh1_block(y, 0, False)(0)
    looped(count, last_block(y))
    tokens_home.start()

    @pl.loop(0, depth)
    def _(k):
        some = gather_vectors(vg[...], k * 8, 8)
        small_bufs[0][0, k] = some.reshape(small_bufs[0].shape[2:])

    small_phases[0]()
    for k in range(33, len(stages)):
        stage(k)
        send_tokens(2)
    values = s_up[...]
    s_up[...] = quarter_columns(values, width, back=True)
    for copy in (
        *[layer_away(i) for i in range(layer_count)], text_away(), text_home(), *[tokens_away(i) for i in range(token_pieces)], tokens_home,
    ):
        copy.wait()


def backward(depth, number, wholes, kept, text_length):
    (
        token_seq, text_seq, normed_one, joined, self_mixed, after_self, normed_two, cross_queries,
        cross_kv, cross_mixed, after_cross, normed_three, active, slope, grad_after_ffn,
        grad_branch, layer_out, vec, lse1, lse2, zgrads,
    ) = kept
    rows, width = self_mixed.shape
    text_rows = cross_kv.shape[0]
    hidden = active.shape[1]
    share = width // (depth * 8)
    half = (2, rows // 2, width)
    low, full = jnp.bfloat16, jnp.float32
    operands = [
        token_seq.reshape(rows, width), text_seq, normed_one, joined, self_mixed, after_self,
        normed_two, cross_queries, cross_kv, cross_mixed, after_cross, normed_three, active, slope,
        grad_after_ffn, grad_branch, layer_out.reshape(half),
    ]

    def vmem(*dims, kind=low):
        return pltpu.VMEM(dims, kind)

    results_low = [jax.ShapeDtypeStruct(s, low) for s in (half, half, text_seq.shape)]
    columns = [w.shape[-1] for w in wholes[:6]]
    sums = [jax.ShapeDtypeStruct((share, c), full) for c in columns]
    sums += [jax.ShapeDtypeStruct((4 * share, width), full), jax.ShapeDtypeStruct((share, 128), full)]
    scratch = [
        vmem(rows, hidden), vmem(rows, hidden), vmem(rows, width, kind=full),
        vmem(rows, width, kind=full), vmem(rows, width), vmem(rows, width), vmem(rows, width),
        vmem(text_rows, 2 * width), vmem(text_rows, 2 * width), vmem(*text_seq.shape),
        vmem(*text_seq.shape), vmem(2, NORM_BLOCK, width, kind=full),
        vmem(32, width, kind=full), vmem(rows, 128, kind=full), vmem(rows, 128, kind=full),
        vmem(WEIGHT_RING, depth, 2, 2, 2, share, width),
    ]
    scratch += ring_scratch(depth, BACK_STRIDE, share, width // 2, low)
    scratch += ring_scratch(depth, 0, share, 128, full)
    pieces = 2 * (sum(c // width for c in columns) + 4)
    scratch += copy_sems(pieces, depth)[:2] + copy_sems(1, depth)[:2]
    scratch += [
        pltpu.SemaphoreType.DMA((3, 16)), pltpu.SemaphoreType.DMA((3, 16)),
        pltpu.SemaphoreType.DMA((5,)), pltpu.SemaphoreType.DMA((16,)),
        pltpu.SemaphoreType.DMA((32,)),
    ]
    in_vmem = pl.BlockSpec(memory_space=pltpu.VMEM)
    results = pl.pallas_call(
        functools.partial(backward_kernel, depth),
        out_shape=results_low + sums,
        in_specs=[ANYWHERE] * (len(wholes) + len(operands))
        + [in_vmem] * 4
        + [pl.BlockSpec(memory_space=pltpu.SMEM)],
        out_specs=[ANYWHERE] * 3 + [in_vmem] * len(sums),
        scratch_shapes=scratch,
        compiler_params=pltpu.CompilerParams(
            collective_id=number, has_side_effects=True, vmem_limit_bytes=BACK_VMEM_LIMIT
        ),
        name="backward",
    )(*wholes, *operands, vec, lse1, lse2, zgrads, text_length)
    return list(results[:3]), list(results[3:])


BACK_VMEM_LIMIT = 63 * 2**20


def pack_vectors(vectors, wide):
    packed = jnp.concatenate([jnp.stack(vectors), wide.reshape(4, -1)])
    return jnp.pad(packed, ((0, 32 - packed.shape[0]), (0, 128 - packed.shape[1])))


def paired_layer(
    depth,
    tokens,
    text_states,
    unit_length,
    text_length,
    cotangent,
    attn_gain,
    attn_shift,
    attn_inputs,
    attn_qbias,
    attn_vbias,
    attn_output,
    attn_obias,
    cross_gain,
    cross_shift,
    cross_query,
    cross_qbias,
    cross_keyval,
    cross_vbias,
    cross_output,
    cross_obias,
    ffn_gain,
    ffn_shift,
    ffn_up,
    ffn_upbias,
    ffn_down,
    ffn_downbias,
    final_gain,
    final_shift,
):
    share = attn_gain.shape[0]
    packed = pack_vectors(
        [
            attn_gain, attn_shift, attn_qbias, attn_vbias, attn_obias, cross_gain, cross_shift,
            cross_qbias, cross_vbias, cross_obias, ffn_gain, ffn_shift, ffn_downbias, final_gain,
            final_shift,
        ],
        ffn_upbias,
    )
    wholes, kept = forward(
        depth, 0, tokens, text_states, cotangent, unit_length, text_length,
        [
            packed, attn_inputs, attn_output, cross_query, cross_keyval, cross_output, ffn_up,
            ffn_down,
        ],
    )
    (layer_out, tokens_grad, text_grad), sums = backward(depth, 1, wholes[1:], kept, text_length)
    s_in, s_out, s_cq, s_ckv, s_co, s_up, s_down, s_small = sums
    s_upbias = s_small[VECTOR_COUNT : VECTOR_COUNT + 4, :share].reshape(-1)
    v = [s_small[i, :share] for i in range(VECTOR_COUNT)]
    return (
        layer_out, tokens_grad, text_grad, v[A_GAIN], v[A_SHIFT], s_in, v[A_QBIAS], v[A_VBIAS],
        s_out, v[A_OBIAS], v[C_GAIN], v[C_SHIFT], s_cq, v[C_QBIAS], s_ckv, v[C_VBIAS], s_co,
        v[C_OBIAS], v[F_GAIN], v[F_SHIFT], s_up, s_upbias, s_down, v[F_DOWNBIAS], v[Z_GAIN],
        v[Z_SHIFT],
    )


def solution(mesh):
    in_specs = (
        P("dp", "seq", None),
        P("dp", "seq", None),
        P("dp"),
        P("dp"),
        P("dp", "seq", None),
        P(("dp", "seq")),
        P(("dp", "seq")),
        P(("dp", "seq"), None),
        P(("dp", "seq")),
        P(("dp", "seq")),
        P(("dp", "seq"), None),
        P(("dp", "seq")),
        P(("dp", "seq")),
        P(("dp", "seq")),
        P(("dp", "seq"), None),
        P(("dp", "seq")),
        P(("dp", "seq"), None),
        P(("dp", "seq")),
        P(("dp", "seq"), None),
        P(("dp", "seq")),
        P(("dp", "seq")),
        P(("dp", "seq")),
        P(("dp", "seq"), None),
        P(("dp", "seq")),
        P(("dp", "seq"), None),
        P(("dp", "seq")),
        P(("dp", "seq")),
        P(("dp", "seq")),
    )
    out_specs = (
        P("dp", "seq", None),
        P("dp", "seq", None),
        P("dp", "seq", None),
        P(("dp", "seq")),
        P(("dp", "seq")),
        P(("dp", "seq"), None),
        P(("dp", "seq")),
        P(("dp", "seq")),
        P(("dp", "seq"), None),
        P(("dp", "seq")),
        P(("dp", "seq")),
        P(("dp", "seq")),
        P(("dp", "seq"), None),
        P(("dp", "seq")),
        P(("dp", "seq"), None),
        P(("dp", "seq")),
        P(("dp", "seq"), None),
        P(("dp", "seq")),
        P(("dp", "seq")),
        P(("dp", "seq")),
        P(("dp", "seq"), None),
        P(("dp", "seq")),
        P(("dp", "seq"), None),
        P(("dp", "seq")),
        P(("dp", "seq")),
        P(("dp", "seq")),
    )
    groups, seq_parts = mesh.shape["dp"], mesh.shape["seq"]

    def layer(*arguments):
        shard = arguments[5].shape[0]
        parts = arguments[0].shape[0]
        if seq_parts == 2 and parts == 2 and groups % 4 == 0 and shard % 32 == 0:
            return paired_layer(groups // 4, *arguments)
        return on_device(*arguments)

    return jax.shard_map(
        layer, mesh=mesh, in_specs=in_specs, out_specs=out_specs, check_vma=False
    )
```

```python
import functools
import math

import jax
import jax.numpy as jnp
from jax import lax
from jax.experimental import pallas as pl
from jax.experimental.pallas import tpu as pltpu
from jax.sharding import PartitionSpec as P

HEADS = 16
HEAD_DIM = 64


EPSILON = 1e-05
MASKED = -1e30


def layer_norm(values, norm_gain, norm_shift):
    center = values - jnp.mean(values, axis=-1, keepdims=True)
    spread = jnp.mean(center * center, axis=-1, keepdims=True)
    return center * lax.rsqrt(spread + EPSILON) * norm_gain + norm_shift


def norm_back(values, norm_gain, norm_shift, upstream):
    result, pullback = jax.vjp(layer_norm, values, norm_gain, norm_shift)
    return pullback(upstream)


def rows_dot(left_side, right_side):
    return jnp.dot(left_side, right_side, preferred_element_type=jnp.float32)


def left_dot(left_side, right_side):
    return lax.dot_general(
        left_side, right_side, (((0,), (0,)), ((), ())), preferred_element_type=jnp.float32
    )


def right_dot(left_side, right_side):
    return lax.dot_general(
        left_side, right_side, (((1,), (1,)), ((), ())), preferred_element_type=jnp.float32
    )


def heads_of(matrix):
    return matrix.reshape(matrix.shape[0], HEADS, HEAD_DIM)


def attend_forward(queries, key_rows, value_rows, allowed):
    score_scale = 1.0 / math.sqrt(HEAD_DIM)
    scores = (
        jnp.einsum(
            "qhd,khd->hqk",
            heads_of(queries),
            heads_of(key_rows),
            preferred_element_type=jnp.float32,
        )
        * score_scale
    )
    scores = jnp.where(allowed[None], scores, MASKED)
    row_max = jnp.max(scores, axis=-1, keepdims=True)
    weights = jnp.exp(scores - row_max)
    row_total = jnp.sum(weights, axis=-1, keepdims=True)
    weights = (weights / row_total).astype(jnp.bfloat16)
    mixed_rows = jnp.einsum(
        "hqk,khd->qhd", weights, heads_of(value_rows), preferred_element_type=jnp.float32
    )
    logsum = (row_max + jnp.log(row_total))[..., 0]
    return (mixed_rows.reshape(queries.shape[0], -1).astype(jnp.bfloat16), logsum)


def attend_back(queries, key_rows, value_rows, allowed, logsum, upstream):
    score_scale = 1.0 / math.sqrt(HEAD_DIM)
    query_heads = heads_of(queries)
    key_heads = heads_of(key_rows)
    upstream_heads = heads_of(upstream)
    scores = (
        jnp.einsum("qhd,khd->hqk", query_heads, key_heads, preferred_element_type=jnp.float32)
        * score_scale
    )
    scores = jnp.where(allowed[None], scores, MASKED)
    weights = jnp.exp(scores - logsum[..., None])
    grad_weights = jnp.einsum(
        "qhd,khd->hqk", upstream_heads, heads_of(value_rows), preferred_element_type=jnp.float32
    )
    row_delta = jnp.sum(weights * grad_weights, axis=-1, keepdims=True)
    grad_scores = (weights * (grad_weights - row_delta)).astype(jnp.bfloat16)
    grad_query = (
        jnp.einsum("hqk,khd->qhd", grad_scores, key_heads, preferred_element_type=jnp.float32)
        * score_scale
    )
    grad_key = (
        jnp.einsum("hqk,qhd->khd", grad_scores, query_heads, preferred_element_type=jnp.float32)
        * score_scale
    )
    grad_value = jnp.einsum(
        "hqk,qhd->khd",
        weights.astype(jnp.bfloat16),
        upstream_heads,
        preferred_element_type=jnp.float32,
    )
    key_count = key_rows.shape[0]
    return (
        grad_query.reshape(queries.shape[0], -1),
        grad_key.reshape(key_count, -1),
        grad_value.reshape(key_count, -1),
    )


def to_float(values):
    return values.astype(jnp.float32)


def on_device(
    tokens,
    text_states,
    unit_length,
    text_length,
    cotangent,
    attn_gain,
    attn_shift,
    attn_inputs,
    attn_qbias,
    attn_vbias,
    attn_output,
    attn_obias,
    cross_gain,
    cross_shift,
    cross_query,
    cross_qbias,
    cross_keyval,
    cross_vbias,
    cross_output,
    cross_obias,
    ffn_gain,
    ffn_shift,
    ffn_up,
    ffn_upbias,
    ffn_down,
    ffn_downbias,
    final_gain,
    final_shift,
):
    seq_count, local_len, model_width = tokens.shape
    row_count = seq_count * local_len
    first_pos = lax.axis_index("seq") * local_len
    zero_bias = jnp.zeros((model_width,), jnp.float32)
    (
        a_gain_full,
        a_shift_full,
        attention_input_weight_whole,
        a_qbias_full,
        a_vbias_full,
        a_output_full,
        a_obias_full,
    ) = (
        lax.all_gather(attn_gain, ("dp", "seq"), axis=0, tiled=True),
        lax.all_gather(attn_shift, ("dp", "seq"), axis=0, tiled=True),
        lax.all_gather(attn_inputs, ("dp", "seq"), axis=0, tiled=True),
        lax.all_gather(attn_qbias, ("dp", "seq"), axis=0, tiled=True),
        lax.all_gather(attn_vbias, ("dp", "seq"), axis=0, tiled=True),
        lax.all_gather(attn_output, ("dp", "seq"), axis=0, tiled=True),
        lax.all_gather(attn_obias, ("dp", "seq"), axis=0, tiled=True),
    )
    inputs = to_float(tokens).reshape(row_count, model_width)
    normed_one = layer_norm(inputs, to_float(a_gain_full), to_float(a_shift_full)).astype(
        jnp.bfloat16
    )
    joined = rows_dot(normed_one, attention_input_weight_whole) + jnp.concatenate(
        [to_float(a_qbias_full), zero_bias, to_float(a_vbias_full)]
    )
    joined = joined.astype(jnp.bfloat16)
    self_queries = joined[:, :model_width].reshape(seq_count, local_len, model_width)
    keyval_local = joined[:, model_width:].reshape(seq_count, local_len, 2 * model_width)
    self_keyval = lax.all_gather(keyval_local, "seq", axis=1, tiled=True)
    full_len = self_keyval.shape[1]
    causal = jnp.arange(full_len)[None, :] <= (first_pos + jnp.arange(local_len))[:, None]

    def self_forward(packed):
        seq_queries, seq_keyval = packed
        return attend_forward(
            seq_queries, seq_keyval[:, :model_width], seq_keyval[:, model_width:], causal
        )

    self_mixed, self_logsum = lax.map(self_forward, (self_queries, self_keyval))
    self_flat = self_mixed.reshape(row_count, model_width)
    after_self = inputs + rows_dot(self_flat, a_output_full) + to_float(a_obias_full)
    (
        c_gain_full,
        c_shift_full,
        c_query_full,
        c_qbias_full,
        c_keyval_full,
        cross_value_bias_whole,
        c_output_full,
        c_obias_full,
    ) = (
        lax.all_gather(cross_gain, ("dp", "seq"), axis=0, tiled=True),
        lax.all_gather(cross_shift, ("dp", "seq"), axis=0, tiled=True),
        lax.all_gather(cross_query, ("dp", "seq"), axis=0, tiled=True),
        lax.all_gather(cross_qbias, ("dp", "seq"), axis=0, tiled=True),
        lax.all_gather(cross_keyval, ("dp", "seq"), axis=0, tiled=True),
        lax.all_gather(cross_vbias, ("dp", "seq"), axis=0, tiled=True),
        lax.all_gather(cross_output, ("dp", "seq"), axis=0, tiled=True),
        lax.all_gather(cross_obias, ("dp", "seq"), axis=0, tiled=True),
    )
    normed_two = layer_norm(after_self, to_float(c_gain_full), to_float(c_shift_full)).astype(
        jnp.bfloat16
    )
    cross_queries = (rows_dot(normed_two, c_query_full) + to_float(c_qbias_full)).astype(
        jnp.bfloat16
    )
    cross_queries = cross_queries.reshape(seq_count, local_len, model_width)
    keyval_bias = jnp.concatenate([zero_bias, to_float(cross_value_bias_whole)])
    text_whole = lax.all_gather(text_states, "seq", axis=1, tiled=True)
    cross_kv = (rows_dot(text_whole.reshape(-1, model_width), c_keyval_full) + keyval_bias).astype(
        jnp.bfloat16
    )
    cross_kv = cross_kv.reshape(seq_count, -1, 2 * model_width)
    text_total = cross_kv.shape[1]
    text_allowed = jnp.arange(text_total)[None, :] < text_length[:, None]

    def cross_forward(packed):
        seq_queries, seq_keyval, seq_allowed = packed
        allowed = jnp.broadcast_to(seq_allowed[None, :], (local_len, text_total))
        return attend_forward(
            seq_queries, seq_keyval[:, :model_width], seq_keyval[:, model_width:], allowed
        )

    cross_blended_rows, cross_logsum = lax.map(
        cross_forward, (cross_queries, cross_kv, text_allowed)
    )
    cross_flat = cross_blended_rows.reshape(row_count, model_width)
    after_cross = after_self + rows_dot(cross_flat, c_output_full) + to_float(c_obias_full)
    (
        f_gain_full,
        feedforward_shift_whole,
        f_up_full,
        f_upbias_full,
        f_down_full,
        f_downbias_full,
        z_gain_full,
        z_shift_full,
    ) = (
        lax.all_gather(ffn_gain, ("dp", "seq"), axis=0, tiled=True),
        lax.all_gather(ffn_shift, ("dp", "seq"), axis=0, tiled=True),
        lax.all_gather(ffn_up, ("dp", "seq"), axis=0, tiled=True),
        lax.all_gather(ffn_upbias, ("dp", "seq"), axis=0, tiled=True),
        lax.all_gather(ffn_down, ("dp", "seq"), axis=0, tiled=True),
        lax.all_gather(ffn_downbias, ("dp", "seq"), axis=0, tiled=True),
        lax.all_gather(final_gain, ("dp", "seq"), axis=0, tiled=True),
        lax.all_gather(final_shift, ("dp", "seq"), axis=0, tiled=True),
    )
    normed_three = layer_norm(
        after_cross, to_float(f_gain_full), to_float(feedforward_shift_whole)
    ).astype(jnp.bfloat16)
    ffn_inner = rows_dot(normed_three, f_up_full) + to_float(f_upbias_full)
    active = jax.nn.gelu(ffn_inner).astype(jnp.bfloat16)
    after_ffn = after_cross + rows_dot(active, f_down_full) + to_float(f_downbias_full)
    valid_rows = ((first_pos + jnp.arange(local_len))[None, :] < unit_length[:, None]).astype(
        jnp.float32
    )
    valid_rows = valid_rows.reshape(row_count, 1)
    final_norm = layer_norm(after_ffn, to_float(z_gain_full), to_float(z_shift_full))
    layer_out = (
        (final_norm * valid_rows).astype(jnp.bfloat16).reshape(seq_count, local_len, model_width)
    )
    (
        f_gain_full,
        feedforward_shift_whole,
        f_up_full,
        f_upbias_full,
        f_down_full,
        f_downbias_full,
        z_gain_full,
        z_shift_full,
    ) = (
        lax.all_gather(ffn_gain, ("dp", "seq"), axis=0, tiled=True),
        lax.all_gather(ffn_shift, ("dp", "seq"), axis=0, tiled=True),
        lax.all_gather(ffn_up, ("dp", "seq"), axis=0, tiled=True),
        lax.all_gather(ffn_upbias, ("dp", "seq"), axis=0, tiled=True),
        lax.all_gather(ffn_down, ("dp", "seq"), axis=0, tiled=True),
        lax.all_gather(ffn_downbias, ("dp", "seq"), axis=0, tiled=True),
        lax.all_gather(final_gain, ("dp", "seq"), axis=0, tiled=True),
        lax.all_gather(final_shift, ("dp", "seq"), axis=0, tiled=True),
    )
    upstream = to_float(cotangent).reshape(row_count, model_width) * valid_rows
    grad_after_ffn, grad_zgain, grad_zshift = norm_back(
        after_ffn, to_float(z_gain_full), to_float(z_shift_full), upstream
    )
    grad_branch = grad_after_ffn.astype(jnp.bfloat16)
    grad_down = left_dot(active, grad_branch)
    grad_downbias = jnp.sum(to_float(grad_branch), axis=0)
    grad_active = right_dot(grad_branch, f_down_full)
    inner_value, gelu_back = jax.vjp(jax.nn.gelu, ffn_inner)
    grad_inner = gelu_back(grad_active)[0].astype(jnp.bfloat16)
    grad_up = left_dot(normed_three, grad_inner)
    grad_upbias = jnp.sum(to_float(grad_inner), axis=0)
    grad_normed_three = right_dot(grad_inner, f_up_full)
    grad_cross_norm, grad_fgain, grad_fshift = norm_back(
        after_cross, to_float(f_gain_full), to_float(feedforward_shift_whole), grad_normed_three
    )
    grad_after_cross = grad_after_ffn + grad_cross_norm
    ffn_sums = (
        lax.psum_scatter(grad_fgain, ("dp", "seq"), scatter_dimension=0, tiled=True),
        lax.psum_scatter(grad_fshift, ("dp", "seq"), scatter_dimension=0, tiled=True),
        lax.psum_scatter(grad_up, ("dp", "seq"), scatter_dimension=0, tiled=True),
        lax.psum_scatter(grad_upbias, ("dp", "seq"), scatter_dimension=0, tiled=True),
        lax.psum_scatter(grad_down, ("dp", "seq"), scatter_dimension=0, tiled=True),
        lax.psum_scatter(grad_downbias, ("dp", "seq"), scatter_dimension=0, tiled=True),
        lax.psum_scatter(grad_zgain, ("dp", "seq"), scatter_dimension=0, tiled=True),
        lax.psum_scatter(grad_zshift, ("dp", "seq"), scatter_dimension=0, tiled=True),
    )
    (
        c_gain_full,
        c_shift_full,
        c_query_full,
        c_qbias_full,
        c_keyval_full,
        cross_value_bias_whole,
        c_output_full,
        c_obias_full,
    ) = (
        lax.all_gather(cross_gain, ("dp", "seq"), axis=0, tiled=True),
        lax.all_gather(cross_shift, ("dp", "seq"), axis=0, tiled=True),
        lax.all_gather(cross_query, ("dp", "seq"), axis=0, tiled=True),
        lax.all_gather(cross_qbias, ("dp", "seq"), axis=0, tiled=True),
        lax.all_gather(cross_keyval, ("dp", "seq"), axis=0, tiled=True),
        lax.all_gather(cross_vbias, ("dp", "seq"), axis=0, tiled=True),
        lax.all_gather(cross_output, ("dp", "seq"), axis=0, tiled=True),
        lax.all_gather(cross_obias, ("dp", "seq"), axis=0, tiled=True),
    )
    cross_branch_gradient = grad_after_cross.astype(jnp.bfloat16)
    grad_coutput = left_dot(cross_flat, cross_branch_gradient)
    grad_cobias = jnp.sum(to_float(cross_branch_gradient), axis=0)
    grad_cross_mixed = right_dot(cross_branch_gradient, c_output_full).astype(jnp.bfloat16)
    grad_cross_mixed = grad_cross_mixed.reshape(seq_count, local_len, model_width)

    def cross_backward(packed):
        seq_queries, seq_keyval, seq_allowed, sequence_log_sum_exp, seq_upstream = packed
        allowed = jnp.broadcast_to(seq_allowed[None, :], (local_len, text_total))
        return attend_back(
            seq_queries,
            seq_keyval[:, :model_width],
            seq_keyval[:, model_width:],
            allowed,
            sequence_log_sum_exp,
            seq_upstream,
        )

    grad_cq, grad_ck, grad_cv = lax.map(
        cross_backward, (cross_queries, cross_kv, text_allowed, cross_logsum, grad_cross_mixed)
    )
    grad_ckv = lax.psum_scatter(
        jnp.concatenate([grad_ck, grad_cv], axis=-1).astype(jnp.bfloat16),
        "seq",
        scatter_dimension=1,
        tiled=True,
    ).astype(jnp.float32)
    grad_ckv = grad_ckv.astype(jnp.bfloat16).reshape(-1, 2 * model_width)
    grad_ckeyval = left_dot(text_states.reshape(-1, model_width), grad_ckv)
    grad_cvbias = jnp.sum(to_float(grad_ckv[:, model_width:]), axis=0)
    text_grad = right_dot(grad_ckv, c_keyval_full).astype(jnp.bfloat16).reshape(text_states.shape)
    grad_cq_low = grad_cq.reshape(row_count, model_width).astype(jnp.bfloat16)
    grad_cquery = left_dot(normed_two, grad_cq_low)
    grad_cqbias = jnp.sum(to_float(grad_cq_low), axis=0)
    grad_normed_two = right_dot(grad_cq_low, c_query_full)
    grad_self_norm, grad_cgain, grad_cshift = norm_back(
        after_self, to_float(c_gain_full), to_float(c_shift_full), grad_normed_two
    )
    grad_after_self = grad_after_cross + grad_self_norm
    cross_sums = (
        lax.psum_scatter(grad_cgain, ("dp", "seq"), scatter_dimension=0, tiled=True),
        lax.psum_scatter(grad_cshift, ("dp", "seq"), scatter_dimension=0, tiled=True),
        lax.psum_scatter(grad_cquery, ("dp", "seq"), scatter_dimension=0, tiled=True),
        lax.psum_scatter(grad_cqbias, ("dp", "seq"), scatter_dimension=0, tiled=True),
        lax.psum_scatter(grad_ckeyval, ("dp", "seq"), scatter_dimension=0, tiled=True),
        lax.psum_scatter(grad_cvbias, ("dp", "seq"), scatter_dimension=0, tiled=True),
        lax.psum_scatter(grad_coutput, ("dp", "seq"), scatter_dimension=0, tiled=True),
        lax.psum_scatter(grad_cobias, ("dp", "seq"), scatter_dimension=0, tiled=True),
    )
    (
        a_gain_full,
        a_shift_full,
        attention_input_weight_whole,
        a_qbias_full,
        a_vbias_full,
        a_output_full,
        a_obias_full,
    ) = (
        lax.all_gather(attn_gain, ("dp", "seq"), axis=0, tiled=True),
        lax.all_gather(attn_shift, ("dp", "seq"), axis=0, tiled=True),
        lax.all_gather(attn_inputs, ("dp", "seq"), axis=0, tiled=True),
        lax.all_gather(attn_qbias, ("dp", "seq"), axis=0, tiled=True),
        lax.all_gather(attn_vbias, ("dp", "seq"), axis=0, tiled=True),
        lax.all_gather(attn_output, ("dp", "seq"), axis=0, tiled=True),
        lax.all_gather(attn_obias, ("dp", "seq"), axis=0, tiled=True),
    )
    grad_self_branch = grad_after_self.astype(jnp.bfloat16)
    grad_aoutput = left_dot(self_flat, grad_self_branch)
    grad_aobias = jnp.sum(to_float(grad_self_branch), axis=0)
    grad_self_mixed = right_dot(grad_self_branch, a_output_full).astype(jnp.bfloat16)
    grad_self_mixed = grad_self_mixed.reshape(seq_count, local_len, model_width)

    def self_backward(packed):
        seq_queries, seq_keyval, sequence_log_sum_exp, seq_upstream = packed
        return attend_back(
            seq_queries,
            seq_keyval[:, :model_width],
            seq_keyval[:, model_width:],
            causal,
            sequence_log_sum_exp,
            seq_upstream,
        )

    gradient_self_query, grad_sk, grad_sv = lax.map(
        self_backward, (self_queries, self_keyval, self_logsum, grad_self_mixed)
    )
    gradient_self_keyvalue = lax.psum_scatter(
        jnp.concatenate([grad_sk, grad_sv], axis=-1).astype(jnp.bfloat16),
        "seq",
        scatter_dimension=1,
        tiled=True,
    ).astype(jnp.float32)
    grad_joined = (
        jnp.concatenate([gradient_self_query, gradient_self_keyvalue], axis=-1)
        .reshape(row_count, 3 * model_width)
        .astype(jnp.bfloat16)
    )
    grad_ainputs = left_dot(normed_one, grad_joined)
    grad_aqbias = jnp.sum(to_float(grad_joined[:, :model_width]), axis=0)
    grad_avbias = jnp.sum(to_float(grad_joined[:, 2 * model_width :]), axis=0)
    grad_normed_one = right_dot(grad_joined, attention_input_weight_whole)
    grad_input_norm, grad_again, grad_ashift = norm_back(
        inputs, to_float(a_gain_full), to_float(a_shift_full), grad_normed_one
    )
    tokens_grad = (
        (grad_after_self + grad_input_norm)
        .astype(jnp.bfloat16)
        .reshape(seq_count, local_len, model_width)
    )
    attn_sums = (
        lax.psum_scatter(grad_again, ("dp", "seq"), scatter_dimension=0, tiled=True),
        lax.psum_scatter(grad_ashift, ("dp", "seq"), scatter_dimension=0, tiled=True),
        lax.psum_scatter(grad_ainputs, ("dp", "seq"), scatter_dimension=0, tiled=True),
        lax.psum_scatter(grad_aqbias, ("dp", "seq"), scatter_dimension=0, tiled=True),
        lax.psum_scatter(grad_avbias, ("dp", "seq"), scatter_dimension=0, tiled=True),
        lax.psum_scatter(grad_aoutput, ("dp", "seq"), scatter_dimension=0, tiled=True),
        lax.psum_scatter(grad_aobias, ("dp", "seq"), scatter_dimension=0, tiled=True),
    )
    return (layer_out, tokens_grad, text_grad, *attn_sums, *cross_sums, *ffn_sums)


MESH_ID = pl.DeviceIdType.MESH
ANYWHERE = pl.BlockSpec(memory_space=pl.ANY)
VMEM_LIMIT = 56 * 2**20


class Place:
    def __init__(self, depth):
        group = lax.axis_index("dp")
        self.depth = depth
        self.z = group // 4
        self.x = lax.rem(group // 2, 2)
        self.core = lax.rem(group, 2)
        self.y = lax.axis_index("seq")

    def device(self, z, x, core, y):
        return {"dp": (z * 2 + x) * 2 + core, "seq": y}

    def along_z(self, step):
        return self.device(lax.rem(self.z + step, self.depth), self.x, self.core, self.y)

    def across_x(self):
        return self.device(self.z, 1 - self.x, self.core, self.y)

    def across_y(self):
        return self.device(self.z, self.x, self.core, 1 - self.y)

    def sibling(self):
        return self.device(self.z, self.x, 1 - self.core, self.y)

    def along(self, axis):
        if axis == "z":
            return [self.along_z(step) for step in range(1, self.depth)]
        return [self.across_x() if axis == "x" else self.across_y()]

    def greet(self):
        partners = [self.along_z(step) for step in range(1, self.depth)]
        partners += [self.across_x(), self.across_y(), self.sibling()]
        barrier = pltpu.get_barrier_semaphore()
        for partner in partners:
            pl.semaphore_signal(barrier, inc=1, device_id=partner, device_id_type=MESH_ID)
        pl.semaphore_wait(barrier, len(partners))


def remote(source, target, sems, item, index, device):
    send, receive = sems
    return pltpu.make_async_remote_copy(
        src_ref=source,
        dst_ref=target,
        send_sem=send.at[item, index],
        recv_sem=receive.at[item, index],
        device_id=device,
        device_id_type=MESH_ID,
    )


def pipelined(phase_lists, stride):
    stages = []
    for first, phases in enumerate(phase_lists):
        for p, phase in enumerate(phases):
            turn = first + stride * p
            while len(stages) <= turn:
                stages.append([])
            stages[turn].append(phase)
    return stages


ORDERS = (("z", "x", "y"), ("y", "z", "x"))


def gather_phases(place, shard, whole, rows, cols, sems, local, stop, item):
    half = rows.size // 2
    halves = (pl.ds(rows.start, half), pl.ds(rows.start + half, half))
    here = {"z": place.z, "x": place.x, "y": place.y}
    every = slice(None)

    def view(done, some_rows, core):
        at = {axis: every if axis in done else here[axis] for axis in here}
        return whole.at[at["z"], at["x"], core, at["y"], some_rows, cols]

    def copies(phase):
        made = []
        if phase == 3:
            both = view("zxy", rows, place.core)
            return [remote(both, both, sems, item, 2 * place.depth + 2, place.sibling())]
        slot = sum(len(place.along(o[p])) for o in ORDERS for p in range(phase))
        for some_rows, order in zip(halves, ORDERS):
            target = view(order[:phase], some_rows, place.core)
            source = shard.at[some_rows, cols] if phase == 0 else target
            for device in place.along(order[phase]):
                made.append(remote(source, target, sems, item, slot, device))
                slot += 1
        return made

    def take():
        return pltpu.make_async_copy(shard.at[rows, cols], stop, local.at[item, 0])

    def put():
        return pltpu.make_async_copy(stop, view("", rows, place.core), local.at[item, 1])

    def start(phase):
        for copy in copies(phase):
            copy.start()

    def wait(phase):
        for copy in copies(phase):
            copy.wait()

    def opening():
        start(0)
        take().start()
        take().wait()
        put().start()

    def turn(phase):
        def run():
            wait(phase - 1)
            if phase == 1:
                put().wait()
            start(phase)

        return run

    return [opening, turn(1), turn(2), turn(3), lambda: wait(3)]


def copy_sems(items, depth):
    width = 2 * depth + 3
    return [
        pltpu.SemaphoreType.DMA((items, width)),
        pltpu.SemaphoreType.DMA((items, width)),
        pltpu.SemaphoreType.DMA((items, 2)),
    ]


ITEM = 512


def weight_items(shape):
    rows, cols = shape
    return [
        (pl.ds(r, 32), pl.ds(c, min(ITEM, cols)))
        for r in range(0, rows, 32)
        for c in range(0, cols, min(ITEM, cols))
    ]


def nt(a, b):
    return lax.dot_general(a, b, (((1,), (1,)), ((), ())), preferred_element_type=jnp.float32)


def nn(a, b):
    return jnp.dot(a, b, preferred_element_type=jnp.float32)


def half_mask(rows):
    return lax.broadcasted_iota(jnp.int32, (rows, 128), 1) < 64


def pick(block, head, first):
    zero = jnp.zeros_like(block)
    return jnp.where(first, block, zero) if head == 0 else jnp.where(first, zero, block)


MOST_KEYS = 256


def segments(causal, qb, keys, size, most):
    if not causal:
        return [(0, keys, False)]
    first = qb * size
    before = [(lo, min(lo + most, first), False) for lo in range(0, first, most)]
    return before + [(first, first + size, True)]


def both(block, first):
    return jnp.concatenate([pick(block, 0, first), pick(block, 1, first)], axis=0)


def diagonal_mask(scored, size):
    r = lax.broadcasted_iota(jnp.int32, scored.shape, 0)
    c = lax.broadcasted_iota(jnp.int32, scored.shape, 1)
    return jnp.where(r <= lax.rem(c, size), scored, MASKED)


def attend_pair(causal, rows, keys, size, get_q, get_k, get_v, bias, put, lse_ref):
    vt = get_v(0, keys).T
    first = half_mask(size)
    for qb in range(rows // size):
        sl = slice(qb * size, (qb + 1) * size)
        qs = both(get_q(sl.start, sl.stop) * jnp.bfloat16(0.125), first)
        parts = []
        for lo, hi, diagonal in segments(causal, qb, keys, size, MOST_KEYS):
            s = nt(get_k(lo, hi), qs)
            if diagonal:
                s = diagonal_mask(s, size)
            if bias is not None:
                s = s + jnp.concatenate([bias] * (2 * size // 128), axis=1)
            parts.append((lo, hi, s))
        m = functools.reduce(jnp.maximum, [jnp.max(s, axis=0, keepdims=True) for _, _, s in parts])
        total, out = None, None
        for lo, hi, s in parts:
            p = jnp.exp(s - m)
            l = jnp.sum(p, axis=0, keepdims=True)
            o = nn(vt[:, lo:hi], p.astype(jnp.bfloat16))
            total = l if total is None else total + l
            out = o if out is None else out + o
        lse = m + jnp.log(total)
        lse_ref[0:1, sl] = lse[:, :size]
        lse_ref[1:2, sl] = lse[:, size:]
        out = out * (1.0 / total)
        out = jnp.concatenate([out[:64, :size], out[64:, size:]], axis=0).T
        put(sl, out.astype(jnp.bfloat16))


def attend_back_pair(
    causal, rows, keys, size, get_q, get_k, get_v, get_o, get_do, lse_ref, bias, put_dq, put_dk,
    put_dv, dk_acc, dv_acc,
):
    kt = (get_k(0, keys) * jnp.bfloat16(0.125)).T
    first = half_mask(size)
    order = list(range(rows // size))
    if causal:
        order = order[::-1]
    for qb in order:
        sl = slice(qb * size, (qb + 1) * size)
        qs = both(get_q(sl.start, sl.stop) * jnp.bfloat16(0.125), first)
        do = get_do(sl.start, sl.stop)
        dos = both(do, first)
        dt = (do.astype(jnp.float32) * get_o(sl.start, sl.stop).astype(jnp.float32)).T
        delta = jnp.concatenate(
            [
                jnp.sum(dt[:64], axis=0, keepdims=True),
                jnp.sum(dt[64:], axis=0, keepdims=True),
            ],
            axis=1,
        )
        lse = jnp.concatenate([lse_ref[0:1, sl], lse_ref[1:2, sl]], axis=1)
        dq = None
        for lo, hi, diagonal in segments(causal, qb, keys, size, MOST_KEYS):
            s = nt(get_k(lo, hi), qs)
            if diagonal:
                s = diagonal_mask(s, size)
            if bias is not None:
                s = s + jnp.concatenate([bias] * (2 * size // 128), axis=1)
            dp = nt(get_v(lo, hi), dos)
            p = jnp.exp(s - lse)
            ds = (p * (dp - delta)).astype(jnp.bfloat16)
            dv = nn(p.astype(jnp.bfloat16), dos)
            dk = nn(ds, qs)
            part = nn(kt[:, lo:hi], ds)
            dq = part if dq is None else dq + part
            if qb == order[0]:
                dv_acc[lo:hi, :] = dv
                dk_acc[lo:hi, :] = dk
            else:
                dv_acc[lo:hi, :] += dv
                dk_acc[lo:hi, :] += dk
        dq = jnp.concatenate([dq[:64, :size], dq[64:, size:]], axis=0).T
        put_dq(sl, dq.astype(jnp.bfloat16))
    put_dk(dk_acc[0:keys, :].astype(jnp.bfloat16))
    put_dv(dv_acc[0:keys, :].astype(jnp.bfloat16))


BLOCK = 256
MATMUL_ROWS = 512
RING = 6

VECTOR_COUNT = 15
(
    A_GAIN, A_SHIFT, A_QBIAS, A_VBIAS, A_OBIAS, C_GAIN, C_SHIFT, C_QBIAS, C_VBIAS, C_OBIAS,
    F_GAIN, F_SHIFT, F_DOWNBIAS, Z_GAIN, Z_SHIFT,
) = range(VECTOR_COUNT)
F_UPBIAS = VECTOR_COUNT
UP_INDEX, DOWN_INDEX = 6, 7
STRIDE = 3
SWAP_PIECES = 16
SELF_QUERIES, CROSS_QUERIES = 512, 1024


def block_rows(index, size):
    return pl.ds(pl.multiple_of(index * size, size), size)


def lanes(index, size):
    return pl.ds(pl.multiple_of(index * size, size), size)


def center_and_scale(values):
    center = values - jnp.mean(values, axis=-1, keepdims=True)
    spread = jnp.mean(center * center, axis=-1, keepdims=True)
    scale = lax.rsqrt(spread + EPSILON)
    return center * scale, scale


def norm_pull(unit, scale, pulled):
    inner = jnp.mean(pulled * unit, axis=-1, keepdims=True)
    return scale * (pulled - jnp.mean(pulled, axis=-1, keepdims=True) - unit * inner)


def gelu_and_slope(values):
    root = math.sqrt(2.0 / math.pi)
    square = values * values
    bend = jnp.tanh(root * (values + 0.044715 * (values * square)))
    rise = root * (1.0 + 3.0 * 0.044715 * square)
    result = 0.5 * values * (1.0 + bend)
    slope = 0.5 * (1.0 + bend) + 0.5 * values * ((1.0 - bend * bend) * rise)
    return result, slope


def spread_vectors(packed):
    rows = packed.shape[0]
    width = rows
    lane = lax.broadcasted_iota(jnp.int32, (128, width), 1)
    source = lax.broadcasted_iota(jnp.int32, (128, width), 0)
    select = jnp.where(lax.rem(lane, 32) == source, 1.0, 0.0).astype(jnp.bfloat16)
    wide = jnp.dot(packed, select, preferred_element_type=jnp.float32)
    row = lax.broadcasted_iota(jnp.int32, (rows, width), 0)
    lane = lax.broadcasted_iota(jnp.int32, (rows, width), 1)
    wide = jnp.where(row // 32 == lane // 32, wide, 0.0)
    return jnp.sum(wide.reshape(rows // 32, 32, width), axis=0)


def quarter_columns(values, width, back=False):
    share = 32
    per = 128 // share
    shards = width // share
    lane = lax.broadcasted_iota(jnp.int32, (values.shape[0], 128), 1) // share
    blocks = [values[:, k * 128 : (k + 1) * 128] for k in range(4 * shards * share // 128)]
    result = []
    for k in range(len(blocks)):
        total = None
        for j in range(per):
            if back:
                source, held = blocks[j * (shards // per) + k // per], k % per
            else:
                source, held = blocks[per * (k % (shards // per)) + j], k // (shards // per)
            moved = source if held == j else pltpu.roll(source, (j - held) * share % 128, 1)
            total = moved if total is None else jnp.where(lane == j, moved, total)
        result.append(total)
    return jnp.concatenate(result, axis=1)


def arrange_columns(target, source, sem, width):
    copy = pltpu.make_async_copy(source, target, sem)
    copy.start()
    copy.wait()
    values = target[...].astype(jnp.float32)
    target[...] = quarter_columns(values, width).astype(target.dtype)


class Copies:
    def __init__(self, sems):
        self.sems = sems
        self.open = {}
        self.used = 0

    def start(self, source, target):
        copy = pltpu.make_async_copy(source, target, self.sems.at[self.used])
        self.used += 1
        copy.start()
        return copy


def forward_kernel(depth, sizes, *refs):
    refs = list(refs)

    def take(count):
        taken = refs[:count]
        del refs[:count]
        return taken

    shard_count = len(sizes)
    tokens, texts, cots, unit_length, text_length = take(5)
    shards = take(7 + 1)
    wholes = take(shard_count)
    (
        o_tokens, o_text, o_h1, o_qkv, o_o1, o_after_self, o_h2, o_cq, o_ckv, o_o2,
        o_after_cross, o_h3, o_active, o_slope, o_gaf, o_gbr, o_layer,
    ) = take(17)
    vec, lse1, lse2, zgrads = take(4)
    tok, txt, cot, x, o1, cq, ckv, o2, resid, h2, ring, slopes, packed = take(13)
    stops = take(sum(len(weight_items(s)) for s in sizes))
    send, receive, local, sw_send, sw_receive, sw_local, loads, outs = take(8)
    (up_stop, up_sem) = take(2)

    place = Place(depth)
    y = place.y
    rows = resid.shape[0]
    width = resid.shape[1]
    part = rows // 2
    copies = Copies(outs)
    sources = list(shards[:DOWN_INDEX])
    sources[UP_INDEX] = up_stop
    share = sizes[0][0]
    sources += [shards[DOWN_INDEX].at[pl.ds(q * share, share)] for q in range(4)]
    phases, chunks, item = [], [], 0
    for index, size in enumerate(sizes):
        for r, c in weight_items(size):
            phases.append(
                gather_phases(
                    place, sources[index], wholes[index], r, c, (send, receive), local,
                    stops[item], item,
                )
            )
            if index > 0 and c.start % width == 0:
                chunks.append((wholes[index], pl.ds(c.start, width)))
            item += 1
    stages = pipelined(phases[1:], STRIDE)
    for k, phase in enumerate(phases[0]):
        stages[STRIDE * k].append(phase)

    def swapping(k, source, target, count, first):
        size = source.shape[1] // count

        def away(i):
            piece = pl.ds(i * size, size)
            return remote(
                source.at[1 - y, piece], target.at[y, piece], (sw_send, sw_receive), k, i,
                place.across_y(),
            )

        home = pltpu.make_async_copy(source.at[y], target.at[y], sw_local.at[k])
        for i in range(count):
            stages[first + i].append(lambda i=i: away(i).start())
        stages[first].append(home.start)

        def closing():
            home.wait()
            for i in range(count):
                away(i).wait()

        return closing

    token_swap = swapping(0, tokens, tok, 8, 0)
    text_swap = swapping(1, texts, txt, 2, 10)
    cot_swap = swapping(2, cots, cot, SWAP_PIECES, 22)

    def load(chunk):
        whole, cols = chunks[chunk]
        return pltpu.make_async_copy(
            whole.at[:, :, :, :, :, cols], ring.at[chunk % RING], loads.at[chunk]
        )

    ran = []

    def stage(k):
        assert len(ran) == k
        ran.append(k)
        for one in stages[k]:
            one()
        ready = k - 4 * STRIDE
        if ready > 0 and ready % 2 == 1:
            load(ready // 2).start()

    def weight(chunk):
        return ring[chunk % RING].reshape(width, width)

    def row(index):
        return vec[index : index + 1, :]

    def looped(count, body, due=()):
        @pl.loop(0, count)
        def _(j):
            for at, k in due:

                @pl.when(j == at)
                def _(k=k):
                    stage(k)

            body(j)

    place.greet()
    for k in range(4):
        stage(k)
    arrange_columns(up_stop, shards[UP_INDEX], up_sem, width)
    for k in range(4, 14):
        stage(k)
    pack = pltpu.make_async_copy(wholes[0], packed, outs.at[copies.used])
    copies.used += 1
    pack.start()
    pack.wait()
    vec[...] = spread_vectors(packed[...].reshape(-1, 128))
    token_swap()
    done_tokens = copies.start(tok, o_tokens)

    def token_block(b):
        half = b // (part // BLOCK)
        inner = lax.rem(b, part // BLOCK)
        return tok[half, block_rows(inner, BLOCK), :].astype(jnp.float32)

    def norm_one(b):
        unit, _ = center_and_scale(token_block(b))
        at = block_rows(b, BLOCK)
        x[at, 3 * width :] = (unit * row(A_GAIN) + row(A_SHIFT)).astype(jnp.bfloat16)
        resid[at, :] = token_block(b)

    looped(rows // BLOCK, norm_one)
    done_h1 = copies.start(x.at[:, pl.ds(3 * width, width)], o_h1)

    def project(chunk):
        bias = (row(A_QBIAS), None, row(A_VBIAS))[chunk]
        load(chunk).wait()

        def block(b):
            at = block_rows(b, MATMUL_ROWS)
            value = nn(x[at, 3 * width :], weight(chunk))
            if bias is not None:
                value = value + bias
            x[at, chunk * width : (chunk + 1) * width] = value.astype(jnp.bfloat16)

        looped(rows // MATMUL_ROWS, block)

    stage(14)
    project(0)
    stage(15)
    project(1)
    stage(16)
    stage(17)
    project(2)
    done_qkv = copies.start(x.at[:, pl.ds(0, 3 * width)], o_qkv)
    pairs = width // 128

    def self_pair(j):
        def part_of(base):
            return lambda lo, hi: x[lo:hi, lanes(j + base * pairs, 128)]

        def put(sl, value):
            o1[sl, lanes(j, 128)] = value

        attend_pair(
            True, rows, rows, min(SELF_QUERIES, rows), part_of(0), part_of(1), part_of(2), None, put, lse1.at[j]
        )

    looped(pairs, self_pair, ((1, 18), (2, 19), (4, 20), (5, 21), (7, 22)))
    done_o1 = copies.start(o1, o_o1)
    load(3).wait()

    def out_block(b):
        at = block_rows(b, MATMUL_ROWS)
        resid[at, :] = resid[at, :] + nn(o1[at, :], weight(3)) + row(A_OBIAS)

    looped(rows // MATMUL_ROWS, out_block)
    stage(23)
    done_after_self = copies.start(resid, o_after_self)

    def norm_two(b):
        at = block_rows(b, BLOCK)
        unit, _ = center_and_scale(resid[at, :])
        h2[at, :] = (unit * row(C_GAIN) + row(C_SHIFT)).astype(jnp.bfloat16)

    looped(rows // BLOCK, norm_two)
    done_h2 = copies.start(h2, o_h2)
    stage(24)
    load(4).wait()

    def cq_block(b):
        at = block_rows(b, MATMUL_ROWS)
        cq[at, :] = (nn(h2[at, :], weight(4)) + row(C_QBIAS)).astype(jnp.bfloat16)

    looped(rows // MATMUL_ROWS, cq_block)
    done_cq = copies.start(cq, o_cq)
    text_swap()
    done_text = copies.start(txt, o_text)
    text = txt[...].reshape(-1, width)
    text_rows = text.shape[0]
    stage(25)
    load(5).wait()
    ckv[:, :width] = nn(text, weight(5)).astype(jnp.bfloat16)
    load(6).wait()
    ckv[:, width:] = (nn(text, weight(6)) + row(C_VBIAS)).astype(jnp.bfloat16)
    done_ckv = copies.start(ckv, o_ckv)
    bias = text_mask(text_rows, text_length[y])

    def cross_pair(j):
        def put(sl, value):
            o2[sl, lanes(j, 128)] = value

        attend_pair(
            False, rows, text_rows, min(CROSS_QUERIES, rows),
            lambda lo, hi: cq[lo:hi, lanes(j, 128)],
            lambda lo, hi: ckv[lo:hi, lanes(j, 128)],
            lambda lo, hi: ckv[lo:hi, lanes(j + pairs, 128)],
            bias, put, lse2.at[j],
        )

    looped(pairs, cross_pair, ((1, 26), (4, 27), (6, 28)))
    done_o2 = copies.start(o2, o_o2)
    load(7).wait()
    done_after_self.wait()

    def cross_out_block(b):
        at = block_rows(b, MATMUL_ROWS)
        resid[at, :] = resid[at, :] + nn(o2[at, :], weight(7)) + row(C_OBIAS)

    looped(rows // MATMUL_ROWS, cross_out_block)
    stage(29)
    done_after_cross = copies.start(resid, o_after_cross)
    done_o1.wait()
    h3 = o1

    def norm_three(b):
        at = block_rows(b, BLOCK)
        unit, _ = center_and_scale(resid[at, :])
        h3[at, :] = (unit * row(F_GAIN) + row(F_SHIFT)).astype(jnp.bfloat16)

    looped(rows // BLOCK, norm_three)
    done_h3 = copies.start(h3, o_h3)
    done_h1.wait()
    done_qkv.wait()
    waiting = []

    def up(q):
        load(8 + q).wait()
        slope_at = slopes.at[q % 2]

        def block(b):
            at = block_rows(b, BLOCK)
            inner = nn(h3[at, :], weight(8 + q)) + row(F_UPBIAS + q)
            active, slope = gelu_and_slope(inner)
            x[at, q * width : (q + 1) * width] = active.astype(jnp.bfloat16)
            slope_at[at, :] = slope.astype(jnp.bfloat16)

        if q >= 2:
            waiting[q - 2].wait()
        looped(rows // BLOCK, block)
        span = pl.ds(q * width, width)
        waiting.append(copies.start(slope_at, o_slope.at[:, span]))

    stage(30)
    stage(31)
    up(0)
    stage(32)
    stage(33)
    up(1)
    stage(34)
    up(2)
    stage(35)
    stage(36)
    up(3)
    stage(37)
    done_active = copies.start(x, o_active)
    done_after_cross.wait()

    def down(q):
        load(12 + q).wait()

        def block(b):
            at = block_rows(b, MATMUL_ROWS)
            resid[at, :] += nn(x[at, q * width : (q + 1) * width], weight(12 + q))

        looped(rows // MATMUL_ROWS, block)

    for q in range(4):
        down(q)
        if q < 3:
            stage(38 + 2 * q)
            stage(39 + 2 * q)
    cot_swap()
    done_cq.wait()
    done_o2.wait()
    valid_count = unit_length[y]
    zgrads[...] = jnp.zeros_like(zgrads)
    gbr, layer = cq, o2

    def last_block(b):
        at = block_rows(b, BLOCK)
        unit, scale = center_and_scale(resid[at, :] + row(F_DOWNBIAS))
        position = b * BLOCK + lax.broadcasted_iota(jnp.int32, (BLOCK, 1), 0)
        valid = jnp.where(position < valid_count, 1.0, 0.0)
        layer[at, :] = ((unit * row(Z_GAIN) + row(Z_SHIFT)) * valid).astype(jnp.bfloat16)
        half = b // (part // BLOCK)
        inner = lax.rem(b, part // BLOCK)
        upstream = cot[half, block_rows(inner, BLOCK), :].astype(jnp.float32) * valid
        zgrads[0:1, :] += jnp.sum(upstream * unit, axis=0, keepdims=True)
        zgrads[1:2, :] += jnp.sum(upstream, axis=0, keepdims=True)
        grad = norm_pull(unit, scale, upstream * row(Z_GAIN))
        low = grad.astype(jnp.bfloat16)
        gbr[at, :] = low
        zgrads[2:3, :] += jnp.sum(low.astype(jnp.float32), axis=0, keepdims=True)
        resid[at, :] = grad

    ending = []
    for b in range(rows // BLOCK):
        last_block(b)
        at = pl.ds(b * BLOCK, BLOCK)
        ending += [
            copies.start(source.at[at, :], target.at[at, :])
            for source, target in ((resid, o_gaf), (gbr, o_gbr), (layer, o_layer))
        ]
    ending += [done_tokens, done_h2, done_text, done_ckv, done_h3, done_active]
    for copy in ending + waiting[2:]:
        copy.wait()


def text_mask(text_rows, count):
    position = lax.broadcasted_iota(jnp.int32, (text_rows, 128), 0)
    return jnp.where(position < count, 0.0, MASKED)


def forward(depth, number, tokens, texts, cots, unit_length, text_length, shards):
    rows, width = 2 * tokens.shape[1], tokens.shape[2]
    text_rows = 2 * texts.shape[1]
    hidden = 4 * width
    pairs = width // 128
    share = shards[0].shape[0]
    sizes = [s.shape for s in shards[:DOWN_INDEX]] + [(share, width)] * 4
    items = sum(len(weight_items(s)) for s in sizes)
    low, full = jnp.bfloat16, jnp.float32

    def shape(*dims, kind=low):
        return jax.ShapeDtypeStruct(dims, kind)

    def vmem(*dims, kind=low):
        return pltpu.VMEM(dims, kind)

    big = shape(rows, width)
    exact = shape(rows, width, kind=full)
    outs = [shape(depth, 2, 2, 2, *s) for s in sizes]
    outs += [
        shape(*tokens.shape), shape(*texts.shape), big, shape(rows, 3 * width), big, exact, big, big,
        shape(text_rows, 2 * width), big, exact, big, shape(rows, hidden), shape(rows, hidden),
        exact, big, big,
    ]
    small = [
        shape(32, width, kind=full), shape(pairs, 2, rows, kind=full),
        shape(pairs, 2, rows, kind=full), shape(8, width, kind=full),
    ]
    scratch = [
        vmem(*tokens.shape), vmem(*texts.shape), vmem(*cots.shape), vmem(rows, hidden),
        vmem(rows, width), vmem(rows, width), vmem(text_rows, 2 * width), vmem(rows, width),
        vmem(rows, width, kind=full), vmem(rows, width), vmem(RING, depth, 2, 2, 2, 32, width),
        vmem(2, rows, width), vmem(depth, 2, 2, 2, *sizes[0]),
    ]
    scratch += [vmem(r.size, c.size) for s in sizes for r, c in weight_items(s)]
    scratch += copy_sems(items, depth)
    scratch += [
        pltpu.SemaphoreType.DMA((3, SWAP_PIECES)), pltpu.SemaphoreType.DMA((3, SWAP_PIECES)),
        pltpu.SemaphoreType.DMA((3,)), pltpu.SemaphoreType.DMA((items,)),
        pltpu.SemaphoreType.DMA((48,)), vmem(*sizes[UP_INDEX]), pltpu.SemaphoreType.DMA,
    ]
    memory = pl.BlockSpec(memory_space=pltpu.SMEM)
    results = pl.pallas_call(
        functools.partial(forward_kernel, depth, sizes),
        out_shape=outs + small,
        in_specs=[ANYWHERE] * 3 + [memory] * 2 + [ANYWHERE] * len(shards),
        out_specs=[ANYWHERE] * len(outs) + [pl.BlockSpec(memory_space=pltpu.VMEM)] * len(small),
        scratch_shapes=scratch,
        compiler_params=pltpu.CompilerParams(
            collective_id=number, has_side_effects=True, vmem_limit_bytes=VMEM_LIMIT
        ),
        name="forward",
    )(tokens, texts, cots, unit_length, text_length, *shards)
    return list(results[: len(sizes)]), list(results[len(sizes) :])


BACK_STRIDE = 3
BACK_RING = 2 * BACK_STRIDE + 2
BACK_QUERIES = 256
WEIGHT_RING = 2
NORM_BLOCK = 128


def ring_scratch(depth, stride, rows, cols, dtype):
    half = rows // 2
    slots = max(1, 3 * stride)
    return [
        pltpu.VMEM((max(1, 2 * stride + 2 * (stride > 0)), depth, 2, 2, 2, rows, cols), dtype),
        pltpu.VMEM((max(1, 2 * stride), depth, 2, 2, rows, cols), dtype),
        pltpu.VMEM((slots, depth, 2, half, cols), dtype),
        pltpu.VMEM((slots, depth, half, cols), dtype),
        pltpu.VMEM((slots, depth - 1, half, cols), dtype),
        pltpu.VMEM((slots, depth, 2, half, cols), dtype),
        pltpu.VMEM((slots, depth - 1, 2, half, cols), dtype),
        pltpu.VMEM((slots, half, cols), dtype),
    ]


def piece_phases(place, put_result, bufs, sems, item):
    depth = bufs[0].shape[1]
    piece, came, a_y, a_x, a_z, b_x, b_z, b_y = (buf.at[item % buf.shape[0]] for buf in bufs)
    half = bufs[7].shape[1]
    low, high = pl.ds(0, half), pl.ds(half, half)
    z, x, core, y = place.z, place.x, place.core, place.y
    every = slice(None)

    def send(a, b, index, device):
        return remote(a, b, sems, item, index, device)

    def copies(phase):
        if phase == 0:
            return [send(piece.at[every, every, 1 - core], came, 0, place.sibling())]
        if phase == 1:
            return [
                send(piece.at[every, every, core, 1 - y, low], a_y, 1, place.across_y()),
                send(piece.at[every, 1 - x, core, every, high], b_x, 2, place.across_x()),
            ]
        if phase == 2:
            return [send(a_y.at[every, 1 - x], a_x, 3, place.across_x())] + [
                send(
                    b_x.at[lax.rem(z + step, depth)], b_z.at[step - 1], 3 + step,
                    place.along_z(step),
                )
                for step in range(1, depth)
            ]
        return [send(b_z.at[0, 1 - y], b_y, 3 + depth, place.across_y())] + [
            send(
                a_x.at[lax.rem(z + step, depth)], a_z.at[step - 1], 3 + depth + step,
                place.along_z(step),
            )
            for step in range(1, depth)
        ]

    def start(phase):
        for copy in copies(phase):
            copy.start()

    def wait(phase):
        for copy in copies(phase):
            copy.wait()

    def wide(values):
        return values.astype(jnp.float32)

    def after_core():
        wait(0)

        @pl.loop(0, depth)
        def _(k):
            for i in range(2):
                for j in range(2):
                    piece[k, i, core, j] = piece[k, i, core, j] + came[k, i, j]

        start(1)

    def after_one():
        wait(1)

        @pl.loop(0, depth)
        def _(k):
            for i in range(2):
                a_y[k, i] = a_y[k, i] + piece[k, i, core, y, low]
                b_x[k, i] = b_x[k, i] + piece[k, x, core, i, high]

        start(2)

    def after_two():
        wait(2)

        @pl.loop(0, depth)
        def _(k):
            a_x[k] = a_x[k] + a_y[k, x]

        for i in range(2):
            total = wide(b_x[z, i])
            for step in range(1, depth):
                total = total + wide(b_z[step - 1, i])
            b_z[0, i] = total.astype(b_z.dtype)
        start(3)

    def closing():
        wait(3)
        total = wide(a_x[z])
        for step in range(1, depth):
            total = total + wide(a_z[step - 1])
        put_result(low, total)
        put_result(high, wide(b_z[0, y]) + wide(b_y[...]))

    return [lambda: start(0), after_core, after_one, after_two, closing]


def gather_vectors(vectors, first, shards):
    width = vectors.shape[1]
    row = first + lax.broadcasted_iota(jnp.int32, (shards, 32, width), 0)
    lane = lax.broadcasted_iota(jnp.int32, (shards, 32, width), 2)
    parts = jnp.where(row == lane // 32, vectors[None], 0.0).reshape(shards * 32, width)
    source = lax.broadcasted_iota(jnp.int32, (width, 128), 0)
    lane = lax.broadcasted_iota(jnp.int32, (width, 128), 1)
    select = jnp.where(lax.rem(source, 32) == lane, 1.0, 0.0).astype(jnp.bfloat16)
    total = None
    for _ in range(3):
        some = parts.astype(jnp.bfloat16)
        parts = parts - some.astype(jnp.float32)
        value = nn(some, select)
        total = value if total is None else total + value
    return total


def backward_kernel(depth, *refs):
    refs = list(refs)

    def take(count):
        taken = refs[:count]
        del refs[:count]
        return taken

    w_in, w_out, w_cq, w_ckv, w_co, w_up = take(6)
    w_downs = take(4)
    (
        i_tokens, i_text, i_h1, i_qkv, i_o1, i_after_self, i_h2, i_cq, i_ckv, i_o2, i_after_cross,
        i_h3, i_active, i_slope, i_gaf, i_gbr, i_layer,
    ) = take(17)
    vec, lse1, lse2, zgrads, text_length = take(5)
    o_layer, o_tokens, o_text = take(3)
    s_in, s_out, s_cq, s_ckv, s_co, s_up, s_down, s_small = take(8)
    p, q_buf, resid, dh, low, h3, extra, ckv, dckv, text, tgrad, src, vg, ka, va = take(15)
    ring = take(1)[0]
    bufs = take(8)
    small_bufs = take(8)
    sems = take(2)
    small_sems = take(2)
    swap_send, swap_receive, swap_local, loads, fetches = take(5)

    place = Place(depth)
    y = place.y
    rows, width = resid.shape
    part_rows = rows // 2
    pairs = width // 128
    shards = depth * 8
    text_rows = ckv.shape[0]
    fetched = Copies(fetches)
    fetch = fetched.start

    half_width = width // 2
    targets = [(s_down, q, h) for q in range(4) for h in (0, 1)]
    targets += [(s_co, 0, h) for h in (0, 1)]
    targets += [(s_up, 0, h) for h in range(8)]
    targets += [(s_cq, 0, h) for h in (0, 1)]
    targets += [(s_ckv, 0, h) for h in range(4)]
    targets += [(s_out, 0, h) for h in (0, 1)]
    targets += [(s_in, 0, 2 * c + h) for h in (0, 1) for c in range(3)]
    share = width // shards

    def keeping(target, quarter, column):
        def put(some_rows, value):
            at = pl.ds(quarter * share + some_rows.start, some_rows.size)
            target[at, column * half_width : (column + 1) * half_width] = value

        return put

    phases = [
        piece_phases(place, keeping(*target), bufs, sems, item)
        for item, target in enumerate(targets)
    ]

    def put_small(some_rows, value):
        s_small[some_rows, :] = value

    small_phases = piece_phases(place, put_small, small_bufs, small_sems, 0)
    stages = pipelined(phases + [[lambda: None] + small_phases[1:]], BACK_STRIDE)
    ran = []

    def stage(k):
        assert len(ran) == k
        ran.append(k)
        for one in stages[k]:
            one()

    def make(item, get_left, *rights):
        @pl.loop(0, 2)
        def _(b):
            left = get_left(lanes(b, half_width))
            slot = item
            for get in rights:
                value = left_dot(left, get()).astype(jnp.bfloat16)
                for k in range(value.shape[1] // half_width):
                    some = value[:, k * half_width : (k + 1) * half_width]
                    piece = bufs[0].at[slot % BACK_RING]
                    piece[pl.ds(b * (depth // 2), depth // 2)] = some.reshape(
                        depth // 2, 2, 2, 2, share, half_width
                    )
                    slot += 1

    def produce(item, get_left, *rights):
        make(item, get_left, *rights)
        stage(item)

    def part(buf, k):
        return lambda: buf[:, k * half_width : (k + 1) * half_width]

    def halves(buf, k):
        return (lambda: buf[:, k * width : (k + 1) * width],)

    order = []
    for k in range(4):
        order += [(w_downs[k], 0), (w_up, k)]
    order += [(w_co, 0), (w_ckv, 0), (w_ckv, 1), (w_cq, 0), (w_out, 0)]
    order += [(w_in, c) for c in range(3)]

    def load(n):
        whole, column = order[n]
        return pltpu.make_async_copy(
            whole.at[:, :, :, :, :, pl.ds(column * width, width)],
            ring.at[n % WEIGHT_RING],
            loads.at[n],
        )

    def weight(n):
        return ring[n % WEIGHT_RING].reshape(width, width)

    def ready(n):
        load(n).wait()

    def finished(n):
        if n + WEIGHT_RING < len(order):
            load(n + WEIGHT_RING).start()

    def row(index):
        return vec[index : index + 1, :]

    def add_row(index, value):
        vg[index : index + 1, :] += jnp.sum(value, axis=0, keepdims=True)

    def looped(count, body):
        @pl.loop(0, count)
        def _(j):
            body(j)

    def by_blocks(body, size=MATMUL_ROWS):
        looped(rows // size, lambda b: body(block_rows(b, size)))

    def column(buf, k):
        return lambda some_lanes: buf[:, pl.ds(k * width + some_lanes.start, some_lanes.size)]

    def plain(buf):
        return lambda some_lanes: buf[:, some_lanes]

    def norm_step(source, gain, shift, next_bias):
        blocks = rows // NORM_BLOCK

        def bring(b, slot):
            return pltpu.make_async_copy(
                source.at[block_rows(b, NORM_BLOCK), :], src.at[slot], swap_local.at[3 + slot]
            )

        bring(0, 0).start()

        def step(b):
            slot = lax.rem(b, 2)
            bring(b, slot).wait()

            @pl.when(b + 1 < blocks)
            def _():
                bring(b + 1, 1 - slot).start()

            at = block_rows(b, NORM_BLOCK)
            unit, scale = center_and_scale(src[slot])
            pulled = dh[at, :]
            add_row(gain, pulled * unit)
            add_row(shift, pulled)
            total = resid[at, :] + norm_pull(unit, scale, pulled * row(gain))
            resid[at, :] = total
            rounded = total.astype(jnp.bfloat16)
            low[at, :] = rounded
            add_row(next_bias, rounded.astype(jnp.float32))

        looped(blocks, step)

    def swap_out(k, get_source, target, local_source):
        def away():
            return remote(
                get_source(1 - y), target.at[y], (swap_send, swap_receive), k, 0, place.across_y()
            )

        def home():
            return pltpu.make_async_copy(local_source, target.at[y], swap_local.at[k])

        return away, home

    place.greet()
    got_low = fetch(i_gbr, low)
    spans = [pl.ds(k * width, width) for k in range(4)]

    def fetch_active(k):
        return fetch(i_active.at[:, spans[k]], p.at[:, spans[k]])

    def fetch_slope(k):
        return fetch(i_slope.at[:, spans[k]], q_buf.at[:, spans[k]])

    got_active = [fetch_active(0)]
    got_low.wait()
    load(0).start()
    got_slope = [fetch_slope(0)]
    load(1).start()
    keep = extra.at[pl.ds(0, part_rows)]
    got_keep = fetch(i_layer.at[y], keep)
    got_active.append(fetch_active(1))
    got_slope.append(fetch_slope(1))
    vg[...] = jnp.zeros_like(vg)
    vg[Z_GAIN : Z_GAIN + 1, :] = zgrads[0:1, :]
    vg[Z_SHIFT : Z_SHIFT + 1, :] = zgrads[1:2, :]
    vg[F_DOWNBIAS : F_DOWNBIAS + 1, :] = zgrads[2:3, :]
    layer_count = 16
    layer_size = part_rows // layer_count

    def layer_away(i):
        piece = pl.ds(i * layer_size, layer_size)
        return remote(
            i_layer.at[1 - y, piece], o_layer.at[y, piece], (swap_send, swap_receive), 0, i,
            place.across_y(),
        )

    layer_home = pltpu.make_async_copy(keep, o_layer.at[y], swap_local.at[0])
    for i in range(layer_count):
        if i < 6:
            layer_away(i).start()
        else:
            stages[i - 5].append(lambda i=i: layer_away(i).start())

    for k in range(4):
        got_active[k].wait()
        produce(2 * k, column(p, k), *halves(low, 0))
        if k == 0:
            got_active += [fetch_active(2), fetch_active(3)]
            got_slope += [fetch_slope(2), fetch_slope(3)]
            got_resid = fetch(i_gaf, resid)
            got_h3 = fetch(i_h3, h3)
            got_ckv = fetch(i_ckv, ckv)
            got_text = fetch(i_text, text)
        n = 2 * k
        got_slope[k].wait()
        ready(n)
        span = slice(k * width, (k + 1) * width)

        def inner_block(at, n=n, span=span, k=k):
            grad = nt(low[at, :], weight(n)) * q_buf[at, span].astype(jnp.float32)
            rounded = grad.astype(jnp.bfloat16)
            q_buf[at, span] = rounded
            add_row(F_UPBIAS + k, rounded.astype(jnp.float32))

        by_blocks(inner_block)
        finished(n)
        stage(2 * k + 1)
        ready(n + 1)

        def up_block(at, n=n, span=span, k=k):
            value = nt(q_buf[at, span], weight(n + 1))
            dh[at, :] = value if k == 0 else dh[at, :] + value

        by_blocks(up_block)
        finished(n + 1)
    cq_at, o2_at, do2_at, h2_at = (slice(k * width, (k + 1) * width) for k in range(4))
    got_cq = fetch(i_cq, p.at[:, pl.ds(0, width)])
    got_o2 = fetch(i_o2, p.at[:, pl.ds(width, width)])
    got_h2 = fetch(i_h2, p.at[:, pl.ds(3 * width, width)])
    got_resid.wait()
    norm_step(i_after_cross, F_GAIN, F_SHIFT, C_OBIAS)
    got_keep.wait()
    layer_home.start()

    got_o2.wait()
    produce(8, column(p, 1), *halves(low, 0))
    ready(8)

    def do2_block(at):
        p[at, do2_at] = nt(low[at, :], weight(8)).astype(jnp.bfloat16)

    by_blocks(do2_block)
    finished(8)
    stage(9)
    got_cq.wait()
    got_h3.wait()
    got_ckv.wait()
    bias = text_mask(text_rows, text_length[y])
    dcq = extra
    layer_home.wait()

    def pair_lanes(buf, j, base):
        return lambda lo, hi: buf[lo:hi, lanes(j + base * pairs, 128)]

    def cross_pair(j):
        for at, k in ((0, 10), (2, 11), (3, 12), (5, 13), (7, 14)):

            @pl.when(j == at)
            def _(k=k):
                if k % 2 == 0:
                    produce(k, plain(h3), *halves(q_buf, (k - 10) // 2))
                else:
                    stage(k)

        def put_dq(sl, value):
            dcq[sl, lanes(j, 128)] = value
            vg[C_QBIAS : C_QBIAS + 1, lanes(j, 128)] += jnp.sum(
                value.astype(jnp.float32), axis=0, keepdims=True
            )

        def put_dk(value):
            dckv[:, lanes(j, 128)] = value

        def put_dv(value):
            dckv[:, lanes(j + pairs, 128)] = value
            vg[C_VBIAS : C_VBIAS + 1, lanes(j, 128)] = jnp.sum(
                value.astype(jnp.float32), axis=0, keepdims=True
            )

        attend_back_pair(
            False, rows, text_rows, BACK_QUERIES, pair_lanes(p, j, 0), pair_lanes(ckv, j, 0),
            pair_lanes(ckv, j, 1), pair_lanes(p, j, 1), pair_lanes(p, j, 2), lse2.at[j], bias,
            put_dq, put_dk, put_dv, ka, va,
        )

    looped(pairs, cross_pair)
    got_qkv = fetch(i_qkv, p.at[:, pl.ds(0, 3 * width)])
    stage(15)
    ready(9)
    text_value = nt(dckv[:, :width], weight(9))
    finished(9)
    ready(10)
    text_value = text_value + nt(dckv[:, width:], weight(10))
    finished(10)
    tgrad[...] = text_value.astype(jnp.bfloat16).reshape(tgrad.shape)
    text_away, text_home = swap_out(1, lambda k: tgrad.at[k], o_text, tgrad.at[y])
    text_away().start()
    text_home().start()
    produce(16, plain(h3), *halves(q_buf, 3))
    ready(11)

    def dh2_block(at):
        dh[at, :] = nt(dcq[at, :], weight(11))

    by_blocks(dh2_block)
    finished(11)
    stage(17)
    got_o1 = fetch(i_o1, q_buf.at[:, pl.ds(3 * width, width)])
    got_tokens = fetch(i_tokens, h3)
    norm_step(i_after_self, C_GAIN, C_SHIFT, A_OBIAS)
    got_h2.wait()
    produce(18, column(p, 3), *halves(dcq, 0))
    got_h1 = fetch(i_h1, p.at[:, pl.ds(3 * width, width)])

    ready(12)
    do1 = extra

    def do1_block(at):
        do1[at, :] = nt(low[at, :], weight(12)).astype(jnp.bfloat16)

    by_blocks(do1_block)
    finished(12)
    stage(19)
    got_text.wait()

    def text_lanes(some_lanes):
        return text[:, :, some_lanes].reshape(text_rows, some_lanes.size)

    got_qkv.wait()
    got_o1.wait()

    def self_pair(j):
        def put_dq(sl, value):
            q_buf[sl, lanes(j, 128)] = value
            vg[A_QBIAS : A_QBIAS + 1, lanes(j, 128)] += jnp.sum(
                value.astype(jnp.float32), axis=0, keepdims=True
            )

        def put_dk(value):
            q_buf[:, lanes(j + pairs, 128)] = value

        def put_dv(value):
            q_buf[:, lanes(j + 2 * pairs, 128)] = value
            vg[A_VBIAS : A_VBIAS + 1, lanes(j, 128)] = jnp.sum(
                value.astype(jnp.float32), axis=0, keepdims=True
            )

        attend_back_pair(
            True, rows, rows, BACK_QUERIES, pair_lanes(p, j, 0), pair_lanes(p, j, 1), pair_lanes(p, j, 2),
            pair_lanes(q_buf, j, 3), lambda lo, hi: do1[lo:hi, lanes(j, 128)], lse1.at[j], None,
            put_dq, put_dk, put_dv, ka, va,
        )

    half_pairs = pairs // 2

    def first_half(j):
        for k in range(4):

            @pl.when(j == k)
            def _(k=k):
                if k % 2 == 0:
                    produce(20 + k, text_lanes, *halves(dckv, k // 2))
                else:
                    stage(20 + k)

        self_pair(j)

    looped(half_pairs, first_half)
    got_h1.wait()

    def second_half(j):
        @pl.when(j == 0)
        def _():
            produce(24, column(q_buf, 3), *halves(low, 0))

        @pl.when(j == 1)
        def _():
            stage(25)

        @pl.when(j == 2)
        def _():
            produce(26, column(p, 3), part(q_buf, 0), part(q_buf, 2))
            stage(27)

        @pl.when(j == 3)
        def _():
            produce(28, column(p, 3), part(q_buf, 4))

        self_pair(j + half_pairs)

    looped(half_pairs, second_half)

    grads = low

    def rows_of(half, b):
        return pl.ds(pl.multiple_of(half * part_rows + b * BLOCK, BLOCK), BLOCK)

    def dh1_block(half, c, first=None):
        fresh = c == 0 if first is None else first

        def block(b):
            at = block_rows(half, part_rows)
            value = nt(q_buf[at, c * width : (c + 1) * width], weight(13 + c))
            dh[at, :] = value if fresh else dh[at, :] + value

        return block

    def last_block(half):
        def block(b):
            at = rows_of(half, b)
            unit, scale = center_and_scale(h3[at, :].astype(jnp.float32))
            pulled = dh[at, :]
            add_row(A_GAIN, pulled * unit)
            add_row(A_SHIFT, pulled)
            total = resid[at, :] + norm_pull(unit, scale, pulled * row(A_GAIN))
            grads[at, :] = total.astype(jnp.bfloat16)

        return block

    token_pieces = 16
    token_size = part_rows // token_pieces

    def tokens_away(i):
        at = pl.multiple_of((1 - y) * part_rows + i * token_size, token_size)
        return remote(
            grads.at[pl.ds(at, token_size), :],
            o_tokens.at[y, pl.ds(i * token_size, token_size)],
            (swap_send, swap_receive), 2, i, place.across_y(),
        )

    tokens_sent = []

    def send_tokens(some):
        for i in range(len(tokens_sent), min(token_pieces, len(tokens_sent) + some)):
            tokens_away(i).start()
            tokens_sent.append(i)

    tokens_home = pltpu.make_async_copy(
        grads.at[block_rows(y, part_rows), :], o_tokens.at[y], swap_local.at[2]
    )
    count = part_rows // BLOCK
    make(29, column(p, 3), part(q_buf, 1), part(q_buf, 3))
    stage(29)
    got_tokens.wait()
    ready(13)
    dh1_block(1 - y, 0)(0)
    load(15).start()
    ready(14)
    dh1_block(1 - y, 1)(0)
    stage(30)
    ready(15)
    dh1_block(1 - y, 2)(0)
    looped(count, last_block(1 - y))
    send_tokens(3)
    make(31, column(p, 3), part(q_buf, 5))
    stage(31)
    send_tokens(2)
    dh1_block(y, 2, True)(0)
    load(13).start()
    dh1_block(y, 1)(0)
    stage(32)
    send_tokens(3)
    ready(13)
    dh1_block(y, 0, False)(0)
    looped(count, last_block(y))
    tokens_home.start()

    @pl.loop(0, depth)
    def _(k):
        some = gather_vectors(vg[...], k * 8, 8)
        small_bufs[0][0, k] = some.reshape(small_bufs[0].shape[2:])

    small_phases[0]()
    for k in range(33, len(stages)):
        stage(k)
        send_tokens(2)
    values = s_up[...]
    s_up[...] = quarter_columns(values, width, back=True)
    for copy in (
        *[layer_away(i) for i in range(layer_count)], text_away(), text_home(), *[tokens_away(i) for i in range(token_pieces)], tokens_home,
    ):
        copy.wait()


def backward(depth, number, wholes, kept, text_length):
    (
        token_seq, text_seq, normed_one, joined, self_mixed, after_self, normed_two, cross_queries,
        cross_kv, cross_mixed, after_cross, normed_three, active, slope, grad_after_ffn,
        grad_branch, layer_out, vec, lse1, lse2, zgrads,
    ) = kept
    rows, width = self_mixed.shape
    text_rows = cross_kv.shape[0]
    hidden = active.shape[1]
    share = width // (depth * 8)
    half = (2, rows // 2, width)
    low, full = jnp.bfloat16, jnp.float32
    operands = [
        token_seq.reshape(rows, width), text_seq, normed_one, joined, self_mixed, after_self,
        normed_two, cross_queries, cross_kv, cross_mixed, after_cross, normed_three, active, slope,
        grad_after_ffn, grad_branch, layer_out.reshape(half),
    ]

    def vmem(*dims, kind=low):
        return pltpu.VMEM(dims, kind)

    results_low = [jax.ShapeDtypeStruct(s, low) for s in (half, half, text_seq.shape)]
    columns = [w.shape[-1] for w in wholes[:6]]
    sums = [jax.ShapeDtypeStruct((share, c), full) for c in columns]
    sums += [jax.ShapeDtypeStruct((4 * share, width), full), jax.ShapeDtypeStruct((share, 128), full)]
    scratch = [
        vmem(rows, hidden), vmem(rows, hidden), vmem(rows, width, kind=full),
        vmem(rows, width, kind=full), vmem(rows, width), vmem(rows, width), vmem(rows, width),
        vmem(text_rows, 2 * width), vmem(text_rows, 2 * width), vmem(*text_seq.shape),
        vmem(*text_seq.shape), vmem(2, NORM_BLOCK, width, kind=full),
        vmem(32, width, kind=full), vmem(rows, 128, kind=full), vmem(rows, 128, kind=full),
        vmem(WEIGHT_RING, depth, 2, 2, 2, share, width),
    ]
    scratch += ring_scratch(depth, BACK_STRIDE, share, width // 2, low)
    scratch += ring_scratch(depth, 0, share, 128, full)
    pieces = 2 * (sum(c // width for c in columns) + 4)
    scratch += copy_sems(pieces, depth)[:2] + copy_sems(1, depth)[:2]
    scratch += [
        pltpu.SemaphoreType.DMA((3, 16)), pltpu.SemaphoreType.DMA((3, 16)),
        pltpu.SemaphoreType.DMA((5,)), pltpu.SemaphoreType.DMA((16,)),
        pltpu.SemaphoreType.DMA((32,)),
    ]
    in_vmem = pl.BlockSpec(memory_space=pltpu.VMEM)
    results = pl.pallas_call(
        functools.partial(backward_kernel, depth),
        out_shape=results_low + sums,
        in_specs=[ANYWHERE] * (len(wholes) + len(operands))
        + [in_vmem] * 4
        + [pl.BlockSpec(memory_space=pltpu.SMEM)],
        out_specs=[ANYWHERE] * 3 + [in_vmem] * len(sums),
        scratch_shapes=scratch,
        compiler_params=pltpu.CompilerParams(
            collective_id=number, has_side_effects=True, vmem_limit_bytes=BACK_VMEM_LIMIT
        ),
        name="backward",
    )(*wholes, *operands, vec, lse1, lse2, zgrads, text_length)
    return list(results[:3]), list(results[3:])


BACK_VMEM_LIMIT = 63 * 2**20


def pack_vectors(vectors, wide):
    packed = jnp.concatenate([jnp.stack(vectors), wide.reshape(4, -1)])
    return jnp.pad(packed, ((0, 32 - packed.shape[0]), (0, 128 - packed.shape[1])))


def settle_kernel(count, *refs):
    ins, outs, held = refs[:count], refs[count : 2 * count], refs[2 * count : 3 * count]
    arrive, leave = refs[3 * count :]
    coming = [pltpu.make_async_copy(a, b, arrive.at[k]) for k, (a, b) in enumerate(zip(ins, held))]
    going = [pltpu.make_async_copy(a, b, leave.at[k]) for k, (a, b) in enumerate(zip(held, outs))]
    for copy in coming:
        copy.start()
    for come, go in zip(coming, going):
        come.wait()
        go.start()
    for copy in going:
        copy.wait()


def settle(arrays):
    count = len(arrays)
    return pl.pallas_call(
        functools.partial(settle_kernel, count),
        out_shape=[jax.ShapeDtypeStruct(a.shape, a.dtype) for a in arrays],
        in_specs=[ANYWHERE] * count,
        out_specs=[ANYWHERE] * count,
        scratch_shapes=[pltpu.VMEM(a.shape, a.dtype) for a in arrays]
        + [pltpu.SemaphoreType.DMA((count,))] * 2,
        compiler_params=pltpu.CompilerParams(vmem_limit_bytes=VMEM_LIMIT),
        name="settle",
    )(*arrays)


def paired_layer(
    depth,
    tokens,
    text_states,
    unit_length,
    text_length,
    cotangent,
    attn_gain,
    attn_shift,
    attn_inputs,
    attn_qbias,
    attn_vbias,
    attn_output,
    attn_obias,
    cross_gain,
    cross_shift,
    cross_query,
    cross_qbias,
    cross_keyval,
    cross_vbias,
    cross_output,
    cross_obias,
    ffn_gain,
    ffn_shift,
    ffn_up,
    ffn_upbias,
    ffn_down,
    ffn_downbias,
    final_gain,
    final_shift,
):
    share = attn_gain.shape[0]
    packed = pack_vectors(
        [
            attn_gain, attn_shift, attn_qbias, attn_vbias, attn_obias, cross_gain, cross_shift,
            cross_qbias, cross_vbias, cross_obias, ffn_gain, ffn_shift, ffn_downbias, final_gain,
            final_shift,
        ],
        ffn_upbias,
    )
    wholes, kept = forward(
        depth, 0, tokens, text_states, cotangent, unit_length, text_length,
        [
            packed, attn_inputs, attn_output, cross_query, cross_keyval, cross_output, ffn_up,
            ffn_down,
        ],
    )
    (layer_out, tokens_grad, text_grad), sums = backward(depth, 1, wholes[1:], kept, text_length)
    *results, s_small = settle([layer_out, tokens_grad, text_grad, *sums])
    layer_out, tokens_grad, text_grad, s_in, s_out, s_cq, s_ckv, s_co, s_up, s_down = results
    s_upbias = s_small[VECTOR_COUNT : VECTOR_COUNT + 4, :share].reshape(-1)
    v = [s_small[i, :share] for i in range(VECTOR_COUNT)]
    return (
        layer_out, tokens_grad, text_grad, v[A_GAIN], v[A_SHIFT], s_in, v[A_QBIAS], v[A_VBIAS],
        s_out, v[A_OBIAS], v[C_GAIN], v[C_SHIFT], s_cq, v[C_QBIAS], s_ckv, v[C_VBIAS], s_co,
        v[C_OBIAS], v[F_GAIN], v[F_SHIFT], s_up, s_upbias, s_down, v[F_DOWNBIAS], v[Z_GAIN],
        v[Z_SHIFT],
    )


def solution(mesh):
    in_specs = (
        P("dp", "seq", None),
        P("dp", "seq", None),
        P("dp"),
        P("dp"),
        P("dp", "seq", None),
        P(("dp", "seq")),
        P(("dp", "seq")),
        P(("dp", "seq"), None),
        P(("dp", "seq")),
        P(("dp", "seq")),
        P(("dp", "seq"), None),
        P(("dp", "seq")),
        P(("dp", "seq")),
        P(("dp", "seq")),
        P(("dp", "seq"), None),
        P(("dp", "seq")),
        P(("dp", "seq"), None),
        P(("dp", "seq")),
        P(("dp", "seq"), None),
        P(("dp", "seq")),
        P(("dp", "seq")),
        P(("dp", "seq")),
        P(("dp", "seq"), None),
        P(("dp", "seq")),
        P(("dp", "seq"), None),
        P(("dp", "seq")),
        P(("dp", "seq")),
        P(("dp", "seq")),
    )
    out_specs = (
        P("dp", "seq", None),
        P("dp", "seq", None),
        P("dp", "seq", None),
        P(("dp", "seq")),
        P(("dp", "seq")),
        P(("dp", "seq"), None),
        P(("dp", "seq")),
        P(("dp", "seq")),
        P(("dp", "seq"), None),
        P(("dp", "seq")),
        P(("dp", "seq")),
        P(("dp", "seq")),
        P(("dp", "seq"), None),
        P(("dp", "seq")),
        P(("dp", "seq"), None),
        P(("dp", "seq")),
        P(("dp", "seq"), None),
        P(("dp", "seq")),
        P(("dp", "seq")),
        P(("dp", "seq")),
        P(("dp", "seq"), None),
        P(("dp", "seq")),
        P(("dp", "seq"), None),
        P(("dp", "seq")),
        P(("dp", "seq")),
        P(("dp", "seq")),
    )
    groups, seq_parts = mesh.shape["dp"], mesh.shape["seq"]

    def layer(*arguments):
        shard = arguments[5].shape[0]
        parts = arguments[0].shape[0]
        if seq_parts == 2 and parts == 2 and groups % 4 == 0 and shard % 32 == 0:
            return paired_layer(groups // 4, *arguments)
        return on_device(*arguments)

    return jax.shard_map(
        layer, mesh=mesh, in_specs=in_specs, out_specs=out_specs, check_vma=False
    )
```

```python
import functools
import math

import jax
import jax.numpy as jnp
from jax import lax
from jax.experimental import pallas as pl
from jax.experimental.pallas import tpu as pltpu
from jax.sharding import PartitionSpec as P

HEADS = 16
HEAD_DIM = 64


EPSILON = 1e-05
MASKED = -1e30


def layer_norm(values, norm_gain, norm_shift):
    center = values - jnp.mean(values, axis=-1, keepdims=True)
    spread = jnp.mean(center * center, axis=-1, keepdims=True)
    return center * lax.rsqrt(spread + EPSILON) * norm_gain + norm_shift


def norm_back(values, norm_gain, norm_shift, upstream):
    result, pullback = jax.vjp(layer_norm, values, norm_gain, norm_shift)
    return pullback(upstream)


def rows_dot(left_side, right_side):
    return jnp.dot(left_side, right_side, preferred_element_type=jnp.float32)


def left_dot(left_side, right_side):
    return lax.dot_general(
        left_side, right_side, (((0,), (0,)), ((), ())), preferred_element_type=jnp.float32
    )


def right_dot(left_side, right_side):
    return lax.dot_general(
        left_side, right_side, (((1,), (1,)), ((), ())), preferred_element_type=jnp.float32
    )


def heads_of(matrix):
    return matrix.reshape(matrix.shape[0], HEADS, HEAD_DIM)


def attend_forward(queries, key_rows, value_rows, allowed):
    score_scale = 1.0 / math.sqrt(HEAD_DIM)
    scores = (
        jnp.einsum(
            "qhd,khd->hqk",
            heads_of(queries),
            heads_of(key_rows),
            preferred_element_type=jnp.float32,
        )
        * score_scale
    )
    scores = jnp.where(allowed[None], scores, MASKED)
    row_max = jnp.max(scores, axis=-1, keepdims=True)
    weights = jnp.exp(scores - row_max)
    row_total = jnp.sum(weights, axis=-1, keepdims=True)
    weights = (weights / row_total).astype(jnp.bfloat16)
    mixed_rows = jnp.einsum(
        "hqk,khd->qhd", weights, heads_of(value_rows), preferred_element_type=jnp.float32
    )
    logsum = (row_max + jnp.log(row_total))[..., 0]
    return (mixed_rows.reshape(queries.shape[0], -1).astype(jnp.bfloat16), logsum)


def attend_back(queries, key_rows, value_rows, allowed, logsum, upstream):
    score_scale = 1.0 / math.sqrt(HEAD_DIM)
    query_heads = heads_of(queries)
    key_heads = heads_of(key_rows)
    upstream_heads = heads_of(upstream)
    scores = (
        jnp.einsum("qhd,khd->hqk", query_heads, key_heads, preferred_element_type=jnp.float32)
        * score_scale
    )
    scores = jnp.where(allowed[None], scores, MASKED)
    weights = jnp.exp(scores - logsum[..., None])
    grad_weights = jnp.einsum(
        "qhd,khd->hqk", upstream_heads, heads_of(value_rows), preferred_element_type=jnp.float32
    )
    row_delta = jnp.sum(weights * grad_weights, axis=-1, keepdims=True)
    grad_scores = (weights * (grad_weights - row_delta)).astype(jnp.bfloat16)
    grad_query = (
        jnp.einsum("hqk,khd->qhd", grad_scores, key_heads, preferred_element_type=jnp.float32)
        * score_scale
    )
    grad_key = (
        jnp.einsum("hqk,qhd->khd", grad_scores, query_heads, preferred_element_type=jnp.float32)
        * score_scale
    )
    grad_value = jnp.einsum(
        "hqk,qhd->khd",
        weights.astype(jnp.bfloat16),
        upstream_heads,
        preferred_element_type=jnp.float32,
    )
    key_count = key_rows.shape[0]
    return (
        grad_query.reshape(queries.shape[0], -1),
        grad_key.reshape(key_count, -1),
        grad_value.reshape(key_count, -1),
    )


def to_float(values):
    return values.astype(jnp.float32)


def on_device(
    tokens,
    text_states,
    unit_length,
    text_length,
    cotangent,
    attn_gain,
    attn_shift,
    attn_inputs,
    attn_qbias,
    attn_vbias,
    attn_output,
    attn_obias,
    cross_gain,
    cross_shift,
    cross_query,
    cross_qbias,
    cross_keyval,
    cross_vbias,
    cross_output,
    cross_obias,
    ffn_gain,
    ffn_shift,
    ffn_up,
    ffn_upbias,
    ffn_down,
    ffn_downbias,
    final_gain,
    final_shift,
):
    seq_count, local_len, model_width = tokens.shape
    row_count = seq_count * local_len
    first_pos = lax.axis_index("seq") * local_len
    zero_bias = jnp.zeros((model_width,), jnp.float32)
    (
        a_gain_full,
        a_shift_full,
        attention_input_weight_whole,
        a_qbias_full,
        a_vbias_full,
        a_output_full,
        a_obias_full,
    ) = (
        lax.all_gather(attn_gain, ("dp", "seq"), axis=0, tiled=True),
        lax.all_gather(attn_shift, ("dp", "seq"), axis=0, tiled=True),
        lax.all_gather(attn_inputs, ("dp", "seq"), axis=0, tiled=True),
        lax.all_gather(attn_qbias, ("dp", "seq"), axis=0, tiled=True),
        lax.all_gather(attn_vbias, ("dp", "seq"), axis=0, tiled=True),
        lax.all_gather(attn_output, ("dp", "seq"), axis=0, tiled=True),
        lax.all_gather(attn_obias, ("dp", "seq"), axis=0, tiled=True),
    )
    inputs = to_float(tokens).reshape(row_count, model_width)
    normed_one = layer_norm(inputs, to_float(a_gain_full), to_float(a_shift_full)).astype(
        jnp.bfloat16
    )
    joined = rows_dot(normed_one, attention_input_weight_whole) + jnp.concatenate(
        [to_float(a_qbias_full), zero_bias, to_float(a_vbias_full)]
    )
    joined = joined.astype(jnp.bfloat16)
    self_queries = joined[:, :model_width].reshape(seq_count, local_len, model_width)
    keyval_local = joined[:, model_width:].reshape(seq_count, local_len, 2 * model_width)
    self_keyval = lax.all_gather(keyval_local, "seq", axis=1, tiled=True)
    full_len = self_keyval.shape[1]
    causal = jnp.arange(full_len)[None, :] <= (first_pos + jnp.arange(local_len))[:, None]

    def self_forward(packed):
        seq_queries, seq_keyval = packed
        return attend_forward(
            seq_queries, seq_keyval[:, :model_width], seq_keyval[:, model_width:], causal
        )

    self_mixed, self_logsum = lax.map(self_forward, (self_queries, self_keyval))
    self_flat = self_mixed.reshape(row_count, model_width)
    after_self = inputs + rows_dot(self_flat, a_output_full) + to_float(a_obias_full)
    (
        c_gain_full,
        c_shift_full,
        c_query_full,
        c_qbias_full,
        c_keyval_full,
        cross_value_bias_whole,
        c_output_full,
        c_obias_full,
    ) = (
        lax.all_gather(cross_gain, ("dp", "seq"), axis=0, tiled=True),
        lax.all_gather(cross_shift, ("dp", "seq"), axis=0, tiled=True),
        lax.all_gather(cross_query, ("dp", "seq"), axis=0, tiled=True),
        lax.all_gather(cross_qbias, ("dp", "seq"), axis=0, tiled=True),
        lax.all_gather(cross_keyval, ("dp", "seq"), axis=0, tiled=True),
        lax.all_gather(cross_vbias, ("dp", "seq"), axis=0, tiled=True),
        lax.all_gather(cross_output, ("dp", "seq"), axis=0, tiled=True),
        lax.all_gather(cross_obias, ("dp", "seq"), axis=0, tiled=True),
    )
    normed_two = layer_norm(after_self, to_float(c_gain_full), to_float(c_shift_full)).astype(
        jnp.bfloat16
    )
    cross_queries = (rows_dot(normed_two, c_query_full) + to_float(c_qbias_full)).astype(
        jnp.bfloat16
    )
    cross_queries = cross_queries.reshape(seq_count, local_len, model_width)
    keyval_bias = jnp.concatenate([zero_bias, to_float(cross_value_bias_whole)])
    text_whole = lax.all_gather(text_states, "seq", axis=1, tiled=True)
    cross_kv = (rows_dot(text_whole.reshape(-1, model_width), c_keyval_full) + keyval_bias).astype(
        jnp.bfloat16
    )
    cross_kv = cross_kv.reshape(seq_count, -1, 2 * model_width)
    text_total = cross_kv.shape[1]
    text_allowed = jnp.arange(text_total)[None, :] < text_length[:, None]

    def cross_forward(packed):
        seq_queries, seq_keyval, seq_allowed = packed
        allowed = jnp.broadcast_to(seq_allowed[None, :], (local_len, text_total))
        return attend_forward(
            seq_queries, seq_keyval[:, :model_width], seq_keyval[:, model_width:], allowed
        )

    cross_blended_rows, cross_logsum = lax.map(
        cross_forward, (cross_queries, cross_kv, text_allowed)
    )
    cross_flat = cross_blended_rows.reshape(row_count, model_width)
    after_cross = after_self + rows_dot(cross_flat, c_output_full) + to_float(c_obias_full)
    (
        f_gain_full,
        feedforward_shift_whole,
        f_up_full,
        f_upbias_full,
        f_down_full,
        f_downbias_full,
        z_gain_full,
        z_shift_full,
    ) = (
        lax.all_gather(ffn_gain, ("dp", "seq"), axis=0, tiled=True),
        lax.all_gather(ffn_shift, ("dp", "seq"), axis=0, tiled=True),
        lax.all_gather(ffn_up, ("dp", "seq"), axis=0, tiled=True),
        lax.all_gather(ffn_upbias, ("dp", "seq"), axis=0, tiled=True),
        lax.all_gather(ffn_down, ("dp", "seq"), axis=0, tiled=True),
        lax.all_gather(ffn_downbias, ("dp", "seq"), axis=0, tiled=True),
        lax.all_gather(final_gain, ("dp", "seq"), axis=0, tiled=True),
        lax.all_gather(final_shift, ("dp", "seq"), axis=0, tiled=True),
    )
    normed_three = layer_norm(
        after_cross, to_float(f_gain_full), to_float(feedforward_shift_whole)
    ).astype(jnp.bfloat16)
    ffn_inner = rows_dot(normed_three, f_up_full) + to_float(f_upbias_full)
    active = jax.nn.gelu(ffn_inner).astype(jnp.bfloat16)
    after_ffn = after_cross + rows_dot(active, f_down_full) + to_float(f_downbias_full)
    valid_rows = ((first_pos + jnp.arange(local_len))[None, :] < unit_length[:, None]).astype(
        jnp.float32
    )
    valid_rows = valid_rows.reshape(row_count, 1)
    final_norm = layer_norm(after_ffn, to_float(z_gain_full), to_float(z_shift_full))
    layer_out = (
        (final_norm * valid_rows).astype(jnp.bfloat16).reshape(seq_count, local_len, model_width)
    )
    (
        f_gain_full,
        feedforward_shift_whole,
        f_up_full,
        f_upbias_full,
        f_down_full,
        f_downbias_full,
        z_gain_full,
        z_shift_full,
    ) = (
        lax.all_gather(ffn_gain, ("dp", "seq"), axis=0, tiled=True),
        lax.all_gather(ffn_shift, ("dp", "seq"), axis=0, tiled=True),
        lax.all_gather(ffn_up, ("dp", "seq"), axis=0, tiled=True),
        lax.all_gather(ffn_upbias, ("dp", "seq"), axis=0, tiled=True),
        lax.all_gather(ffn_down, ("dp", "seq"), axis=0, tiled=True),
        lax.all_gather(ffn_downbias, ("dp", "seq"), axis=0, tiled=True),
        lax.all_gather(final_gain, ("dp", "seq"), axis=0, tiled=True),
        lax.all_gather(final_shift, ("dp", "seq"), axis=0, tiled=True),
    )
    upstream = to_float(cotangent).reshape(row_count, model_width) * valid_rows
    grad_after_ffn, grad_zgain, grad_zshift = norm_back(
        after_ffn, to_float(z_gain_full), to_float(z_shift_full), upstream
    )
    grad_branch = grad_after_ffn.astype(jnp.bfloat16)
    grad_down = left_dot(active, grad_branch)
    grad_downbias = jnp.sum(to_float(grad_branch), axis=0)
    grad_active = right_dot(grad_branch, f_down_full)
    inner_value, gelu_back = jax.vjp(jax.nn.gelu, ffn_inner)
    grad_inner = gelu_back(grad_active)[0].astype(jnp.bfloat16)
    grad_up = left_dot(normed_three, grad_inner)
    grad_upbias = jnp.sum(to_float(grad_inner), axis=0)
    grad_normed_three = right_dot(grad_inner, f_up_full)
    grad_cross_norm, grad_fgain, grad_fshift = norm_back(
        after_cross, to_float(f_gain_full), to_float(feedforward_shift_whole), grad_normed_three
    )
    grad_after_cross = grad_after_ffn + grad_cross_norm
    ffn_sums = (
        lax.psum_scatter(grad_fgain, ("dp", "seq"), scatter_dimension=0, tiled=True),
        lax.psum_scatter(grad_fshift, ("dp", "seq"), scatter_dimension=0, tiled=True),
        lax.psum_scatter(grad_up, ("dp", "seq"), scatter_dimension=0, tiled=True),
        lax.psum_scatter(grad_upbias, ("dp", "seq"), scatter_dimension=0, tiled=True),
        lax.psum_scatter(grad_down, ("dp", "seq"), scatter_dimension=0, tiled=True),
        lax.psum_scatter(grad_downbias, ("dp", "seq"), scatter_dimension=0, tiled=True),
        lax.psum_scatter(grad_zgain, ("dp", "seq"), scatter_dimension=0, tiled=True),
        lax.psum_scatter(grad_zshift, ("dp", "seq"), scatter_dimension=0, tiled=True),
    )
    (
        c_gain_full,
        c_shift_full,
        c_query_full,
        c_qbias_full,
        c_keyval_full,
        cross_value_bias_whole,
        c_output_full,
        c_obias_full,
    ) = (
        lax.all_gather(cross_gain, ("dp", "seq"), axis=0, tiled=True),
        lax.all_gather(cross_shift, ("dp", "seq"), axis=0, tiled=True),
        lax.all_gather(cross_query, ("dp", "seq"), axis=0, tiled=True),
        lax.all_gather(cross_qbias, ("dp", "seq"), axis=0, tiled=True),
        lax.all_gather(cross_keyval, ("dp", "seq"), axis=0, tiled=True),
        lax.all_gather(cross_vbias, ("dp", "seq"), axis=0, tiled=True),
        lax.all_gather(cross_output, ("dp", "seq"), axis=0, tiled=True),
        lax.all_gather(cross_obias, ("dp", "seq"), axis=0, tiled=True),
    )
    cross_branch_gradient = grad_after_cross.astype(jnp.bfloat16)
    grad_coutput = left_dot(cross_flat, cross_branch_gradient)
    grad_cobias = jnp.sum(to_float(cross_branch_gradient), axis=0)
    grad_cross_mixed = right_dot(cross_branch_gradient, c_output_full).astype(jnp.bfloat16)
    grad_cross_mixed = grad_cross_mixed.reshape(seq_count, local_len, model_width)

    def cross_backward(packed):
        seq_queries, seq_keyval, seq_allowed, sequence_log_sum_exp, seq_upstream = packed
        allowed = jnp.broadcast_to(seq_allowed[None, :], (local_len, text_total))
        return attend_back(
            seq_queries,
            seq_keyval[:, :model_width],
            seq_keyval[:, model_width:],
            allowed,
            sequence_log_sum_exp,
            seq_upstream,
        )

    grad_cq, grad_ck, grad_cv = lax.map(
        cross_backward, (cross_queries, cross_kv, text_allowed, cross_logsum, grad_cross_mixed)
    )
    grad_ckv = lax.psum_scatter(
        jnp.concatenate([grad_ck, grad_cv], axis=-1).astype(jnp.bfloat16),
        "seq",
        scatter_dimension=1,
        tiled=True,
    ).astype(jnp.float32)
    grad_ckv = grad_ckv.astype(jnp.bfloat16).reshape(-1, 2 * model_width)
    grad_ckeyval = left_dot(text_states.reshape(-1, model_width), grad_ckv)
    grad_cvbias = jnp.sum(to_float(grad_ckv[:, model_width:]), axis=0)
    text_grad = right_dot(grad_ckv, c_keyval_full).astype(jnp.bfloat16).reshape(text_states.shape)
    grad_cq_low = grad_cq.reshape(row_count, model_width).astype(jnp.bfloat16)
    grad_cquery = left_dot(normed_two, grad_cq_low)
    grad_cqbias = jnp.sum(to_float(grad_cq_low), axis=0)
    grad_normed_two = right_dot(grad_cq_low, c_query_full)
    grad_self_norm, grad_cgain, grad_cshift = norm_back(
        after_self, to_float(c_gain_full), to_float(c_shift_full), grad_normed_two
    )
    grad_after_self = grad_after_cross + grad_self_norm
    cross_sums = (
        lax.psum_scatter(grad_cgain, ("dp", "seq"), scatter_dimension=0, tiled=True),
        lax.psum_scatter(grad_cshift, ("dp", "seq"), scatter_dimension=0, tiled=True),
        lax.psum_scatter(grad_cquery, ("dp", "seq"), scatter_dimension=0, tiled=True),
        lax.psum_scatter(grad_cqbias, ("dp", "seq"), scatter_dimension=0, tiled=True),
        lax.psum_scatter(grad_ckeyval, ("dp", "seq"), scatter_dimension=0, tiled=True),
        lax.psum_scatter(grad_cvbias, ("dp", "seq"), scatter_dimension=0, tiled=True),
        lax.psum_scatter(grad_coutput, ("dp", "seq"), scatter_dimension=0, tiled=True),
        lax.psum_scatter(grad_cobias, ("dp", "seq"), scatter_dimension=0, tiled=True),
    )
    (
        a_gain_full,
        a_shift_full,
        attention_input_weight_whole,
        a_qbias_full,
        a_vbias_full,
        a_output_full,
        a_obias_full,
    ) = (
        lax.all_gather(attn_gain, ("dp", "seq"), axis=0, tiled=True),
        lax.all_gather(attn_shift, ("dp", "seq"), axis=0, tiled=True),
        lax.all_gather(attn_inputs, ("dp", "seq"), axis=0, tiled=True),
        lax.all_gather(attn_qbias, ("dp", "seq"), axis=0, tiled=True),
        lax.all_gather(attn_vbias, ("dp", "seq"), axis=0, tiled=True),
        lax.all_gather(attn_output, ("dp", "seq"), axis=0, tiled=True),
        lax.all_gather(attn_obias, ("dp", "seq"), axis=0, tiled=True),
    )
    grad_self_branch = grad_after_self.astype(jnp.bfloat16)
    grad_aoutput = left_dot(self_flat, grad_self_branch)
    grad_aobias = jnp.sum(to_float(grad_self_branch), axis=0)
    grad_self_mixed = right_dot(grad_self_branch, a_output_full).astype(jnp.bfloat16)
    grad_self_mixed = grad_self_mixed.reshape(seq_count, local_len, model_width)

    def self_backward(packed):
        seq_queries, seq_keyval, sequence_log_sum_exp, seq_upstream = packed
        return attend_back(
            seq_queries,
            seq_keyval[:, :model_width],
            seq_keyval[:, model_width:],
            causal,
            sequence_log_sum_exp,
            seq_upstream,
        )

    gradient_self_query, grad_sk, grad_sv = lax.map(
        self_backward, (self_queries, self_keyval, self_logsum, grad_self_mixed)
    )
    gradient_self_keyvalue = lax.psum_scatter(
        jnp.concatenate([grad_sk, grad_sv], axis=-1).astype(jnp.bfloat16),
        "seq",
        scatter_dimension=1,
        tiled=True,
    ).astype(jnp.float32)
    grad_joined = (
        jnp.concatenate([gradient_self_query, gradient_self_keyvalue], axis=-1)
        .reshape(row_count, 3 * model_width)
        .astype(jnp.bfloat16)
    )
    grad_ainputs = left_dot(normed_one, grad_joined)
    grad_aqbias = jnp.sum(to_float(grad_joined[:, :model_width]), axis=0)
    grad_avbias = jnp.sum(to_float(grad_joined[:, 2 * model_width :]), axis=0)
    grad_normed_one = right_dot(grad_joined, attention_input_weight_whole)
    grad_input_norm, grad_again, grad_ashift = norm_back(
        inputs, to_float(a_gain_full), to_float(a_shift_full), grad_normed_one
    )
    tokens_grad = (
        (grad_after_self + grad_input_norm)
        .astype(jnp.bfloat16)
        .reshape(seq_count, local_len, model_width)
    )
    attn_sums = (
        lax.psum_scatter(grad_again, ("dp", "seq"), scatter_dimension=0, tiled=True),
        lax.psum_scatter(grad_ashift, ("dp", "seq"), scatter_dimension=0, tiled=True),
        lax.psum_scatter(grad_ainputs, ("dp", "seq"), scatter_dimension=0, tiled=True),
        lax.psum_scatter(grad_aqbias, ("dp", "seq"), scatter_dimension=0, tiled=True),
        lax.psum_scatter(grad_avbias, ("dp", "seq"), scatter_dimension=0, tiled=True),
        lax.psum_scatter(grad_aoutput, ("dp", "seq"), scatter_dimension=0, tiled=True),
        lax.psum_scatter(grad_aobias, ("dp", "seq"), scatter_dimension=0, tiled=True),
    )
    return (layer_out, tokens_grad, text_grad, *attn_sums, *cross_sums, *ffn_sums)


MESH_ID = pl.DeviceIdType.MESH
ANYWHERE = pl.BlockSpec(memory_space=pl.ANY)
VMEM_LIMIT = 56 * 2**20


class Place:
    def __init__(self, depth):
        group = lax.axis_index("dp")
        self.depth = depth
        self.z = group // 4
        self.x = lax.rem(group // 2, 2)
        self.core = lax.rem(group, 2)
        self.y = lax.axis_index("seq")

    def device(self, z, x, core, y):
        return {"dp": (z * 2 + x) * 2 + core, "seq": y}

    def along_z(self, step):
        return self.device(lax.rem(self.z + step, self.depth), self.x, self.core, self.y)

    def across_x(self):
        return self.device(self.z, 1 - self.x, self.core, self.y)

    def across_y(self):
        return self.device(self.z, self.x, self.core, 1 - self.y)

    def sibling(self):
        return self.device(self.z, self.x, 1 - self.core, self.y)

    def along(self, axis):
        if axis == "z":
            return [self.along_z(step) for step in range(1, self.depth)]
        return [self.across_x() if axis == "x" else self.across_y()]

    def greet(self):
        partners = [self.along_z(step) for step in range(1, self.depth)]
        partners += [self.across_x(), self.across_y(), self.sibling()]
        barrier = pltpu.get_barrier_semaphore()
        for partner in partners:
            pl.semaphore_signal(barrier, inc=1, device_id=partner, device_id_type=MESH_ID)
        pl.semaphore_wait(barrier, len(partners))


def remote(source, target, sems, item, index, device):
    send, receive = sems
    return pltpu.make_async_remote_copy(
        src_ref=source,
        dst_ref=target,
        send_sem=send.at[item, index],
        recv_sem=receive.at[item, index],
        device_id=device,
        device_id_type=MESH_ID,
    )


def pipelined(phase_lists, stride):
    stages = []
    for first, phases in enumerate(phase_lists):
        for p, phase in enumerate(phases):
            turn = first + stride * p
            while len(stages) <= turn:
                stages.append([])
            stages[turn].append(phase)
    return stages


ORDERS = (("z", "x", "y"), ("y", "z", "x"))


def gather_phases(place, shard, whole, rows, cols, sems, local, stop, item):
    half = rows.size // 2
    halves = (pl.ds(rows.start, half), pl.ds(rows.start + half, half))
    here = {"z": place.z, "x": place.x, "y": place.y}
    every = slice(None)

    def view(done, some_rows, core):
        at = {axis: every if axis in done else here[axis] for axis in here}
        return whole.at[at["z"], at["x"], core, at["y"], some_rows, cols]

    def copies(phase):
        made = []
        if phase == 3:
            both = view("zxy", rows, place.core)
            return [remote(both, both, sems, item, 2 * place.depth + 2, place.sibling())]
        slot = sum(len(place.along(o[p])) for o in ORDERS for p in range(phase))
        for some_rows, order in zip(halves, ORDERS):
            target = view(order[:phase], some_rows, place.core)
            source = shard.at[some_rows, cols] if phase == 0 else target
            for device in place.along(order[phase]):
                made.append(remote(source, target, sems, item, slot, device))
                slot += 1
        return made

    def take():
        return pltpu.make_async_copy(shard.at[rows, cols], stop, local.at[item, 0])

    def put():
        return pltpu.make_async_copy(stop, view("", rows, place.core), local.at[item, 1])

    def start(phase):
        for copy in copies(phase):
            copy.start()

    def wait(phase):
        for copy in copies(phase):
            copy.wait()

    def opening():
        start(0)
        take().start()
        take().wait()
        put().start()

    def turn(phase):
        def run():
            wait(phase - 1)
            if phase == 1:
                put().wait()
            start(phase)

        return run

    return [opening, turn(1), turn(2), turn(3), lambda: wait(3)]


def copy_sems(items, depth):
    width = 2 * depth + 3
    return [
        pltpu.SemaphoreType.DMA((items, width)),
        pltpu.SemaphoreType.DMA((items, width)),
        pltpu.SemaphoreType.DMA((items, 2)),
    ]


ITEM = 512


def weight_items(shape):
    rows, cols = shape
    return [
        (pl.ds(r, 32), pl.ds(c, min(ITEM, cols)))
        for r in range(0, rows, 32)
        for c in range(0, cols, min(ITEM, cols))
    ]


def nt(a, b):
    return lax.dot_general(a, b, (((1,), (1,)), ((), ())), preferred_element_type=jnp.float32)


def nn(a, b):
    return jnp.dot(a, b, preferred_element_type=jnp.float32)


def half_mask(rows):
    return lax.broadcasted_iota(jnp.int32, (rows, 128), 1) < 64


def pick(block, head, first):
    zero = jnp.zeros_like(block)
    return jnp.where(first, block, zero) if head == 0 else jnp.where(first, zero, block)


MOST_KEYS = 256


def segments(causal, qb, keys, size, most):
    if not causal:
        return [(0, keys, False)]
    first = qb * size
    before = [(lo, min(lo + most, first), False) for lo in range(0, first, most)]
    return before + [(first, first + size, True)]


def both(block, first):
    return jnp.concatenate([pick(block, 0, first), pick(block, 1, first)], axis=0)


def diagonal_mask(scored, size):
    r = lax.broadcasted_iota(jnp.int32, scored.shape, 0)
    c = lax.broadcasted_iota(jnp.int32, scored.shape, 1)
    return jnp.where(r <= lax.rem(c, size), scored, MASKED)


def attend_pair(causal, rows, keys, size, get_q, get_k, get_v, bias, put, lse_ref):
    vt = get_v(0, keys).T
    first = half_mask(size)
    for qb in range(rows // size):
        sl = slice(qb * size, (qb + 1) * size)
        qs = both(get_q(sl.start, sl.stop) * jnp.bfloat16(0.125), first)
        parts = []
        for lo, hi, diagonal in segments(causal, qb, keys, size, MOST_KEYS):
            s = nt(get_k(lo, hi), qs)
            if diagonal:
                s = diagonal_mask(s, size)
            if bias is not None:
                s = s + jnp.concatenate([bias] * (2 * size // 128), axis=1)
            parts.append((lo, hi, s))
        m = functools.reduce(jnp.maximum, [jnp.max(s, axis=0, keepdims=True) for _, _, s in parts])
        total, out = None, None
        for lo, hi, s in parts:
            p = jnp.exp(s - m)
            l = jnp.sum(p, axis=0, keepdims=True)
            o = nn(vt[:, lo:hi], p.astype(jnp.bfloat16))
            total = l if total is None else total + l
            out = o if out is None else out + o
        lse = m + jnp.log(total)
        lse_ref[0:1, sl] = lse[:, :size]
        lse_ref[1:2, sl] = lse[:, size:]
        out = out * (1.0 / total)
        out = jnp.concatenate([out[:64, :size], out[64:, size:]], axis=0).T
        put(sl, out.astype(jnp.bfloat16))


def attend_back_pair(
    causal, rows, keys, size, get_q, get_k, get_v, get_o, get_do, lse_ref, bias, put_dq, put_dk,
    put_dv, dk_acc, dv_acc,
):
    kt = (get_k(0, keys) * jnp.bfloat16(0.125)).T
    first = half_mask(size)
    order = list(range(rows // size))
    if causal:
        order = order[::-1]
    for qb in order:
        sl = slice(qb * size, (qb + 1) * size)
        qs = both(get_q(sl.start, sl.stop) * jnp.bfloat16(0.125), first)
        do = get_do(sl.start, sl.stop)
        dos = both(do, first)
        dt = (do.astype(jnp.float32) * get_o(sl.start, sl.stop).astype(jnp.float32)).T
        delta = jnp.concatenate(
            [
                jnp.sum(dt[:64], axis=0, keepdims=True),
                jnp.sum(dt[64:], axis=0, keepdims=True),
            ],
            axis=1,
        )
        lse = jnp.concatenate([lse_ref[0:1, sl], lse_ref[1:2, sl]], axis=1)
        dq = None
        for lo, hi, diagonal in segments(causal, qb, keys, size, MOST_KEYS):
            s = nt(get_k(lo, hi), qs)
            if diagonal:
                s = diagonal_mask(s, size)
            if bias is not None:
                s = s + jnp.concatenate([bias] * (2 * size // 128), axis=1)
            dp = nt(get_v(lo, hi), dos)
            p = jnp.exp(s - lse)
            ds = (p * (dp - delta)).astype(jnp.bfloat16)
            dv = nn(p.astype(jnp.bfloat16), dos)
            dk = nn(ds, qs)
            part = nn(kt[:, lo:hi], ds)
            dq = part if dq is None else dq + part
            if qb == order[0]:
                dv_acc[lo:hi, :] = dv
                dk_acc[lo:hi, :] = dk
            else:
                dv_acc[lo:hi, :] += dv
                dk_acc[lo:hi, :] += dk
        dq = jnp.concatenate([dq[:64, :size], dq[64:, size:]], axis=0).T
        put_dq(sl, dq.astype(jnp.bfloat16))
    put_dk(dk_acc[0:keys, :].astype(jnp.bfloat16))
    put_dv(dv_acc[0:keys, :].astype(jnp.bfloat16))


BLOCK = 256
MATMUL_ROWS = 512
RING = 6

VECTOR_COUNT = 15
(
    A_GAIN, A_SHIFT, A_QBIAS, A_VBIAS, A_OBIAS, C_GAIN, C_SHIFT, C_QBIAS, C_VBIAS, C_OBIAS,
    F_GAIN, F_SHIFT, F_DOWNBIAS, Z_GAIN, Z_SHIFT,
) = range(VECTOR_COUNT)
F_UPBIAS = VECTOR_COUNT
UP_INDEX, DOWN_INDEX = 6, 7
STRIDE = 3
SWAP_PIECES = 16
SELF_QUERIES, CROSS_QUERIES = 512, 1024


def block_rows(index, size):
    return pl.ds(pl.multiple_of(index * size, size), size)


def lanes(index, size):
    return pl.ds(pl.multiple_of(index * size, size), size)


def center_and_scale(values):
    center = values - jnp.mean(values, axis=-1, keepdims=True)
    spread = jnp.mean(center * center, axis=-1, keepdims=True)
    scale = lax.rsqrt(spread + EPSILON)
    return center * scale, scale


def norm_pull(unit, scale, pulled):
    inner = jnp.mean(pulled * unit, axis=-1, keepdims=True)
    return scale * (pulled - jnp.mean(pulled, axis=-1, keepdims=True) - unit * inner)


def gelu_and_slope(values):
    root = math.sqrt(2.0 / math.pi)
    square = values * values
    bend = jnp.tanh(root * (values + 0.044715 * (values * square)))
    rise = root * (1.0 + 3.0 * 0.044715 * square)
    result = 0.5 * values * (1.0 + bend)
    slope = 0.5 * (1.0 + bend) + 0.5 * values * ((1.0 - bend * bend) * rise)
    return result, slope


def spread_vectors(packed):
    rows = packed.shape[0]
    width = rows
    lane = lax.broadcasted_iota(jnp.int32, (128, width), 1)
    source = lax.broadcasted_iota(jnp.int32, (128, width), 0)
    select = jnp.where(lax.rem(lane, 32) == source, 1.0, 0.0).astype(jnp.bfloat16)
    wide = jnp.dot(packed, select, preferred_element_type=jnp.float32)
    row = lax.broadcasted_iota(jnp.int32, (rows, width), 0)
    lane = lax.broadcasted_iota(jnp.int32, (rows, width), 1)
    wide = jnp.where(row // 32 == lane // 32, wide, 0.0)
    return jnp.sum(wide.reshape(rows // 32, 32, width), axis=0)


def quarter_columns(values, width, back=False):
    share = 32
    per = 128 // share
    shards = width // share
    lane = lax.broadcasted_iota(jnp.int32, (values.shape[0], 128), 1) // share
    blocks = [values[:, k * 128 : (k + 1) * 128] for k in range(4 * shards * share // 128)]
    result = []
    for k in range(len(blocks)):
        total = None
        for j in range(per):
            if back:
                source, held = blocks[j * (shards // per) + k // per], k % per
            else:
                source, held = blocks[per * (k % (shards // per)) + j], k // (shards // per)
            moved = source if held == j else pltpu.roll(source, (j - held) * share % 128, 1)
            total = moved if total is None else jnp.where(lane == j, moved, total)
        result.append(total)
    return jnp.concatenate(result, axis=1)


def arrange_columns(target, source, sem, width):
    copy = pltpu.make_async_copy(source, target, sem)
    copy.start()
    copy.wait()
    values = target[...].astype(jnp.float32)
    target[...] = quarter_columns(values, width).astype(target.dtype)


class Copies:
    def __init__(self, sems):
        self.sems = sems
        self.open = {}
        self.used = 0

    def start(self, source, target):
        copy = pltpu.make_async_copy(source, target, self.sems.at[self.used])
        self.used += 1
        copy.start()
        return copy


def forward_kernel(depth, sizes, *refs):
    refs = list(refs)

    def take(count):
        taken = refs[:count]
        del refs[:count]
        return taken

    shard_count = len(sizes)
    tokens, texts, cots, unit_length, text_length = take(5)
    shards = take(7 + 1)
    wholes = take(shard_count)
    (
        o_tokens, o_text, o_h1, o_qkv, o_o1, o_after_self, o_h2, o_cq, o_ckv, o_o2,
        o_after_cross, o_h3, o_active, o_slope, o_gaf, o_gbr, o_layer,
    ) = take(17)
    vec, lse1, lse2, zgrads = take(4)
    tok, txt, cot, x, o1, cq, ckv, o2, resid, h2, ring, slopes, packed = take(13)
    stops = take(sum(len(weight_items(s)) for s in sizes))
    send, receive, local, sw_send, sw_receive, sw_local, loads, outs = take(8)
    (up_stop, up_sem) = take(2)

    place = Place(depth)
    y = place.y
    rows = resid.shape[0]
    width = resid.shape[1]
    part = rows // 2
    copies = Copies(outs)
    sources = list(shards[:DOWN_INDEX])
    sources[UP_INDEX] = up_stop
    share = sizes[0][0]
    sources += [shards[DOWN_INDEX].at[pl.ds(q * share, share)] for q in range(4)]
    phases, chunks, item = [], [], 0
    for index, size in enumerate(sizes):
        for r, c in weight_items(size):
            phases.append(
                gather_phases(
                    place, sources[index], wholes[index], r, c, (send, receive), local,
                    stops[item], item,
                )
            )
            if index > 0 and c.start % width == 0:
                chunks.append((wholes[index], pl.ds(c.start, width)))
            item += 1
    stages = pipelined(phases[1:], STRIDE)
    for k, phase in enumerate(phases[0]):
        stages[STRIDE * k].append(phase)

    def swapping(k, source, target, count, first):
        size = source.shape[1] // count

        def away(i):
            piece = pl.ds(i * size, size)
            return remote(
                source.at[1 - y, piece], target.at[y, piece], (sw_send, sw_receive), k, i,
                place.across_y(),
            )

        home = pltpu.make_async_copy(source.at[y], target.at[y], sw_local.at[k])
        for i in range(count):
            stages[first + i].append(lambda i=i: away(i).start())
        stages[first].append(home.start)

        def closing():
            home.wait()
            for i in range(count):
                away(i).wait()

        return closing

    token_swap = swapping(0, tokens, tok, 8, 0)
    text_swap = swapping(1, texts, txt, 2, 10)
    cot_swap = swapping(2, cots, cot, SWAP_PIECES, 27)

    def load(chunk):
        whole, cols = chunks[chunk]
        return pltpu.make_async_copy(
            whole.at[:, :, :, :, :, cols], ring.at[chunk % RING], loads.at[chunk]
        )

    ran = []

    def stage(k):
        assert len(ran) == k
        ran.append(k)
        for one in stages[k]:
            one()
        ready = k - 4 * STRIDE
        if ready > 0 and ready % 2 == 1:
            load(ready // 2).start()

    def weight(chunk):
        return ring[chunk % RING].reshape(width, width)

    def row(index):
        return vec[index : index + 1, :]

    def looped(count, body, due=()):
        @pl.loop(0, count)
        def _(j):
            for at, k in due:

                @pl.when(j == at)
                def _(k=k):
                    stage(k)

            body(j)

    place.greet()
    for k in range(4):
        stage(k)
    arrange_columns(up_stop, shards[UP_INDEX], up_sem, width)
    for k in range(4, 14):
        stage(k)
    pack = pltpu.make_async_copy(wholes[0], packed, outs.at[copies.used])
    copies.used += 1
    pack.start()
    pack.wait()
    vec[...] = spread_vectors(packed[...].reshape(-1, 128))
    token_swap()
    done_tokens = copies.start(tok, o_tokens)

    def token_block(b):
        half = b // (part // BLOCK)
        inner = lax.rem(b, part // BLOCK)
        return tok[half, block_rows(inner, BLOCK), :].astype(jnp.float32)

    def norm_one(b):
        unit, _ = center_and_scale(token_block(b))
        at = block_rows(b, BLOCK)
        x[at, 3 * width :] = (unit * row(A_GAIN) + row(A_SHIFT)).astype(jnp.bfloat16)
        resid[at, :] = token_block(b)

    looped(rows // BLOCK, norm_one)
    done_h1 = copies.start(x.at[:, pl.ds(3 * width, width)], o_h1)

    def project(chunk):
        bias = (row(A_QBIAS), None, row(A_VBIAS))[chunk]
        load(chunk).wait()

        def block(b):
            at = block_rows(b, MATMUL_ROWS)
            value = nn(x[at, 3 * width :], weight(chunk))
            if bias is not None:
                value = value + bias
            x[at, chunk * width : (chunk + 1) * width] = value.astype(jnp.bfloat16)

        looped(rows // MATMUL_ROWS, block)

    stage(14)
    project(0)
    stage(15)
    project(1)
    stage(16)
    stage(17)
    project(2)
    done_qkv = copies.start(x.at[:, pl.ds(0, 3 * width)], o_qkv)
    pairs = width // 128

    def self_pair(j):
        def part_of(base):
            return lambda lo, hi: x[lo:hi, lanes(j + base * pairs, 128)]

        def put(sl, value):
            o1[sl, lanes(j, 128)] = value

        attend_pair(
            True, rows, rows, min(SELF_QUERIES, rows), part_of(0), part_of(1), part_of(2), None, put, lse1.at[j]
        )

    looped(pairs, self_pair, ((1, 18), (2, 19), (4, 20), (5, 21), (7, 22)))
    done_o1 = copies.start(o1, o_o1)
    load(3).wait()

    def out_block(b):
        at = block_rows(b, MATMUL_ROWS)
        resid[at, :] = resid[at, :] + nn(o1[at, :], weight(3)) + row(A_OBIAS)

    looped(rows // MATMUL_ROWS, out_block)
    stage(23)
    done_after_self = copies.start(resid, o_after_self)

    def norm_two(b):
        at = block_rows(b, BLOCK)
        unit, _ = center_and_scale(resid[at, :])
        h2[at, :] = (unit * row(C_GAIN) + row(C_SHIFT)).astype(jnp.bfloat16)

    looped(rows // BLOCK, norm_two)
    done_h2 = copies.start(h2, o_h2)
    stage(24)
    load(4).wait()

    def cq_block(b):
        at = block_rows(b, MATMUL_ROWS)
        cq[at, :] = (nn(h2[at, :], weight(4)) + row(C_QBIAS)).astype(jnp.bfloat16)

    looped(rows // MATMUL_ROWS, cq_block)
    done_cq = copies.start(cq, o_cq)
    text_swap()
    done_text = copies.start(txt, o_text)
    text = txt[...].reshape(-1, width)
    text_rows = text.shape[0]
    stage(25)
    load(5).wait()
    ckv[:, :width] = nn(text, weight(5)).astype(jnp.bfloat16)
    load(6).wait()
    ckv[:, width:] = (nn(text, weight(6)) + row(C_VBIAS)).astype(jnp.bfloat16)
    done_ckv = copies.start(ckv, o_ckv)
    bias = text_mask(text_rows, text_length[y])

    def cross_pair(j):
        def put(sl, value):
            o2[sl, lanes(j, 128)] = value

        attend_pair(
            False, rows, text_rows, min(CROSS_QUERIES, rows),
            lambda lo, hi: cq[lo:hi, lanes(j, 128)],
            lambda lo, hi: ckv[lo:hi, lanes(j, 128)],
            lambda lo, hi: ckv[lo:hi, lanes(j + pairs, 128)],
            bias, put, lse2.at[j],
        )

    looped(pairs, cross_pair, ((1, 26), (4, 27), (6, 28)))
    done_o2 = copies.start(o2, o_o2)
    load(7).wait()
    done_after_self.wait()

    def cross_out_block(b):
        at = block_rows(b, MATMUL_ROWS)
        resid[at, :] = resid[at, :] + nn(o2[at, :], weight(7)) + row(C_OBIAS)

    looped(rows // MATMUL_ROWS, cross_out_block)
    stage(29)
    done_after_cross = copies.start(resid, o_after_cross)
    done_o1.wait()
    h3 = o1

    def norm_three(b):
        at = block_rows(b, BLOCK)
        unit, _ = center_and_scale(resid[at, :])
        h3[at, :] = (unit * row(F_GAIN) + row(F_SHIFT)).astype(jnp.bfloat16)

    looped(rows // BLOCK, norm_three)
    done_h3 = copies.start(h3, o_h3)
    done_h1.wait()
    done_qkv.wait()
    waiting = []

    def up(q):
        load(8 + q).wait()
        slope_at = slopes.at[q % 2]

        def block(b):
            at = block_rows(b, BLOCK)
            inner = nn(h3[at, :], weight(8 + q)) + row(F_UPBIAS + q)
            active, slope = gelu_and_slope(inner)
            x[at, q * width : (q + 1) * width] = active.astype(jnp.bfloat16)
            slope_at[at, :] = slope.astype(jnp.bfloat16)

        if q >= 2:
            waiting[q - 2].wait()
        looped(rows // BLOCK, block)
        span = pl.ds(q * width, width)
        waiting.append(copies.start(slope_at, o_slope.at[:, span]))

    stage(30)
    stage(31)
    up(0)
    stage(32)
    stage(33)
    up(1)
    stage(34)
    up(2)
    stage(35)
    stage(36)
    up(3)
    stage(37)
    done_active = copies.start(x, o_active)
    done_after_cross.wait()

    def down(q):
        load(12 + q).wait()

        def block(b):
            at = block_rows(b, MATMUL_ROWS)
            resid[at, :] += nn(x[at, q * width : (q + 1) * width], weight(12 + q))

        looped(rows // MATMUL_ROWS, block)

    for q in range(4):
        down(q)
        if q < 3:
            stage(38 + 2 * q)
            stage(39 + 2 * q)
    cot_swap()
    done_cq.wait()
    done_o2.wait()
    valid_count = unit_length[y]
    zgrads[...] = jnp.zeros_like(zgrads)
    gbr, layer = cq, o2

    def last_block(b):
        at = block_rows(b, BLOCK)
        unit, scale = center_and_scale(resid[at, :] + row(F_DOWNBIAS))
        position = b * BLOCK + lax.broadcasted_iota(jnp.int32, (BLOCK, 1), 0)
        valid = jnp.where(position < valid_count, 1.0, 0.0)
        layer[at, :] = ((unit * row(Z_GAIN) + row(Z_SHIFT)) * valid).astype(jnp.bfloat16)
        half = b // (part // BLOCK)
        inner = lax.rem(b, part // BLOCK)
        upstream = cot[half, block_rows(inner, BLOCK), :].astype(jnp.float32) * valid
        zgrads[0:1, :] += jnp.sum(upstream * unit, axis=0, keepdims=True)
        zgrads[1:2, :] += jnp.sum(upstream, axis=0, keepdims=True)
        grad = norm_pull(unit, scale, upstream * row(Z_GAIN))
        low = grad.astype(jnp.bfloat16)
        gbr[at, :] = low
        zgrads[2:3, :] += jnp.sum(low.astype(jnp.float32), axis=0, keepdims=True)
        resid[at, :] = grad

    ending = []
    for b in range(rows // BLOCK):
        last_block(b)
        at = pl.ds(b * BLOCK, BLOCK)
        ending += [
            copies.start(source.at[at, :], target.at[at, :])
            for source, target in ((resid, o_gaf), (gbr, o_gbr), (layer, o_layer))
        ]
    ending += [done_tokens, done_h2, done_text, done_ckv, done_h3, done_active]
    for copy in ending + waiting[2:]:
        copy.wait()


def text_mask(text_rows, count):
    position = lax.broadcasted_iota(jnp.int32, (text_rows, 128), 0)
    return jnp.where(position < count, 0.0, MASKED)


def forward(depth, number, tokens, texts, cots, unit_length, text_length, shards):
    rows, width = 2 * tokens.shape[1], tokens.shape[2]
    text_rows = 2 * texts.shape[1]
    hidden = 4 * width
    pairs = width // 128
    share = shards[0].shape[0]
    sizes = [s.shape for s in shards[:DOWN_INDEX]] + [(share, width)] * 4
    items = sum(len(weight_items(s)) for s in sizes)
    low, full = jnp.bfloat16, jnp.float32

    def shape(*dims, kind=low):
        return jax.ShapeDtypeStruct(dims, kind)

    def vmem(*dims, kind=low):
        return pltpu.VMEM(dims, kind)

    big = shape(rows, width)
    exact = shape(rows, width, kind=full)
    outs = [shape(depth, 2, 2, 2, *s) for s in sizes]
    outs += [
        shape(*tokens.shape), shape(*texts.shape), big, shape(rows, 3 * width), big, exact, big, big,
        shape(text_rows, 2 * width), big, exact, big, shape(rows, hidden), shape(rows, hidden),
        exact, big, big,
    ]
    small = [
        shape(32, width, kind=full), shape(pairs, 2, rows, kind=full),
        shape(pairs, 2, rows, kind=full), shape(8, width, kind=full),
    ]
    scratch = [
        vmem(*tokens.shape), vmem(*texts.shape), vmem(*cots.shape), vmem(rows, hidden),
        vmem(rows, width), vmem(rows, width), vmem(text_rows, 2 * width), vmem(rows, width),
        vmem(rows, width, kind=full), vmem(rows, width), vmem(RING, depth, 2, 2, 2, 32, width),
        vmem(2, rows, width), vmem(depth, 2, 2, 2, *sizes[0]),
    ]
    scratch += [vmem(r.size, c.size) for s in sizes for r, c in weight_items(s)]
    scratch += copy_sems(items, depth)
    scratch += [
        pltpu.SemaphoreType.DMA((3, SWAP_PIECES)), pltpu.SemaphoreType.DMA((3, SWAP_PIECES)),
        pltpu.SemaphoreType.DMA((3,)), pltpu.SemaphoreType.DMA((items,)),
        pltpu.SemaphoreType.DMA((48,)), vmem(*sizes[UP_INDEX]), pltpu.SemaphoreType.DMA,
    ]
    memory = pl.BlockSpec(memory_space=pltpu.SMEM)
    results = pl.pallas_call(
        functools.partial(forward_kernel, depth, sizes),
        out_shape=outs + small,
        in_specs=[ANYWHERE] * 3 + [memory] * 2 + [ANYWHERE] * len(shards),
        out_specs=[ANYWHERE] * len(outs) + [pl.BlockSpec(memory_space=pltpu.VMEM)] * len(small),
        scratch_shapes=scratch,
        compiler_params=pltpu.CompilerParams(
            collective_id=number, has_side_effects=True, vmem_limit_bytes=VMEM_LIMIT
        ),
        name="forward",
    )(tokens, texts, cots, unit_length, text_length, *shards)
    return list(results[: len(sizes)]), list(results[len(sizes) :])


BACK_STRIDE = 3
BACK_RING = 2 * BACK_STRIDE + 2
BACK_QUERIES = 256
WEIGHT_RING = 2
NORM_BLOCK = 128


def ring_scratch(depth, stride, rows, cols, dtype):
    half = rows // 2
    slots = max(1, 3 * stride)
    return [
        pltpu.VMEM((max(1, 2 * stride + 2 * (stride > 0)), depth, 2, 2, 2, rows, cols), dtype),
        pltpu.VMEM((max(1, 2 * stride), depth, 2, 2, rows, cols), dtype),
        pltpu.VMEM((slots, depth, 2, half, cols), dtype),
        pltpu.VMEM((slots, depth, half, cols), dtype),
        pltpu.VMEM((slots, depth - 1, half, cols), dtype),
        pltpu.VMEM((slots, depth, 2, half, cols), dtype),
        pltpu.VMEM((slots, depth - 1, 2, half, cols), dtype),
        pltpu.VMEM((slots, half, cols), dtype),
    ]


def piece_phases(place, put_result, bufs, sems, item):
    depth = bufs[0].shape[1]
    piece, came, a_y, a_x, a_z, b_x, b_z, b_y = (buf.at[item % buf.shape[0]] for buf in bufs)
    half = bufs[7].shape[1]
    low, high = pl.ds(0, half), pl.ds(half, half)
    z, x, core, y = place.z, place.x, place.core, place.y
    every = slice(None)

    def send(a, b, index, device):
        return remote(a, b, sems, item, index, device)

    def copies(phase):
        if phase == 0:
            return [send(piece.at[every, every, 1 - core], came, 0, place.sibling())]
        if phase == 1:
            return [
                send(piece.at[every, every, core, 1 - y, low], a_y, 1, place.across_y()),
                send(piece.at[every, 1 - x, core, every, high], b_x, 2, place.across_x()),
            ]
        if phase == 2:
            return [send(a_y.at[every, 1 - x], a_x, 3, place.across_x())] + [
                send(
                    b_x.at[lax.rem(z + step, depth)], b_z.at[step - 1], 3 + step,
                    place.along_z(step),
                )
                for step in range(1, depth)
            ]
        return [send(b_z.at[0, 1 - y], b_y, 3 + depth, place.across_y())] + [
            send(
                a_x.at[lax.rem(z + step, depth)], a_z.at[step - 1], 3 + depth + step,
                place.along_z(step),
            )
            for step in range(1, depth)
        ]

    def start(phase):
        for copy in copies(phase):
            copy.start()

    def wait(phase):
        for copy in copies(phase):
            copy.wait()

    def wide(values):
        return values.astype(jnp.float32)

    def after_core():
        wait(0)

        @pl.loop(0, depth)
        def _(k):
            for i in range(2):
                for j in range(2):
                    piece[k, i, core, j] = piece[k, i, core, j] + came[k, i, j]

        start(1)

    def after_one():
        wait(1)

        @pl.loop(0, depth)
        def _(k):
            for i in range(2):
                a_y[k, i] = a_y[k, i] + piece[k, i, core, y, low]
                b_x[k, i] = b_x[k, i] + piece[k, x, core, i, high]

        start(2)

    def after_two():
        wait(2)

        @pl.loop(0, depth)
        def _(k):
            a_x[k] = a_x[k] + a_y[k, x]

        for i in range(2):
            total = wide(b_x[z, i])
            for step in range(1, depth):
                total = total + wide(b_z[step - 1, i])
            b_z[0, i] = total.astype(b_z.dtype)
        start(3)

    def closing():
        wait(3)
        total = wide(a_x[z])
        for step in range(1, depth):
            total = total + wide(a_z[step - 1])
        put_result(low, total)
        put_result(high, wide(b_z[0, y]) + wide(b_y[...]))

    return [lambda: start(0), after_core, after_one, after_two, closing]


def gather_vectors(vectors, first, shards):
    width = vectors.shape[1]
    row = first + lax.broadcasted_iota(jnp.int32, (shards, 32, width), 0)
    lane = lax.broadcasted_iota(jnp.int32, (shards, 32, width), 2)
    parts = jnp.where(row == lane // 32, vectors[None], 0.0).reshape(shards * 32, width)
    source = lax.broadcasted_iota(jnp.int32, (width, 128), 0)
    lane = lax.broadcasted_iota(jnp.int32, (width, 128), 1)
    select = jnp.where(lax.rem(source, 32) == lane, 1.0, 0.0).astype(jnp.bfloat16)
    total = None
    for _ in range(3):
        some = parts.astype(jnp.bfloat16)
        parts = parts - some.astype(jnp.float32)
        value = nn(some, select)
        total = value if total is None else total + value
    return total


def backward_kernel(depth, *refs):
    refs = list(refs)

    def take(count):
        taken = refs[:count]
        del refs[:count]
        return taken

    w_in, w_out, w_cq, w_ckv, w_co, w_up = take(6)
    w_downs = take(4)
    (
        i_tokens, i_text, i_h1, i_qkv, i_o1, i_after_self, i_h2, i_cq, i_ckv, i_o2, i_after_cross,
        i_h3, i_active, i_slope, i_gaf, i_gbr, i_layer,
    ) = take(17)
    vec, lse1, lse2, zgrads, text_length = take(5)
    o_layer, o_tokens, o_text = take(3)
    s_in, s_out, s_cq, s_ckv, s_co, s_up, s_down, s_small = take(8)
    p, q_buf, resid, dh, low, h3, extra, ckv, dckv, text, tgrad, src, vg, ka, va = take(15)
    ring = take(1)[0]
    bufs = take(8)
    small_bufs = take(8)
    sems = take(2)
    small_sems = take(2)
    swap_send, swap_receive, swap_local, loads, fetches = take(5)

    place = Place(depth)
    y = place.y
    rows, width = resid.shape
    part_rows = rows // 2
    pairs = width // 128
    shards = depth * 8
    text_rows = ckv.shape[0]
    fetched = Copies(fetches)
    fetch = fetched.start

    half_width = width // 2
    targets = [(s_down, q, h) for q in range(4) for h in (0, 1)]
    targets += [(s_co, 0, h) for h in (0, 1)]
    targets += [(s_up, 0, h) for h in range(8)]
    targets += [(s_cq, 0, h) for h in (0, 1)]
    targets += [(s_ckv, 0, h) for h in range(4)]
    targets += [(s_out, 0, h) for h in (0, 1)]
    targets += [(s_in, 0, 2 * c + h) for h in (0, 1) for c in range(3)]
    share = width // shards

    def keeping(target, quarter, column):
        def put(some_rows, value):
            at = pl.ds(quarter * share + some_rows.start, some_rows.size)
            target[at, column * half_width : (column + 1) * half_width] = value

        return put

    phases = [
        piece_phases(place, keeping(*target), bufs, sems, item)
        for item, target in enumerate(targets)
    ]

    def put_small(some_rows, value):
        s_small[some_rows, :] = value

    small_phases = piece_phases(place, put_small, small_bufs, small_sems, 0)
    stages = pipelined(phases + [[lambda: None] + small_phases[1:]], BACK_STRIDE)
    ran = []

    def stage(k):
        assert len(ran) == k
        ran.append(k)
        for one in stages[k]:
            one()

    def make(item, get_left, *rights):
        @pl.loop(0, 2)
        def _(b):
            left = get_left(lanes(b, half_width))
            slot = item
            for get in rights:
                value = left_dot(left, get()).astype(jnp.bfloat16)
                for k in range(value.shape[1] // half_width):
                    some = value[:, k * half_width : (k + 1) * half_width]
                    piece = bufs[0].at[slot % BACK_RING]
                    piece[pl.ds(b * (depth // 2), depth // 2)] = some.reshape(
                        depth // 2, 2, 2, 2, share, half_width
                    )
                    slot += 1

    def produce(item, get_left, *rights):
        make(item, get_left, *rights)
        stage(item)

    def part(buf, k):
        return lambda: buf[:, k * half_width : (k + 1) * half_width]

    def halves(buf, k):
        return (lambda: buf[:, k * width : (k + 1) * width],)

    order = []
    for k in range(4):
        order += [(w_downs[k], 0), (w_up, k)]
    order += [(w_co, 0), (w_ckv, 0), (w_ckv, 1), (w_cq, 0), (w_out, 0)]
    order += [(w_in, c) for c in range(3)]

    def load(n):
        whole, column = order[n]
        return pltpu.make_async_copy(
            whole.at[:, :, :, :, :, pl.ds(column * width, width)],
            ring.at[n % WEIGHT_RING],
            loads.at[n],
        )

    def weight(n):
        return ring[n % WEIGHT_RING].reshape(width, width)

    def ready(n):
        load(n).wait()

    def finished(n):
        if n + WEIGHT_RING < len(order):
            load(n + WEIGHT_RING).start()

    def row(index):
        return vec[index : index + 1, :]

    def add_row(index, value):
        vg[index : index + 1, :] += jnp.sum(value, axis=0, keepdims=True)

    def looped(count, body):
        @pl.loop(0, count)
        def _(j):
            body(j)

    def by_blocks(body, size=MATMUL_ROWS):
        looped(rows // size, lambda b: body(block_rows(b, size)))

    def column(buf, k):
        return lambda some_lanes: buf[:, pl.ds(k * width + some_lanes.start, some_lanes.size)]

    def plain(buf):
        return lambda some_lanes: buf[:, some_lanes]

    def norm_step(source, gain, shift, next_bias):
        blocks = rows // NORM_BLOCK

        def bring(b, slot):
            return pltpu.make_async_copy(
                source.at[block_rows(b, NORM_BLOCK), :], src.at[slot], swap_local.at[3 + slot]
            )

        bring(0, 0).start()

        def step(b):
            slot = lax.rem(b, 2)
            bring(b, slot).wait()

            @pl.when(b + 1 < blocks)
            def _():
                bring(b + 1, 1 - slot).start()

            at = block_rows(b, NORM_BLOCK)
            unit, scale = center_and_scale(src[slot])
            pulled = dh[at, :]
            add_row(gain, pulled * unit)
            add_row(shift, pulled)
            total = resid[at, :] + norm_pull(unit, scale, pulled * row(gain))
            resid[at, :] = total
            rounded = total.astype(jnp.bfloat16)
            low[at, :] = rounded
            add_row(next_bias, rounded.astype(jnp.float32))

        looped(blocks, step)

    def swap_out(k, get_source, target, local_source):
        def away():
            return remote(
                get_source(1 - y), target.at[y], (swap_send, swap_receive), k, 0, place.across_y()
            )

        def home():
            return pltpu.make_async_copy(local_source, target.at[y], swap_local.at[k])

        return away, home

    place.greet()
    got_low = fetch(i_gbr, low)
    spans = [pl.ds(k * width, width) for k in range(4)]

    def fetch_active(k):
        return fetch(i_active.at[:, spans[k]], p.at[:, spans[k]])

    def fetch_slope(k):
        return fetch(i_slope.at[:, spans[k]], q_buf.at[:, spans[k]])

    got_active = [fetch_active(0)]
    got_low.wait()
    load(0).start()
    got_slope = [fetch_slope(0)]
    load(1).start()
    keep = extra.at[pl.ds(0, part_rows)]
    got_keep = fetch(i_layer.at[y], keep)
    got_active.append(fetch_active(1))
    got_slope.append(fetch_slope(1))
    vg[...] = jnp.zeros_like(vg)
    vg[Z_GAIN : Z_GAIN + 1, :] = zgrads[0:1, :]
    vg[Z_SHIFT : Z_SHIFT + 1, :] = zgrads[1:2, :]
    vg[F_DOWNBIAS : F_DOWNBIAS + 1, :] = zgrads[2:3, :]
    layer_count = 16
    layer_size = part_rows // layer_count

    def layer_away(i):
        piece = pl.ds(i * layer_size, layer_size)
        return remote(
            i_layer.at[1 - y, piece], o_layer.at[y, piece], (swap_send, swap_receive), 0, i,
            place.across_y(),
        )

    layer_home = pltpu.make_async_copy(keep, o_layer.at[y], swap_local.at[0])
    for i in range(layer_count):
        if i < 6:
            layer_away(i).start()
        else:
            stages[i - 5].append(lambda i=i: layer_away(i).start())

    for k in range(4):
        got_active[k].wait()
        produce(2 * k, column(p, k), *halves(low, 0))
        if k == 0:
            got_active += [fetch_active(2), fetch_active(3)]
            got_slope += [fetch_slope(2), fetch_slope(3)]
            got_resid = fetch(i_gaf, resid)
            got_h3 = fetch(i_h3, h3)
            got_ckv = fetch(i_ckv, ckv)
            got_text = fetch(i_text, text)
        n = 2 * k
        got_slope[k].wait()
        ready(n)
        span = slice(k * width, (k + 1) * width)

        def inner_block(at, n=n, span=span, k=k):
            grad = nt(low[at, :], weight(n)) * q_buf[at, span].astype(jnp.float32)
            rounded = grad.astype(jnp.bfloat16)
            q_buf[at, span] = rounded
            add_row(F_UPBIAS + k, rounded.astype(jnp.float32))

        by_blocks(inner_block)
        finished(n)
        stage(2 * k + 1)
        ready(n + 1)

        def up_block(at, n=n, span=span, k=k):
            value = nt(q_buf[at, span], weight(n + 1))
            dh[at, :] = value if k == 0 else dh[at, :] + value

        by_blocks(up_block)
        finished(n + 1)
    cq_at, o2_at, do2_at, h2_at = (slice(k * width, (k + 1) * width) for k in range(4))
    got_cq = fetch(i_cq, p.at[:, pl.ds(0, width)])
    got_o2 = fetch(i_o2, p.at[:, pl.ds(width, width)])
    got_h2 = fetch(i_h2, p.at[:, pl.ds(3 * width, width)])
    got_resid.wait()
    norm_step(i_after_cross, F_GAIN, F_SHIFT, C_OBIAS)
    got_keep.wait()
    layer_home.start()

    got_o2.wait()
    produce(8, column(p, 1), *halves(low, 0))
    ready(8)

    def do2_block(at):
        p[at, do2_at] = nt(low[at, :], weight(8)).astype(jnp.bfloat16)

    by_blocks(do2_block)
    finished(8)
    stage(9)
    got_cq.wait()
    got_h3.wait()
    got_ckv.wait()
    bias = text_mask(text_rows, text_length[y])
    dcq = extra
    layer_home.wait()

    def pair_lanes(buf, j, base):
        return lambda lo, hi: buf[lo:hi, lanes(j + base * pairs, 128)]

    def cross_pair(j):
        for at, k in ((0, 10), (2, 11), (3, 12), (5, 13), (7, 14)):

            @pl.when(j == at)
            def _(k=k):
                if k % 2 == 0:
                    produce(k, plain(h3), *halves(q_buf, (k - 10) // 2))
                else:
                    stage(k)

        def put_dq(sl, value):
            dcq[sl, lanes(j, 128)] = value
            vg[C_QBIAS : C_QBIAS + 1, lanes(j, 128)] += jnp.sum(
                value.astype(jnp.float32), axis=0, keepdims=True
            )

        def put_dk(value):
            dckv[:, lanes(j, 128)] = value

        def put_dv(value):
            dckv[:, lanes(j + pairs, 128)] = value
            vg[C_VBIAS : C_VBIAS + 1, lanes(j, 128)] = jnp.sum(
                value.astype(jnp.float32), axis=0, keepdims=True
            )

        attend_back_pair(
            False, rows, text_rows, BACK_QUERIES, pair_lanes(p, j, 0), pair_lanes(ckv, j, 0),
            pair_lanes(ckv, j, 1), pair_lanes(p, j, 1), pair_lanes(p, j, 2), lse2.at[j], bias,
            put_dq, put_dk, put_dv, ka, va,
        )

    looped(pairs, cross_pair)
    got_qkv = fetch(i_qkv, p.at[:, pl.ds(0, 3 * width)])
    stage(15)
    ready(9)
    text_value = nt(dckv[:, :width], weight(9))
    finished(9)
    ready(10)
    text_value = text_value + nt(dckv[:, width:], weight(10))
    finished(10)
    tgrad[...] = text_value.astype(jnp.bfloat16).reshape(tgrad.shape)
    text_away, text_home = swap_out(1, lambda k: tgrad.at[k], o_text, tgrad.at[y])
    text_away().start()
    text_home().start()
    produce(16, plain(h3), *halves(q_buf, 3))
    ready(11)

    def dh2_block(at):
        dh[at, :] = nt(dcq[at, :], weight(11))

    by_blocks(dh2_block)
    finished(11)
    stage(17)
    got_o1 = fetch(i_o1, q_buf.at[:, pl.ds(3 * width, width)])
    got_tokens = fetch(i_tokens, h3)
    norm_step(i_after_self, C_GAIN, C_SHIFT, A_OBIAS)
    got_h2.wait()
    produce(18, column(p, 3), *halves(dcq, 0))
    got_h1 = fetch(i_h1, p.at[:, pl.ds(3 * width, width)])

    ready(12)
    do1 = extra

    def do1_block(at):
        do1[at, :] = nt(low[at, :], weight(12)).astype(jnp.bfloat16)

    by_blocks(do1_block)
    finished(12)
    stage(19)
    got_text.wait()

    def text_lanes(some_lanes):
        return text[:, :, some_lanes].reshape(text_rows, some_lanes.size)

    got_qkv.wait()
    got_o1.wait()

    def self_pair(j):
        def put_dq(sl, value):
            q_buf[sl, lanes(j, 128)] = value
            vg[A_QBIAS : A_QBIAS + 1, lanes(j, 128)] += jnp.sum(
                value.astype(jnp.float32), axis=0, keepdims=True
            )

        def put_dk(value):
            q_buf[:, lanes(j + pairs, 128)] = value

        def put_dv(value):
            q_buf[:, lanes(j + 2 * pairs, 128)] = value
            vg[A_VBIAS : A_VBIAS + 1, lanes(j, 128)] = jnp.sum(
                value.astype(jnp.float32), axis=0, keepdims=True
            )

        attend_back_pair(
            True, rows, rows, BACK_QUERIES, pair_lanes(p, j, 0), pair_lanes(p, j, 1), pair_lanes(p, j, 2),
            pair_lanes(q_buf, j, 3), lambda lo, hi: do1[lo:hi, lanes(j, 128)], lse1.at[j], None,
            put_dq, put_dk, put_dv, ka, va,
        )

    half_pairs = pairs // 2

    def first_half(j):
        for k in range(4):

            @pl.when(j == k)
            def _(k=k):
                if k % 2 == 0:
                    produce(20 + k, text_lanes, *halves(dckv, k // 2))
                else:
                    stage(20 + k)

        self_pair(j)

    looped(half_pairs, first_half)
    got_h1.wait()

    def second_half(j):
        @pl.when(j == 0)
        def _():
            produce(24, column(q_buf, 3), *halves(low, 0))

        @pl.when(j == 1)
        def _():
            stage(25)

        @pl.when(j == 2)
        def _():
            produce(26, column(p, 3), part(q_buf, 0), part(q_buf, 2))
            stage(27)

        @pl.when(j == 3)
        def _():
            produce(28, column(p, 3), part(q_buf, 4))

        self_pair(j + half_pairs)

    looped(half_pairs, second_half)

    grads = low

    def rows_of(half, b):
        return pl.ds(pl.multiple_of(half * part_rows + b * BLOCK, BLOCK), BLOCK)

    def dh1_block(half, c, first=None):
        fresh = c == 0 if first is None else first

        def block(b):
            at = block_rows(half, part_rows)
            value = nt(q_buf[at, c * width : (c + 1) * width], weight(13 + c))
            dh[at, :] = value if fresh else dh[at, :] + value

        return block

    def last_block(half):
        def block(b):
            at = rows_of(half, b)
            unit, scale = center_and_scale(h3[at, :].astype(jnp.float32))
            pulled = dh[at, :]
            add_row(A_GAIN, pulled * unit)
            add_row(A_SHIFT, pulled)
            total = resid[at, :] + norm_pull(unit, scale, pulled * row(A_GAIN))
            grads[at, :] = total.astype(jnp.bfloat16)

        return block

    token_pieces = 16
    token_size = part_rows // token_pieces

    def tokens_away(i):
        at = pl.multiple_of((1 - y) * part_rows + i * token_size, token_size)
        return remote(
            grads.at[pl.ds(at, token_size), :],
            o_tokens.at[y, pl.ds(i * token_size, token_size)],
            (swap_send, swap_receive), 2, i, place.across_y(),
        )

    tokens_sent = []

    def send_tokens(some):
        for i in range(len(tokens_sent), min(token_pieces, len(tokens_sent) + some)):
            tokens_away(i).start()
            tokens_sent.append(i)

    tokens_home = pltpu.make_async_copy(
        grads.at[block_rows(y, part_rows), :], o_tokens.at[y], swap_local.at[2]
    )
    count = part_rows // BLOCK
    make(29, column(p, 3), part(q_buf, 1), part(q_buf, 3))
    stage(29)
    got_tokens.wait()
    ready(13)
    dh1_block(1 - y, 0)(0)
    load(15).start()
    ready(14)
    dh1_block(1 - y, 1)(0)
    stage(30)
    ready(15)
    dh1_block(1 - y, 2)(0)
    looped(count, last_block(1 - y))
    send_tokens(3)
    make(31, column(p, 3), part(q_buf, 5))
    stage(31)
    send_tokens(2)
    dh1_block(y, 2, True)(0)
    load(13).start()
    dh1_block(y, 1)(0)
    stage(32)
    send_tokens(3)
    ready(13)
    dh1_block(y, 0, False)(0)
    looped(count, last_block(y))
    tokens_home.start()

    @pl.loop(0, depth)
    def _(k):
        some = gather_vectors(vg[...], k * 8, 8)
        small_bufs[0][0, k] = some.reshape(small_bufs[0].shape[2:])

    small_phases[0]()
    for k in range(33, len(stages)):
        stage(k)
        send_tokens(2)
    values = s_up[...]
    s_up[...] = quarter_columns(values, width, back=True)
    for copy in (
        *[layer_away(i) for i in range(layer_count)], text_away(), text_home(), *[tokens_away(i) for i in range(token_pieces)], tokens_home,
    ):
        copy.wait()


def backward(depth, number, wholes, kept, text_length):
    (
        token_seq, text_seq, normed_one, joined, self_mixed, after_self, normed_two, cross_queries,
        cross_kv, cross_mixed, after_cross, normed_three, active, slope, grad_after_ffn,
        grad_branch, layer_out, vec, lse1, lse2, zgrads,
    ) = kept
    rows, width = self_mixed.shape
    text_rows = cross_kv.shape[0]
    hidden = active.shape[1]
    share = width // (depth * 8)
    half = (2, rows // 2, width)
    low, full = jnp.bfloat16, jnp.float32
    operands = [
        token_seq.reshape(rows, width), text_seq, normed_one, joined, self_mixed, after_self,
        normed_two, cross_queries, cross_kv, cross_mixed, after_cross, normed_three, active, slope,
        grad_after_ffn, grad_branch, layer_out.reshape(half),
    ]

    def vmem(*dims, kind=low):
        return pltpu.VMEM(dims, kind)

    results_low = [jax.ShapeDtypeStruct(s, low) for s in (half, half, text_seq.shape)]
    columns = [w.shape[-1] for w in wholes[:6]]
    sums = [jax.ShapeDtypeStruct((share, c), full) for c in columns]
    sums += [jax.ShapeDtypeStruct((4 * share, width), full), jax.ShapeDtypeStruct((share, 128), full)]
    scratch = [
        vmem(rows, hidden), vmem(rows, hidden), vmem(rows, width, kind=full),
        vmem(rows, width, kind=full), vmem(rows, width), vmem(rows, width), vmem(rows, width),
        vmem(text_rows, 2 * width), vmem(text_rows, 2 * width), vmem(*text_seq.shape),
        vmem(*text_seq.shape), vmem(2, NORM_BLOCK, width, kind=full),
        vmem(32, width, kind=full), vmem(rows, 128, kind=full), vmem(rows, 128, kind=full),
        vmem(WEIGHT_RING, depth, 2, 2, 2, share, width),
    ]
    scratch += ring_scratch(depth, BACK_STRIDE, share, width // 2, low)
    scratch += ring_scratch(depth, 0, share, 128, full)
    pieces = 2 * (sum(c // width for c in columns) + 4)
    scratch += copy_sems(pieces, depth)[:2] + copy_sems(1, depth)[:2]
    scratch += [
        pltpu.SemaphoreType.DMA((3, 16)), pltpu.SemaphoreType.DMA((3, 16)),
        pltpu.SemaphoreType.DMA((5,)), pltpu.SemaphoreType.DMA((16,)),
        pltpu.SemaphoreType.DMA((32,)),
    ]
    in_vmem = pl.BlockSpec(memory_space=pltpu.VMEM)
    results = pl.pallas_call(
        functools.partial(backward_kernel, depth),
        out_shape=results_low + sums,
        in_specs=[ANYWHERE] * (len(wholes) + len(operands))
        + [in_vmem] * 4
        + [pl.BlockSpec(memory_space=pltpu.SMEM)],
        out_specs=[ANYWHERE] * 3 + [in_vmem] * len(sums),
        scratch_shapes=scratch,
        compiler_params=pltpu.CompilerParams(
            collective_id=number, has_side_effects=True, vmem_limit_bytes=BACK_VMEM_LIMIT
        ),
        name="backward",
    )(*wholes, *operands, vec, lse1, lse2, zgrads, text_length)
    return list(results[:3]), list(results[3:])


BACK_VMEM_LIMIT = 63 * 2**20


def pack_vectors(vectors, wide):
    packed = jnp.concatenate([jnp.stack(vectors), wide.reshape(4, -1)])
    return jnp.pad(packed, ((0, 32 - packed.shape[0]), (0, 128 - packed.shape[1])))


def settle_kernel(count, *refs):
    ins, outs, held = refs[:count], refs[count : 2 * count], refs[2 * count : 3 * count]
    arrive, leave = refs[3 * count :]
    coming = [pltpu.make_async_copy(a, b, arrive.at[k]) for k, (a, b) in enumerate(zip(ins, held))]
    going = [pltpu.make_async_copy(a, b, leave.at[k]) for k, (a, b) in enumerate(zip(held, outs))]
    for copy in coming:
        copy.start()
    for come, go in zip(coming, going):
        come.wait()
        go.start()
    for copy in going:
        copy.wait()


def settle(arrays):
    count = len(arrays)
    return pl.pallas_call(
        functools.partial(settle_kernel, count),
        out_shape=[jax.ShapeDtypeStruct(a.shape, a.dtype) for a in arrays],
        in_specs=[ANYWHERE] * count,
        out_specs=[ANYWHERE] * count,
        scratch_shapes=[pltpu.VMEM(a.shape, a.dtype) for a in arrays]
        + [pltpu.SemaphoreType.DMA((count,))] * 2,
        compiler_params=pltpu.CompilerParams(vmem_limit_bytes=VMEM_LIMIT),
        name="settle",
    )(*arrays)


def paired_layer(
    depth,
    tokens,
    text_states,
    unit_length,
    text_length,
    cotangent,
    attn_gain,
    attn_shift,
    attn_inputs,
    attn_qbias,
    attn_vbias,
    attn_output,
    attn_obias,
    cross_gain,
    cross_shift,
    cross_query,
    cross_qbias,
    cross_keyval,
    cross_vbias,
    cross_output,
    cross_obias,
    ffn_gain,
    ffn_shift,
    ffn_up,
    ffn_upbias,
    ffn_down,
    ffn_downbias,
    final_gain,
    final_shift,
):
    share = attn_gain.shape[0]
    packed = pack_vectors(
        [
            attn_gain, attn_shift, attn_qbias, attn_vbias, attn_obias, cross_gain, cross_shift,
            cross_qbias, cross_vbias, cross_obias, ffn_gain, ffn_shift, ffn_downbias, final_gain,
            final_shift,
        ],
        ffn_upbias,
    )
    wholes, kept = forward(
        depth, 0, tokens, text_states, cotangent, unit_length, text_length,
        [
            packed, attn_inputs, attn_output, cross_query, cross_keyval, cross_output, ffn_up,
            ffn_down,
        ],
    )
    (layer_out, tokens_grad, text_grad), sums = backward(depth, 1, wholes[1:], kept, text_length)
    *results, s_small = settle([layer_out, tokens_grad, text_grad, *sums])
    layer_out, tokens_grad, text_grad, s_in, s_out, s_cq, s_ckv, s_co, s_up, s_down = results
    s_upbias = s_small[VECTOR_COUNT : VECTOR_COUNT + 4, :share].reshape(-1)
    v = [s_small[i, :share] for i in range(VECTOR_COUNT)]
    return (
        layer_out, tokens_grad, text_grad, v[A_GAIN], v[A_SHIFT], s_in, v[A_QBIAS], v[A_VBIAS],
        s_out, v[A_OBIAS], v[C_GAIN], v[C_SHIFT], s_cq, v[C_QBIAS], s_ckv, v[C_VBIAS], s_co,
        v[C_OBIAS], v[F_GAIN], v[F_SHIFT], s_up, s_upbias, s_down, v[F_DOWNBIAS], v[Z_GAIN],
        v[Z_SHIFT],
    )


def solution(mesh):
    in_specs = (
        P("dp", "seq", None),
        P("dp", "seq", None),
        P("dp"),
        P("dp"),
        P("dp", "seq", None),
        P(("dp", "seq")),
        P(("dp", "seq")),
        P(("dp", "seq"), None),
        P(("dp", "seq")),
        P(("dp", "seq")),
        P(("dp", "seq"), None),
        P(("dp", "seq")),
        P(("dp", "seq")),
        P(("dp", "seq")),
        P(("dp", "seq"), None),
        P(("dp", "seq")),
        P(("dp", "seq"), None),
        P(("dp", "seq")),
        P(("dp", "seq"), None),
        P(("dp", "seq")),
        P(("dp", "seq")),
        P(("dp", "seq")),
        P(("dp", "seq"), None),
        P(("dp", "seq")),
        P(("dp", "seq"), None),
        P(("dp", "seq")),
        P(("dp", "seq")),
        P(("dp", "seq")),
    )
    out_specs = (
        P("dp", "seq", None),
        P("dp", "seq", None),
        P("dp", "seq", None),
        P(("dp", "seq")),
        P(("dp", "seq")),
        P(("dp", "seq"), None),
        P(("dp", "seq")),
        P(("dp", "seq")),
        P(("dp", "seq"), None),
        P(("dp", "seq")),
        P(("dp", "seq")),
        P(("dp", "seq")),
        P(("dp", "seq"), None),
        P(("dp", "seq")),
        P(("dp", "seq"), None),
        P(("dp", "seq")),
        P(("dp", "seq"), None),
        P(("dp", "seq")),
        P(("dp", "seq")),
        P(("dp", "seq")),
        P(("dp", "seq"), None),
        P(("dp", "seq")),
        P(("dp", "seq"), None),
        P(("dp", "seq")),
        P(("dp", "seq")),
        P(("dp", "seq")),
    )
    groups, seq_parts = mesh.shape["dp"], mesh.shape["seq"]

    def layer(*arguments):
        shard = arguments[5].shape[0]
        parts = arguments[0].shape[0]
        if seq_parts == 2 and parts == 2 and groups % 4 == 0 and shard % 32 == 0:
            return paired_layer(groups // 4, *arguments)
        return on_device(*arguments)

    return jax.shard_map(
        layer, mesh=mesh, in_specs=in_specs, out_specs=out_specs, check_vma=False
    )
```
